32 devices in a mesh: seq: 8 (over z, x), head: 4 (over y, core).
Axes of the slice: x: 2, y: 2, z: 4, core: 2. Of those that a mesh axis runs over, the one named last changes fastest.
Arguments:
- queries: bfloat16 [2048, 16, 128], P(('seq', 'head')), may hold values from -6 to 6
- key_vectors: bfloat16 [2048, 16, 128], P(('seq', 'head')), may hold values from -6 to 6
- value_vectors: bfloat16 [2048, 32, 128], P(('seq', 'head')), may hold values from -6 to 6
- output_gate: bfloat16 [2048, 32, 128], P(('seq', 'head')), may hold values from -6 to 6
- write_strength: bfloat16 [2048, 32], P(('seq', 'head'))
- norm_gain: bfloat16 [128], replicated, may hold values from 0.099609375 to 1.8984375
- output_weight: bfloat16 [4096, 2048], P('head'), may hold values from -0.09375 to 0.09375
Outputs:
- projected: bfloat16 [2048, 2048], P(('seq', 'head'))
The draws below stay inside these ranges and needn't reach their ends.
All inputs are finite; a program needn't handle non-finite values.
Results may differ from the reference program's by a relative error of at most 0.017.
Values may be sent and summed in bfloat16 or wider, within the bound.
No kernel may reach another device: no remote copies, remote signals or barrier semaphores. Data moves between devices by JAX's collectives and lax.ppermute only.
A program may use at most 128 MiB of HBM per device.

```python
import jax
import jax.numpy as jnp
from jax import lax

MODEL_DIM = 2048
HK = 16
HV = 32
DK = 128
SPAN = 64
TOKENS = 2048
N_HEAD = 4


def draw_write_strength(key, part):
    pick_key, slow_key, fast_key, rough_key = jax.random.split(key, 4)
    slow_share = 0.5
    slow_heads = jax.random.uniform(pick_key, (HV,)) < slow_share
    slow_rate = jax.random.uniform(slow_key, (HV,), minval=0.25, maxval=2.0) * (DK / TOKENS)
    fast_rate = jnp.exp(jax.random.uniform(fast_key, (HV,), minval=jnp.log(0.1), maxval=jnp.log(0.9)))
    base_rate = jnp.where(slow_heads, slow_rate, fast_rate)
    roughness = jax.random.uniform(rough_key, (TOKENS, HV), minval=0.5, maxval=1.5)
    return jnp.minimum(base_rate[None, :] * roughness, 1.0).astype(jnp.bfloat16)


def block_scale(stream_key, extent, shards, smallest, high):
    factor_of = 1.0
    for position, parts in shards:
        steps = jax.random.uniform(jax.random.fold_in(jax.random.fold_in(stream_key, 6), position), (parts,), jnp.float32, smallest / len(shards), high / len(shards))
        factor_of = factor_of * jnp.repeat(jnp.exp(steps), extent[position] // parts).reshape((-1,) + (1,) * (len(extent) - 1 - position))
    return factor_of


def normal_values(own_key, extent, spread, most, cuts=(), held_as=jnp.bfloat16):
    factor_of = block_scale(own_key, extent, cuts, -0.22, 0.18) if cuts else 1.0
    drawn = jax.random.normal(own_key, extent, jnp.float32) * spread * factor_of
    return jnp.minimum(jnp.maximum(drawn, -most), most).astype(held_as)


def setup_inputs(seed: int = 0) -> dict:
    seeds = jax.random.split(jax.random.key(seed), 8)
    return {
        "queries": normal_values(seeds[0], (TOKENS, HK, DK), 1.0, 6.0, ((0, 32),)),
        "key_vectors": normal_values(seeds[1], (TOKENS, HK, DK), 1.0, 6.0, ((0, 32),)),
        "value_vectors": normal_values(seeds[2], (TOKENS, HV, DK), 1.0, 6.0, ((0, 32),)),
        "output_gate": normal_values(seeds[3], (TOKENS, HV, DK), 1.0, 6.0, ((0, 32),)),
        "write_strength": draw_write_strength(jax.random.fold_in(seeds[7], 71), 0),
        "norm_gain": jnp.clip(1.0 + 0.18 * jax.random.normal(seeds[5], (DK,), jnp.float32), 0.099609375, 1.8984375).astype(jnp.bfloat16),
        "output_weight": normal_values(seeds[6], (HV * DK, MODEL_DIM), (HV * DK) ** -0.5, 0.09375, ((0, 4),)),
    }


precise = lax.Precision.HIGHEST
epsilon = 1e-06

def unit_rows(values_in):
    return values_in * lax.rsqrt(lax.optimization_barrier(jnp.sum(values_in * values_in, -1, keepdims=True)) + epsilon)

def span_factors(key_blocks, value_blocks, strength_blocks):
    key_gram = jnp.einsum('...cd,...md->...cm', key_blocks, key_blocks, precision=precise)
    below_diagonal = jnp.tril(key_gram * strength_blocks[..., :, None], -1)
    block_size = key_blocks.shape[-2]
    system = below_diagonal + jnp.eye(block_size, dtype=key_blocks.dtype)
    right_sides = jnp.concatenate([key_blocks * strength_blocks[..., None], value_blocks * strength_blocks[..., None]], -1)
    solved = jax.scipy.linalg.solve_triangular(system, right_sides, lower=True, unit_diagonal=True)
    head_width = key_blocks.shape[-1]
    return (solved[..., :head_width], solved[..., head_width:])

def span_step(carried, pieces):
    query_c, key_c, w_c, u_c = pieces
    scores = jnp.tril(jnp.einsum('...cd,...md->...cm', query_c, key_c, precision=precise))
    corrected = u_c - jnp.einsum('...cd,...de->...ce', w_c, carried, precision=precise)
    outputs = jnp.einsum('...cd,...de->...ce', query_c, carried, precision=precise) + jnp.einsum('...cm,...me->...ce', scores, corrected, precision=precise)
    carried = carried + jnp.einsum('...cd,...ce->...de', key_c, corrected, precision=precise)
    return (carried, outputs)

def reference(queries, key_vectors, value_vectors, output_gate, write_strength, norm_gain, output_weight):
    head_ratio = HV // HK
    query_unit = unit_rows(queries.astype(jnp.float32)) * DK ** (-0.5)
    key_unit = unit_rows(key_vectors.astype(jnp.float32))
    span_count = TOKENS // SPAN

    def one_head(head_index):
        key_index = head_index // head_ratio
        query_rows = lax.dynamic_index_in_dim(query_unit, key_index, 1, False)
        key_rows = lax.dynamic_index_in_dim(key_unit, key_index, 1, False)
        value_rows = lax.dynamic_index_in_dim(value_vectors, head_index, 1, False).astype(jnp.float32)
        strength_rows = lax.dynamic_index_in_dim(write_strength, head_index, 1, False).astype(jnp.float32)
        query_blocks = query_rows.reshape(span_count, SPAN, DK)
        key_blocks = key_rows.reshape(span_count, SPAN, DK)
        value_blocks = value_rows.reshape(span_count, SPAN, DK)
        strength_blocks = strength_rows.reshape(span_count, SPAN)
        w_blocks, u_blocks = span_factors(key_blocks, value_blocks, strength_blocks)
        initial = jnp.zeros((DK, DK), jnp.float32)
        final_state, outputs = lax.scan(span_step, initial, (query_blocks, key_blocks, w_blocks, u_blocks))
        return outputs.reshape(TOKENS, DK)
    core = jnp.transpose(lax.map(one_head, jnp.arange(HV, dtype=jnp.int32)), (1, 0, 2))
    mean_square = lax.optimization_barrier(jnp.mean(core * core, -1, keepdims=True))
    normed = core * lax.rsqrt(mean_square + epsilon) * norm_gain.astype(jnp.float32) * jax.nn.silu(output_gate.astype(jnp.float32))
    gated = normed.astype(jnp.bfloat16).reshape(TOKENS, HV * DK)
    group_rows = HV * DK // N_HEAD
    running = jnp.zeros((TOKENS, MODEL_DIM), jnp.float32)
    for group in range(N_HEAD):
        group_terms = jnp.dot(gated[:, group * group_rows:(group + 1) * group_rows].astype(jnp.float32), output_weight[group * group_rows:(group + 1) * group_rows].astype(jnp.float32), preferred_element_type=jnp.float32)
        running = running + lax.optimization_barrier(group_terms.astype(jnp.bfloat16)).astype(jnp.float32)
    return running.astype(jnp.bfloat16)
```

```python
import functools

import jax
import jax.numpy as jnp
from jax import lax
from jax.experimental import pallas as pl
from jax.experimental.pallas import tpu as pltpu
from jax.sharding import Mesh, PartitionSpec as P

SPAN = 128
EPSILON = 1e-06
F32 = jnp.float32
BF16 = jnp.bfloat16
ROW_TILE = 16
VMEM = pl.BlockSpec(memory_space=pltpu.VMEM)


def dot(left, right):
    return jnp.dot(left, right, preferred_element_type=F32)


def dot_nt(left, right):
    return lax.dot_general(left, right, (((1,), (1,)), ((), ())), preferred_element_type=F32)


def params(megabytes=48):
    return pltpu.CompilerParams(vmem_limit_bytes=megabytes * 2**20)


def pack_kernel(sub, q_ref, k_ref, v_ref, b_ref, out_ref):
    tokens, key_heads, width = q_ref.shape
    value_heads = v_ref.shape[1]
    ratio = value_heads // key_heads
    n_head = key_heads // sub
    q_t = jnp.transpose(q_ref[...], (1, 0, 2))
    k_t = jnp.transpose(k_ref[...], (1, 0, 2))
    v_t = jnp.transpose(v_ref[...], (1, 0, 2))
    strength = jnp.transpose(b_ref[...].astype(F32), (1, 0))
    strength = jnp.concatenate([strength] * (width // tokens), axis=1)
    strength = jnp.concatenate([strength, jnp.zeros((ROW_TILE, width), F32)], axis=0)
    for peer in range(key_heads):
        head = (peer % n_head) * sub + peer // n_head
        out_ref[peer, 0:tokens] = q_t[head]
        out_ref[peer, tokens : 2 * tokens] = k_t[head]
        for r in range(ratio):
            out_ref[peer, (2 + r) * tokens : (3 + r) * tokens] = v_t[head * ratio + r]
        out_ref[peer, (2 + ratio) * tokens :] = strength[
            head * ratio : head * ratio + ROW_TILE
        ].astype(BF16)


def block_rows(got_ref, block, per, tokens, part):
    rows = got_ref[pl.ds(block * per, per), part * tokens : (part + 1) * tokens]
    return rows.reshape(per * tokens, rows.shape[-1])


def block_inverse(below):
    size = below[0].shape[0]
    rows = lax.broadcasted_iota(jnp.int32, (size, size), 0)
    cols = lax.broadcasted_iota(jnp.int32, (size, size), 1)
    zero = jnp.zeros((size, size), F32)
    step = 1
    solved = None
    while step < size:
        joins = (rows // (2 * step) == cols // (2 * step)) & (rows // step > cols // step)
        parts = [jnp.where(joins, matrix, zero) for matrix in below]
        if step == 1:
            solved = [
                jnp.where(rows == cols, jnp.ones_like(zero), -part).astype(BF16) for part in parts
            ]
        else:
            inner = [dot(part.astype(BF16), now).astype(BF16) for part, now in zip(parts, solved)]
            solved = [now - dot(now, mid).astype(BF16) for now, mid in zip(solved, inner)]
        step *= 2
    return solved


def factor_kernel(
    tokens, ratio, group, got_ref, state_ref, scores_ref, w_ref, u_ref, trans_ref, prefix_ref, unit_ref, add_ref
):
    width = got_ref.shape[-1]
    per = SPAN // tokens
    blocks = got_ref.shape[0] // per
    rows = lax.broadcasted_iota(jnp.int32, (SPAN, SPAN), 0)
    cols = lax.broadcasted_iota(jnp.int32, (SPAN, SPAN), 1)
    lane = lax.broadcasted_iota(jnp.int32, (1, SPAN), 1)

    def factors(outer, unused):
        below, held = [], []
        for inner in range(group):
            block = outer * group + inner
            query = block_rows(got_ref, block, per, tokens, 0)
            key = block_rows(got_ref, block, per, tokens, 1)
            gram = dot_nt(key, key)
            scores = dot_nt(query, key)
            scores_ref[block] = jnp.where(rows >= cols, scores, 0.0).astype(BF16)
            squares = jnp.where(rows == cols, gram, 0.0)
            key_row = lax.rsqrt(jnp.sum(squares, 0, keepdims=True) + EPSILON)
            key_col = lax.rsqrt(jnp.sum(squares, 1, keepdims=True) + EPSILON)
            query_f = query.astype(F32)
            query_col = lax.rsqrt(jnp.sum(query_f * query_f, 1, keepdims=True) + EPSILON) * width ** (-0.5)
            unit_ref[block] = jnp.broadcast_to(query_col, (SPAN, width))
            lower = jnp.where(rows > cols, gram, 0.0) * key_row
            for r in range(ratio):
                strength = jnp.zeros((1, SPAN), F32)
                for place in range(per):
                    first = (2 + ratio) * tokens
                    piece = got_ref[block * per + place, first : first + ROW_TILE].astype(F32)[r : r + 1]
                    strength = jnp.where(lane // tokens == place, piece, strength)
                scaled = strength * key_row
                scaled_col = jnp.sum(jnp.where(rows == cols, scaled, 0.0), 1, keepdims=True)
                below.append(lower * scaled_col)
                held.append((block, r, key, key_col, key_row, strength))
        solved = block_inverse(below)
        for now, (block, r, key, key_col, key_row, strength) in zip(solved, held):
            value = block_rows(got_ref, block, per, tokens, 2 + r)
            weighted = now.astype(F32) * key_col * strength
            u_now = dot(weighted.astype(BF16), value)
            w_now = dot((weighted * key_row).astype(BF16), key).astype(BF16)
            both = dot(key.T, jnp.concatenate([w_now, u_now.astype(BF16)], axis=1))
            w_ref[block, r] = w_now
            u_ref[block, r] = u_now
            trans_ref[block, r] = both[:, :width].astype(BF16)
            add_ref[block, r] = both[:, width:]
        return unused

    lax.fori_loop(0, blocks // group, factors, 0)

    states = [jnp.zeros((width, width), F32) for r in range(ratio)]
    for block in range(blocks):
        for r in range(ratio):
            held = states[r].astype(BF16)
            prefix_ref[block, r] = held
            if block == 0:
                states[r] = add_ref[block, r]
            else:
                states[r] = states[r] + add_ref[block, r] - dot(trans_ref[block, r], held)
    for r in range(ratio):
        state_ref[r] = states[r].astype(state_ref.dtype)


def spread_kernel(
    tokens, ratio, got_ref, scores_ref, w_ref, u_ref, trans_ref, prefix_ref, unit_ref, local_ref, reach_ref, total_ref
):
    width = got_ref.shape[-1]
    per = SPAN // tokens
    blocks = got_ref.shape[0] // per
    rows = lax.broadcasted_iota(jnp.int32, (width, width), 0)
    cols = lax.broadcasted_iota(jnp.int32, (width, width), 1)
    identity = jnp.where(rows == cols, 1.0, 0.0).astype(F32)
    carried = [identity for r in range(ratio)]
    for block in range(blocks):
        query = block_rows(got_ref, block, per, tokens, 0)
        for r in range(ratio):
            held = carried[r].astype(BF16)
            if block == 0:
                carried[r] = identity - trans_ref[block, r].astype(F32)
            else:
                carried[r] = carried[r] - dot(trans_ref[block, r], held)
            starts = jnp.concatenate([prefix_ref[block, r], held], axis=1)
            passed = dot(w_ref[block, r], starts)
            corrected = jnp.concatenate([u_ref[block, r] - passed[:, :width], -passed[:, width:]], axis=1)
            left = jnp.concatenate([query, scores_ref[block]], axis=1)
            right = jnp.concatenate([starts, corrected.astype(BF16)], axis=0)
            out = dot(left, right)
            local_ref[r, block] = out[:, :width] * unit_ref[block]
            reach_ref[r, block] = (out[:, width:] * unit_ref[block]).astype(BF16)
    for r in range(ratio):
        total_ref[r] = carried[r]


def join_kernel(state_ref, local_ref, reach_ref, out_ref):
    ratio, blocks, span, width = local_ref.shape
    for r in range(ratio):
        held = state_ref[r].astype(BF16)
        for block in range(blocks):
            core = local_ref[r, block] + dot(reach_ref[r, block], held)
            mean_square = jnp.mean(core * core, 1, keepdims=True)
            out_ref[block, r] = (core * lax.rsqrt(mean_square + EPSILON)).astype(BF16)


def project_kernel(core_ref, gate_ref, gain_ref, weight_ref, out_ref, gated_ref):
    heads, pieces, span, width = core_ref.shape
    sources, unused, tokens, unused = gate_ref.shape

    @pl.when(pl.program_id(0) == 0)
    def _():
        gain = gain_ref[...].astype(F32)
        for head in range(heads):
            core = core_ref[head].reshape(pieces * span, width).astype(F32)
            gate = gate_ref[:, head].reshape(sources * tokens, width).astype(F32)
            gated = core * gain * (gate / (1.0 + jnp.exp(-gate)))
            gated_ref[:, head * width : (head + 1) * width] = gated.astype(BF16)

    out_ref[...] = dot(gated_ref[...], weight_ref[...]).astype(BF16)


def per_device(
    outer, sub, n_head, queries, key_vectors, value_vectors, output_gate, write_strength, norm_gain, output_weight
):
    tokens, key_heads, width = queries.shape
    value_heads = value_vectors.shape[1]
    ratio = value_heads // key_heads
    sources = sub * n_head
    shard = tokens * sources
    blocks = shard // SPAN
    shard_tokens = tokens * n_head
    packed_rows = (2 + ratio) * tokens + ROW_TILE
    shape = jax.ShapeDtypeStruct

    with jax.named_scope("pack"):
        packed = pl.pallas_call(
            functools.partial(pack_kernel, sub),
            out_shape=shape((sources, packed_rows, width), BF16),
            in_specs=[VMEM] * 4,
            out_specs=VMEM,
            compiler_params=params(),
        )(queries, key_vectors, value_vectors, write_strength)
    got = lax.all_to_all(packed, ("sub", "head"), split_axis=0, concat_axis=0, tiled=True)
    gate_t = jnp.transpose(output_gate, (1, 0, 2)).reshape(n_head, value_heads // n_head, tokens, width)
    gate = lax.all_to_all(gate_t, "head", split_axis=0, concat_axis=0, tiled=True)

    state_type = BF16 if outer == 2 else F32
    square = (blocks, ratio, width, width)
    with jax.named_scope("factors"):
        state, scores, w, u, trans, prefix, unit = pl.pallas_call(
            functools.partial(factor_kernel, tokens, ratio, 2),
            out_shape=[
                shape((ratio, width, width), state_type),
                shape((blocks, SPAN, SPAN), BF16),
                shape((blocks, ratio, SPAN, width), BF16),
                shape((blocks, ratio, SPAN, width), F32),
                shape(square, BF16),
                shape(square, BF16),
                shape((blocks, SPAN, width), F32),
            ],
            in_specs=[VMEM],
            out_specs=[VMEM] * 7,
            scratch_shapes=[pltpu.VMEM(square, F32)],
            compiler_params=params(),
        )(got)

    onward = [(place, place + 1) for place in range(outer - 1)]
    incoming = lax.ppermute(state, "outer", onward)
    with jax.named_scope("spread"):
        local, reach, total = pl.pallas_call(
            functools.partial(spread_kernel, tokens, ratio),
            out_shape=[
                shape((ratio, blocks, SPAN, width), F32),
                shape((ratio, blocks, SPAN, width), BF16),
                shape((ratio, width, width), F32),
            ],
            in_specs=[VMEM] * 7,
            out_specs=[VMEM] * 3,
            compiler_params=params(),
            cost_estimate=pl.CostEstimate(flops=10**9, bytes_accessed=8 * 10**6, transcendentals=0),
        )(got, scores, w, u, trans, prefix, unit)
    for hop in range(outer - 2):
        passed = jnp.einsum("hde,hef->hdf", total, incoming, precision=lax.Precision.HIGHEST)
        incoming = lax.ppermute(state + passed, "outer", onward)

    with jax.named_scope("join"):
        normed = pl.pallas_call(
            join_kernel,
            out_shape=shape((blocks, ratio, SPAN, width), BF16),
            in_specs=[VMEM] * 3,
            out_specs=VMEM,
            compiler_params=params(),
        )(incoming, local, reach)
    pieces = shard_tokens // SPAN
    normed = jnp.transpose(normed.reshape(sub, pieces, ratio, SPAN, width), (0, 2, 1, 3, 4))
    mine = lax.all_to_all(normed, "sub", split_axis=0, concat_axis=0, tiled=True)
    heads = sub * ratio
    mine = mine.reshape(heads, pieces, SPAN, width)

    columns = output_weight.shape[1]
    tile = 512
    with jax.named_scope("project"):
        partial = pl.pallas_call(
            project_kernel,
            grid=(columns // tile,),
            out_shape=shape((shard_tokens, columns), BF16),
            in_specs=[
                pl.BlockSpec((heads, pieces, SPAN, width), lambda i: (0, 0, 0, 0)),
                pl.BlockSpec((n_head, heads, tokens, width), lambda i: (0, 0, 0, 0)),
                pl.BlockSpec((1, width), lambda i: (0, 0)),
                pl.BlockSpec((heads * width, tile), lambda i: (0, i)),
            ],
            out_specs=pl.BlockSpec((shard_tokens, tile), lambda i: (0, i)),
            scratch_shapes=[pltpu.VMEM((shard_tokens, heads * width), BF16)],
            compiler_params=params(),
        )(mine, gate, norm_gain.reshape(1, width), output_weight)
    shares = lax.all_to_all(
        partial.reshape(n_head, tokens, columns), "head", split_axis=0, concat_axis=0, tiled=True
    )
    return jnp.sum(shares.astype(F32), 0).astype(BF16)


def solution(mesh):
    n_seq, n_head = mesh.shape["seq"], mesh.shape["head"]

    def run(queries, key_vectors, value_vectors, output_gate, write_strength, norm_gain, output_weight):
        sub = queries.shape[1] // n_head
        outer = n_seq // sub
        split = Mesh(mesh.devices.reshape(outer, sub, n_head), ("outer", "sub", "head"))
        every = ("outer", "sub", "head")
        placed = (
            P(every, None, None),
            P(every, None, None),
            P(every, None, None),
            P(every, None, None),
            P(every, None),
            P(),
            P("head", None),
        )
        return jax.shard_map(
            functools.partial(per_device, outer, sub, n_head),
            mesh=split,
            in_specs=placed,
            out_specs=P(every, None),
            check_vma=False,
        )(queries, key_vectors, value_vectors, output_gate, write_strength, norm_gain, output_weight)

    return run
```

```python
import functools

import jax
import jax.numpy as jnp
from jax import lax
from jax.experimental import pallas as pl
from jax.experimental.pallas import tpu as pltpu
from jax.sharding import Mesh, PartitionSpec as P

SPAN = 128
EPSILON = 1e-06
F32 = jnp.float32
BF16 = jnp.bfloat16
ROW_TILE = 16
VMEM = pl.BlockSpec(memory_space=pltpu.VMEM)
SMEM = pl.BlockSpec(memory_space=pltpu.SMEM)
ANY = pl.BlockSpec(memory_space=pl.ANY)


def dot(left, right):
    return jnp.dot(left, right, preferred_element_type=F32)


def dot_nt(left, right):
    return lax.dot_general(left, right, (((1,), (1,)), ((), ())), preferred_element_type=F32)


def params(megabytes=48):
    return pltpu.CompilerParams(vmem_limit_bytes=megabytes * 2**20)


def turned(ref):
    return jnp.transpose(ref[...], (1, 0, 2))


def pack_write_kernel(sub, k_hbm, v_hbm, b_hbm, out_ref, k_ref, v_ref, b_ref, done):
    tokens, key_heads, width = k_ref.shape
    value_heads = v_ref.shape[1]
    ratio = value_heads // key_heads
    n_head = key_heads // sub
    copies = [
        pltpu.make_async_copy(source, target, done.at[place])
        for place, (source, target) in enumerate(((b_hbm, b_ref), (k_hbm, k_ref), (v_hbm, v_ref)))
    ]
    for copy in copies:
        copy.start()
    copies[0].wait()
    strength = jnp.concatenate([b_ref[...].astype(F32)] * (width // tokens), axis=1)
    strength = jnp.concatenate([strength, jnp.zeros((ROW_TILE, width), F32)], axis=0)
    copies[1].wait()
    k_t = turned(k_ref)
    heads = [(peer % n_head) * sub + peer // n_head for peer in range(key_heads)]
    for peer, head in enumerate(heads):
        out_ref[peer, 0:tokens] = k_t[head]
        out_ref[peer, (1 + ratio) * tokens :] = strength[
            head * ratio : head * ratio + ROW_TILE
        ].astype(BF16)
    copies[2].wait()
    v_t = turned(v_ref)
    for peer, head in enumerate(heads):
        for r in range(ratio):
            out_ref[peer, (1 + r) * tokens : (2 + r) * tokens] = v_t[head * ratio + r]


def pack_read_kernel(sub, q_hbm, g_hbm, out_ref, q_ref, g_ref, done):
    tokens, key_heads, width = q_ref.shape
    ratio = g_ref.shape[1] // key_heads
    n_head = key_heads // sub
    copies = [
        pltpu.make_async_copy(source, target, done.at[place])
        for place, (source, target) in enumerate(((q_hbm, q_ref), (g_hbm, g_ref)))
    ]
    for copy in copies:
        copy.start()
    heads = [(peer % n_head) * sub + peer // n_head for peer in range(key_heads)]
    copies[0].wait()
    q_t = turned(q_ref)
    for peer, head in enumerate(heads):
        out_ref[peer, 0:tokens] = q_t[head]
    copies[1].wait()
    g_t = turned(g_ref)
    for peer, head in enumerate(heads):
        for r in range(ratio):
            out_ref[peer, (1 + r) * tokens : (2 + r) * tokens] = g_t[head * ratio + r]


def block_rows(got_ref, block, per, tokens, part):
    rows = got_ref[pl.ds(block * per, per), part * tokens : (part + 1) * tokens]
    return rows.reshape(per * tokens, rows.shape[-1])


def block_inverse(below):
    size = below[0].shape[0]
    rows = lax.broadcasted_iota(jnp.int32, (size, size), 0)
    cols = lax.broadcasted_iota(jnp.int32, (size, size), 1)
    zero = jnp.zeros((size, size), F32)
    step = 1
    solved = None
    while step < size:
        joins = (rows // (2 * step) == cols // (2 * step)) & (rows // step > cols // step)
        parts = [jnp.where(joins, matrix, zero) for matrix in below]
        if step == 1:
            solved = [
                jnp.where(rows == cols, jnp.ones_like(zero), -part).astype(BF16) for part in parts
            ]
        else:
            inner = [dot(part.astype(BF16), now).astype(BF16) for part, now in zip(parts, solved)]
            solved = [now - dot(now, mid).astype(BF16) for now, mid in zip(solved, inner)]
        step *= 2
    return solved


def factor_kernel(tokens, ratio, group, got_ref, state_ref, w_ref, u_ref, trans_ref, prefix_ref, add_ref):
    width = got_ref.shape[-1]
    per = SPAN // tokens
    blocks = got_ref.shape[0] // per
    rows = lax.broadcasted_iota(jnp.int32, (SPAN, SPAN), 0)
    cols = lax.broadcasted_iota(jnp.int32, (SPAN, SPAN), 1)
    lane = lax.broadcasted_iota(jnp.int32, (1, SPAN), 1)
    first = (1 + ratio) * tokens

    def factors(outer):
        below, held = [], []
        for inner in range(group):
            block = outer * group + inner
            key = block_rows(got_ref, block, per, tokens, 0)
            gram = dot_nt(key, key)
            squares = jnp.where(rows == cols, gram, 0.0)
            key_row = lax.rsqrt(jnp.sum(squares, 0, keepdims=True) + EPSILON)
            key_col = lax.rsqrt(jnp.sum(squares, 1, keepdims=True) + EPSILON)
            lower = jnp.where(rows > cols, gram, 0.0) * key_row
            for r in range(ratio):
                strength = jnp.zeros((1, SPAN), F32)
                for place in range(per):
                    piece = got_ref[block * per + place, first : first + ROW_TILE].astype(F32)[r : r + 1]
                    strength = jnp.where(lane // tokens == place, piece, strength)
                scaled_col = jnp.sum(jnp.where(rows == cols, strength * key_row, 0.0), 1, keepdims=True)
                below.append(lower * scaled_col)
                held.append((block, r, key, key_col, key_row, strength))
        solved = block_inverse(below)
        for now, (block, r, key, key_col, key_row, strength) in zip(solved, held):
            value = block_rows(got_ref, block, per, tokens, 1 + r)
            weighted = now.astype(F32) * key_col * strength
            u_now = dot(weighted.astype(BF16), value)
            w_now = dot((weighted * key_row).astype(BF16), key).astype(BF16)
            both = dot(key.T, jnp.concatenate([w_now, u_now.astype(BF16)], axis=1))
            w_ref[block, r] = w_now
            u_ref[block, r] = u_now
            trans_ref[block, r] = both[:, :width].astype(BF16)
            add_ref[block, r] = both[:, width:]

    for outer in range(blocks // group):
        factors(outer)

    states = [jnp.zeros((width, width), F32) for r in range(ratio)]
    for block in range(blocks):
        for r in range(ratio):
            held = states[r].astype(BF16)
            prefix_ref[block, r] = held
            if block == 0:
                states[r] = add_ref[block, r]
            else:
                states[r] = states[r] + add_ref[block, r] - dot(trans_ref[block, r], held)
    for r in range(ratio):
        state_ref[r] = states[r].astype(state_ref.dtype)


def spread_kernel(
    tokens, ratio, got_ref, read_ref, w_ref, u_ref, trans_ref, prefix_ref, local_ref, reach_ref, total_ref
):
    width = got_ref.shape[-1]
    per = SPAN // tokens
    blocks = got_ref.shape[0] // per
    rows = lax.broadcasted_iota(jnp.int32, (SPAN, SPAN), 0)
    cols = lax.broadcasted_iota(jnp.int32, (SPAN, SPAN), 1)
    wide_rows = lax.broadcasted_iota(jnp.int32, (width, width), 0)
    wide_cols = lax.broadcasted_iota(jnp.int32, (width, width), 1)
    identity = jnp.where(wide_rows == wide_cols, 1.0, 0.0).astype(F32)
    carried = [identity for r in range(ratio)]
    for block in range(blocks):
        query = block_rows(read_ref, block, per, tokens, 0)
        key = block_rows(got_ref, block, per, tokens, 0)
        scores = jnp.where(rows >= cols, dot_nt(query, key), 0.0).astype(BF16)
        query_f = query.astype(F32)
        squares = jnp.sum(query_f * query_f, 1, keepdims=True)
        unit = lax.rsqrt(squares + EPSILON) * width ** (-0.5)
        left = jnp.concatenate([query, scores], axis=1)
        for r in range(ratio):
            held = carried[r].astype(BF16)
            if block == 0:
                carried[r] = identity - trans_ref[block, r].astype(F32)
            else:
                carried[r] = carried[r] - dot(trans_ref[block, r], held)
            starts = jnp.concatenate([prefix_ref[block, r], held], axis=1)
            passed = dot(w_ref[block, r], starts)
            corrected = jnp.concatenate([u_ref[block, r] - passed[:, :width], -passed[:, width:]], axis=1)
            right = jnp.concatenate([starts, corrected.astype(BF16)], axis=0)
            out = dot(left, right) * unit
            local_ref[r, block] = out[:, :width]
            reach_ref[r, block] = out[:, width:].astype(BF16)
    for r in range(ratio):
        total_ref[r] = carried[r]


def join_kernel(tokens, place_ref, state_ref, local_ref, reach_ref, read_ref, gain_ref, *out_refs):
    ratio, blocks, span, width = local_ref.shape
    per = span // tokens
    pieces = blocks // len(out_refs)
    gain = gain_ref[...].astype(F32)
    mine = place_ref[0]
    for distance, out_ref in enumerate(out_refs):
        target = mine ^ distance
        for piece in range(pieces):
            block = target * pieces + piece
            for r in range(ratio):
                core = local_ref[r, block] + dot(reach_ref[r, block], state_ref[r].astype(BF16))
                mean_square = jnp.mean(core * core, 1, keepdims=True)
                gate = block_rows(read_ref, block, per, tokens, 1 + r).astype(F32)
                gated = core * lax.rsqrt(mean_square + EPSILON) * gain * (gate / (1.0 + jnp.exp(-gate)))
                out_ref[piece, r] = gated.astype(BF16)


def project_kernel(tokens, parts, place_ref, *refs):
    gated_refs, weight_ref, send_ref, keep_ref, rows_ref = refs[:parts], refs[parts], *refs[parts + 1 :]
    pieces, ratio, span, width = gated_refs[0].shape
    per = span // tokens
    half = pieces * per // 2

    @pl.when(pl.program_id(0) == 0)
    def _():
        for distance, gated_ref in enumerate(gated_refs):
            source = place_ref[0] ^ distance
            for r in range(ratio):
                lanes = pl.ds(pl.multiple_of((source * ratio + r) * width, width), width)
                for kept in range(2):
                    for place in range(half):
                        share = 2 * place + ((place_ref[1] + 1 + kept) & 1)
                        block = gated_ref[share // per, r, pl.ds(pl.multiple_of(share % per * tokens, tokens), tokens)]
                        first = (kept * half + place) * tokens
                        rows_ref[first : first + tokens, lanes] = block

    out = dot(rows_ref[...], weight_ref[...]).reshape(2, half, tokens, weight_ref.shape[1])
    send_ref[...] = out[0].astype(BF16)
    keep_ref[...] = out[1]


def halve_kernel(stage, place_ref, keep_ref, got_ref, send_ref, left_ref):
    bit = (place_ref[1] >> stage) & 1
    for place in range(keep_ref.shape[0] // 2):
        there, here = 2 * place + 1 - bit, 2 * place + bit
        send_ref[place] = (keep_ref[there] + got_ref[there].astype(F32)).astype(BF16)
        left_ref[place] = keep_ref[here] + got_ref[here].astype(F32)


def per_device(
    outer, sub, n_head, queries, key_vectors, value_vectors, output_gate, write_strength, norm_gain, output_weight
):
    tokens, key_heads, width = queries.shape
    value_heads = value_vectors.shape[1]
    ratio = value_heads // key_heads
    sources = sub * n_head
    shard = tokens * sources
    blocks = shard // SPAN
    shard_tokens = tokens * n_head
    shape = jax.ShapeDtypeStruct
    place = jnp.stack([lax.axis_index("sub"), lax.axis_index("head")]).astype(jnp.int32)

    with jax.named_scope("pack_write"):
        write = pl.pallas_call(
            functools.partial(pack_write_kernel, sub),
            out_shape=shape((sources, (1 + ratio) * tokens + ROW_TILE, width), BF16),
            in_specs=[ANY] * 3,
            out_specs=VMEM,
            scratch_shapes=[
                pltpu.VMEM(key_vectors.shape, BF16),
                pltpu.VMEM(value_vectors.shape, BF16),
                pltpu.VMEM((value_heads, tokens), BF16),
                pltpu.SemaphoreType.DMA((3,)),
            ],
            compiler_params=params(60),
        )(key_vectors, value_vectors, write_strength.T)
    got = lax.all_to_all(write, ("sub", "head"), split_axis=0, concat_axis=0, tiled=True)
    with jax.named_scope("pack_read"):
        read = pl.pallas_call(
            functools.partial(pack_read_kernel, sub),
            out_shape=shape((sources, (1 + ratio) * tokens, width), BF16),
            in_specs=[ANY] * 2,
            out_specs=VMEM,
            scratch_shapes=[
                pltpu.VMEM(queries.shape, BF16),
                pltpu.VMEM(output_gate.shape, BF16),
                pltpu.SemaphoreType.DMA((2,)),
            ],
            compiler_params=params(60),
        )(queries, output_gate)
    got_read = lax.all_to_all(read, ("sub", "head"), split_axis=0, concat_axis=0, tiled=True)

    state_type = BF16 if outer == 2 else F32
    square = (blocks, ratio, width, width)
    with jax.named_scope("factors"):
        state, w, u, trans, prefix = pl.pallas_call(
            functools.partial(factor_kernel, tokens, ratio, blocks),
            out_shape=[
                shape((ratio, width, width), state_type),
                shape((blocks, ratio, SPAN, width), BF16),
                shape((blocks, ratio, SPAN, width), F32),
                shape(square, BF16),
                shape(square, BF16),
            ],
            in_specs=[VMEM],
            out_specs=[VMEM] * 5,
            scratch_shapes=[pltpu.VMEM(square, F32)],
            compiler_params=params(),
            cost_estimate=pl.CostEstimate(flops=5 * 10**9, bytes_accessed=4 * 10**6, transcendentals=0),
        )(got)

    onward = [(here, here + 1) for here in range(outer - 1)]
    incoming = lax.ppermute(state, "outer", onward)
    with jax.named_scope("spread"):
        local, reach, total = pl.pallas_call(
            functools.partial(spread_kernel, tokens, ratio),
            out_shape=[
                shape((ratio, blocks, SPAN, width), F32),
                shape((ratio, blocks, SPAN, width), BF16),
                shape((ratio, width, width), F32),
            ],
            in_specs=[VMEM] * 6,
            out_specs=[VMEM] * 3,
            compiler_params=params(),
            cost_estimate=pl.CostEstimate(flops=10**9, bytes_accessed=8 * 10**6, transcendentals=0),
        )(got, got_read, w, u, trans, prefix)
    for hop in range(outer - 2):
        passed = jnp.einsum("hde,hef->hdf", total, incoming, precision=lax.Precision.HIGHEST)
        incoming = lax.ppermute(state + passed, "outer", onward)

    pieces = shard_tokens // SPAN
    with jax.named_scope("join"):
        gated = pl.pallas_call(
            functools.partial(join_kernel, tokens),
            out_shape=[shape((pieces, ratio, SPAN, width), BF16)] * sub,
            in_specs=[SMEM] + [VMEM] * 5,
            out_specs=[VMEM] * sub,
            compiler_params=params(),
        )(place, incoming, local, reach, got_read, norm_gain.reshape(1, width))
    gated = list(gated)
    for distance in reversed(range(1, sub)):
        pairs = [(here, here ^ distance) for here in range(sub)]
        gated[distance] = lax.ppermute(gated[distance], "sub", pairs)

    columns = output_weight.shape[1]
    tile = 512
    chunks = 2
    steps = columns // chunks // tile
    depth = sub * ratio * width
    half = n_head // 2
    summed = []
    for chunk in range(chunks):
        with jax.named_scope("project"):
            send, keep = pl.pallas_call(
                functools.partial(project_kernel, tokens, sub),
                grid=(steps,),
                out_shape=[
                    shape((half, tokens, columns // chunks), BF16),
                    shape((half, tokens, columns // chunks), F32),
                ],
                in_specs=[SMEM]
                + [pl.BlockSpec((pieces, ratio, SPAN, width), lambda i: (0, 0, 0, 0))] * sub
                + [pl.BlockSpec((depth, tile), lambda i, first=chunk * steps: (0, i + first))],
                out_specs=[pl.BlockSpec((half, tokens, tile), lambda i: (0, 0, i))] * 2,
                scratch_shapes=[pltpu.VMEM((shard_tokens, depth), BF16)],
                compiler_params=params(),
                cost_estimate=pl.CostEstimate(flops=10**9, bytes_accessed=4 * 10**6, transcendentals=0),
            )(place, *gated, output_weight)
        stage = 0
        while True:
            pairs = [(here, here ^ (1 << stage)) for here in range(n_head)]
            arrived = lax.ppermute(send, "head", pairs)
            if keep.shape[0] == 1:
                summed.append((keep[0] + arrived[0].astype(F32)).astype(BF16))
                break
            stage += 1
            with jax.named_scope("halve"):
                left = (keep.shape[0] // 2,) + keep.shape[1:]
                send, keep = pl.pallas_call(
                    functools.partial(halve_kernel, stage),
                    out_shape=[shape(left, BF16), shape(left, F32)],
                    in_specs=[SMEM, VMEM, VMEM],
                    out_specs=[VMEM] * 2,
                    compiler_params=params(),
                )(place, keep, arrived)
    return jnp.concatenate(summed, axis=1)


def solution(mesh):
    n_seq, n_head = mesh.shape["seq"], mesh.shape["head"]

    def run(queries, key_vectors, value_vectors, output_gate, write_strength, norm_gain, output_weight):
        sub = queries.shape[1] // n_head
        outer = n_seq // sub
        split = Mesh(mesh.devices.reshape(outer, sub, n_head), ("outer", "sub", "head"))
        every = ("outer", "sub", "head")
        placed = (
            P(every, None, None),
            P(every, None, None),
            P(every, None, None),
            P(every, None, None),
            P(every, None),
            P(),
            P("head", None),
        )
        return jax.shard_map(
            functools.partial(per_device, outer, sub, n_head),
            mesh=split,
            in_specs=placed,
            out_specs=P(every, None),
            check_vma=False,
        )(queries, key_vectors, value_vectors, output_gate, write_strength, norm_gain, output_weight)

    return run
```

```python
import functools

import jax
import jax.numpy as jnp
from jax import lax
from jax.experimental import pallas as pl
from jax.experimental.pallas import tpu as pltpu
from jax.sharding import Mesh, PartitionSpec as P

SPAN = 128
EPSILON = 1e-06
F32 = jnp.float32
BF16 = jnp.bfloat16
ROW_TILE = 16
VMEM = pl.BlockSpec(memory_space=pltpu.VMEM)
SMEM = pl.BlockSpec(memory_space=pltpu.SMEM)
ANY = pl.BlockSpec(memory_space=pl.ANY)


def dot(left, right):
    return jnp.dot(left, right, preferred_element_type=F32)


def dot_nt(left, right):
    return lax.dot_general(left, right, (((1,), (1,)), ((), ())), preferred_element_type=F32)


def params(megabytes=24):
    return pltpu.CompilerParams(vmem_limit_bytes=megabytes * 2**20)


def turned(values):
    return jnp.transpose(values, (1, 0, 2))


def pack_kernel(sub, place_ref, q_hbm, k_hbm, v_hbm, b_hbm, *refs):
    tokens, key_heads, width = q_hbm.shape
    ratio = v_hbm.shape[1] // key_heads
    n_head = key_heads // sub
    out_refs = refs[:key_heads]
    q_ref, k_ref, v_ref, b_ref, q_turned, k_turned, v_turned, b_turned, done = refs[key_heads:]
    copies = [
        pltpu.make_async_copy(source, target, done.at[number])
        for number, (source, target) in enumerate(
            ((b_hbm, b_ref), (k_hbm, k_ref), (q_hbm, q_ref), (v_hbm, v_ref))
        )
    ]
    for copy in copies:
        copy.start()
    copies[0].wait()
    strength = jnp.concatenate([b_ref[...].astype(F32)] * (width // tokens), axis=1)
    strength = jnp.concatenate([strength, jnp.zeros((ROW_TILE, width), F32)], axis=0)
    for head in range(key_heads):
        b_turned[head] = strength[head * ratio : head * ratio + ROW_TILE].astype(BF16)
    for copy, source, target in zip(copies[1:], (k_ref, q_ref, v_ref), (k_turned, q_turned, v_turned)):
        copy.wait()
        target[...] = turned(source[...])
    mine = place_ref[0] * n_head + place_ref[1]
    for distance, out_ref in enumerate(out_refs):
        peer = mine ^ distance
        head = (peer % n_head) * sub + peer // n_head
        out_ref[0:tokens] = q_turned[head]
        out_ref[tokens : 2 * tokens] = k_turned[head]
        for r in range(ratio):
            out_ref[(2 + r) * tokens : (3 + r) * tokens] = v_turned[head * ratio + r]
        out_ref[(2 + ratio) * tokens :] = b_turned[head]


def gate_kernel(place_ref, gate_ref, gain_ref, unused_ref, *refs):
    out_refs, gates = refs[:-1], refs[-1]
    gate = gate_ref[...].astype(F32)
    gated = gain_ref[...].astype(F32)[:, None] * (gate / (1.0 + jnp.exp(-gate)))
    gates[...] = turned(gated.astype(BF16))
    for distance, out_ref in enumerate(out_refs):
        heads = out_ref.shape[0]
        out_ref[...] = gates[pl.ds((place_ref[1] ^ distance) * heads, heads)]


def block_rows(got_ref, block, per, tokens, part):
    rows = got_ref[pl.ds(block * per, per), part * tokens : (part + 1) * tokens]
    return rows.reshape(per * tokens, rows.shape[-1])


def block_inverse(below):
    size = below[0].shape[0]
    rows = lax.broadcasted_iota(jnp.int32, (size, size), 0)
    cols = lax.broadcasted_iota(jnp.int32, (size, size), 1)
    zero = jnp.zeros((size, size), F32)
    step = 1
    solved = None
    while step < size:
        joins = (rows // (2 * step) == cols // (2 * step)) & (rows // step > cols // step)
        parts = [jnp.where(joins, matrix, zero) for matrix in below]
        if step == 1:
            solved = [
                jnp.where(rows == cols, jnp.ones_like(zero), -part).astype(BF16) for part in parts
            ]
        else:
            inner = [dot(part.astype(BF16), now).astype(BF16) for part, now in zip(parts, solved)]
            solved = [now - dot(now, mid).astype(BF16) for now, mid in zip(solved, inner)]
        step *= 2
    return solved


def factor_kernel(tokens, ratio, n_head, place_ref, *refs):
    sources = len(refs) - 7
    slab_refs = refs[:sources]
    got_ref, state_ref, w_ref, u_ref, trans_ref, prefix_ref, add_ref = refs[sources:]
    mine = place_ref[0] * n_head + place_ref[1]
    for distance, slab_ref in enumerate(slab_refs):
        got_ref[mine ^ distance] = slab_ref[...]

    width = got_ref.shape[-1]
    per = SPAN // tokens
    blocks = got_ref.shape[0] // per
    rows = lax.broadcasted_iota(jnp.int32, (SPAN, SPAN), 0)
    cols = lax.broadcasted_iota(jnp.int32, (SPAN, SPAN), 1)
    lane = lax.broadcasted_iota(jnp.int32, (1, SPAN), 1)
    first = (2 + ratio) * tokens
    below, held = [], []
    for block in range(blocks):
        key = block_rows(got_ref, block, per, tokens, 1)
        gram = dot_nt(key, key)
        squares = jnp.where(rows == cols, gram, 0.0)
        key_row = lax.rsqrt(jnp.sum(squares, 0, keepdims=True) + EPSILON)
        key_col = lax.rsqrt(jnp.sum(squares, 1, keepdims=True) + EPSILON)
        lower = jnp.where(rows > cols, gram, 0.0) * key_row
        for r in range(ratio):
            strength = jnp.zeros((1, SPAN), F32)
            for place in range(per):
                piece = got_ref[block * per + place, first : first + ROW_TILE].astype(F32)[r : r + 1]
                strength = jnp.where(lane // tokens == place, piece, strength)
            scaled_col = jnp.sum(jnp.where(rows == cols, strength * key_row, 0.0), 1, keepdims=True)
            below.append(lower * scaled_col)
            held.append((block, r, key, key_col, key_row, strength))
    solved = block_inverse(below)
    for now, (block, r, key, key_col, key_row, strength) in zip(solved, held):
        value = block_rows(got_ref, block, per, tokens, 2 + r)
        weighted = now.astype(F32) * key_col * strength
        u_now = dot(weighted.astype(BF16), value)
        w_now = dot((weighted * key_row).astype(BF16), key).astype(BF16)
        both = dot(key.T, jnp.concatenate([w_now, u_now.astype(BF16)], axis=1))
        w_ref[block, r] = w_now
        u_ref[block, r] = u_now
        trans_ref[block, r] = both[:, :width].astype(BF16)
        add_ref[block, r] = both[:, width:]

    states = [jnp.zeros((width, width), F32) for r in range(ratio)]
    for block in range(blocks):
        for r in range(ratio):
            held = states[r].astype(BF16)
            prefix_ref[block, r] = held
            if block == 0:
                states[r] = add_ref[block, r]
            else:
                states[r] = states[r] + add_ref[block, r] - dot(trans_ref[block, r], held)
    for r in range(ratio):
        state_ref[r] = states[r].astype(state_ref.dtype)


def spread_kernel(
    tokens, ratio, got_ref, w_ref, u_ref, trans_ref, prefix_ref, local_ref, reach_ref, total_ref
):
    width = got_ref.shape[-1]
    per = SPAN // tokens
    blocks = got_ref.shape[0] // per
    rows = lax.broadcasted_iota(jnp.int32, (SPAN, SPAN), 0)
    cols = lax.broadcasted_iota(jnp.int32, (SPAN, SPAN), 1)
    wide_rows = lax.broadcasted_iota(jnp.int32, (width, width), 0)
    wide_cols = lax.broadcasted_iota(jnp.int32, (width, width), 1)
    identity = jnp.where(wide_rows == wide_cols, 1.0, 0.0).astype(F32)
    carried = [identity for r in range(ratio)]
    for block in range(blocks):
        query = block_rows(got_ref, block, per, tokens, 0)
        key = block_rows(got_ref, block, per, tokens, 1)
        scores = jnp.where(rows >= cols, dot_nt(query, key), 0.0).astype(BF16)
        query_f = query.astype(F32)
        squares = jnp.sum(query_f * query_f, 1, keepdims=True)
        unit = lax.rsqrt(squares + EPSILON) * width ** (-0.5)
        left = jnp.concatenate([query, scores], axis=1)
        for r in range(ratio):
            held = carried[r].astype(BF16)
            if block == 0:
                carried[r] = identity - trans_ref[block, r].astype(F32)
            else:
                carried[r] = carried[r] - dot(trans_ref[block, r], held)
            starts = jnp.concatenate([prefix_ref[block, r], held], axis=1)
            passed = dot(w_ref[block, r], starts)
            corrected = jnp.concatenate([u_ref[block, r] - passed[:, :width], -passed[:, width:]], axis=1)
            right = jnp.concatenate([starts, corrected.astype(BF16)], axis=0)
            out = dot(left, right) * unit
            local_ref[r, block] = out[:, :width]
            reach_ref[r, block] = out[:, width:].astype(BF16)
    for r in range(ratio):
        total_ref[r] = carried[r]


def join_kernel(place_ref, state_ref, local_ref, reach_ref, *out_refs):
    ratio, blocks, span, width = local_ref.shape
    pieces = blocks // len(out_refs)
    for distance, out_ref in enumerate(out_refs):
        target = place_ref[0] ^ distance
        for piece in range(pieces):
            block = target * pieces + piece
            for r in range(ratio):
                core = local_ref[r, block] + dot(reach_ref[r, block], state_ref[r].astype(BF16))
                mean_square = jnp.mean(core * core, 1, keepdims=True)
                out_ref[piece, r] = (core * lax.rsqrt(mean_square + EPSILON)).astype(BF16)


def project(chunk, rows, weight_ref, send_ref, keep_ref):
    half, tokens, columns = keep_ref.shape
    out = dot(rows, weight_ref[:, chunk * columns : (chunk + 1) * columns]).reshape(2, half, tokens, columns)
    send_ref[...] = out[0].astype(BF16)
    keep_ref[...] = out[1]


def project_kernel(parts, chunk, place_ref, *refs):
    normed_refs, gate_refs, (weight_ref, send_ref, keep_ref, rows_ref) = refs[:parts], refs[parts:-4], refs[-4:]
    pieces, ratio, span, width = normed_refs[0].shape
    tokens = gate_refs[0].shape[1]
    per = span // tokens
    half = len(gate_refs) // 2
    for distance, normed_ref in enumerate(normed_refs):
        source = place_ref[0] ^ distance
        for apart, gate_ref in enumerate(gate_refs):
            share = place_ref[1] ^ apart
            first = ((1 - apart % 2) * half + share // 2) * tokens
            place = pl.ds(pl.multiple_of(first, tokens), tokens)
            from_rows = pl.ds(pl.multiple_of(share % per * tokens, tokens), tokens)
            for r in range(ratio):
                lanes = pl.ds(pl.multiple_of((source * ratio + r) * width, width), width)
                normed = normed_ref[share // per, r, from_rows].astype(F32)
                gate = gate_ref[source * ratio + r].astype(F32)
                rows_ref[place, lanes] = (normed * gate).astype(BF16)
    project(chunk, rows_ref[...], weight_ref, send_ref, keep_ref)


def project_more_kernel(chunk, rows_ref, weight_ref, send_ref, keep_ref):
    project(chunk, rows_ref[...], weight_ref, send_ref, keep_ref)


def halve_kernel(stage, place_ref, keep_ref, got_ref, send_ref, left_ref):
    bit = (place_ref[1] >> stage) & 1
    for place in range(keep_ref.shape[0] // 2):
        there, here = 2 * place + 1 - bit, 2 * place + bit
        send_ref[place] = (keep_ref[there] + got_ref[there].astype(F32)).astype(BF16)
        left_ref[place] = keep_ref[here] + got_ref[here].astype(F32)


def finish_kernel(*refs):
    out_ref = refs[-1]
    keep_refs, got_refs = refs[: len(refs) // 2], refs[len(refs) // 2 : -1]
    first = 0
    for keep_ref, got_ref in zip(keep_refs, got_refs):
        columns = keep_ref.shape[-1]
        out_ref[:, first : first + columns] = (keep_ref[0] + got_ref[0].astype(F32)).astype(BF16)
        first += columns


def per_device(
    outer, sub, n_head, queries, key_vectors, value_vectors, output_gate, write_strength, norm_gain, output_weight
):
    tokens, key_heads, width = queries.shape
    value_heads = value_vectors.shape[1]
    ratio = value_heads // key_heads
    sources = sub * n_head
    shard = tokens * sources
    blocks = shard // SPAN
    shard_tokens = tokens * n_head
    shape = jax.ShapeDtypeStruct
    place = jnp.stack([lax.axis_index("sub"), lax.axis_index("head")]).astype(jnp.int32)

    with jax.named_scope("pack"):
        slab = shape(((2 + ratio) * tokens + ROW_TILE, width), BF16)
        slabs = pl.pallas_call(
            functools.partial(pack_kernel, sub),
            out_shape=[slab] * sources,
            in_specs=[SMEM] + [ANY] * 4,
            out_specs=[VMEM] * sources,
            scratch_shapes=[
                pltpu.VMEM(queries.shape, BF16),
                pltpu.VMEM(key_vectors.shape, BF16),
                pltpu.VMEM(value_vectors.shape, BF16),
                pltpu.VMEM((value_heads, tokens), BF16),
                pltpu.VMEM((key_heads, tokens, width), BF16),
                pltpu.VMEM((key_heads, tokens, width), BF16),
                pltpu.VMEM((value_heads, tokens, width), BF16),
                pltpu.VMEM((key_heads, ROW_TILE, width), BF16),
                pltpu.SemaphoreType.DMA((4,)),
            ],
            compiler_params=params(60),
        )(place, queries, key_vectors, value_vectors, write_strength.T)
    slabs = list(slabs)
    for distance in reversed(range(1, sources)):
        pairs = [(here, here ^ distance) for here in range(sources)]
        slabs[distance] = lax.ppermute(slabs[distance], ("sub", "head"), pairs)

    state_type = BF16 if outer == 2 else F32
    square = (blocks, ratio, width, width)
    with jax.named_scope("factors"):
        got, state, w, u, trans, prefix = pl.pallas_call(
            functools.partial(factor_kernel, tokens, ratio, n_head),
            out_shape=[
                shape((sources,) + slab.shape, BF16),
                shape((ratio, width, width), state_type),
                shape((blocks, ratio, SPAN, width), BF16),
                shape((blocks, ratio, SPAN, width), F32),
                shape(square, BF16),
                shape(square, BF16),
            ],
            in_specs=[SMEM] + [VMEM] * sources,
            out_specs=[VMEM] * 6,
            scratch_shapes=[pltpu.VMEM(square, F32)],
            compiler_params=params(),
            cost_estimate=pl.CostEstimate(flops=4 * 10**9, bytes_accessed=4 * 10**6, transcendentals=0),
        )(place, *slabs)

    onward = [(here, here + 1) for here in range(outer - 1)]
    incoming = lax.ppermute(state, "outer", onward)
    with jax.named_scope("spread"):
        local, reach, total = pl.pallas_call(
            functools.partial(spread_kernel, tokens, ratio),
            out_shape=[
                shape((ratio, blocks, SPAN, width), F32),
                shape((ratio, blocks, SPAN, width), BF16),
                shape((ratio, width, width), F32),
            ],
            in_specs=[VMEM] * 5,
            out_specs=[VMEM] * 3,
            compiler_params=params(),
            cost_estimate=pl.CostEstimate(flops=2 * 10**9, bytes_accessed=8 * 10**6, transcendentals=0),
        )(got, w, u, trans, prefix)
    heads = sub * ratio
    with jax.named_scope("gates"):
        gates = pl.pallas_call(
            gate_kernel,
            out_shape=[shape((heads, tokens, width), BF16)] * n_head,
            in_specs=[SMEM, VMEM, VMEM, ANY],
            out_specs=[VMEM] * n_head,
            scratch_shapes=[pltpu.VMEM((value_heads, tokens, width), BF16)],
            compiler_params=params(),
            cost_estimate=pl.CostEstimate(flops=10**9, bytes_accessed=8 * 10**6, transcendentals=0),
        )(place, output_gate, norm_gain.reshape(1, width), state)
    gates = list(gates)
    for distance in reversed(range(1, n_head)):
        pairs = [(here, here ^ distance) for here in range(n_head)]
        gates[distance] = lax.ppermute(gates[distance], "head", pairs)
    for hop in range(outer - 2):
        passed = jnp.einsum("hde,hef->hdf", total, incoming, precision=lax.Precision.HIGHEST)
        incoming = lax.ppermute(state + passed, "outer", onward)

    pieces = shard_tokens // SPAN
    with jax.named_scope("join"):
        normed = pl.pallas_call(
            join_kernel,
            out_shape=[shape((pieces, ratio, SPAN, width), BF16)] * sub,
            in_specs=[SMEM] + [VMEM] * 3,
            out_specs=[VMEM] * sub,
            compiler_params=params(),
        )(place, incoming, local, reach)
    normed = list(normed)
    for distance in reversed(range(1, sub)):
        pairs = [(here, here ^ distance) for here in range(sub)]
        normed[distance] = lax.ppermute(normed[distance], "sub", pairs)

    chunks = 2
    columns = output_weight.shape[1] // chunks
    half = n_head // 2
    out_shape = [shape((half, tokens, columns), BF16), shape((half, tokens, columns), F32)]
    kept, arrivals, rows = [], [], None
    for chunk in range(chunks):
        cost = pl.CostEstimate(flops=10**9, bytes_accessed=4 * 10**6, transcendentals=0)
        with jax.named_scope("project"):
            if chunk == 0:
                send, keep, rows = pl.pallas_call(
                    functools.partial(project_kernel, sub, chunk),
                    out_shape=out_shape + [shape((shard_tokens, heads * width), BF16)],
                    in_specs=[SMEM] + [VMEM] * (sub + n_head + 1),
                    out_specs=[VMEM] * 3,
                    compiler_params=params(),
                    cost_estimate=cost,
                )(place, *normed, *gates, output_weight)
            else:
                send, keep = pl.pallas_call(
                    functools.partial(project_more_kernel, chunk),
                    out_shape=out_shape,
                    in_specs=[VMEM] * 2,
                    out_specs=[VMEM] * 2,
                    compiler_params=params(),
                    cost_estimate=cost,
                )(rows, output_weight)
        stage = 0
        while True:
            pairs = [(here, here ^ (1 << stage)) for here in range(n_head)]
            arrived = lax.ppermute(send, "head", pairs)
            if keep.shape[0] == 1:
                kept.append(keep)
                arrivals.append(arrived)
                break
            stage += 1
            with jax.named_scope("halve"):
                left = (keep.shape[0] // 2,) + keep.shape[1:]
                send, keep = pl.pallas_call(
                    functools.partial(halve_kernel, stage),
                    out_shape=[shape(left, BF16), shape(left, F32)],
                    in_specs=[SMEM, VMEM, VMEM],
                    out_specs=[VMEM] * 2,
                    compiler_params=params(),
                )(place, keep, arrived)
    with jax.named_scope("finish"):
        return pl.pallas_call(
            finish_kernel,
            out_shape=shape((tokens, output_weight.shape[1]), BF16),
            in_specs=[VMEM] * (2 * chunks),
            out_specs=VMEM,
            compiler_params=params(),
        )(*kept, *arrivals)


def solution(mesh):
    n_seq, n_head = mesh.shape["seq"], mesh.shape["head"]

    def run(queries, key_vectors, value_vectors, output_gate, write_strength, norm_gain, output_weight):
        sub = queries.shape[1] // n_head
        outer = n_seq // sub
        split = Mesh(mesh.devices.reshape(outer, sub, n_head), ("outer", "sub", "head"))
        every = ("outer", "sub", "head")
        placed = (
            P(every, None, None),
            P(every, None, None),
            P(every, None, None),
            P(every, None, None),
            P(every, None),
            P(),
            P("head", None),
        )
        return jax.shard_map(
            functools.partial(per_device, outer, sub, n_head),
            mesh=split,
            in_specs=placed,
            out_specs=P(every, None),
            check_vma=False,
        )(queries, key_vectors, value_vectors, output_gate, write_strength, norm_gain, output_weight)

    return run
```

```python
import functools

import jax
import jax.numpy as jnp
from jax import lax
from jax.experimental import pallas as pl
from jax.experimental.pallas import tpu as pltpu
from jax.sharding import Mesh, PartitionSpec as P

SPAN = 128
EPSILON = 1e-06
F32 = jnp.float32
BF16 = jnp.bfloat16
ROW_TILE = 16
VMEM = pl.BlockSpec(memory_space=pltpu.VMEM)
SMEM = pl.BlockSpec(memory_space=pltpu.SMEM)
ANY = pl.BlockSpec(memory_space=pl.ANY)


def dot(left, right):
    return jnp.dot(left, right, preferred_element_type=F32)


def dot_nt(left, right):
    return lax.dot_general(left, right, (((1,), (1,)), ((), ())), preferred_element_type=F32)


def params(megabytes=24):
    return pltpu.CompilerParams(vmem_limit_bytes=megabytes * 2**20)


def turned(values):
    return jnp.transpose(values, (1, 0, 2))


def position():
    return lax.axis_index("sub"), lax.axis_index("head")


def chip_order(chips):
    return sorted(range(chips), key=lambda distance: -bin(distance).count("1") if distance else -chips)


def pack_kernel(sub, q_hbm, k_hbm, v_hbm, b_hbm, *refs):
    tokens, key_heads, width = q_hbm.shape
    ratio = v_hbm.shape[1] // key_heads
    n_head = key_heads // sub
    q_ref, k_ref, v_ref, b_ref, q_turned, k_turned, v_turned, b_turned, done = refs[key_heads // 2 :]
    copies = [
        pltpu.make_async_copy(source, target, done.at[number])
        for number, (source, target) in enumerate(
            ((b_hbm, b_ref), (k_hbm, k_ref), (q_hbm, q_ref), (v_hbm, v_ref))
        )
    ]
    for copy in copies:
        copy.start()
    copies[0].wait()
    strength = jnp.concatenate([b_ref[...].astype(F32)] * (width // tokens), axis=1)
    strength = jnp.concatenate([strength, jnp.zeros((ROW_TILE, width), F32)], axis=0)
    for head in range(key_heads):
        b_turned[head] = strength[head * ratio : head * ratio + ROW_TILE].astype(BF16)
    for copy, source, target in zip(copies[1:], (k_ref, q_ref, v_ref), (k_turned, q_turned, v_turned)):
        copy.wait()
        target[...] = turned(source[...])
    along_sub, along_head = position()
    mine = along_sub * n_head + along_head
    for distance in range(key_heads):
        peer = mine ^ distance
        head = (peer % n_head) * sub + peer // n_head
        out_ref = refs[chip_order(key_heads // 2).index(distance // 2)].at[distance % 2]
        out_ref[0:tokens] = q_turned[head]
        out_ref[tokens : 2 * tokens] = k_turned[head]
        for r in range(ratio):
            out_ref[(2 + r) * tokens : (3 + r) * tokens] = v_turned[head * ratio + r]
        out_ref[(2 + ratio) * tokens :] = b_turned[head]


def other_core_kernel(*refs):
    slab_refs, out_ref = refs[:-2], refs[-1]
    for place, slab_ref in enumerate(slab_refs):
        out_ref[place] = slab_ref[1]


def gate_kernel(gate_ref, gain_ref, after_ref, *refs):
    unused, along_head = position()
    out_refs, gates = refs[:-1], refs[-1]
    gate = gate_ref[...].astype(F32)
    gated = gain_ref[...].astype(F32)[:, None] * (gate / (1.0 + jnp.exp(-gate)))
    gates[...] = turned(gated.astype(BF16))
    for distance, out_ref in enumerate(out_refs):
        heads = out_ref.shape[0]
        out_ref[...] = gates[pl.ds((along_head ^ distance) * heads, heads)]


def block_rows(got_ref, block, per, tokens, part):
    rows = got_ref[pl.ds(block * per, per), part * tokens : (part + 1) * tokens]
    return rows.reshape(per * tokens, rows.shape[-1])


def block_inverse(below):
    size = below[0].shape[0]
    rows = lax.broadcasted_iota(jnp.int32, (size, size), 0)
    cols = lax.broadcasted_iota(jnp.int32, (size, size), 1)
    zero = jnp.zeros((size, size), F32)
    step = 1
    solved = None
    while step < size:
        joins = (rows // (2 * step) == cols // (2 * step)) & (rows // step > cols // step)
        parts = [jnp.where(joins, matrix, zero) for matrix in below]
        if step == 1:
            solved = [
                jnp.where(rows == cols, jnp.ones_like(zero), -part).astype(BF16) for part in parts
            ]
        else:
            inner = [dot(part.astype(BF16), now).astype(BF16) for part, now in zip(parts, solved)]
            solved = [now - dot(now, mid).astype(BF16) for now, mid in zip(solved, inner)]
        step *= 2
    return solved


def factor_kernel(tokens, ratio, sub, n_head, *refs):
    chips = sub * n_head // 2
    got_ref, state_ref, w_ref, u_ref, trans_ref, prefix_ref, add_ref = refs[-7:]
    along_sub, along_head = position()
    mine = along_sub * n_head + along_head
    for number, distance in enumerate(chip_order(chips)):
        got_ref[mine ^ (2 * distance)] = refs[number][0]
        got_ref[mine ^ (2 * distance + 1)] = refs[chips][number]
    width = got_ref.shape[-1]
    per = SPAN // tokens
    blocks = got_ref.shape[0] // per
    rows = lax.broadcasted_iota(jnp.int32, (SPAN, SPAN), 0)
    cols = lax.broadcasted_iota(jnp.int32, (SPAN, SPAN), 1)
    lane = lax.broadcasted_iota(jnp.int32, (1, SPAN), 1)
    first = (2 + ratio) * tokens
    below, held = [], []
    for block in range(blocks):
        key = block_rows(got_ref, block, per, tokens, 1)
        gram = dot_nt(key, key)
        squares = jnp.where(rows == cols, gram, 0.0)
        key_row = lax.rsqrt(jnp.sum(squares, 0, keepdims=True) + EPSILON)
        key_col = lax.rsqrt(jnp.sum(squares, 1, keepdims=True) + EPSILON)
        lower = jnp.where(rows > cols, gram, 0.0) * key_row
        for r in range(ratio):
            strength = jnp.zeros((1, SPAN), F32)
            for place in range(per):
                piece = got_ref[block * per + place, first : first + ROW_TILE].astype(F32)[r : r + 1]
                strength = jnp.where(lane // tokens == place, piece, strength)
            scaled_col = jnp.sum(jnp.where(rows == cols, strength * key_row, 0.0), 1, keepdims=True)
            below.append(lower * scaled_col)
            held.append((block, r, key, key_col, key_row, strength))
    solved = block_inverse(below)
    for now, (block, r, key, key_col, key_row, strength) in zip(solved, held):
        value = block_rows(got_ref, block, per, tokens, 2 + r)
        weighted = now.astype(F32) * key_col * strength
        u_now = dot(weighted.astype(BF16), value)
        w_now = dot((weighted * key_row).astype(BF16), key).astype(BF16)
        both = dot(key.T, jnp.concatenate([w_now, u_now.astype(BF16)], axis=1))
        w_ref[block, r] = w_now
        u_ref[block, r] = u_now
        trans_ref[block, r] = both[:, :width].astype(BF16)
        add_ref[block, r] = both[:, width:]

    states = [jnp.zeros((width, width), F32) for r in range(ratio)]
    for block in range(blocks):
        for r in range(ratio):
            held = states[r].astype(BF16)
            prefix_ref[block, r] = held
            if block == 0:
                states[r] = add_ref[block, r]
            else:
                states[r] = states[r] + add_ref[block, r] - dot(trans_ref[block, r], held)
    for r in range(ratio):
        state_ref[r] = states[r].astype(state_ref.dtype)


def spread_kernel(
    tokens, ratio, got_ref, w_ref, u_ref, trans_ref, prefix_ref, local_ref, reach_ref, total_ref
):
    width = got_ref.shape[-1]
    per = SPAN // tokens
    blocks = got_ref.shape[0] // per
    rows = lax.broadcasted_iota(jnp.int32, (SPAN, SPAN), 0)
    cols = lax.broadcasted_iota(jnp.int32, (SPAN, SPAN), 1)
    wide_rows = lax.broadcasted_iota(jnp.int32, (width, width), 0)
    wide_cols = lax.broadcasted_iota(jnp.int32, (width, width), 1)
    identity = jnp.where(wide_rows == wide_cols, 1.0, 0.0).astype(F32)
    carried = [identity for r in range(ratio)]
    for block in range(blocks):
        query = block_rows(got_ref, block, per, tokens, 0)
        key = block_rows(got_ref, block, per, tokens, 1)
        scores = jnp.where(rows >= cols, dot_nt(query, key), 0.0).astype(BF16)
        query_f = query.astype(F32)
        squares = jnp.sum(query_f * query_f, 1, keepdims=True)
        unit = lax.rsqrt(squares + EPSILON) * width ** (-0.5)
        left = jnp.concatenate([query, scores], axis=1)
        for r in range(ratio):
            held = carried[r].astype(BF16)
            if block == 0:
                carried[r] = identity - trans_ref[block, r].astype(F32)
            else:
                carried[r] = carried[r] - dot(trans_ref[block, r], held)
            starts = jnp.concatenate([prefix_ref[block, r], held], axis=1)
            passed = dot(w_ref[block, r], starts)
            corrected = jnp.concatenate([u_ref[block, r] - passed[:, :width], -passed[:, width:]], axis=1)
            right = jnp.concatenate([starts, corrected.astype(BF16)], axis=0)
            out = dot(left, right) * unit
            local_ref[r, block] = out[:, :width]
            reach_ref[r, block] = out[:, width:].astype(BF16)
    for r in range(ratio):
        total_ref[r] = carried[r]


def join_kernel(flip, pieces, state_ref, local_ref, reach_ref, *out_refs):
    ratio, blocks, span, width = local_ref.shape
    along_sub, along_head = position()
    upper = along_head // (lax.axis_size("head") // 2)
    for distance, out_ref in enumerate(out_refs):
        target = along_sub ^ distance
        for piece in range(pieces):
            block = (target * 2 + (upper ^ flip)) * pieces + piece
            for r in range(ratio):
                core = local_ref[r, block] + dot(reach_ref[r, block], state_ref[r].astype(BF16))
                mean_square = jnp.mean(core * core, 1, keepdims=True)
                out_ref[piece, r] = (core * lax.rsqrt(mean_square + EPSILON)).astype(BF16)


def project_kernel(parts, after_ref, *refs):
    normed_refs, gate_refs, (weight_ref, send_ref, keep_ref, rows_ref) = refs[:parts], refs[parts:-4], refs[-4:]
    pieces, ratio, span, width = normed_refs[0].shape
    tokens = gate_refs[0].shape[1]
    per = span // tokens
    shares = len(gate_refs)
    along_sub, along_head = position()
    for distance, normed_ref in enumerate(normed_refs):
        source = along_sub ^ distance
        for apart, gate_ref in enumerate(gate_refs):
            share = (along_head ^ apart) & (shares - 1)
            first = ((1 - apart % 2) * (shares // 2) + share // 2) * tokens
            place = pl.ds(pl.multiple_of(first, tokens), tokens)
            from_rows = pl.ds(pl.multiple_of(share % per * tokens, tokens), tokens)
            for r in range(ratio):
                lanes = pl.ds(pl.multiple_of((source * ratio + r) * width, width), width)
                normed = normed_ref[share // per, r, from_rows].astype(F32)
                gate = gate_ref[source * ratio + r].astype(F32)
                rows_ref[place, lanes] = (normed * gate).astype(BF16)
    out = dot(rows_ref[...], weight_ref[...]).reshape((2,) + keep_ref.shape)
    send_ref[...] = out[0].astype(BF16)
    keep_ref[...] = out[1]


def sum_kernel(keep_ref, *refs):
    total = keep_ref[...]
    for got_ref in refs[:-1]:
        total = total + got_ref[...].astype(F32)
    refs[-1][...] = total.astype(refs[-1].dtype)


def per_device(
    outer, sub, n_head, queries, key_vectors, value_vectors, output_gate, write_strength, norm_gain, output_weight
):
    tokens, key_heads, width = queries.shape
    value_heads = value_vectors.shape[1]
    ratio = value_heads // key_heads
    sources = sub * n_head
    shard = tokens * sources
    blocks = shard // SPAN
    shard_tokens = tokens * n_head
    shape = jax.ShapeDtypeStruct

    with jax.named_scope("pack"):
        slab = ((2 + ratio) * tokens + ROW_TILE, width)
        slabs = pl.pallas_call(
            functools.partial(pack_kernel, sub),
            out_shape=[shape((2,) + slab, BF16)] * (sources // 2),
            in_specs=[ANY] * 4,
            out_specs=[VMEM] * (sources // 2),
            scratch_shapes=[
                pltpu.VMEM(queries.shape, BF16),
                pltpu.VMEM(key_vectors.shape, BF16),
                pltpu.VMEM(value_vectors.shape, BF16),
                pltpu.VMEM((value_heads, tokens), BF16),
                pltpu.VMEM((key_heads, tokens, width), BF16),
                pltpu.VMEM((key_heads, tokens, width), BF16),
                pltpu.VMEM((value_heads, tokens, width), BF16),
                pltpu.VMEM((key_heads, ROW_TILE, width), BF16),
                pltpu.SemaphoreType.DMA((4,)),
            ],
            compiler_params=params(60),
        )(queries, key_vectors, value_vectors, write_strength.T)
    group = ("sub", "head")
    slabs = list(slabs)
    for number, distance in enumerate(chip_order(sources // 2)):
        if distance:
            pairs = [(here, here ^ (2 * distance)) for here in range(sources)]
            slabs[number] = lax.ppermute(slabs[number], group, pairs)

    heads = sub * ratio
    with jax.named_scope("gates"):
        gates = pl.pallas_call(
            gate_kernel,
            out_shape=[shape((heads, tokens, width), BF16)] * n_head,
            in_specs=[VMEM, VMEM, ANY],
            out_specs=[VMEM] * n_head,
            scratch_shapes=[pltpu.VMEM((value_heads, tokens, width), BF16)],
            compiler_params=params(),
            cost_estimate=pl.CostEstimate(flops=10**9, bytes_accessed=8 * 10**6, transcendentals=0),
        )(output_gate, norm_gain.reshape(1, width), slabs[1])
    gates = list(gates)
    for distance in reversed(range(1, n_head)):
        pairs = [(here, here ^ distance) for here in range(n_head)]
        gates[distance] = lax.ppermute(gates[distance], "head", pairs)

    with jax.named_scope("other_core"):
        passed = pl.pallas_call(
            other_core_kernel,
            out_shape=shape((len(slabs),) + slab, BF16),
            in_specs=[VMEM] * len(slabs) + [ANY],
            out_specs=VMEM,
            compiler_params=params(),
        )(*slabs, gates[0])
    passed = lax.ppermute(passed, group, [(here, here ^ 1) for here in range(sources)])

    state_type = BF16 if outer == 2 else F32
    square = (blocks, ratio, width, width)
    with jax.named_scope("factors"):
        got, state, w, u, trans, prefix = pl.pallas_call(
            functools.partial(factor_kernel, tokens, ratio, sub, n_head),
            out_shape=[
                shape((sources,) + slab, BF16),
                shape((ratio, width, width), state_type),
                shape((blocks, ratio, SPAN, width), BF16),
                shape((blocks, ratio, SPAN, width), F32),
                shape(square, BF16),
                shape(square, BF16),
            ],
            in_specs=[VMEM] * (sources // 2 + 1),
            out_specs=[VMEM] * 6,
            scratch_shapes=[pltpu.VMEM(square, F32)],
            compiler_params=params(),
            cost_estimate=pl.CostEstimate(flops=4 * 10**9, bytes_accessed=4 * 10**6, transcendentals=0),
        )(*slabs, passed)

    onward = [(here, here + 1) for here in range(outer - 1)]
    incoming = lax.ppermute(state, "outer", onward)
    with jax.named_scope("spread"):
        local, reach, total = pl.pallas_call(
            functools.partial(spread_kernel, tokens, ratio),
            out_shape=[
                shape((ratio, blocks, SPAN, width), F32),
                shape((ratio, blocks, SPAN, width), BF16),
                shape((ratio, width, width), F32),
            ],
            in_specs=[VMEM] * 5,
            out_specs=[VMEM] * 3,
            compiler_params=params(),
            cost_estimate=pl.CostEstimate(flops=2 * 10**9, bytes_accessed=8 * 10**6, transcendentals=0),
        )(got, w, u, trans, prefix)
    for hop in range(outer - 2):
        passed = jnp.einsum("hde,hef->hdf", total, incoming, precision=lax.Precision.HIGHEST)
        incoming = lax.ppermute(state + passed, "outer", onward)

    pieces = shard_tokens // SPAN // 2
    columns = output_weight.shape[1]
    quarter = (n_head // 4, tokens, columns)
    by_core = [(here, here ^ 1) for here in range(n_head)]
    half = n_head // 2
    halves = []
    for flip in (1, 0):
        with jax.named_scope("join"):
            normed = pl.pallas_call(
                functools.partial(join_kernel, flip, pieces),
                out_shape=[shape((pieces, ratio, SPAN, width), BF16)] * sub,
                in_specs=[VMEM] * 3,
                out_specs=[VMEM] * sub,
                compiler_params=params(),
            )(incoming, local, reach)
        halves.append(list(normed))
    after = halves[1][0]
    for flip, normed in zip((1, 0), halves):
        for distance in reversed(range(1, sub)):
            pairs = [(here, here ^ distance) for here in range(sub)]
            normed[distance] = lax.ppermute(normed[distance], "sub", pairs)
    for flip, normed in zip((1, 0), halves):
        with jax.named_scope("project"):
            send, keep = pl.pallas_call(
                functools.partial(project_kernel, sub),
                out_shape=[shape(quarter, BF16), shape(quarter, F32)],
                in_specs=[ANY] + [VMEM] * (sub + half + 1),
                out_specs=[VMEM] * 2,
                scratch_shapes=[pltpu.VMEM((shard_tokens // 2, heads * width), BF16)],
                compiler_params=params(),
                cost_estimate=pl.CostEstimate(flops=10**9, bytes_accessed=4 * 10**6, transcendentals=0),
            )(after, *normed, *gates[half * flip : half * (flip + 1)], output_weight)
        arrived = lax.ppermute(send, "head", by_core)
        last = n_head == 4 and flip == 0
        with jax.named_scope("sum"):
            summed = pl.pallas_call(
                sum_kernel,
                out_shape=shape(quarter, BF16 if flip or last else F32),
                in_specs=[VMEM] * (3 - flip),
                out_specs=VMEM,
                compiler_params=params(),
            )(keep, arrived, *([] if flip else [passed_on]))
        if flip:
            after = summed
            passed_on = lax.ppermute(summed, "head", [(here, here ^ half) for here in range(n_head)])
    bit = 2
    while bit < half:
        mine = (lax.axis_index("head") // bit) % 2
        split = summed.reshape((summed.shape[0] // 2, 2) + summed.shape[1:])
        send = lax.dynamic_index_in_dim(split, 1 - mine, 1, False).astype(BF16)
        keep = lax.dynamic_index_in_dim(split, mine, 1, False)
        summed = keep + lax.ppermute(send, "head", [(here, here ^ bit) for here in range(n_head)]).astype(F32)
        bit *= 2
    return summed[0].astype(BF16)


def solution(mesh):
    n_seq, n_head = mesh.shape["seq"], mesh.shape["head"]

    def run(queries, key_vectors, value_vectors, output_gate, write_strength, norm_gain, output_weight):
        sub = queries.shape[1] // n_head
        outer = n_seq // sub
        split = Mesh(mesh.devices.reshape(outer, sub, n_head), ("outer", "sub", "head"))
        every = ("outer", "sub", "head")
        placed = (
            P(every, None, None),
            P(every, None, None),
            P(every, None, None),
            P(every, None, None),
            P(every, None),
            P(),
            P("head", None),
        )
        return jax.shard_map(
            functools.partial(per_device, outer, sub, n_head),
            mesh=split,
            in_specs=placed,
            out_specs=P(every, None),
            check_vma=False,
        )(queries, key_vectors, value_vectors, output_gate, write_strength, norm_gain, output_weight)

    return run
```

```python
import functools

import jax
import jax.numpy as jnp
from jax import lax
from jax.experimental import pallas as pl
from jax.experimental.pallas import tpu as pltpu
from jax.sharding import Mesh, PartitionSpec as P

SPAN = 128
EPSILON = 1e-06
F32 = jnp.float32
BF16 = jnp.bfloat16
ROW_TILE = 16
VMEM = pl.BlockSpec(memory_space=pltpu.VMEM)
SMEM = pl.BlockSpec(memory_space=pltpu.SMEM)
ANY = pl.BlockSpec(memory_space=pl.ANY)
LIGHT = pl.CostEstimate(flops=1, bytes_accessed=1, transcendentals=0)


def dot(left, right):
    return jnp.dot(left, right, preferred_element_type=F32)


def dot_nt(left, right):
    return lax.dot_general(left, right, (((1,), (1,)), ((), ())), preferred_element_type=F32)


def params(megabytes=24):
    return pltpu.CompilerParams(vmem_limit_bytes=megabytes * 2**20)


def turned(values):
    return jnp.transpose(values, (1, 0, 2))


def position():
    return lax.axis_index("sub"), lax.axis_index("head")


def pack_kernel(sub, q_hbm, k_hbm, v_hbm, b_hbm, out_ref, q_ref, k_ref, v_ref, b_ref, done):
    tokens, key_heads, width = q_hbm.shape
    ratio = v_hbm.shape[1] // key_heads
    n_head = key_heads // sub
    copies = [
        pltpu.make_async_copy(source, target, done.at[number])
        for number, (source, target) in enumerate(
            ((b_hbm, b_ref), (k_hbm, k_ref), (q_hbm, q_ref), (v_hbm, v_ref))
        )
    ]
    for copy in copies:
        copy.start()
    heads = [(peer % n_head) * sub + peer // n_head for peer in range(key_heads)]
    copies[0].wait()
    strength = jnp.concatenate([b_ref[...].astype(F32)] * (width // tokens), axis=1)
    strength = jnp.concatenate([strength, jnp.zeros((ROW_TILE, width), F32)], axis=0)
    for peer, head in enumerate(heads):
        tile = strength[head * ratio : head * ratio + ROW_TILE]
        out_ref[peer, (2 + ratio) * tokens :] = tile.astype(BF16)
    copies[1].wait()
    rows = turned(k_ref[...])
    for peer, head in enumerate(heads):
        out_ref[peer, tokens : 2 * tokens] = rows[head]
    copies[2].wait()
    rows = turned(q_ref[...])
    for peer, head in enumerate(heads):
        out_ref[peer, 0:tokens] = rows[head]
    copies[3].wait()
    rows = turned(v_ref[...])
    for peer, head in enumerate(heads):
        for r in range(ratio):
            out_ref[peer, (2 + r) * tokens : (3 + r) * tokens] = rows[head * ratio + r]


def gate_kernel(gate_ref, gain_ref, after_ref, *refs):
    unused, along_head = position()
    out_refs, gates = refs[:-1], refs[-1]
    gate = gate_ref[...].astype(F32)
    gated = gain_ref[...].astype(F32)[:, None] * (gate / (1.0 + jnp.exp(-gate)))
    gates[...] = turned(gated.astype(BF16))
    for distance, out_ref in enumerate(out_refs):
        heads = out_ref.shape[0]
        out_ref[...] = gates[pl.ds((along_head ^ distance) * heads, heads)]


def block_rows(got_ref, block, per, tokens, part):
    rows = got_ref[pl.ds(block * per, per), part * tokens : (part + 1) * tokens]
    return rows.reshape(per * tokens, rows.shape[-1])


def block_inverse(below):
    size = below[0].shape[0]
    rows = lax.broadcasted_iota(jnp.int32, (size, size), 0)
    cols = lax.broadcasted_iota(jnp.int32, (size, size), 1)
    zero = jnp.zeros((size, size), F32)
    step = 1
    solved = None
    while step < size:
        joins = (rows // (2 * step) == cols // (2 * step)) & (rows // step > cols // step)
        parts = [jnp.where(joins, matrix, zero) for matrix in below]
        if step == 1:
            solved = [
                jnp.where(rows == cols, jnp.ones_like(zero), -part).astype(BF16) for part in parts
            ]
        else:
            inner = [dot(part.astype(BF16), now).astype(BF16) for part, now in zip(parts, solved)]
            solved = [now - dot(now, mid).astype(BF16) for now, mid in zip(solved, inner)]
        step *= 2
    return solved


def factor_kernel(tokens, ratio, got_ref, state_ref, w_ref, u_ref, trans_ref, prefix_ref, add_ref):
    width = got_ref.shape[-1]
    per = SPAN // tokens
    blocks = got_ref.shape[0] // per
    rows = lax.broadcasted_iota(jnp.int32, (SPAN, SPAN), 0)
    cols = lax.broadcasted_iota(jnp.int32, (SPAN, SPAN), 1)
    lane = lax.broadcasted_iota(jnp.int32, (1, SPAN), 1)
    first = (2 + ratio) * tokens
    below, held = [], []
    for block in range(blocks):
        key = block_rows(got_ref, block, per, tokens, 1)
        gram = dot_nt(key, key)
        squares = jnp.where(rows == cols, gram, 0.0)
        key_row = lax.rsqrt(jnp.sum(squares, 0, keepdims=True) + EPSILON)
        key_col = lax.rsqrt(jnp.sum(squares, 1, keepdims=True) + EPSILON)
        lower = jnp.where(rows > cols, gram, 0.0) * key_row
        for r in range(ratio):
            strength = jnp.zeros((1, SPAN), F32)
            for place in range(per):
                piece = got_ref[block * per + place, first : first + ROW_TILE].astype(F32)[r : r + 1]
                strength = jnp.where(lane // tokens == place, piece, strength)
            scaled_col = jnp.sum(jnp.where(rows == cols, strength * key_row, 0.0), 1, keepdims=True)
            below.append(lower * scaled_col)
            held.append((block, r, key, key_col, key_row, strength))
    solved = block_inverse(below)
    for now, (block, r, key, key_col, key_row, strength) in zip(solved, held):
        value = block_rows(got_ref, block, per, tokens, 2 + r)
        weighted = now.astype(F32) * key_col * strength
        u_now = dot(weighted.astype(BF16), value)
        w_now = dot((weighted * key_row).astype(BF16), key).astype(BF16)
        both = dot(key.T, jnp.concatenate([w_now, u_now.astype(BF16)], axis=1))
        w_ref[block, r] = w_now
        u_ref[block, r] = u_now
        trans_ref[block, r] = both[:, :width].astype(BF16)
        add_ref[block, r] = both[:, width:]

    states = [jnp.zeros((width, width), F32) for r in range(ratio)]
    for block in range(blocks):
        for r in range(ratio):
            held = states[r].astype(BF16)
            prefix_ref[block, r] = held
            if block == 0:
                states[r] = add_ref[block, r]
            else:
                states[r] = states[r] + add_ref[block, r] - dot(trans_ref[block, r], held)
    for r in range(ratio):
        state_ref[r] = states[r].astype(state_ref.dtype)


def spread_kernel(
    tokens, ratio, got_ref, w_ref, u_ref, trans_ref, prefix_ref, after_ref, local_ref, reach_ref, total_ref
):
    width = got_ref.shape[-1]
    per = SPAN // tokens
    blocks = got_ref.shape[0] // per
    rows = lax.broadcasted_iota(jnp.int32, (SPAN, SPAN), 0)
    cols = lax.broadcasted_iota(jnp.int32, (SPAN, SPAN), 1)
    wide_rows = lax.broadcasted_iota(jnp.int32, (width, width), 0)
    wide_cols = lax.broadcasted_iota(jnp.int32, (width, width), 1)
    identity = jnp.where(wide_rows == wide_cols, 1.0, 0.0).astype(F32)
    carried = [identity for r in range(ratio)]
    for block in range(blocks):
        query = block_rows(got_ref, block, per, tokens, 0)
        key = block_rows(got_ref, block, per, tokens, 1)
        scores = jnp.where(rows >= cols, dot_nt(query, key), 0.0).astype(BF16)
        query_f = query.astype(F32)
        squares = jnp.sum(query_f * query_f, 1, keepdims=True)
        unit = lax.rsqrt(squares + EPSILON) * width ** (-0.5)
        left = jnp.concatenate([query, scores], axis=1)
        for r in range(ratio):
            held = carried[r].astype(BF16)
            if block == 0:
                carried[r] = identity - trans_ref[block, r].astype(F32)
            else:
                carried[r] = carried[r] - dot(trans_ref[block, r], held)
            starts = jnp.concatenate([prefix_ref[block, r], held], axis=1)
            passed = dot(w_ref[block, r], starts)
            corrected = jnp.concatenate([u_ref[block, r] - passed[:, :width], -passed[:, width:]], axis=1)
            right = jnp.concatenate([starts, corrected.astype(BF16)], axis=0)
            out = dot(left, right) * unit
            local_ref[r, block] = out[:, :width]
            reach_ref[r, block] = out[:, width:].astype(BF16)
    for r in range(ratio):
        total_ref[r] = carried[r]


def join_kernel(state_ref, local_ref, reach_ref, *out_refs):
    ratio, blocks, span, width = local_ref.shape
    pieces = out_refs[0].shape[1]
    along_sub, along_head = position()
    upper = along_head // (lax.axis_size("head") // 2)
    for distance, out_ref in enumerate(out_refs):
        target = along_sub ^ distance
        for kept in range(2):
            for piece in range(pieces):
                block = (target * 2 + (upper ^ (1 - kept))) * pieces + piece
                for r in range(ratio):
                    core = local_ref[r, block] + dot(reach_ref[r, block], state_ref[r].astype(BF16))
                    mean_square = jnp.mean(core * core, 1, keepdims=True)
                    out_ref[kept, piece, r] = (core * lax.rsqrt(mean_square + EPSILON)).astype(BF16)


def project_kernel(parts, kept, *refs):
    shares = (len(refs) - parts - 4) // 2
    normed_refs, gate_refs = refs[:parts], refs[parts : parts + shares]
    weight_ref, send_ref, keep_ref, rows_ref = refs[-4:]
    unused, pieces, ratio, span, width = normed_refs[0].shape
    tokens = gate_refs[0].shape[1]
    per = span // tokens
    along_sub, along_head = position()
    for distance, normed_ref in enumerate(normed_refs):
        source = along_sub ^ distance
        for apart, gate_ref in enumerate(gate_refs):
            share = (along_head ^ apart) & (shares - 1)
            first = ((1 - apart % 2) * (shares // 2) + share // 2) * tokens
            place = pl.ds(pl.multiple_of(first, tokens), tokens)
            from_rows = pl.ds(pl.multiple_of(share % per * tokens, tokens), tokens)
            for r in range(ratio):
                lanes = pl.ds(pl.multiple_of((source * ratio + r) * width, width), width)
                normed = normed_ref[kept, share // per, r, from_rows].astype(F32)
                gate = gate_ref[source * ratio + r].astype(F32)
                rows_ref[place, lanes] = (normed * gate).astype(BF16)
    out = dot(rows_ref[...], weight_ref[...]).reshape((2,) + keep_ref.shape)
    send_ref[...] = out[0].astype(BF16)
    keep_ref[...] = out[1]


def sum_kernel(keep_ref, *refs):
    total = keep_ref[...]
    for got_ref in refs[:-1]:
        total = total + got_ref[...].astype(F32)
    refs[-1][...] = total.astype(refs[-1].dtype)


def per_device(
    outer, sub, n_head, queries, key_vectors, value_vectors, output_gate, write_strength, norm_gain, output_weight
):
    tokens, key_heads, width = queries.shape
    value_heads = value_vectors.shape[1]
    ratio = value_heads // key_heads
    sources = sub * n_head
    shard = tokens * sources
    blocks = shard // SPAN
    shard_tokens = tokens * n_head
    shape = jax.ShapeDtypeStruct

    with jax.named_scope("pack"):
        slab = ((2 + ratio) * tokens + ROW_TILE, width)
        packed = pl.pallas_call(
            functools.partial(pack_kernel, sub),
            out_shape=shape((sources,) + slab, BF16),
            in_specs=[ANY] * 4,
            out_specs=VMEM,
            scratch_shapes=[
                pltpu.VMEM(queries.shape, BF16),
                pltpu.VMEM(key_vectors.shape, BF16),
                pltpu.VMEM(value_vectors.shape, BF16),
                pltpu.VMEM((value_heads, tokens), BF16),
                pltpu.SemaphoreType.DMA((4,)),
            ],
            compiler_params=params(60),
        )(queries, key_vectors, value_vectors, write_strength.T)
    got = lax.all_to_all(packed, ("sub", "head"), split_axis=0, concat_axis=0, tiled=True)

    state_type = BF16 if outer == 2 else F32
    square = (blocks, ratio, width, width)
    with jax.named_scope("factors"):
        state, w, u, trans, prefix = pl.pallas_call(
            functools.partial(factor_kernel, tokens, ratio),
            out_shape=[
                shape((ratio, width, width), state_type),
                shape((blocks, ratio, SPAN, width), BF16),
                shape((blocks, ratio, SPAN, width), F32),
                shape(square, BF16),
                shape(square, BF16),
            ],
            in_specs=[VMEM],
            out_specs=[VMEM] * 5,
            scratch_shapes=[pltpu.VMEM(square, F32)],
            compiler_params=params(),
            cost_estimate=LIGHT,
        )(got)

    onward = [(here, here + 1) for here in range(outer - 1)]
    incoming = lax.ppermute(state, "outer", onward)
    heads = sub * ratio
    with jax.named_scope("gates"):
        gates = pl.pallas_call(
            gate_kernel,
            out_shape=[shape((heads, tokens, width), BF16)] * n_head,
            in_specs=[VMEM, VMEM, ANY],
            out_specs=[VMEM] * n_head,
            scratch_shapes=[pltpu.VMEM((value_heads, tokens, width), BF16)],
            compiler_params=params(),
            cost_estimate=LIGHT,
        )(output_gate, norm_gain.reshape(1, width), state)
    gates = list(gates)
    for distance in reversed(range(1, n_head)):
        pairs = [(here, here ^ distance) for here in range(n_head)]
        gates[distance] = lax.ppermute(gates[distance], "head", pairs)
    with jax.named_scope("spread"):
        local, reach, total = pl.pallas_call(
            functools.partial(spread_kernel, tokens, ratio),
            out_shape=[
                shape((ratio, blocks, SPAN, width), F32),
                shape((ratio, blocks, SPAN, width), BF16),
                shape((ratio, width, width), F32),
            ],
            in_specs=[VMEM] * 5 + [ANY],
            out_specs=[VMEM] * 3,
            compiler_params=params(),
            cost_estimate=LIGHT,
        )(got, w, u, trans, prefix, gates[0])
    for hop in range(outer - 2):
        passed = jnp.einsum("hde,hef->hdf", total, incoming, precision=lax.Precision.HIGHEST)
        incoming = lax.ppermute(state + passed, "outer", onward)

    pieces = shard_tokens // SPAN // 2
    columns = output_weight.shape[1]
    quarter = (n_head // 4, tokens, columns)
    by_core = [(here, here ^ 1) for here in range(n_head)]
    half = n_head // 2
    with jax.named_scope("join"):
        normed = pl.pallas_call(
            join_kernel,
            out_shape=[shape((2, pieces, ratio, SPAN, width), BF16)] * sub,
            in_specs=[VMEM] * 3,
            out_specs=[VMEM] * sub,
            compiler_params=params(),
            cost_estimate=LIGHT,
        )(incoming, local, reach)
    normed = list(normed)
    for distance in reversed(range(1, sub)):
        pairs = [(here, here ^ distance) for here in range(sub)]
        normed[distance] = lax.ppermute(normed[distance], "sub", pairs)
    for kept in range(2):
        with jax.named_scope("project"):
            send, keep = pl.pallas_call(
                functools.partial(project_kernel, sub, kept),
                out_shape=[shape(quarter, BF16), shape(quarter, F32)],
                in_specs=[VMEM] * (sub + half) + [ANY] * half + [VMEM],
                out_specs=[VMEM] * 2,
                scratch_shapes=[pltpu.VMEM((shard_tokens // 2, heads * width), BF16)],
                compiler_params=params(),
                cost_estimate=pl.CostEstimate(flops=10**9, bytes_accessed=1, transcendentals=0),
            )(*normed, *gates[half * (1 - kept) :], *gates[: half * (1 - kept)], output_weight)
        arrived = lax.ppermute(send, "head", by_core)
        last = n_head == 4 and kept == 1
        with jax.named_scope("sum"):
            summed = pl.pallas_call(
                sum_kernel,
                out_shape=shape(quarter, F32 if kept and not last else BF16),
                in_specs=[VMEM] * (2 + kept),
                out_specs=VMEM,
                compiler_params=params(),
                cost_estimate=LIGHT,
            )(keep, arrived, *([passed_on] if kept else []))
        if not kept:
            passed_on = lax.ppermute(summed, "head", [(here, here ^ half) for here in range(n_head)])
    bit = 2
    while bit < half:
        mine = (lax.axis_index("head") // bit) % 2
        split = summed.reshape((summed.shape[0] // 2, 2) + summed.shape[1:])
        send = lax.dynamic_index_in_dim(split, 1 - mine, 1, False).astype(BF16)
        keep = lax.dynamic_index_in_dim(split, mine, 1, False)
        summed = keep + lax.ppermute(send, "head", [(here, here ^ bit) for here in range(n_head)]).astype(F32)
        bit *= 2
    return summed[0].astype(BF16)


def solution(mesh):
    n_seq, n_head = mesh.shape["seq"], mesh.shape["head"]

    def run(queries, key_vectors, value_vectors, output_gate, write_strength, norm_gain, output_weight):
        sub = queries.shape[1] // n_head
        outer = n_seq // sub
        split = Mesh(mesh.devices.reshape(outer, sub, n_head), ("outer", "sub", "head"))
        every = ("outer", "sub", "head")
        placed = (
            P(every, None, None),
            P(every, None, None),
            P(every, None, None),
            P(every, None, None),
            P(every, None),
            P(),
            P("head", None),
        )
        return jax.shard_map(
            functools.partial(per_device, outer, sub, n_head),
            mesh=split,
            in_specs=placed,
            out_specs=P(every, None),
            check_vma=False,
        )(queries, key_vectors, value_vectors, output_gate, write_strength, norm_gain, output_weight)

    return run
```

```python
import functools

import jax
import jax.numpy as jnp
from jax import lax
from jax.experimental import pallas as pl
from jax.experimental.pallas import tpu as pltpu
from jax.sharding import Mesh, PartitionSpec as P

SPAN = 128
EPSILON = 1e-06
F32 = jnp.float32
BF16 = jnp.bfloat16
ROW_TILE = 16
VMEM = pl.BlockSpec(memory_space=pltpu.VMEM)
SMEM = pl.BlockSpec(memory_space=pltpu.SMEM)
ANY = pl.BlockSpec(memory_space=pl.ANY)
LIGHT = pl.CostEstimate(flops=1, bytes_accessed=1, transcendentals=0)


def dot(left, right):
    return jnp.dot(left, right, preferred_element_type=F32)


def dot_nt(left, right):
    return lax.dot_general(left, right, (((1,), (1,)), ((), ())), preferred_element_type=F32)


def params(megabytes=24):
    return pltpu.CompilerParams(vmem_limit_bytes=megabytes * 2**20)


def turned(values):
    return jnp.transpose(values, (1, 0, 2))


def position():
    return lax.axis_index("sub"), lax.axis_index("head")


def pack_kernel(sub, q_hbm, k_hbm, v_hbm, b_hbm, out_ref, q_ref, k_ref, v_ref, b_ref, done):
    tokens, key_heads, width = q_hbm.shape
    ratio = v_hbm.shape[1] // key_heads
    n_head = key_heads // sub
    copies = [
        pltpu.make_async_copy(source, target, done.at[number])
        for number, (source, target) in enumerate(
            ((b_hbm, b_ref), (k_hbm, k_ref), (q_hbm, q_ref), (v_hbm, v_ref))
        )
    ]
    for copy in copies:
        copy.start()
    heads = [(peer % n_head) * sub + peer // n_head for peer in range(key_heads)]
    copies[0].wait()
    strength = jnp.concatenate([b_ref[...].astype(F32)] * (width // tokens), axis=1)
    strength = jnp.concatenate([strength, jnp.zeros((ROW_TILE, width), F32)], axis=0)
    for peer, head in enumerate(heads):
        tile = strength[head * ratio : head * ratio + ROW_TILE]
        out_ref[peer, (2 + ratio) * tokens :] = tile.astype(BF16)
    copies[1].wait()
    rows = turned(k_ref[...])
    for peer, head in enumerate(heads):
        out_ref[peer, tokens : 2 * tokens] = rows[head]
    copies[2].wait()
    rows = turned(q_ref[...])
    for peer, head in enumerate(heads):
        out_ref[peer, 0:tokens] = rows[head]
    copies[3].wait()
    rows = turned(v_ref[...])
    for peer, head in enumerate(heads):
        for r in range(ratio):
            out_ref[peer, (2 + r) * tokens : (3 + r) * tokens] = rows[head * ratio + r]


def gate_kernel(gate_ref, gain_ref, *refs):
    unused, along_head = position()
    out_refs, gates = refs[:-1], refs[-1]
    gate = gate_ref[...].astype(F32)
    gated = gain_ref[...].astype(F32)[:, None] * (gate / (1.0 + jnp.exp(-gate)))
    gates[...] = turned(gated.astype(BF16))
    for distance, out_ref in enumerate(out_refs):
        heads = out_ref.shape[0]
        out_ref[...] = gates[pl.ds((along_head ^ distance) * heads, heads)]


def block_rows(got_ref, block, per, tokens, part):
    rows = got_ref[pl.ds(block * per, per), part * tokens : (part + 1) * tokens]
    return rows.reshape(per * tokens, rows.shape[-1])


def block_inverse(below):
    size = below[0].shape[0]
    rows = lax.broadcasted_iota(jnp.int32, (size, size), 0)
    cols = lax.broadcasted_iota(jnp.int32, (size, size), 1)
    zero = jnp.zeros((size, size), F32)
    step = 1
    solved = None
    while step < size:
        joins = (rows // (2 * step) == cols // (2 * step)) & (rows // step > cols // step)
        parts = [jnp.where(joins, matrix, zero) for matrix in below]
        if step == 1:
            solved = [
                jnp.where(rows == cols, jnp.ones_like(zero), -part).astype(BF16) for part in parts
            ]
        else:
            inner = [dot(part.astype(BF16), now).astype(BF16) for part, now in zip(parts, solved)]
            solved = [now - dot(now, mid).astype(BF16) for now, mid in zip(solved, inner)]
        step *= 2
    return solved


def factor_kernel(tokens, ratio, n_head, got_ref, *refs):
    state_ref, w_ref, u_ref, trans_ref, prefix_ref = refs[n_head : n_head + 5]
    add_ref = refs[-1]
    width = got_ref.shape[-1]
    per = SPAN // tokens
    blocks = got_ref.shape[0] // per
    rows = lax.broadcasted_iota(jnp.int32, (SPAN, SPAN), 0)
    cols = lax.broadcasted_iota(jnp.int32, (SPAN, SPAN), 1)
    lane = lax.broadcasted_iota(jnp.int32, (1, SPAN), 1)
    first = (2 + ratio) * tokens
    below, held = [], []
    for block in range(blocks):
        key = block_rows(got_ref, block, per, tokens, 1)
        gram = dot_nt(key, key)
        squares = jnp.where(rows == cols, gram, 0.0)
        key_row = lax.rsqrt(jnp.sum(squares, 0, keepdims=True) + EPSILON)
        key_col = lax.rsqrt(jnp.sum(squares, 1, keepdims=True) + EPSILON)
        lower = jnp.where(rows > cols, gram, 0.0) * key_row
        for r in range(ratio):
            strength = jnp.zeros((1, SPAN), F32)
            for place in range(per):
                piece = got_ref[block * per + place, first : first + ROW_TILE].astype(F32)[r : r + 1]
                strength = jnp.where(lane // tokens == place, piece, strength)
            scaled_col = jnp.sum(jnp.where(rows == cols, strength * key_row, 0.0), 1, keepdims=True)
            below.append(lower * scaled_col)
            held.append((block, r, key, key_col, key_row, strength))
    solved = block_inverse(below)
    for now, (block, r, key, key_col, key_row, strength) in zip(solved, held):
        value = block_rows(got_ref, block, per, tokens, 2 + r)
        weighted = now.astype(F32) * key_col * strength
        u_now = dot(weighted.astype(BF16), value)
        w_now = dot((weighted * key_row).astype(BF16), key).astype(BF16)
        both = dot(key.T, jnp.concatenate([w_now, u_now.astype(BF16)], axis=1))
        w_ref[block, r] = w_now
        u_ref[block, r] = u_now
        trans_ref[block, r] = both[:, :width].astype(BF16)
        add_ref[block, r] = both[:, width:]

    states = [jnp.zeros((width, width), F32) for r in range(ratio)]
    for block in range(blocks):
        for r in range(ratio):
            held = states[r].astype(BF16)
            prefix_ref[block, r] = held
            if block == 0:
                states[r] = add_ref[block, r]
            else:
                states[r] = states[r] + add_ref[block, r] - dot(trans_ref[block, r], held)
    for r in range(ratio):
        state_ref[r] = states[r].astype(state_ref.dtype)


def spread_kernel(
    tokens, ratio, got_ref, w_ref, u_ref, trans_ref, prefix_ref, local_ref, reach_ref, total_ref
):
    width = got_ref.shape[-1]
    per = SPAN // tokens
    blocks = got_ref.shape[0] // per
    rows = lax.broadcasted_iota(jnp.int32, (SPAN, SPAN), 0)
    cols = lax.broadcasted_iota(jnp.int32, (SPAN, SPAN), 1)
    wide_rows = lax.broadcasted_iota(jnp.int32, (width, width), 0)
    wide_cols = lax.broadcasted_iota(jnp.int32, (width, width), 1)
    identity = jnp.where(wide_rows == wide_cols, 1.0, 0.0).astype(F32)
    carried = [identity for r in range(ratio)]
    for block in range(blocks):
        query = block_rows(got_ref, block, per, tokens, 0)
        key = block_rows(got_ref, block, per, tokens, 1)
        scores = jnp.where(rows >= cols, dot_nt(query, key), 0.0).astype(BF16)
        query_f = query.astype(F32)
        squares = jnp.sum(query_f * query_f, 1, keepdims=True)
        unit = lax.rsqrt(squares + EPSILON) * width ** (-0.5)
        left = jnp.concatenate([query, scores], axis=1)
        for r in range(ratio):
            held = carried[r].astype(BF16)
            if block == 0:
                carried[r] = identity - trans_ref[block, r].astype(F32)
            else:
                carried[r] = carried[r] - dot(trans_ref[block, r], held)
            starts = jnp.concatenate([prefix_ref[block, r], held], axis=1)
            passed = dot(w_ref[block, r], starts)
            corrected = jnp.concatenate([u_ref[block, r] - passed[:, :width], -passed[:, width:]], axis=1)
            right = jnp.concatenate([starts, corrected.astype(BF16)], axis=0)
            out = dot(left, right) * unit
            local_ref[r, block] = out[:, :width]
            reach_ref[r, block] = out[:, width:].astype(BF16)
    for r in range(ratio):
        total_ref[r] = carried[r]


def join_kernel(state_ref, local_ref, reach_ref, *out_refs):
    ratio, blocks, span, width = local_ref.shape
    pieces, parts = out_refs[0].shape[0], len(out_refs) // 2
    along_sub, along_head = position()
    upper = along_head // (lax.axis_size("head") // 2)
    for number, out_ref in enumerate(out_refs):
        target = along_sub ^ (number % parts)
        for piece in range(pieces):
            block = (target * 2 + (upper ^ (1 - number // parts))) * pieces + piece
            for r in range(ratio):
                core = local_ref[r, block] + dot(reach_ref[r, block], state_ref[r].astype(BF16))
                mean_square = jnp.mean(core * core, 1, keepdims=True)
                out_ref[piece, r] = (core * lax.rsqrt(mean_square + EPSILON)).astype(BF16)


def project_kernel(parts, shares, *refs):
    normed_refs, gate_refs = refs[:parts], refs[parts : parts + shares]
    weight_ref, *send_refs, keep_ref, rows_ref = refs[parts + 2 * shares :]
    pieces, ratio, span, width = normed_refs[0].shape
    tokens = gate_refs[0].shape[1]
    per = span // tokens
    along_sub, along_head = position()
    for distance, normed_ref in enumerate(normed_refs):
        source = along_sub ^ distance
        for apart, gate_ref in enumerate(gate_refs):
            share = (along_head ^ apart) & (shares - 1)
            first = ((1 - apart % 2) * (shares // 2) + share // 2) * tokens
            place = pl.ds(pl.multiple_of(first, tokens), tokens)
            from_rows = pl.ds(pl.multiple_of(share % per * tokens, tokens), tokens)
            for r in range(ratio):
                lanes = pl.ds(pl.multiple_of((source * ratio + r) * width, width), width)
                normed = normed_ref[share // per, r, from_rows].astype(F32)
                gate = gate_ref[source * ratio + r].astype(F32)
                rows_ref[place, lanes] = (normed * gate).astype(BF16)
    out = dot(rows_ref[...], weight_ref[...]).reshape((2,) + keep_ref.shape)
    first = 0
    for send_ref in send_refs:
        columns = send_ref.shape[-1]
        send_ref[...] = out[0, :, :, first : first + columns].astype(BF16)
        first += columns
    keep_ref[...] = out[1]


def sum_kernel(keep_ref, *refs):
    out_ref = refs[-1]
    first = 0
    for number, got_ref in enumerate(refs[:-1]):
        columns = got_ref.shape[-1]
        if first == keep_ref.shape[-1]:
            break
        total = keep_ref[:, :, first : first + columns] + got_ref[...].astype(F32)
        for more_ref in refs[:-1]:
            if more_ref.shape[-1] == keep_ref.shape[-1] and more_ref is not got_ref:
                total = total + more_ref[:, :, first : first + columns].astype(F32)
        out_ref[:, :, first : first + columns] = total.astype(out_ref.dtype)
        first += columns


def per_device(
    outer, sub, n_head, queries, key_vectors, value_vectors, output_gate, write_strength, norm_gain, output_weight
):
    tokens, key_heads, width = queries.shape
    value_heads = value_vectors.shape[1]
    ratio = value_heads // key_heads
    sources = sub * n_head
    shard = tokens * sources
    blocks = shard // SPAN
    shard_tokens = tokens * n_head
    shape = jax.ShapeDtypeStruct

    with jax.named_scope("pack"):
        slab = ((2 + ratio) * tokens + ROW_TILE, width)
        packed = pl.pallas_call(
            functools.partial(pack_kernel, sub),
            out_shape=shape((sources,) + slab, BF16),
            in_specs=[ANY] * 4,
            out_specs=VMEM,
            scratch_shapes=[
                pltpu.VMEM(queries.shape, BF16),
                pltpu.VMEM(key_vectors.shape, BF16),
                pltpu.VMEM(value_vectors.shape, BF16),
                pltpu.VMEM((value_heads, tokens), BF16),
                pltpu.SemaphoreType.DMA((4,)),
            ],
            compiler_params=params(60),
        )(queries, key_vectors, value_vectors, write_strength.T)
    got = lax.all_to_all(packed, ("sub", "head"), split_axis=0, concat_axis=0, tiled=True)

    heads = sub * ratio
    with jax.named_scope("gates"):
        gates = pl.pallas_call(
            gate_kernel,
            out_shape=[shape((heads, tokens, width), BF16)] * n_head,
            in_specs=[VMEM] * 2,
            out_specs=[VMEM] * n_head,
            scratch_shapes=[pltpu.VMEM((value_heads, tokens, width), BF16)],
            compiler_params=params(),
            cost_estimate=LIGHT,
        )(output_gate, norm_gain.reshape(1, width))

    state_type = BF16 if outer == 2 else F32
    square = (blocks, ratio, width, width)
    with jax.named_scope("factors"):
        state, w, u, trans, prefix, *gates = pl.pallas_call(
            functools.partial(factor_kernel, tokens, ratio, n_head),
            out_shape=[
                shape((ratio, width, width), state_type),
                shape((blocks, ratio, SPAN, width), BF16),
                shape((blocks, ratio, SPAN, width), F32),
                shape(square, BF16),
                shape(square, BF16),
            ]
            + [shape((heads, tokens, width), BF16)] * n_head,
            in_specs=[VMEM] + [ANY] * n_head,
            out_specs=[VMEM] * 5 + [ANY] * n_head,
            input_output_aliases={1 + number: 5 + number for number in range(n_head)},
            scratch_shapes=[pltpu.VMEM(square, F32)],
            compiler_params=params(),
            cost_estimate=LIGHT,
        )(got, *gates)

    onward = [(here, here + 1) for here in range(outer - 1)]
    incoming = lax.ppermute(state, "outer", onward)
    for distance in reversed(range(1, n_head)):
        pairs = [(here, here ^ distance) for here in range(n_head)]
        gates[distance] = lax.ppermute(gates[distance], "head", pairs)
    with jax.named_scope("spread"):
        local, reach, total = pl.pallas_call(
            functools.partial(spread_kernel, tokens, ratio),
            out_shape=[
                shape((ratio, blocks, SPAN, width), F32),
                shape((ratio, blocks, SPAN, width), BF16),
                shape((ratio, width, width), F32),
            ],
            in_specs=[VMEM] * 5,
            out_specs=[VMEM] * 3,
            compiler_params=params(),
            cost_estimate=LIGHT,
        )(got, w, u, trans, prefix)
    for hop in range(outer - 2):
        passed = jnp.einsum("hde,hef->hdf", total, incoming, precision=lax.Precision.HIGHEST)
        incoming = lax.ppermute(state + passed, "outer", onward)

    pieces = shard_tokens // SPAN // 2
    columns = output_weight.shape[1]
    quarter = (n_head // 4, tokens, columns)
    by_core = [(here, here ^ 1) for here in range(n_head)]
    half = n_head // 2
    with jax.named_scope("join"):
        normed = pl.pallas_call(
            join_kernel,
            out_shape=[shape((pieces, ratio, SPAN, width), BF16)] * (2 * sub),
            in_specs=[VMEM] * 3,
            out_specs=[VMEM] * (2 * sub),
            compiler_params=params(),
            cost_estimate=LIGHT,
        )(incoming, local, reach)
    for kept in range(2):
        mine = list(normed[kept * sub : (kept + 1) * sub])
        for distance in reversed(range(1, sub)):
            pairs = [(here, here ^ distance) for here in range(sub)]
            mine[distance] = lax.ppermute(mine[distance], "sub", pairs)
        cuts = 1 + kept
        with jax.named_scope("project"):
            *sends, keep = pl.pallas_call(
                functools.partial(project_kernel, sub, half),
                out_shape=[shape(quarter[:-1] + (columns // cuts,), BF16)] * cuts + [shape(quarter, F32)],
                in_specs=[VMEM] * (sub + half) + [ANY] * half + [VMEM],
                out_specs=[VMEM] * (cuts + 1),
                scratch_shapes=[pltpu.VMEM((shard_tokens // 2, heads * width), BF16)],
                compiler_params=params(),
                cost_estimate=LIGHT,
            )(*mine, *gates[half * (1 - kept) :], *gates[: half * (1 - kept)], output_weight)
        arrived = [lax.ppermute(send, "head", by_core) for send in sends]
        last = n_head == 4 and kept == 1
        with jax.named_scope("sum"):
            summed = pl.pallas_call(
                sum_kernel,
                out_shape=shape(quarter, F32 if kept and not last else BF16),
                in_specs=[VMEM] * (1 + cuts + kept),
                out_specs=VMEM,
                compiler_params=params(),
                cost_estimate=LIGHT,
            )(keep, *arrived, *([passed_on] if kept else []))
        if not kept:
            passed_on = lax.ppermute(summed, "head", [(here, here ^ half) for here in range(n_head)])
    bit = 2
    while bit < half:
        mine = (lax.axis_index("head") // bit) % 2
        split = summed.reshape((summed.shape[0] // 2, 2) + summed.shape[1:])
        send = lax.dynamic_index_in_dim(split, 1 - mine, 1, False).astype(BF16)
        keep = lax.dynamic_index_in_dim(split, mine, 1, False)
        summed = keep + lax.ppermute(send, "head", [(here, here ^ bit) for here in range(n_head)]).astype(F32)
        bit *= 2
    return summed[0].astype(BF16)


def solution(mesh):
    n_seq, n_head = mesh.shape["seq"], mesh.shape["head"]

    def run(queries, key_vectors, value_vectors, output_gate, write_strength, norm_gain, output_weight):
        sub = queries.shape[1] // n_head
        outer = n_seq // sub
        split = Mesh(mesh.devices.reshape(outer, sub, n_head), ("outer", "sub", "head"))
        every = ("outer", "sub", "head")
        placed = (
            P(every, None, None),
            P(every, None, None),
            P(every, None, None),
            P(every, None, None),
            P(every, None),
            P(),
            P("head", None),
        )
        return jax.shard_map(
            functools.partial(per_device, outer, sub, n_head),
            mesh=split,
            in_specs=placed,
            out_specs=P(every, None),
            check_vma=False,
        )(queries, key_vectors, value_vectors, output_gate, write_strength, norm_gain, output_weight)

    return run
```

```python
import functools

import jax
import jax.numpy as jnp
from jax import lax
from jax.experimental import pallas as pl
from jax.experimental.pallas import tpu as pltpu
from jax.sharding import Mesh, PartitionSpec as P

SPAN = 128
EPSILON = 1e-06
F32 = jnp.float32
BF16 = jnp.bfloat16
ROW_TILE = 16
VMEM = pl.BlockSpec(memory_space=pltpu.VMEM)
SMEM = pl.BlockSpec(memory_space=pltpu.SMEM)
ANY = pl.BlockSpec(memory_space=pl.ANY)
LIGHT = pl.CostEstimate(flops=1, bytes_accessed=1, transcendentals=0)


def dot(left, right):
    return jnp.dot(left, right, preferred_element_type=F32)


def dot_nt(left, right):
    return lax.dot_general(left, right, (((1,), (1,)), ((), ())), preferred_element_type=F32)


def params(megabytes=24):
    return pltpu.CompilerParams(vmem_limit_bytes=megabytes * 2**20)


def turned(values):
    return jnp.transpose(values, (1, 0, 2))


def position():
    return lax.axis_index("sub"), lax.axis_index("head")


def pack_kernel(sub, q_hbm, k_hbm, v_hbm, b_hbm, out_ref, q_ref, k_ref, v_ref, b_ref, done):
    tokens, key_heads, width = q_hbm.shape
    ratio = v_hbm.shape[1] // key_heads
    n_head = key_heads // sub
    copies = [
        pltpu.make_async_copy(source, target, done.at[number])
        for number, (source, target) in enumerate(
            ((b_hbm, b_ref), (k_hbm, k_ref), (q_hbm, q_ref), (v_hbm, v_ref))
        )
    ]
    for copy in copies:
        copy.start()
    heads = [(peer % n_head) * sub + peer // n_head for peer in range(key_heads)]
    copies[0].wait()
    strength = jnp.concatenate([b_ref[...].astype(F32)] * (width // tokens), axis=1)
    strength = jnp.concatenate([strength, jnp.zeros((ROW_TILE, width), F32)], axis=0)
    for peer, head in enumerate(heads):
        tile = strength[head * ratio : head * ratio + ROW_TILE]
        out_ref[peer, (2 + ratio) * tokens :] = tile.astype(BF16)
    copies[1].wait()
    rows = turned(k_ref[...])
    for peer, head in enumerate(heads):
        out_ref[peer, tokens : 2 * tokens] = rows[head]
    copies[2].wait()
    rows = turned(q_ref[...])
    for peer, head in enumerate(heads):
        out_ref[peer, 0:tokens] = rows[head]
    copies[3].wait()
    rows = turned(v_ref[...])
    for peer, head in enumerate(heads):
        for r in range(ratio):
            out_ref[peer, (2 + r) * tokens : (3 + r) * tokens] = rows[head * ratio + r]


def gate_kernel(gate_ref, gain_ref, *refs):
    unused, along_head = position()
    out_refs, gates = refs[:-1], refs[-1]
    gate = gate_ref[...].astype(F32)
    gated = gain_ref[...].astype(F32)[:, None] * (gate / (1.0 + jnp.exp(-gate)))
    gates[...] = turned(gated.astype(BF16))
    for distance, out_ref in enumerate(out_refs):
        heads = out_ref.shape[0]
        out_ref[...] = gates[pl.ds((along_head ^ distance) * heads, heads)]


def block_rows(got_ref, block, per, tokens, part):
    rows = got_ref[pl.ds(block * per, per), part * tokens : (part + 1) * tokens]
    return rows.reshape(per * tokens, rows.shape[-1])


def beside(matrices):
    return jnp.concatenate(matrices, axis=1)


def diagonal(matrices):
    zero = jnp.zeros_like(matrices[0])
    return jnp.concatenate(
        [beside([m if row == col else zero for col, m in enumerate(matrices)]) for row in range(len(matrices))], axis=0
    )


def parts_of(wide, count):
    width = wide.shape[1] // count
    return [wide[:, part * width : (part + 1) * width] for part in range(count)]


def block_inverse(below, count):
    size, wide = below[0].shape
    rows = lax.broadcasted_iota(jnp.int32, (size, wide), 0)
    cols = lax.broadcasted_iota(jnp.int32, (size, wide), 1) % size
    step = 1
    solved = None
    while step < size:
        joins = (rows // (2 * step) == cols // (2 * step)) & (rows // step > cols // step)
        parts = [jnp.where(joins, matrix, 0.0) for matrix in below]
        if step == 1:
            solved = [jnp.where(rows == cols, 1.0, -part).astype(BF16) for part in parts]
        else:
            inner = [
                dot(part.astype(BF16), diagonal(parts_of(now, count))).astype(BF16) for part, now in zip(parts, solved)
            ]
            solved = [
                now - dot(now, diagonal(parts_of(mid, count))).astype(BF16) for now, mid in zip(solved, inner)
            ]
        step *= 2
    return solved


def factor_kernel(tokens, ratio, n_head, got_ref, *refs):
    state_ref, w_ref, u_ref, trans_ref, prefix_ref = refs[n_head : n_head + 5]
    add_ref = refs[-1]
    width = got_ref.shape[-1]
    per = SPAN // tokens
    blocks = got_ref.shape[0] // per
    rows = lax.broadcasted_iota(jnp.int32, (SPAN, SPAN), 0)
    cols = lax.broadcasted_iota(jnp.int32, (SPAN, SPAN), 1)
    lane = lax.broadcasted_iota(jnp.int32, (1, SPAN), 1)
    first = (2 + ratio) * tokens
    below, held = [], []
    for block in range(blocks):
        key = block_rows(got_ref, block, per, tokens, 1)
        gram = dot_nt(key, key)
        squares = jnp.where(rows == cols, gram, 0.0)
        key_row = lax.rsqrt(jnp.sum(squares, 0, keepdims=True) + EPSILON)
        key_col = lax.rsqrt(jnp.sum(squares, 1, keepdims=True) + EPSILON)
        lower = jnp.where(rows > cols, gram, 0.0) * key_row
        strengths, systems = [], []
        for r in range(ratio):
            strength = jnp.zeros((1, SPAN), F32)
            for place in range(per):
                piece = got_ref[block * per + place, first : first + ROW_TILE].astype(F32)[r : r + 1]
                strength = jnp.where(lane // tokens == place, piece, strength)
            scaled_col = jnp.sum(jnp.where(rows == cols, strength * key_row, 0.0), 1, keepdims=True)
            systems.append(lower * scaled_col)
            strengths.append(strength)
        below.append(beside(systems))
        held.append((block, key, key_col, key_row, strengths))
    solved = block_inverse(below, ratio)
    for now, (block, key, key_col, key_row, strengths) in zip(solved, held):
        products = []
        for r, inverse in enumerate(parts_of(now, ratio)):
            value = block_rows(got_ref, block, per, tokens, 2 + r)
            weighted = inverse.astype(F32) * key_col * strengths[r]
            left = beside([(weighted * key_row).astype(BF16), weighted.astype(BF16)])
            w_now, u_now = parts_of(dot(left, diagonal([key, value])), 2)
            w_now = w_now.astype(BF16)
            w_ref[block, r] = w_now
            u_ref[block, r] = u_now
            products += [w_now, u_now.astype(BF16)]
        key_t = key.T
        for r in range(ratio):
            trans, add = parts_of(dot(key_t, beside(products[2 * r : 2 * r + 2])), 2)
            trans_ref[block, r] = trans.astype(BF16)
            add_ref[block, r] = add

    states = [jnp.zeros((width, width), F32) for r in range(ratio)]
    for block in range(blocks):
        for r in range(ratio):
            held = states[r].astype(BF16)
            prefix_ref[block, r] = held
            if block == 0:
                states[r] = add_ref[block, r]
            else:
                states[r] = states[r] + add_ref[block, r] - dot(trans_ref[block, r], held)
    for r in range(ratio):
        state_ref[r] = states[r].astype(state_ref.dtype)


def spread_kernel(
    tokens, ratio, got_ref, w_ref, u_ref, trans_ref, prefix_ref, local_ref, reach_ref, total_ref
):
    width = got_ref.shape[-1]
    per = SPAN // tokens
    blocks = got_ref.shape[0] // per
    rows = lax.broadcasted_iota(jnp.int32, (SPAN, SPAN), 0)
    cols = lax.broadcasted_iota(jnp.int32, (SPAN, SPAN), 1)
    wide_rows = lax.broadcasted_iota(jnp.int32, (width, width), 0)
    wide_cols = lax.broadcasted_iota(jnp.int32, (width, width), 1)
    identity = jnp.where(wide_rows == wide_cols, 1.0, 0.0).astype(F32)
    carried = [identity for r in range(ratio)]
    for block in range(blocks):
        query = block_rows(got_ref, block, per, tokens, 0)
        key = block_rows(got_ref, block, per, tokens, 1)
        scores = jnp.where(rows >= cols, dot_nt(query, key), 0.0).astype(BF16)
        query_f = query.astype(F32)
        squares = jnp.sum(query_f * query_f, 1, keepdims=True)
        unit = lax.rsqrt(squares + EPSILON) * width ** (-0.5)
        left = jnp.concatenate([query, scores], axis=1)
        for r in range(ratio):
            held = carried[r].astype(BF16)
            if block == 0:
                carried[r] = identity - trans_ref[block, r].astype(F32)
            else:
                carried[r] = carried[r] - dot(trans_ref[block, r], held)
            starts = jnp.concatenate([prefix_ref[block, r], held], axis=1)
            passed = dot(w_ref[block, r], starts)
            corrected = jnp.concatenate([u_ref[block, r] - passed[:, :width], -passed[:, width:]], axis=1)
            right = jnp.concatenate([starts, corrected.astype(BF16)], axis=0)
            out = dot(left, right) * unit
            local_ref[r, block] = out[:, :width]
            reach_ref[r, block] = out[:, width:].astype(BF16)
    for r in range(ratio):
        total_ref[r] = carried[r]


def join_kernel(order, state_ref, local_ref, reach_ref, *out_refs):
    ratio, blocks, span, width = local_ref.shape
    pieces = out_refs[0].shape[1]
    along_sub, along_head = position()
    upper = along_head // (lax.axis_size("head") // 2)
    follows = lax.axis_index("outer") > 0
    states = [jnp.where(follows, state_ref[r].astype(F32), 0.0).astype(BF16) for r in range(ratio)]
    for distance, out_ref in zip(order, out_refs):
        target = along_sub ^ distance
        for kept in range(2):
            for piece in range(pieces):
                block = (target * 2 + (upper ^ (1 - kept))) * pieces + piece
                for r in range(ratio):
                    core = local_ref[r, block] + dot(reach_ref[r, block], states[r])
                    mean_square = jnp.mean(core * core, 1, keepdims=True)
                    out_ref[kept, piece, r] = (core * lax.rsqrt(mean_square + EPSILON)).astype(BF16)


def project_kernel(order, shares, kept, *refs):
    parts = len(order)
    normed_refs, gate_refs = refs[:parts], refs[parts : parts + shares]
    weight_ref, *send_refs, keep_ref, rows_ref = refs[parts + 2 * shares :]
    unused, pieces, ratio, span, width = normed_refs[0].shape
    tokens = gate_refs[0].shape[1]
    per = span // tokens
    along_sub, along_head = position()
    for distance, normed_ref in zip(order, normed_refs):
        source = along_sub ^ distance
        for apart, gate_ref in enumerate(gate_refs):
            share = (along_head ^ apart) & (shares - 1)
            first = ((1 - apart % 2) * (shares // 2) + share // 2) * tokens
            place = pl.ds(pl.multiple_of(first, tokens), tokens)
            from_rows = pl.ds(pl.multiple_of(share % per * tokens, tokens), tokens)
            for r in range(ratio):
                lanes = pl.ds(pl.multiple_of((source * ratio + r) * width, width), width)
                normed = normed_ref[kept, share // per, r, from_rows].astype(F32)
                gate = gate_ref[source * ratio + r].astype(F32)
                rows_ref[place, lanes] = (normed * gate).astype(BF16)
    out = dot(rows_ref[...], weight_ref[...]).reshape((2,) + keep_ref.shape)
    first = 0
    for send_ref in send_refs:
        columns = send_ref.shape[-1]
        send_ref[...] = out[0, :, :, first : first + columns].astype(BF16)
        first += columns
    keep_ref[...] = out[1]


def sum_kernel(keep_ref, *refs):
    out_ref = refs[-1]
    first = 0
    for number, got_ref in enumerate(refs[:-1]):
        columns = got_ref.shape[-1]
        if first == keep_ref.shape[-1]:
            break
        total = keep_ref[:, :, first : first + columns] + got_ref[...].astype(F32)
        for more_ref in refs[:-1]:
            if more_ref.shape[-1] == keep_ref.shape[-1] and more_ref is not got_ref:
                total = total + more_ref[:, :, first : first + columns].astype(F32)
        out_ref[:, :, first : first + columns] = total.astype(out_ref.dtype)
        first += columns


def per_device(
    outer, sub, n_head, queries, key_vectors, value_vectors, output_gate, write_strength, norm_gain, output_weight
):
    tokens, key_heads, width = queries.shape
    value_heads = value_vectors.shape[1]
    ratio = value_heads // key_heads
    sources = sub * n_head
    shard = tokens * sources
    blocks = shard // SPAN
    shard_tokens = tokens * n_head
    shape = jax.ShapeDtypeStruct

    with jax.named_scope("pack"):
        slab = ((2 + ratio) * tokens + ROW_TILE, width)
        packed = pl.pallas_call(
            functools.partial(pack_kernel, sub),
            out_shape=shape((sources,) + slab, BF16),
            in_specs=[ANY] * 4,
            out_specs=VMEM,
            scratch_shapes=[
                pltpu.VMEM(queries.shape, BF16),
                pltpu.VMEM(key_vectors.shape, BF16),
                pltpu.VMEM(value_vectors.shape, BF16),
                pltpu.VMEM((value_heads, tokens), BF16),
                pltpu.SemaphoreType.DMA((4,)),
            ],
            compiler_params=params(60),
        )(queries, key_vectors, value_vectors, write_strength.T)
    got = lax.all_to_all(packed, ("sub", "head"), split_axis=0, concat_axis=0, tiled=True)

    heads = sub * ratio
    with jax.named_scope("gates"):
        gates = pl.pallas_call(
            gate_kernel,
            out_shape=[shape((heads, tokens, width), BF16)] * n_head,
            in_specs=[VMEM] * 2,
            out_specs=[VMEM] * n_head,
            scratch_shapes=[pltpu.VMEM((value_heads, tokens, width), BF16)],
            compiler_params=params(),
            cost_estimate=LIGHT,
        )(output_gate, norm_gain.reshape(1, width))

    state_type = BF16 if outer == 2 else F32
    square = (blocks, ratio, width, width)
    with jax.named_scope("factors"):
        state, w, u, trans, prefix, *gates = pl.pallas_call(
            functools.partial(factor_kernel, tokens, ratio, n_head),
            out_shape=[
                shape((ratio, width, width), state_type),
                shape((blocks, ratio, SPAN, width), BF16),
                shape((blocks, ratio, SPAN, width), F32),
                shape(square, BF16),
                shape(square, BF16),
            ]
            + [shape((heads, tokens, width), BF16)] * n_head,
            in_specs=[VMEM] + [ANY] * n_head,
            out_specs=[VMEM] * 5 + [ANY] * n_head,
            input_output_aliases={1 + number: 5 + number for number in range(n_head)},
            scratch_shapes=[pltpu.VMEM(square, F32)],
            compiler_params=params(),
            cost_estimate=LIGHT,
        )(got, *gates)

    onward = [(here, (here + 1) % outer) for here in range(outer)]
    incoming = lax.ppermute(state, "outer", onward)
    for distance in reversed(range(1, n_head)):
        pairs = [(here, here ^ distance) for here in range(n_head)]
        gates[distance] = lax.ppermute(gates[distance], "head", pairs)
    with jax.named_scope("spread"):
        local, reach, total = pl.pallas_call(
            functools.partial(spread_kernel, tokens, ratio),
            out_shape=[
                shape((ratio, blocks, SPAN, width), F32),
                shape((ratio, blocks, SPAN, width), BF16),
                shape((ratio, width, width), F32),
            ],
            in_specs=[VMEM] * 5,
            out_specs=[VMEM] * 3,
            compiler_params=params(),
            cost_estimate=LIGHT,
        )(got, w, u, trans, prefix)
    for hop in range(outer - 2):
        incoming = jnp.where(lax.axis_index("outer") == 0, 0.0, incoming)
        passed = jnp.einsum("hde,hef->hdf", total, incoming, precision=lax.Precision.HIGHEST)
        incoming = lax.ppermute(state + passed, "outer", onward)

    pieces = shard_tokens // SPAN // 2
    columns = output_weight.shape[1]
    quarter = (n_head // 4, tokens, columns)
    by_core = [(here, here ^ 1) for here in range(n_head)]
    half = n_head // 2
    order = [0] + sorted(range(1, sub), reverse=True)
    with jax.named_scope("join"):
        normed = pl.pallas_call(
            functools.partial(join_kernel, order),
            out_shape=[shape((2, pieces, ratio, SPAN, width), BF16)] * sub,
            in_specs=[VMEM] * 3,
            out_specs=[VMEM] * sub,
            compiler_params=params(),
            cost_estimate=LIGHT,
        )(incoming, local, reach)
    normed = [
        lax.ppermute(part, "sub", [(here, here ^ distance) for here in range(sub)]) if distance else part
        for distance, part in zip(order, normed)
    ]
    for kept in range(2):
        cuts = 1 + kept
        with jax.named_scope("project"):
            *sends, keep = pl.pallas_call(
                functools.partial(project_kernel, order, half, kept),
                out_shape=[shape(quarter[:-1] + (columns // cuts,), BF16)] * cuts + [shape(quarter, F32)],
                in_specs=[VMEM] * (sub + half) + [ANY] * half + [VMEM],
                out_specs=[VMEM] * (cuts + 1),
                scratch_shapes=[pltpu.VMEM((shard_tokens // 2, heads * width), BF16)],
                compiler_params=params(),
                cost_estimate=LIGHT,
            )(*normed, *gates[half * (1 - kept) :], *gates[: half * (1 - kept)], output_weight)
        arrived = [lax.ppermute(send, "head", by_core) for send in sends]
        last = n_head == 4 and kept == 1
        with jax.named_scope("sum"):
            summed = pl.pallas_call(
                sum_kernel,
                out_shape=shape(quarter, F32 if kept and not last else BF16),
                in_specs=[VMEM] * (1 + cuts + kept),
                out_specs=VMEM,
                compiler_params=params(),
                cost_estimate=LIGHT,
            )(keep, *arrived, *([passed_on] if kept else []))
        if not kept:
            passed_on = lax.ppermute(summed, "head", [(here, here ^ half) for here in range(n_head)])
    bit = 2
    while bit < half:
        mine = (lax.axis_index("head") // bit) % 2
        split = summed.reshape((summed.shape[0] // 2, 2) + summed.shape[1:])
        send = lax.dynamic_index_in_dim(split, 1 - mine, 1, False).astype(BF16)
        keep = lax.dynamic_index_in_dim(split, mine, 1, False)
        summed = keep + lax.ppermute(send, "head", [(here, here ^ bit) for here in range(n_head)]).astype(F32)
        bit *= 2
    return summed[0].astype(BF16)


def solution(mesh):
    n_seq, n_head = mesh.shape["seq"], mesh.shape["head"]

    def run(queries, key_vectors, value_vectors, output_gate, write_strength, norm_gain, output_weight):
        sub = queries.shape[1] // n_head
        outer = n_seq // sub
        split = Mesh(mesh.devices.reshape(outer, sub, n_head), ("outer", "sub", "head"))
        every = ("outer", "sub", "head")
        placed = (
            P(every, None, None),
            P(every, None, None),
            P(every, None, None),
            P(every, None, None),
            P(every, None),
            P(),
            P("head", None),
        )
        return jax.shard_map(
            functools.partial(per_device, outer, sub, n_head),
            mesh=split,
            in_specs=placed,
            out_specs=P(every, None),
            check_vma=False,
        )(queries, key_vectors, value_vectors, output_gate, write_strength, norm_gain, output_weight)

    return run
```

```python
import functools

import jax
import jax.numpy as jnp
from jax import lax
from jax.experimental import pallas as pl
from jax.experimental.pallas import tpu as pltpu
from jax.sharding import Mesh, PartitionSpec as P

SPAN = 128
EPSILON = 1e-06
F32 = jnp.float32
BF16 = jnp.bfloat16
ROW_TILE = 16
VMEM = pl.BlockSpec(memory_space=pltpu.VMEM)
SMEM = pl.BlockSpec(memory_space=pltpu.SMEM)
ANY = pl.BlockSpec(memory_space=pl.ANY)
LIGHT = pl.CostEstimate(flops=1, bytes_accessed=1, transcendentals=0)


def dot(left, right):
    return jnp.dot(left, right, preferred_element_type=F32)


def dot_nt(left, right):
    return lax.dot_general(left, right, (((1,), (1,)), ((), ())), preferred_element_type=F32)


def params(megabytes=24):
    return pltpu.CompilerParams(vmem_limit_bytes=megabytes * 2**20)


def turned(values):
    return jnp.transpose(values, (1, 0, 2))


def position():
    return lax.axis_index("sub"), lax.axis_index("head")


def pack_kernel(sub, q_hbm, k_hbm, v_hbm, b_hbm, out_hbm, q_ref, k_ref, v_ref, b_ref, out_ref, came, left):
    tokens, key_heads, width = q_hbm.shape
    ratio = v_hbm.shape[1] // key_heads
    n_head = key_heads // sub
    copies = [
        pltpu.make_async_copy(source, target, came.at[number])
        for number, (source, target) in enumerate(
            ((b_hbm, b_ref), (k_hbm, k_ref), (q_hbm, q_ref), (v_hbm, v_ref))
        )
    ]
    for copy in copies:
        copy.start()
    heads = [(peer % n_head) * sub + peer // n_head for peer in range(key_heads)]
    leaving = []

    def leave(first, size):
        rows = pl.ds(first, size)
        leaving.append(pltpu.make_async_copy(out_ref.at[:, rows], out_hbm.at[:, rows], left.at[len(leaving)]))
        leaving[-1].start()

    copies[0].wait()
    strength = jnp.concatenate([b_ref[...].astype(F32)] * (width // tokens), axis=1)
    strength = jnp.concatenate([strength, jnp.zeros((ROW_TILE, width), F32)], axis=0)
    for peer, head in enumerate(heads):
        tile = strength[head * ratio : head * ratio + ROW_TILE]
        out_ref[peer, (2 + ratio) * tokens :] = tile.astype(BF16)
    leave((2 + ratio) * tokens, ROW_TILE)
    for place, copy, ref in ((1, copies[1], k_ref), (0, copies[2], q_ref)):
        copy.wait()
        rows = turned(ref[...])
        for peer, head in enumerate(heads):
            out_ref[peer, place * tokens : (place + 1) * tokens] = rows[head]
        leave(place * tokens, tokens)
    copies[3].wait()
    rows = turned(v_ref[...])
    for r in range(ratio):
        for peer, head in enumerate(heads):
            out_ref[peer, (2 + r) * tokens : (3 + r) * tokens] = rows[head * ratio + r]
        leave((2 + r) * tokens, tokens)
    for copy in leaving:
        copy.wait()


def gate_kernel(gate_ref, gain_ref, *refs):
    unused, along_head = position()
    out_refs, gates = refs[:-1], refs[-1]
    gate = gate_ref[...].astype(F32)
    gated = gain_ref[...].astype(F32)[:, None] * (gate / (1.0 + jnp.exp(-gate)))
    gates[...] = turned(gated.astype(BF16))
    for distance, out_ref in enumerate(out_refs):
        heads = out_ref.shape[0]
        out_ref[...] = gates[pl.ds((along_head ^ distance) * heads, heads)]


def block_rows(got_ref, block, per, tokens, part):
    rows = got_ref[pl.ds(block * per, per), part * tokens : (part + 1) * tokens]
    return rows.reshape(per * tokens, rows.shape[-1])


def beside(matrices):
    return jnp.concatenate(matrices, axis=1)


def parts_of(wide, count):
    width = wide.shape[1] // count
    return [wide[:, part * width : (part + 1) * width] for part in range(count)]


def block_inverse(below):
    size = below[0].shape[0]
    half = size // 2
    rows = lax.broadcasted_iota(jnp.int32, (half, size), 0)
    cols = lax.broadcasted_iota(jnp.int32, (half, size), 1)
    first = cols < half
    cols = cols % half

    def stacked(wide):
        return jnp.concatenate(parts_of(wide, 2), axis=0)

    def side(tall):
        return jnp.where(first, tall[:half], tall[half:])

    systems = [side(matrix) for matrix in below]
    step = 1
    solved = None
    while step < half:
        joins = (rows // (2 * step) == cols // (2 * step)) & (rows // step > cols // step)
        parts = [jnp.where(joins, system, 0.0) for system in systems]
        if step == 1:
            solved = [jnp.where(rows == cols, 1.0, -part).astype(BF16) for part in parts]
        else:
            inner = [side(dot(stacked(part).astype(BF16), now)).astype(BF16) for part, now in zip(parts, solved)]
            solved = [now - side(dot(stacked(now), mid)).astype(BF16) for now, mid in zip(solved, inner)]
        step *= 2
    joined = []
    for matrix, now in zip(below, solved):
        inner = dot(matrix[half:, :half].astype(BF16), now).astype(BF16)
        outer = dot(now[:, half:], inner).astype(BF16)
        zero = jnp.zeros_like(now)
        joined.append(jnp.concatenate([jnp.where(first, now, zero), jnp.where(first, -outer, now)], axis=0))
    return joined


def factor_kernel(tokens, ratio, n_head, got_ref, *refs):
    state_ref, both_ref, trans_ref, prefix_ref = refs[n_head : n_head + 4]
    add_ref = refs[-1]
    width = got_ref.shape[-1]
    per = SPAN // tokens
    blocks = got_ref.shape[0] // per
    rows = lax.broadcasted_iota(jnp.int32, (SPAN, SPAN), 0)
    cols = lax.broadcasted_iota(jnp.int32, (SPAN, SPAN), 1)
    lane = lax.broadcasted_iota(jnp.int32, (1, SPAN), 1)
    first = (2 + ratio) * tokens
    below, held = [], []
    for block in range(blocks):
        key = block_rows(got_ref, block, per, tokens, 1)
        gram = dot_nt(key, key)
        squares = jnp.where(rows == cols, gram, 0.0)
        key_row = lax.rsqrt(jnp.sum(squares, 0, keepdims=True) + EPSILON)
        key_col = lax.rsqrt(jnp.sum(squares, 1, keepdims=True) + EPSILON)
        lower = jnp.where(rows > cols, gram, 0.0) * key_row
        strengths = []
        for r in range(ratio):
            strength = jnp.zeros((1, SPAN), F32)
            for place in range(per):
                piece = got_ref[block * per + place, first : first + ROW_TILE].astype(F32)[r : r + 1]
                strength = jnp.where(lane // tokens == place, piece, strength)
            scaled_col = jnp.sum(jnp.where(rows == cols, strength * key_row, 0.0), 1, keepdims=True)
            below.append(lower * scaled_col)
            strengths.append(strength)
        held.append((block, key, key_col, key_row, strengths))
    solved = block_inverse(below)
    for number, (block, key, key_col, key_row, strengths) in enumerate(held):
        weighted = [
            inverse.astype(F32) * key_col * strength
            for inverse, strength in zip(solved[number * ratio : (number + 1) * ratio], strengths)
        ]
        w_all = dot(jnp.concatenate([(part * key_row).astype(BF16) for part in weighted], axis=0), key).astype(BF16)
        key_t = key.T
        for r, part in enumerate(weighted):
            value = block_rows(got_ref, block, per, tokens, 2 + r)
            u_now = dot(part.astype(BF16), value).astype(BF16)
            both = beside([w_all[r * SPAN : (r + 1) * SPAN], u_now])
            both_ref[block, r] = both
            trans, add = parts_of(dot(key_t, both), 2)
            trans_ref[block, r] = trans.astype(BF16)
            add_ref[block, r] = add

    states = [jnp.zeros((width, width), F32) for r in range(ratio)]
    for block in range(blocks):
        for r in range(ratio):
            held = states[r].astype(BF16)
            prefix_ref[block, r] = held
            if block == 0:
                states[r] = add_ref[block, r]
            else:
                states[r] = states[r] + add_ref[block, r] - dot(trans_ref[block, r], held)
    for r in range(ratio):
        state_ref[r] = states[r].astype(state_ref.dtype)


def spread_kernel(
    tokens, ratio, total_too, got_ref, both_ref, trans_ref, prefix_ref, local_ref, reach_ref, total_ref
):
    width = got_ref.shape[-1]
    per = SPAN // tokens
    blocks = got_ref.shape[0] // per
    rows = lax.broadcasted_iota(jnp.int32, (SPAN, SPAN), 0)
    cols = lax.broadcasted_iota(jnp.int32, (SPAN, SPAN), 1)
    wide_rows = lax.broadcasted_iota(jnp.int32, (width, width), 0)
    wide_cols = lax.broadcasted_iota(jnp.int32, (width, width), 1)
    identity = jnp.where(wide_rows == wide_cols, 1.0, 0.0).astype(F32)
    carried = [identity for r in range(ratio)]
    for block in range(blocks):
        query = block_rows(got_ref, block, per, tokens, 0)
        key = block_rows(got_ref, block, per, tokens, 1)
        scores = jnp.where(rows >= cols, dot_nt(query, key), 0.0).astype(BF16)
        query_f = query.astype(F32)
        squares = jnp.sum(query_f * query_f, 1, keepdims=True)
        unit = lax.rsqrt(squares + EPSILON) * width ** (-0.5)
        passed = dot(scores, beside([both_ref[block, r] for r in range(ratio)]))
        for r, part in enumerate(parts_of(passed, ratio)):
            through, added = parts_of(part, 2)
            held = carried[r].astype(BF16)
            if block == 0:
                carried[r] = identity - trans_ref[block, r].astype(F32)
            elif total_too or block < blocks - 1:
                carried[r] = carried[r] - dot(trans_ref[block, r], held)
            starts = beside([prefix_ref[block, r], held])
            out = dot((query_f - through).astype(BF16), starts)
            local_ref[r, block] = (out[:, :width] + added) * unit
            reach_ref[r, block] = (out[:, width:] * unit).astype(BF16)
    for r in range(ratio):
        total_ref[r] = carried[r]


def join_kernel(order, state_ref, local_ref, reach_ref, *out_refs):
    ratio, blocks, span, width = local_ref.shape
    pieces = out_refs[0].shape[1]
    along_sub, along_head = position()
    upper = along_head // (lax.axis_size("head") // 2)
    follows = lax.axis_index("outer") > 0
    states = [jnp.where(follows, state_ref[r].astype(F32), 0.0).astype(BF16) for r in range(ratio)]
    for distance, out_ref in zip(order, out_refs):
        target = along_sub ^ distance
        for kept in range(2):
            for piece in range(pieces):
                block = (target * 2 + (upper ^ (1 - kept))) * pieces + piece
                for r in range(ratio):
                    core = local_ref[r, block] + dot(reach_ref[r, block], states[r])
                    mean_square = jnp.mean(core * core, 1, keepdims=True)
                    out_ref[kept, piece, r] = (core * lax.rsqrt(mean_square + EPSILON)).astype(BF16)


def project_kernel(order, shares, kept, *refs):
    parts = len(order)
    normed_refs, gate_refs = refs[:parts], refs[parts : parts + shares]
    weight_ref, *send_refs, keep_ref, rows_ref = refs[parts + 2 * shares :]
    unused, pieces, ratio, span, width = normed_refs[0].shape
    tokens = gate_refs[0].shape[1]
    per = span // tokens
    along_sub, along_head = position()
    for distance, normed_ref in zip(order, normed_refs):
        source = along_sub ^ distance
        for apart, gate_ref in enumerate(gate_refs):
            share = (along_head ^ apart) & (shares - 1)
            first = ((1 - apart % 2) * (shares // 2) + share // 2) * tokens
            place = pl.ds(pl.multiple_of(first, tokens), tokens)
            from_rows = pl.ds(pl.multiple_of(share % per * tokens, tokens), tokens)
            for r in range(ratio):
                lanes = pl.ds(pl.multiple_of((source * ratio + r) * width, width), width)
                normed = normed_ref[kept, share // per, r, from_rows].astype(F32)
                gate = gate_ref[source * ratio + r].astype(F32)
                rows_ref[place, lanes] = (normed * gate).astype(BF16)
    out = dot(rows_ref[...], weight_ref[...]).reshape((2,) + keep_ref.shape)
    first = 0
    for send_ref in send_refs:
        columns = send_ref.shape[-1]
        send_ref[...] = out[0, :, :, first : first + columns].astype(BF16)
        first += columns
    keep_ref[...] = out[1]


def sum_kernel(keep_ref, *refs):
    out_ref = refs[-1]
    first = 0
    for number, got_ref in enumerate(refs[:-1]):
        columns = got_ref.shape[-1]
        if first == keep_ref.shape[-1]:
            break
        total = keep_ref[:, :, first : first + columns] + got_ref[...].astype(F32)
        for more_ref in refs[:-1]:
            if more_ref.shape[-1] == keep_ref.shape[-1] and more_ref is not got_ref:
                total = total + more_ref[:, :, first : first + columns].astype(F32)
        out_ref[:, :, first : first + columns] = total.astype(out_ref.dtype)
        first += columns


def per_device(
    outer, sub, n_head, queries, key_vectors, value_vectors, output_gate, write_strength, norm_gain, output_weight
):
    tokens, key_heads, width = queries.shape
    value_heads = value_vectors.shape[1]
    ratio = value_heads // key_heads
    sources = sub * n_head
    shard = tokens * sources
    blocks = shard // SPAN
    shard_tokens = tokens * n_head
    shape = jax.ShapeDtypeStruct

    with jax.named_scope("pack"):
        slab = ((2 + ratio) * tokens + ROW_TILE, width)
        packed = pl.pallas_call(
            functools.partial(pack_kernel, sub),
            out_shape=shape((sources,) + slab, BF16),
            in_specs=[ANY] * 4,
            out_specs=ANY,
            scratch_shapes=[
                pltpu.VMEM(queries.shape, BF16),
                pltpu.VMEM(key_vectors.shape, BF16),
                pltpu.VMEM(value_vectors.shape, BF16),
                pltpu.VMEM((value_heads, tokens), BF16),
                pltpu.VMEM((sources,) + slab, BF16),
                pltpu.SemaphoreType.DMA((4,)),
                pltpu.SemaphoreType.DMA((3 + ratio,)),
            ],
            compiler_params=params(60),
        )(queries, key_vectors, value_vectors, write_strength.T)
    got = lax.all_to_all(packed, ("sub", "head"), split_axis=0, concat_axis=0, tiled=True)

    heads = sub * ratio
    with jax.named_scope("gates"):
        gates = pl.pallas_call(
            gate_kernel,
            out_shape=[shape((heads, tokens, width), BF16)] * n_head,
            in_specs=[VMEM] * 2,
            out_specs=[VMEM] * n_head,
            scratch_shapes=[pltpu.VMEM((value_heads, tokens, width), BF16)],
            compiler_params=params(),
            cost_estimate=LIGHT,
        )(output_gate, norm_gain.reshape(1, width))

    state_type = BF16 if outer == 2 else F32
    square = (blocks, ratio, width, width)
    with jax.named_scope("factors"):
        state, both, trans, prefix, *gates = pl.pallas_call(
            functools.partial(factor_kernel, tokens, ratio, n_head),
            out_shape=[
                shape((ratio, width, width), state_type),
                shape((blocks, ratio, SPAN, 2 * width), BF16),
                shape(square, BF16),
                shape(square, BF16),
            ]
            + [shape((heads, tokens, width), BF16)] * n_head,
            in_specs=[VMEM] + [ANY] * n_head,
            out_specs=[VMEM] * 4 + [ANY] * n_head,
            input_output_aliases={1 + number: 4 + number for number in range(n_head)},
            scratch_shapes=[pltpu.VMEM(square, F32)],
            compiler_params=params(),
            cost_estimate=LIGHT,
        )(got, *gates)

    onward = [(here, (here + 1) % outer) for here in range(outer)]
    incoming = lax.ppermute(state, "outer", onward)
    for distance in reversed(range(1, n_head)):
        pairs = [(here, here ^ distance) for here in range(n_head)]
        gates[distance] = lax.ppermute(gates[distance], "head", pairs)
    with jax.named_scope("spread"):
        local, reach, total = pl.pallas_call(
            functools.partial(spread_kernel, tokens, ratio, outer > 2),
            out_shape=[
                shape((ratio, blocks, SPAN, width), F32),
                shape((ratio, blocks, SPAN, width), BF16),
                shape((ratio, width, width), F32),
            ],
            in_specs=[VMEM] * 4,
            out_specs=[VMEM] * 3,
            compiler_params=params(),
            cost_estimate=LIGHT,
        )(got, both, trans, prefix)
    for hop in range(outer - 2):
        incoming = jnp.where(lax.axis_index("outer") == 0, 0.0, incoming)
        passed = jnp.einsum("hde,hef->hdf", total, incoming, precision=lax.Precision.HIGHEST)
        incoming = lax.ppermute(state + passed, "outer", onward)

    pieces = shard_tokens // SPAN // 2
    columns = output_weight.shape[1]
    quarter = (n_head // 4, tokens, columns)
    by_core = [(here, here ^ 1) for here in range(n_head)]
    half = n_head // 2
    order = [0] + sorted(range(1, sub), reverse=True)
    with jax.named_scope("join"):
        normed = pl.pallas_call(
            functools.partial(join_kernel, order),
            out_shape=[shape((2, pieces, ratio, SPAN, width), BF16)] * sub,
            in_specs=[VMEM] * 3,
            out_specs=[VMEM] * sub,
            compiler_params=params(),
            cost_estimate=LIGHT,
        )(incoming, local, reach)
    normed = [
        lax.ppermute(part, "sub", [(here, here ^ distance) for here in range(sub)]) if distance else part
        for distance, part in zip(order, normed)
    ]
    for kept in range(2):
        cuts = 1 + kept
        with jax.named_scope("project"):
            *sends, keep = pl.pallas_call(
                functools.partial(project_kernel, order, half, kept),
                out_shape=[shape(quarter[:-1] + (columns // cuts,), BF16)] * cuts + [shape(quarter, F32)],
                in_specs=[VMEM] * (sub + half) + [ANY] * half + [VMEM],
                out_specs=[VMEM] * (cuts + 1),
                scratch_shapes=[pltpu.VMEM((shard_tokens // 2, heads * width), BF16)],
                compiler_params=params(),
                cost_estimate=LIGHT,
            )(*normed, *gates[half * (1 - kept) :], *gates[: half * (1 - kept)], output_weight)
        arrived = [lax.ppermute(send, "head", by_core) for send in sends]
        last = n_head == 4 and kept == 1
        with jax.named_scope("sum"):
            summed = pl.pallas_call(
                sum_kernel,
                out_shape=shape(quarter, F32 if kept and not last else BF16),
                in_specs=[VMEM] * (1 + cuts + kept),
                out_specs=VMEM,
                compiler_params=params(),
                cost_estimate=LIGHT,
            )(keep, *arrived, *([passed_on] if kept else []))
        if not kept:
            passed_on = lax.ppermute(summed, "head", [(here, here ^ half) for here in range(n_head)])
    bit = 2
    while bit < half:
        mine = (lax.axis_index("head") // bit) % 2
        split = summed.reshape((summed.shape[0] // 2, 2) + summed.shape[1:])
        send = lax.dynamic_index_in_dim(split, 1 - mine, 1, False).astype(BF16)
        keep = lax.dynamic_index_in_dim(split, mine, 1, False)
        summed = keep + lax.ppermute(send, "head", [(here, here ^ bit) for here in range(n_head)]).astype(F32)
        bit *= 2
    return summed[0].astype(BF16)


def solution(mesh):
    n_seq, n_head = mesh.shape["seq"], mesh.shape["head"]

    def run(queries, key_vectors, value_vectors, output_gate, write_strength, norm_gain, output_weight):
        sub = queries.shape[1] // n_head
        outer = n_seq // sub
        split = Mesh(mesh.devices.reshape(outer, sub, n_head), ("outer", "sub", "head"))
        every = ("outer", "sub", "head")
        placed = (
            P(every, None, None),
            P(every, None, None),
            P(every, None, None),
            P(every, None, None),
            P(every, None),
            P(),
            P("head", None),
        )
        return jax.shard_map(
            functools.partial(per_device, outer, sub, n_head),
            mesh=split,
            in_specs=placed,
            out_specs=P(every, None),
            check_vma=False,
        )(queries, key_vectors, value_vectors, output_gate, write_strength, norm_gain, output_weight)

    return run
```

```python
import functools

import jax
import jax.numpy as jnp
from jax import lax
from jax.experimental import pallas as pl
from jax.experimental.pallas import tpu as pltpu
from jax.sharding import Mesh, PartitionSpec as P

SPAN = 128
EPSILON = 1e-06
F32 = jnp.float32
BF16 = jnp.bfloat16
ROW_TILE = 16
VMEM = pl.BlockSpec(memory_space=pltpu.VMEM)
SMEM = pl.BlockSpec(memory_space=pltpu.SMEM)
ANY = pl.BlockSpec(memory_space=pl.ANY)
LIGHT = pl.CostEstimate(flops=1, bytes_accessed=1, transcendentals=0)


def dot(left, right):
    return jnp.dot(left, right, preferred_element_type=F32)


def dot_nt(left, right):
    return lax.dot_general(left, right, (((1,), (1,)), ((), ())), preferred_element_type=F32)


def params(megabytes=24):
    return pltpu.CompilerParams(vmem_limit_bytes=megabytes * 2**20)


def turned(values):
    return jnp.transpose(values, (1, 0, 2))


def position():
    return lax.axis_index("sub"), lax.axis_index("head")


def pack_kernel(sub, q_hbm, k_hbm, v_hbm, b_hbm, out_hbm, q_ref, k_ref, v_ref, b_ref, out_ref, came, left):
    tokens, key_heads, width = q_hbm.shape
    ratio = v_hbm.shape[1] // key_heads
    n_head = key_heads // sub
    copies = [
        pltpu.make_async_copy(source, target, came.at[number])
        for number, (source, target) in enumerate(
            ((b_hbm, b_ref), (k_hbm, k_ref), (q_hbm, q_ref), (v_hbm, v_ref))
        )
    ]
    for copy in copies:
        copy.start()
    heads = [(peer % n_head) * sub + peer // n_head for peer in range(key_heads)]
    leaving = []

    def leave(first, size):
        rows = pl.ds(first, size)
        leaving.append(pltpu.make_async_copy(out_ref.at[:, rows], out_hbm.at[:, rows], left.at[len(leaving)]))
        leaving[-1].start()

    copies[0].wait()
    strength = jnp.concatenate([b_ref[...].astype(F32)] * (width // tokens), axis=1)
    strength = jnp.concatenate([strength, jnp.zeros((ROW_TILE, width), F32)], axis=0)
    for peer, head in enumerate(heads):
        tile = strength[head * ratio : head * ratio + ROW_TILE]
        out_ref[peer, (2 + ratio) * tokens :] = tile.astype(BF16)
    leave((2 + ratio) * tokens, ROW_TILE)
    for place, copy, ref in ((1, copies[1], k_ref), (0, copies[2], q_ref)):
        copy.wait()
        rows = turned(ref[...])
        for peer, head in enumerate(heads):
            out_ref[peer, place * tokens : (place + 1) * tokens] = rows[head]
        leave(place * tokens, tokens)
    copies[3].wait()
    rows = turned(v_ref[...])
    for r in range(ratio):
        for peer, head in enumerate(heads):
            out_ref[peer, (2 + r) * tokens : (3 + r) * tokens] = rows[head * ratio + r]
        leave((2 + r) * tokens, tokens)
    for copy in leaving:
        copy.wait()


def gate_kernel(gate_ref, gain_ref, *refs):
    unused, along_head = position()
    out_refs, gates = refs[:-1], refs[-1]
    gate = gate_ref[...].astype(F32)
    gated = gain_ref[...].astype(F32)[:, None] * (gate / (1.0 + jnp.exp(-gate)))
    gates[...] = turned(gated.astype(BF16))
    for distance, out_ref in enumerate(out_refs):
        heads = out_ref.shape[0]
        out_ref[...] = gates[pl.ds((along_head ^ distance) * heads, heads)]


def block_rows(got_ref, block, per, tokens, part):
    rows = got_ref[pl.ds(block * per, per), part * tokens : (part + 1) * tokens]
    return rows.reshape(per * tokens, rows.shape[-1])


def beside(matrices):
    return jnp.concatenate(matrices, axis=1)


def parts_of(wide, count):
    width = wide.shape[1] // count
    return [wide[:, part * width : (part + 1) * width] for part in range(count)]


def block_inverse(below):
    size = below[0].shape[0]
    rows = lax.broadcasted_iota(jnp.int32, (size, size), 0)
    cols = lax.broadcasted_iota(jnp.int32, (size, size), 1)
    zero = jnp.zeros((size, size), F32)
    step = 1
    solved = None
    while step < size:
        joins = (rows // (2 * step) == cols // (2 * step)) & (rows // step > cols // step)
        parts = [jnp.where(joins, matrix, zero) for matrix in below]
        if step == 1:
            solved = [
                jnp.where(rows == cols, jnp.ones_like(zero), -part).astype(BF16) for part in parts
            ]
        else:
            inner = [dot(part.astype(BF16), now).astype(BF16) for part, now in zip(parts, solved)]
            solved = [now - dot(now, mid).astype(BF16) for now, mid in zip(solved, inner)]
        step *= 2
    return solved


def factor_kernel(tokens, ratio, n_head, total_too, got_ref, *refs):
    state_ref, w_ref, u_ref, *tree_refs = refs[n_head : len(refs) - n_head]
    width = got_ref.shape[-1]
    per = SPAN // tokens
    blocks = got_ref.shape[0] // per
    rows = lax.broadcasted_iota(jnp.int32, (SPAN, SPAN), 0)
    cols = lax.broadcasted_iota(jnp.int32, (SPAN, SPAN), 1)
    lane = lax.broadcasted_iota(jnp.int32, (1, SPAN), 1)
    first = (2 + ratio) * tokens
    below, held = [], []
    for block in range(blocks):
        key = block_rows(got_ref, block, per, tokens, 1)
        gram = dot_nt(key, key)
        squares = jnp.where(rows == cols, gram, 0.0)
        key_row = lax.rsqrt(jnp.sum(squares, 0, keepdims=True) + EPSILON)
        key_col = lax.rsqrt(jnp.sum(squares, 1, keepdims=True) + EPSILON)
        lower = jnp.where(rows > cols, gram, 0.0) * key_row
        strengths = []
        for r in range(ratio):
            strength = jnp.zeros((1, SPAN), F32)
            for place in range(per):
                piece = got_ref[block * per + place, first : first + ROW_TILE].astype(F32)[r : r + 1]
                strength = jnp.where(lane // tokens == place, piece, strength)
            scaled_col = jnp.sum(jnp.where(rows == cols, strength * key_row, 0.0), 1, keepdims=True)
            below.append(lower * scaled_col)
            strengths.append(strength)
        held.append((block, key, key_col, key_row, strengths))
    solved = block_inverse(below)
    flat = [(block, r) for block in range(blocks) for r in range(ratio)]
    weighted = []
    for inverse, (block, r) in zip(solved, flat):
        unused, key, key_col, key_row, strengths = held[block]
        weighted.append(inverse.astype(F32) * key_col * strengths[r])
    for part, (block, r) in zip(weighted, flat):
        value = block_rows(got_ref, block, per, tokens, 2 + r)
        u_ref[block, r] = dot(part.astype(BF16), value)
    for part, (block, r) in zip(weighted, flat):
        unused, key, key_col, key_row, strengths = held[block]
        w_ref[block, r] = dot((part * key_row).astype(BF16), key).astype(BF16)
    turns, adds = [], []
    for block in range(blocks):
        key_t = held[block][1].T
        for r in range(ratio):
            turn, add = parts_of(dot(key_t, beside([w_ref[block, r], u_ref[block, r].astype(BF16)])), 2)
            turns.append(turn)
            adds.append(add)

    level = 0
    while len(adds) > ratio:
        count = len(adds) // ratio
        trans_ref, add_ref = tree_refs[2 * level : 2 * level + 2]
        for number in range(len(adds)):
            trans_ref[number // ratio, number % ratio] = turns[number].astype(BF16)
            add_ref[number // ratio, number % ratio] = adds[number]
        longer_turns, longer_adds = [], []
        for pair in range(count // 2):
            for r in range(ratio):
                left, right = 2 * pair * ratio + r, (2 * pair + 1) * ratio + r
                if count > 2 or total_too:
                    both = beside([turns[left], adds[left]])
                    turn, add = parts_of(both - dot(turns[right].astype(BF16), both.astype(BF16)), 2)
                    longer_turns.append(turns[right] + turn)
                else:
                    add = adds[left] - dot(turns[right].astype(BF16), adds[left].astype(BF16))
                longer_adds.append(add + adds[right])
        turns, adds = longer_turns, longer_adds
        level += 1
    for r in range(ratio):
        state_ref[r] = adds[r].astype(state_ref.dtype)
        if total_too:
            tree_refs[-1][r] = turns[r]


def tree_starts(ratio, width, tree_refs):
    rows = lax.broadcasted_iota(jnp.int32, (width, 2 * width), 0)
    cols = lax.broadcasted_iota(jnp.int32, (width, 2 * width), 1)
    neutral = jnp.where(cols == rows + width, 1.0, 0.0).astype(F32)
    starts = [None] * ratio
    for level in reversed(range(len(tree_refs) // 2)):
        trans_ref, add_ref = tree_refs[2 * level : 2 * level + 2]
        longer = []
        for number, start in enumerate(starts):
            place, r = 2 * (number // ratio), number % ratio
            add = beside([add_ref[place, r], jnp.zeros((width, width), F32)])
            if start is None:
                turn = beside([jnp.zeros((width, width), F32), trans_ref[place, r].astype(F32)])
                longer.append((start, neutral - turn + add))
            else:
                longer.append((start, start - dot(trans_ref[place, r], start.astype(BF16)) + add))
        starts = []
        for pair in range(len(longer) // ratio):
            for side in range(2):
                starts += [longer[pair * ratio + r][side] for r in range(ratio)]
    return [neutral if start is None else start for start in starts]


def spread_kernel(tokens, ratio, got_ref, w_ref, u_ref, *refs):
    tree_refs, (local_ref, reach_ref) = refs[:-2], refs[-2:]
    width = got_ref.shape[-1]
    per = SPAN // tokens
    blocks = got_ref.shape[0] // per
    rows = lax.broadcasted_iota(jnp.int32, (SPAN, SPAN), 0)
    cols = lax.broadcasted_iota(jnp.int32, (SPAN, SPAN), 1)
    starts = [start.astype(BF16) for start in tree_starts(ratio, width, tree_refs)]
    lefts, units = [], []
    for block in range(blocks):
        query = block_rows(got_ref, block, per, tokens, 0)
        key = block_rows(got_ref, block, per, tokens, 1)
        scores = jnp.where(rows >= cols, dot_nt(query, key), 0.0).astype(BF16)
        query_f = query.astype(F32)
        squares = jnp.sum(query_f * query_f, 1, keepdims=True)
        units.append(lax.rsqrt(squares + EPSILON) * width ** (-0.5))
        lefts.append(beside([query, scores]))
    flat = [(block, r) for block in range(blocks) for r in range(ratio)]
    rights = []
    for start, (block, r) in zip(starts, flat):
        through, reached = parts_of(dot(w_ref[block, r], start), 2)
        corrected = beside([u_ref[block, r] - through, -reached]).astype(BF16)
        rights.append(jnp.concatenate([start, corrected], axis=0))
    for right, (block, r) in zip(rights, flat):
        out = dot(lefts[block], right) * units[block]
        local_ref[r, block] = out[:, :width]
        reach_ref[r, block] = out[:, width:].astype(BF16)


def join_kernel(order, state_ref, local_ref, reach_ref, *out_refs):
    ratio, blocks, span, width = local_ref.shape
    pieces = out_refs[0].shape[1]
    along_sub, along_head = position()
    upper = along_head // (lax.axis_size("head") // 2)
    follows = lax.axis_index("outer") > 0
    states = [jnp.where(follows, state_ref[r].astype(F32), 0.0).astype(BF16) for r in range(ratio)]
    for distance, out_ref in zip(order, out_refs):
        target = along_sub ^ distance
        for kept in range(2):
            for piece in range(pieces):
                block = (target * 2 + (upper ^ (1 - kept))) * pieces + piece
                for r in range(ratio):
                    core = local_ref[r, block] + dot(reach_ref[r, block], states[r])
                    mean_square = jnp.mean(core * core, 1, keepdims=True)
                    out_ref[kept, piece, r] = (core * lax.rsqrt(mean_square + EPSILON)).astype(BF16)


def project_kernel(order, shares, kept, *refs):
    parts = len(order)
    normed_refs, gate_refs = refs[:parts], refs[parts : parts + shares]
    weight_ref, *send_refs, keep_ref, rows_ref = refs[parts + 2 * shares :]
    unused, pieces, ratio, span, width = normed_refs[0].shape
    tokens = gate_refs[0].shape[1]
    per = span // tokens
    along_sub, along_head = position()
    for distance, normed_ref in zip(order, normed_refs):
        source = along_sub ^ distance
        for apart, gate_ref in enumerate(gate_refs):
            share = (along_head ^ apart) & (shares - 1)
            first = ((1 - apart % 2) * (shares // 2) + share // 2) * tokens
            place = pl.ds(pl.multiple_of(first, tokens), tokens)
            from_rows = pl.ds(pl.multiple_of(share % per * tokens, tokens), tokens)
            for r in range(ratio):
                lanes = pl.ds(pl.multiple_of((source * ratio + r) * width, width), width)
                normed = normed_ref[kept, share // per, r, from_rows].astype(F32)
                gate = gate_ref[source * ratio + r].astype(F32)
                rows_ref[place, lanes] = (normed * gate).astype(BF16)
    out = dot(rows_ref[...], weight_ref[...]).reshape((2,) + keep_ref.shape)
    first = 0
    for send_ref in send_refs:
        columns = send_ref.shape[-1]
        send_ref[...] = out[0, :, :, first : first + columns].astype(BF16)
        first += columns
    keep_ref[...] = out[1]


def sum_kernel(keep_ref, *refs):
    out_ref = refs[-1]
    first = 0
    for number, got_ref in enumerate(refs[:-1]):
        columns = got_ref.shape[-1]
        if first == keep_ref.shape[-1]:
            break
        total = keep_ref[:, :, first : first + columns] + got_ref[...].astype(F32)
        for more_ref in refs[:-1]:
            if more_ref.shape[-1] == keep_ref.shape[-1] and more_ref is not got_ref:
                total = total + more_ref[:, :, first : first + columns].astype(F32)
        out_ref[:, :, first : first + columns] = total.astype(out_ref.dtype)
        first += columns


def per_device(
    outer, sub, n_head, queries, key_vectors, value_vectors, output_gate, write_strength, norm_gain, output_weight
):
    tokens, key_heads, width = queries.shape
    value_heads = value_vectors.shape[1]
    ratio = value_heads // key_heads
    sources = sub * n_head
    shard = tokens * sources
    blocks = shard // SPAN
    shard_tokens = tokens * n_head
    shape = jax.ShapeDtypeStruct

    with jax.named_scope("pack"):
        slab = ((2 + ratio) * tokens + ROW_TILE, width)
        packed = pl.pallas_call(
            functools.partial(pack_kernel, sub),
            out_shape=shape((sources,) + slab, BF16),
            in_specs=[ANY] * 4,
            out_specs=ANY,
            scratch_shapes=[
                pltpu.VMEM(queries.shape, BF16),
                pltpu.VMEM(key_vectors.shape, BF16),
                pltpu.VMEM(value_vectors.shape, BF16),
                pltpu.VMEM((value_heads, tokens), BF16),
                pltpu.VMEM((sources,) + slab, BF16),
                pltpu.SemaphoreType.DMA((4,)),
                pltpu.SemaphoreType.DMA((3 + ratio,)),
            ],
            compiler_params=params(60),
        )(queries, key_vectors, value_vectors, write_strength.T)
    got = lax.all_to_all(packed, ("sub", "head"), split_axis=0, concat_axis=0, tiled=True)

    heads = sub * ratio
    with jax.named_scope("gates"):
        gates = pl.pallas_call(
            gate_kernel,
            out_shape=[shape((heads, tokens, width), BF16)] * n_head,
            in_specs=[VMEM] * 2,
            out_specs=[VMEM] * n_head,
            scratch_shapes=[pltpu.VMEM((value_heads, tokens, width), BF16)],
            compiler_params=params(),
            cost_estimate=LIGHT,
        )(output_gate, norm_gain.reshape(1, width))

    state_type = BF16 if outer == 2 else F32
    with jax.named_scope("factors"):
        depths = []
        while blocks >> len(depths) > 1:
            depths.append(blocks >> len(depths))
        tree = []
        for depth in depths:
            tree += [shape((depth, ratio, width, width), BF16), shape((depth, ratio, width, width), F32)]
        if outer > 2:
            tree.append(shape((ratio, width, width), F32))
        out_shape = [
            shape((ratio, width, width), state_type),
            shape((blocks, ratio, SPAN, width), BF16),
            shape((blocks, ratio, SPAN, width), F32),
        ] + tree
        state, w, u, *rest = pl.pallas_call(
            functools.partial(factor_kernel, tokens, ratio, n_head, outer > 2),
            out_shape=out_shape + [shape((heads, tokens, width), BF16)] * n_head,
            in_specs=[VMEM] + [ANY] * n_head,
            out_specs=[VMEM] * len(out_shape) + [ANY] * n_head,
            input_output_aliases={1 + number: len(out_shape) + number for number in range(n_head)},
            compiler_params=params(),
            cost_estimate=LIGHT,
        )(got, *gates)
        tree, gates = rest[:-n_head], rest[-n_head:]

    onward = [(here, (here + 1) % outer) for here in range(outer)]
    incoming = lax.ppermute(state, "outer", onward)
    for distance in reversed(range(1, n_head)):
        pairs = [(here, here ^ distance) for here in range(n_head)]
        gates[distance] = lax.ppermute(gates[distance], "head", pairs)
    with jax.named_scope("spread"):
        local, reach = pl.pallas_call(
            functools.partial(spread_kernel, tokens, ratio),
            out_shape=[
                shape((ratio, blocks, SPAN, width), F32),
                shape((ratio, blocks, SPAN, width), BF16),
            ],
            in_specs=[VMEM] * (3 + 2 * len(depths)),
            out_specs=[VMEM] * 2,
            compiler_params=params(),
            cost_estimate=LIGHT,
        )(got, w, u, *tree[: 2 * len(depths)])
    for hop in range(outer - 2):
        incoming = jnp.where(lax.axis_index("outer") == 0, 0.0, incoming)
        turned_by = jnp.einsum("hde,hef->hdf", tree[-1], incoming, precision=lax.Precision.HIGHEST)
        incoming = lax.ppermute(state + incoming - turned_by, "outer", onward)

    pieces = shard_tokens // SPAN // 2
    columns = output_weight.shape[1]
    quarter = (n_head // 4, tokens, columns)
    by_core = [(here, here ^ 1) for here in range(n_head)]
    half = n_head // 2
    order = [0] + sorted(range(1, sub), reverse=True)
    with jax.named_scope("join"):
        normed = pl.pallas_call(
            functools.partial(join_kernel, order),
            out_shape=[shape((2, pieces, ratio, SPAN, width), BF16)] * sub,
            in_specs=[VMEM] * 3,
            out_specs=[VMEM] * sub,
            compiler_params=params(),
            cost_estimate=LIGHT,
        )(incoming, local, reach)
    normed = [
        lax.ppermute(part, "sub", [(here, here ^ distance) for here in range(sub)]) if distance else part
        for distance, part in zip(order, normed)
    ]
    for kept in range(2):
        cuts = 1 + kept
        with jax.named_scope("project"):
            *sends, keep = pl.pallas_call(
                functools.partial(project_kernel, order, half, kept),
                out_shape=[shape(quarter[:-1] + (columns // cuts,), BF16)] * cuts + [shape(quarter, F32)],
                in_specs=[VMEM] * (sub + half) + [ANY] * half + [VMEM],
                out_specs=[VMEM] * (cuts + 1),
                scratch_shapes=[pltpu.VMEM((shard_tokens // 2, heads * width), BF16)],
                compiler_params=params(),
                cost_estimate=LIGHT,
            )(*normed, *gates[half * (1 - kept) :], *gates[: half * (1 - kept)], output_weight)
        arrived = [lax.ppermute(send, "head", by_core) for send in sends]
        last = n_head == 4 and kept == 1
        with jax.named_scope("sum"):
            summed = pl.pallas_call(
                sum_kernel,
                out_shape=shape(quarter, F32 if kept and not last else BF16),
                in_specs=[VMEM] * (1 + cuts + kept),
                out_specs=VMEM,
                compiler_params=params(),
                cost_estimate=LIGHT,
            )(keep, *arrived, *([passed_on] if kept else []))
        if not kept:
            passed_on = lax.ppermute(summed, "head", [(here, here ^ half) for here in range(n_head)])
    bit = 2
    while bit < half:
        mine = (lax.axis_index("head") // bit) % 2
        split = summed.reshape((summed.shape[0] // 2, 2) + summed.shape[1:])
        send = lax.dynamic_index_in_dim(split, 1 - mine, 1, False).astype(BF16)
        keep = lax.dynamic_index_in_dim(split, mine, 1, False)
        summed = keep + lax.ppermute(send, "head", [(here, here ^ bit) for here in range(n_head)]).astype(F32)
        bit *= 2
    return summed[0].astype(BF16)


def solution(mesh):
    n_seq, n_head = mesh.shape["seq"], mesh.shape["head"]

    def run(queries, key_vectors, value_vectors, output_gate, write_strength, norm_gain, output_weight):
        sub = queries.shape[1] // n_head
        outer = n_seq // sub
        split = Mesh(mesh.devices.reshape(outer, sub, n_head), ("outer", "sub", "head"))
        every = ("outer", "sub", "head")
        placed = (
            P(every, None, None),
            P(every, None, None),
            P(every, None, None),
            P(every, None, None),
            P(every, None),
            P(),
            P("head", None),
        )
        return jax.shard_map(
            functools.partial(per_device, outer, sub, n_head),
            mesh=split,
            in_specs=placed,
            out_specs=P(every, None),
            check_vma=False,
        )(queries, key_vectors, value_vectors, output_gate, write_strength, norm_gain, output_weight)

    return run
```

```python
import functools

import jax
import jax.numpy as jnp
from jax import lax
from jax.experimental import pallas as pl
from jax.experimental.pallas import tpu as pltpu
from jax.sharding import Mesh, PartitionSpec as P

SPAN = 128
EPSILON = 1e-06
F32 = jnp.float32
BF16 = jnp.bfloat16
ROW_TILE = 16
VMEM = pl.BlockSpec(memory_space=pltpu.VMEM)
SMEM = pl.BlockSpec(memory_space=pltpu.SMEM)
ANY = pl.BlockSpec(memory_space=pl.ANY)
LIGHT = pl.CostEstimate(flops=1, bytes_accessed=1, transcendentals=0)


def dot(left, right):
    return jnp.dot(left, right, preferred_element_type=F32)


def dot_nt(left, right):
    return lax.dot_general(left, right, (((1,), (1,)), ((), ())), preferred_element_type=F32)


def params(megabytes=24):
    return pltpu.CompilerParams(vmem_limit_bytes=megabytes * 2**20)


def turned(values):
    return jnp.transpose(values, (1, 0, 2))


def position():
    return lax.axis_index("sub"), lax.axis_index("head")


def pack_kernel(sub, q_hbm, k_hbm, v_hbm, b_hbm, out_hbm, q_ref, k_ref, v_ref, b_ref, out_ref, came, left):
    tokens, key_heads, width = q_hbm.shape
    ratio = v_hbm.shape[1] // key_heads
    n_head = key_heads // sub
    copies = [
        pltpu.make_async_copy(source, target, came.at[number])
        for number, (source, target) in enumerate(
            ((b_hbm, b_ref), (k_hbm, k_ref), (q_hbm, q_ref), (v_hbm, v_ref))
        )
    ]
    for copy in copies:
        copy.start()
    heads = [(peer % n_head) * sub + peer // n_head for peer in range(key_heads)]
    leaving = []

    def leave(first, size):
        rows = pl.ds(first, size)
        leaving.append(pltpu.make_async_copy(out_ref.at[:, rows], out_hbm.at[:, rows], left.at[len(leaving)]))
        leaving[-1].start()

    copies[0].wait()
    strength = jnp.concatenate([b_ref[...].astype(F32)] * (width // tokens), axis=1)
    strength = jnp.concatenate([strength, jnp.zeros((ROW_TILE, width), F32)], axis=0)
    for peer, head in enumerate(heads):
        tile = strength[head * ratio : head * ratio + ROW_TILE]
        out_ref[peer, (2 + ratio) * tokens :] = tile.astype(BF16)
    leave((2 + ratio) * tokens, ROW_TILE)
    for place, copy, ref in ((1, copies[1], k_ref), (0, copies[2], q_ref)):
        copy.wait()
        rows = turned(ref[...])
        for peer, head in enumerate(heads):
            out_ref[peer, place * tokens : (place + 1) * tokens] = rows[head]
        leave(place * tokens, tokens)
    copies[3].wait()
    rows = turned(v_ref[...])
    for r in range(ratio):
        for peer, head in enumerate(heads):
            out_ref[peer, (2 + r) * tokens : (3 + r) * tokens] = rows[head * ratio + r]
        leave((2 + r) * tokens, tokens)
    for copy in leaving:
        copy.wait()


def gate_kernel(gate_ref, gain_ref, *refs):
    unused, along_head = position()
    out_refs, gates = refs[:-1], refs[-1]
    gate = gate_ref[...].astype(F32)
    gated = gain_ref[...].astype(F32)[:, None] * (gate / (1.0 + jnp.exp(-gate)))
    gates[...] = turned(gated.astype(BF16))
    for distance, out_ref in enumerate(out_refs):
        heads = out_ref.shape[0]
        out_ref[...] = gates[pl.ds((along_head ^ distance) * heads, heads)]


def block_rows(got_ref, block, per, tokens, part):
    rows = got_ref[pl.ds(block * per, per), part * tokens : (part + 1) * tokens]
    return rows.reshape(per * tokens, rows.shape[-1])


def beside(matrices):
    return jnp.concatenate(matrices, axis=1)


def parts_of(wide, count):
    width = wide.shape[1] // count
    return [wide[:, part * width : (part + 1) * width] for part in range(count)]


def block_inverse(below):
    size = below[0].shape[0]
    rows = lax.broadcasted_iota(jnp.int32, (size, size), 0)
    cols = lax.broadcasted_iota(jnp.int32, (size, size), 1)
    zero = jnp.zeros((size, size), F32)
    step = 1
    solved = None
    while step < size:
        joins = (rows // (2 * step) == cols // (2 * step)) & (rows // step > cols // step)
        parts = [jnp.where(joins, matrix, zero) for matrix in below]
        if step == 1:
            solved = [
                jnp.where(rows == cols, jnp.ones_like(zero), -part).astype(BF16) for part in parts
            ]
        else:
            inner = [dot(part.astype(BF16), now).astype(BF16) for part, now in zip(parts, solved)]
            solved = [now - dot(now, mid).astype(BF16) for now, mid in zip(solved, inner)]
        step *= 2
    return solved


def factor_kernel(tokens, ratio, n_head, total_too, got_ref, *refs):
    state_ref, w_ref, u_ref, *tree_refs = refs[n_head:]
    width = got_ref.shape[-1]
    per = SPAN // tokens
    blocks = got_ref.shape[0] // per
    rows = lax.broadcasted_iota(jnp.int32, (SPAN, SPAN), 0)
    cols = lax.broadcasted_iota(jnp.int32, (SPAN, SPAN), 1)
    lane = lax.broadcasted_iota(jnp.int32, (1, SPAN), 1)
    first = (2 + ratio) * tokens
    below, held = [], []
    for block in range(blocks):
        key = block_rows(got_ref, block, per, tokens, 1)
        gram = dot_nt(key, key)
        squares = jnp.where(rows == cols, gram, 0.0)
        key_row = lax.rsqrt(jnp.sum(squares, 0, keepdims=True) + EPSILON)
        key_col = lax.rsqrt(jnp.sum(squares, 1, keepdims=True) + EPSILON)
        lower = jnp.where(rows > cols, gram, 0.0) * key_row
        strengths = []
        for r in range(ratio):
            strength = jnp.zeros((1, SPAN), F32)
            for place in range(per):
                piece = got_ref[block * per + place, first : first + ROW_TILE].astype(F32)[r : r + 1]
                strength = jnp.where(lane // tokens == place, piece, strength)
            scaled_col = jnp.sum(jnp.where(rows == cols, strength * key_row, 0.0), 1, keepdims=True)
            below.append(lower * scaled_col)
            strengths.append(strength)
        held.append((block, key, key_col, key_row, strengths))
    solved = block_inverse(below)
    flat = [(block, r) for block in range(blocks) for r in range(ratio)]
    weighted = []
    for inverse, (block, r) in zip(solved, flat):
        unused, key, key_col, key_row, strengths = held[block]
        weighted.append(inverse.astype(F32) * key_col * strengths[r])
    for part, (block, r) in zip(weighted, flat):
        value = block_rows(got_ref, block, per, tokens, 2 + r)
        u_ref[block, r] = dot(part.astype(BF16), value)
    for part, (block, r) in zip(weighted, flat):
        unused, key, key_col, key_row, strengths = held[block]
        w_ref[block, r] = dot((part * key_row).astype(BF16), key).astype(BF16)
    turns, adds = [], []
    for block in range(blocks):
        key_t = held[block][1].T
        for r in range(ratio):
            turn, add = parts_of(dot(key_t, beside([w_ref[block, r], u_ref[block, r].astype(BF16)])), 2)
            turns.append(turn)
            adds.append(add)

    level = 0
    while len(adds) > ratio:
        count = len(adds) // ratio
        trans_ref, add_ref = tree_refs[2 * level : 2 * level + 2]
        for number in range(len(adds)):
            trans_ref[number // ratio, number % ratio] = turns[number].astype(BF16)
            add_ref[number // ratio, number % ratio] = adds[number]
        longer_turns, longer_adds = [], []
        for pair in range(count // 2):
            for r in range(ratio):
                left, right = 2 * pair * ratio + r, (2 * pair + 1) * ratio + r
                if count > 2 or total_too:
                    both = beside([turns[left], adds[left]])
                    turn, add = parts_of(both - dot(turns[right].astype(BF16), both.astype(BF16)), 2)
                    longer_turns.append(turns[right] + turn)
                else:
                    add = adds[left] - dot(turns[right].astype(BF16), adds[left].astype(BF16))
                longer_adds.append(add + adds[right])
        turns, adds = longer_turns, longer_adds
        level += 1
    for r in range(ratio):
        state_ref[r] = adds[r].astype(state_ref.dtype)
        if total_too:
            tree_refs[-1][r] = turns[r]


def tree_starts(ratio, width, tree_refs):
    rows = lax.broadcasted_iota(jnp.int32, (width, 2 * width), 0)
    cols = lax.broadcasted_iota(jnp.int32, (width, 2 * width), 1)
    neutral = jnp.where(cols == rows + width, 1.0, 0.0).astype(F32)
    starts = [None] * ratio
    for level in reversed(range(len(tree_refs) // 2)):
        trans_ref, add_ref = tree_refs[2 * level : 2 * level + 2]
        longer = []
        for number, start in enumerate(starts):
            place, r = 2 * (number // ratio), number % ratio
            add = beside([add_ref[place, r], jnp.zeros((width, width), F32)])
            if start is None:
                turn = beside([jnp.zeros((width, width), F32), trans_ref[place, r].astype(F32)])
                longer.append((start, neutral - turn + add))
            else:
                longer.append((start, start - dot(trans_ref[place, r], start.astype(BF16)) + add))
        starts = []
        for pair in range(len(longer) // ratio):
            for side in range(2):
                starts += [longer[pair * ratio + r][side] for r in range(ratio)]
    return [neutral if start is None else start for start in starts]


def spread_kernel(tokens, ratio, got_ref, w_ref, u_ref, *refs):
    tree_refs, (local_ref, reach_ref) = refs[:-2], refs[-2:]
    width = got_ref.shape[-1]
    per = SPAN // tokens
    blocks = got_ref.shape[0] // per
    rows = lax.broadcasted_iota(jnp.int32, (SPAN, SPAN), 0)
    cols = lax.broadcasted_iota(jnp.int32, (SPAN, SPAN), 1)
    starts = [start.astype(BF16) for start in tree_starts(ratio, width, tree_refs)]
    lefts, units = [], []
    for block in range(blocks):
        query = block_rows(got_ref, block, per, tokens, 0)
        key = block_rows(got_ref, block, per, tokens, 1)
        scores = jnp.where(rows >= cols, dot_nt(query, key), 0.0).astype(BF16)
        query_f = query.astype(F32)
        squares = jnp.sum(query_f * query_f, 1, keepdims=True)
        units.append(lax.rsqrt(squares + EPSILON) * width ** (-0.5))
        lefts.append(beside([query, scores]))
    flat = [(block, r) for block in range(blocks) for r in range(ratio)]
    rights = []
    for start, (block, r) in zip(starts, flat):
        through, reached = parts_of(dot(w_ref[block, r], start), 2)
        corrected = beside([u_ref[block, r] - through, -reached]).astype(BF16)
        rights.append(jnp.concatenate([start, corrected], axis=0))
    for right, (block, r) in zip(rights, flat):
        out = dot(lefts[block], right) * units[block]
        local_ref[r, block] = out[:, :width]
        reach_ref[r, block] = out[:, width:].astype(BF16)


def join_kernel(order, state_ref, local_ref, reach_ref, *out_refs):
    ratio, blocks, span, width = local_ref.shape
    pieces = out_refs[0].shape[1]
    along_sub, along_head = position()
    upper = along_head // (lax.axis_size("head") // 2)
    follows = lax.axis_index("outer") > 0
    states = [jnp.where(follows, state_ref[r].astype(F32), 0.0).astype(BF16) for r in range(ratio)]
    for distance, out_ref in zip(order, out_refs):
        target = along_sub ^ distance
        for kept in range(2):
            for piece in range(pieces):
                block = (target * 2 + (upper ^ (1 - kept))) * pieces + piece
                for r in range(ratio):
                    core = local_ref[r, block] + dot(reach_ref[r, block], states[r])
                    mean_square = jnp.mean(core * core, 1, keepdims=True)
                    out_ref[kept, piece, r] = (core * lax.rsqrt(mean_square + EPSILON)).astype(BF16)


def project_kernel(order, shares, kept, *refs):
    parts = len(order)
    normed_refs, gate_refs = refs[:parts], refs[parts : parts + shares]
    weight_ref, *send_refs, keep_ref, rows_ref = refs[parts + 2 * shares :]
    unused, pieces, ratio, span, width = normed_refs[0].shape
    tokens = gate_refs[0].shape[1]
    per = span // tokens
    along_sub, along_head = position()
    for distance, normed_ref in zip(order, normed_refs):
        source = along_sub ^ distance
        for apart, gate_ref in enumerate(gate_refs):
            share = (along_head ^ apart) & (shares - 1)
            first = ((1 - apart % 2) * (shares // 2) + share // 2) * tokens
            place = pl.ds(pl.multiple_of(first, tokens), tokens)
            from_rows = pl.ds(pl.multiple_of(share % per * tokens, tokens), tokens)
            for r in range(ratio):
                lanes = pl.ds(pl.multiple_of((source * ratio + r) * width, width), width)
                normed = normed_ref[kept, share // per, r, from_rows].astype(F32)
                gate = gate_ref[source * ratio + r].astype(F32)
                rows_ref[place, lanes] = (normed * gate).astype(BF16)
    out = dot(rows_ref[...], weight_ref[...]).reshape((2,) + keep_ref.shape)
    first = 0
    for send_ref in send_refs:
        columns = send_ref.shape[-1]
        send_ref[...] = out[0, :, :, first : first + columns].astype(BF16)
        first += columns
    keep_ref[...] = out[1]


def sum_kernel(keep_ref, *refs):
    out_ref = refs[-1]
    first = 0
    for number, got_ref in enumerate(refs[:-1]):
        columns = got_ref.shape[-1]
        if first == keep_ref.shape[-1]:
            break
        total = keep_ref[:, :, first : first + columns] + got_ref[...].astype(F32)
        for more_ref in refs[:-1]:
            if more_ref.shape[-1] == keep_ref.shape[-1] and more_ref is not got_ref:
                total = total + more_ref[:, :, first : first + columns].astype(F32)
        out_ref[:, :, first : first + columns] = total.astype(out_ref.dtype)
        first += columns


def per_device(
    outer, sub, n_head, queries, key_vectors, value_vectors, output_gate, write_strength, norm_gain, output_weight
):
    tokens, key_heads, width = queries.shape
    value_heads = value_vectors.shape[1]
    ratio = value_heads // key_heads
    sources = sub * n_head
    shard = tokens * sources
    blocks = shard // SPAN
    shard_tokens = tokens * n_head
    shape = jax.ShapeDtypeStruct

    with jax.named_scope("pack"):
        slab = ((2 + ratio) * tokens + ROW_TILE, width)
        packed = pl.pallas_call(
            functools.partial(pack_kernel, sub),
            out_shape=shape((sources,) + slab, BF16),
            in_specs=[ANY] * 4,
            out_specs=ANY,
            scratch_shapes=[
                pltpu.VMEM(queries.shape, BF16),
                pltpu.VMEM(key_vectors.shape, BF16),
                pltpu.VMEM(value_vectors.shape, BF16),
                pltpu.VMEM((value_heads, tokens), BF16),
                pltpu.VMEM((sources,) + slab, BF16),
                pltpu.SemaphoreType.DMA((4,)),
                pltpu.SemaphoreType.DMA((3 + ratio,)),
            ],
            compiler_params=params(60),
        )(queries, key_vectors, value_vectors, write_strength.T)
    got = lax.all_to_all(packed, ("sub", "head"), split_axis=0, concat_axis=0, tiled=True)

    heads = sub * ratio
    with jax.named_scope("gates"):
        gates = pl.pallas_call(
            gate_kernel,
            out_shape=[shape((heads, tokens, width), BF16)] * n_head,
            in_specs=[VMEM] * 2,
            out_specs=[VMEM] * n_head,
            scratch_shapes=[pltpu.VMEM((value_heads, tokens, width), BF16)],
            compiler_params=params(),
            cost_estimate=LIGHT,
        )(output_gate, norm_gain.reshape(1, width))

    gates = list(gates)
    for distance in reversed(range(1, n_head)):
        pairs = [(here, here ^ distance) for here in range(n_head)]
        gates[distance] = lax.ppermute(gates[distance], "head", pairs)

    state_type = BF16 if outer == 2 else F32
    with jax.named_scope("factors"):
        depths = []
        while blocks >> len(depths) > 1:
            depths.append(blocks >> len(depths))
        tree = []
        for depth in depths:
            tree += [shape((depth, ratio, width, width), BF16), shape((depth, ratio, width, width), F32)]
        if outer > 2:
            tree.append(shape((ratio, width, width), F32))
        out_shape = [
            shape((ratio, width, width), state_type),
            shape((blocks, ratio, SPAN, width), BF16),
            shape((blocks, ratio, SPAN, width), F32),
        ] + tree
        state, w, u, *tree = pl.pallas_call(
            functools.partial(factor_kernel, tokens, ratio, n_head, outer > 2),
            out_shape=out_shape,
            in_specs=[VMEM] + [ANY] * n_head,
            out_specs=[VMEM] * len(out_shape),
            compiler_params=params(),
            cost_estimate=LIGHT,
        )(got, *gates)

    onward = [(here, (here + 1) % outer) for here in range(outer)]
    incoming = lax.ppermute(state, "outer", onward)
    with jax.named_scope("spread"):
        local, reach = pl.pallas_call(
            functools.partial(spread_kernel, tokens, ratio),
            out_shape=[
                shape((ratio, blocks, SPAN, width), F32),
                shape((ratio, blocks, SPAN, width), BF16),
            ],
            in_specs=[VMEM] * (3 + 2 * len(depths)),
            out_specs=[VMEM] * 2,
            compiler_params=params(),
            cost_estimate=LIGHT,
        )(got, w, u, *tree[: 2 * len(depths)])
    for hop in range(outer - 2):
        incoming = jnp.where(lax.axis_index("outer") == 0, 0.0, incoming)
        turned_by = jnp.einsum("hde,hef->hdf", tree[-1], incoming, precision=lax.Precision.HIGHEST)
        incoming = lax.ppermute(state + incoming - turned_by, "outer", onward)

    pieces = shard_tokens // SPAN // 2
    columns = output_weight.shape[1]
    quarter = (n_head // 4, tokens, columns)
    by_core = [(here, here ^ 1) for here in range(n_head)]
    half = n_head // 2
    order = [0] + sorted(range(1, sub), reverse=True)
    with jax.named_scope("join"):
        normed = pl.pallas_call(
            functools.partial(join_kernel, order),
            out_shape=[shape((2, pieces, ratio, SPAN, width), BF16)] * sub,
            in_specs=[VMEM] * 3,
            out_specs=[VMEM] * sub,
            compiler_params=params(),
            cost_estimate=LIGHT,
        )(incoming, local, reach)
    normed = [
        lax.ppermute(part, "sub", [(here, here ^ distance) for here in range(sub)]) if distance else part
        for distance, part in zip(order, normed)
    ]
    for kept in range(2):
        cuts = 1 + kept
        with jax.named_scope("project"):
            *sends, keep = pl.pallas_call(
                functools.partial(project_kernel, order, half, kept),
                out_shape=[shape(quarter[:-1] + (columns // cuts,), BF16)] * cuts + [shape(quarter, F32)],
                in_specs=[VMEM] * (sub + half) + [ANY] * half + [VMEM],
                out_specs=[VMEM] * (cuts + 1),
                scratch_shapes=[pltpu.VMEM((shard_tokens // 2, heads * width), BF16)],
                compiler_params=params(),
                cost_estimate=LIGHT,
            )(*normed, *gates[half * (1 - kept) :], *gates[: half * (1 - kept)], output_weight)
        arrived = [lax.ppermute(send, "head", by_core) for send in sends]
        last = n_head == 4 and kept == 1
        with jax.named_scope("sum"):
            summed = pl.pallas_call(
                sum_kernel,
                out_shape=shape(quarter, F32 if kept and not last else BF16),
                in_specs=[VMEM] * (1 + cuts + kept),
                out_specs=VMEM,
                compiler_params=params(),
                cost_estimate=LIGHT,
            )(keep, *arrived, *([passed_on] if kept else []))
        if not kept:
            passed_on = lax.ppermute(summed, "head", [(here, here ^ half) for here in range(n_head)])
    bit = 2
    while bit < half:
        mine = (lax.axis_index("head") // bit) % 2
        split = summed.reshape((summed.shape[0] // 2, 2) + summed.shape[1:])
        send = lax.dynamic_index_in_dim(split, 1 - mine, 1, False).astype(BF16)
        keep = lax.dynamic_index_in_dim(split, mine, 1, False)
        summed = keep + lax.ppermute(send, "head", [(here, here ^ bit) for here in range(n_head)]).astype(F32)
        bit *= 2
    return summed[0].astype(BF16)


def solution(mesh):
    n_seq, n_head = mesh.shape["seq"], mesh.shape["head"]

    def run(queries, key_vectors, value_vectors, output_gate, write_strength, norm_gain, output_weight):
        sub = queries.shape[1] // n_head
        outer = n_seq // sub
        split = Mesh(mesh.devices.reshape(outer, sub, n_head), ("outer", "sub", "head"))
        every = ("outer", "sub", "head")
        placed = (
            P(every, None, None),
            P(every, None, None),
            P(every, None, None),
            P(every, None, None),
            P(every, None),
            P(),
            P("head", None),
        )
        return jax.shard_map(
            functools.partial(per_device, outer, sub, n_head),
            mesh=split,
            in_specs=placed,
            out_specs=P(every, None),
            check_vma=False,
        )(queries, key_vectors, value_vectors, output_gate, write_strength, norm_gain, output_weight)

    return run
```

```python
import functools

import jax
import jax.numpy as jnp
from jax import lax
from jax.experimental import pallas as pl
from jax.experimental.pallas import tpu as pltpu
from jax.sharding import Mesh, PartitionSpec as P

SPAN = 128
EPSILON = 1e-06
F32 = jnp.float32
BF16 = jnp.bfloat16
ROW_TILE = 16
VMEM = pl.BlockSpec(memory_space=pltpu.VMEM)
SMEM = pl.BlockSpec(memory_space=pltpu.SMEM)
ANY = pl.BlockSpec(memory_space=pl.ANY)
LIGHT = pl.CostEstimate(flops=1, bytes_accessed=1, transcendentals=0)


def dot(left, right):
    return jnp.dot(left, right, preferred_element_type=F32)


def dot_nt(left, right):
    return lax.dot_general(left, right, (((1,), (1,)), ((), ())), preferred_element_type=F32)


def params(megabytes=24):
    return pltpu.CompilerParams(vmem_limit_bytes=megabytes * 2**20)


def turned(values):
    return jnp.transpose(values, (1, 0, 2))


def position():
    return lax.axis_index("sub"), lax.axis_index("head")


def pack_kernel(q_hbm, k_hbm, v_hbm, b_hbm, out_hbm, q_ref, k_ref, v_ref, b_ref, out_ref, came, left):
    tokens, key_heads, width = q_hbm.shape
    ratio = v_hbm.shape[1] // key_heads
    copies = [
        pltpu.make_async_copy(source, target, came.at[number])
        for number, (source, target) in enumerate(
            ((b_hbm, b_ref), (k_hbm, k_ref), (q_hbm, q_ref), (v_hbm, v_ref))
        )
    ]
    for copy in copies:
        copy.start()
    heads = range(key_heads)
    leaving = []

    def leave(first, size):
        rows = pl.ds(first, size)
        leaving.append(pltpu.make_async_copy(out_ref.at[:, rows], out_hbm.at[:, rows], left.at[len(leaving)]))
        leaving[-1].start()

    copies[0].wait()
    strength = jnp.concatenate([b_ref[...].astype(F32)] * (width // tokens), axis=1)
    strength = jnp.concatenate([strength, jnp.zeros((ROW_TILE, width), F32)], axis=0)
    for peer, head in enumerate(heads):
        tile = strength[head * ratio : head * ratio + ROW_TILE]
        out_ref[peer, (2 + ratio) * tokens :] = tile.astype(BF16)
    leave((2 + ratio) * tokens, ROW_TILE)
    for place, copy, ref in ((1, copies[1], k_ref), (0, copies[2], q_ref)):
        copy.wait()
        rows = turned(ref[...])
        for peer, head in enumerate(heads):
            out_ref[peer, place * tokens : (place + 1) * tokens] = rows[head]
        leave(place * tokens, tokens)
    copies[3].wait()
    rows = turned(v_ref[...])
    for r in range(ratio):
        for peer, head in enumerate(heads):
            out_ref[peer, (2 + r) * tokens : (3 + r) * tokens] = rows[head * ratio + r]
        leave((2 + r) * tokens, tokens)
    for copy in leaving:
        copy.wait()


def gate_kernel(gate_ref, gain_ref, *refs):
    unused, along_head = position()
    out_refs, gates = refs[:-1], refs[-1]
    gate = gate_ref[...].astype(F32)
    gated = gain_ref[...].astype(F32)[:, None] * (gate / (1.0 + jnp.exp(-gate)))
    gates[...] = turned(gated.astype(BF16))
    for distance, out_ref in enumerate(out_refs):
        heads = out_ref.shape[0]
        out_ref[...] = gates[pl.ds((along_head ^ distance) * heads, heads)]


def block_slabs(blocks, sub, sources):
    n_head = sources // sub
    places = [source % n_head * sub + source // n_head for source in range(sources)]
    per = sources // blocks
    return [places[block * per : (block + 1) * per] for block in range(blocks)]


def block_rows(got_ref, slabs, tokens, part):
    return jnp.concatenate([got_ref[slab, part * tokens : (part + 1) * tokens] for slab in slabs], axis=0)


def beside(matrices):
    return jnp.concatenate(matrices, axis=1)


def parts_of(wide, count):
    width = wide.shape[1] // count
    return [wide[:, part * width : (part + 1) * width] for part in range(count)]


def block_inverse(below):
    size = below[0].shape[0]
    rows = lax.broadcasted_iota(jnp.int32, (size, size), 0)
    cols = lax.broadcasted_iota(jnp.int32, (size, size), 1)
    zero = jnp.zeros((size, size), F32)
    step = 1
    solved = None
    while step < size:
        joins = (rows // (2 * step) == cols // (2 * step)) & (rows // step > cols // step)
        parts = [jnp.where(joins, matrix, zero) for matrix in below]
        if step == 1:
            solved = [
                jnp.where(rows == cols, jnp.ones_like(zero), -part).astype(BF16) for part in parts
            ]
        else:
            inner = [dot(part.astype(BF16), now).astype(BF16) for part, now in zip(parts, solved)]
            solved = [now - dot(now, mid).astype(BF16) for now, mid in zip(solved, inner)]
        step *= 2
    return solved


def factor_kernel(tokens, ratio, sub, n_head, total_too, got_ref, *refs):
    state_ref, w_ref, u_ref, *tree_refs = refs[n_head : len(refs) - n_head]
    width = got_ref.shape[-1]
    per = SPAN // tokens
    blocks = got_ref.shape[0] // per
    slabs = block_slabs(blocks, sub, got_ref.shape[0])
    rows = lax.broadcasted_iota(jnp.int32, (SPAN, SPAN), 0)
    cols = lax.broadcasted_iota(jnp.int32, (SPAN, SPAN), 1)
    lane = lax.broadcasted_iota(jnp.int32, (1, SPAN), 1)
    first = (2 + ratio) * tokens
    below, held = [], []
    for block in range(blocks):
        key = block_rows(got_ref, slabs[block], tokens, 1)
        gram = dot_nt(key, key)
        squares = jnp.where(rows == cols, gram, 0.0)
        key_row = lax.rsqrt(jnp.sum(squares, 0, keepdims=True) + EPSILON)
        key_col = lax.rsqrt(jnp.sum(squares, 1, keepdims=True) + EPSILON)
        lower = jnp.where(rows > cols, gram, 0.0) * key_row
        strengths = []
        for r in range(ratio):
            strength = jnp.zeros((1, SPAN), F32)
            for place in range(per):
                piece = got_ref[slabs[block][place], first : first + ROW_TILE].astype(F32)[r : r + 1]
                strength = jnp.where(lane // tokens == place, piece, strength)
            scaled_col = jnp.sum(jnp.where(rows == cols, strength * key_row, 0.0), 1, keepdims=True)
            below.append(lower * scaled_col)
            strengths.append(strength)
        held.append((block, key, key_col, key_row, strengths))
    solved = block_inverse(below)
    flat = [(block, r) for block in range(blocks) for r in range(ratio)]
    weighted = []
    for inverse, (block, r) in zip(solved, flat):
        unused, key, key_col, key_row, strengths = held[block]
        weighted.append(inverse.astype(F32) * key_col * strengths[r])
    for part, (block, r) in zip(weighted, flat):
        value = block_rows(got_ref, slabs[block], tokens, 2 + r)
        u_ref[block, r] = dot(part.astype(BF16), value)
    for part, (block, r) in zip(weighted, flat):
        unused, key, key_col, key_row, strengths = held[block]
        w_ref[block, r] = dot((part * key_row).astype(BF16), key).astype(BF16)
    turns, adds = [], []
    for block in range(blocks):
        key_t = held[block][1].T
        for r in range(ratio):
            turn, add = parts_of(dot(key_t, beside([w_ref[block, r], u_ref[block, r].astype(BF16)])), 2)
            turns.append(turn)
            adds.append(add)

    level = 0
    while len(adds) > ratio:
        count = len(adds) // ratio
        trans_ref, add_ref = tree_refs[2 * level : 2 * level + 2]
        for number in range(len(adds)):
            trans_ref[number // ratio, number % ratio] = turns[number].astype(BF16)
            add_ref[number // ratio, number % ratio] = adds[number]
        longer_turns, longer_adds = [], []
        for pair in range(count // 2):
            for r in range(ratio):
                left, right = 2 * pair * ratio + r, (2 * pair + 1) * ratio + r
                if count > 2 or total_too:
                    both = beside([turns[left], adds[left]])
                    turn, add = parts_of(both - dot(turns[right].astype(BF16), both.astype(BF16)), 2)
                    longer_turns.append(turns[right] + turn)
                else:
                    add = adds[left] - dot(turns[right].astype(BF16), adds[left].astype(BF16))
                longer_adds.append(add + adds[right])
        turns, adds = longer_turns, longer_adds
        level += 1
    for r in range(ratio):
        state_ref[r] = adds[r].astype(state_ref.dtype)
        if total_too:
            tree_refs[-1][r] = turns[r]


def tree_starts(ratio, width, tree_refs):
    rows = lax.broadcasted_iota(jnp.int32, (width, 2 * width), 0)
    cols = lax.broadcasted_iota(jnp.int32, (width, 2 * width), 1)
    neutral = jnp.where(cols == rows + width, 1.0, 0.0).astype(F32)
    starts = [None] * ratio
    for level in reversed(range(len(tree_refs) // 2)):
        trans_ref, add_ref = tree_refs[2 * level : 2 * level + 2]
        longer = []
        for number, start in enumerate(starts):
            place, r = 2 * (number // ratio), number % ratio
            add = beside([add_ref[place, r], jnp.zeros((width, width), F32)])
            if start is None:
                turn = beside([jnp.zeros((width, width), F32), trans_ref[place, r].astype(F32)])
                longer.append((start, neutral - turn + add))
            else:
                longer.append((start, start - dot(trans_ref[place, r], start.astype(BF16)) + add))
        starts = []
        for pair in range(len(longer) // ratio):
            for side in range(2):
                starts += [longer[pair * ratio + r][side] for r in range(ratio)]
    return [neutral if start is None else start for start in starts]


def spread_kernel(tokens, ratio, sub, got_ref, w_ref, u_ref, *refs):
    tree_refs, (local_ref, reach_ref) = refs[:-2], refs[-2:]
    width = got_ref.shape[-1]
    per = SPAN // tokens
    blocks = got_ref.shape[0] // per
    slabs = block_slabs(blocks, sub, got_ref.shape[0])
    rows = lax.broadcasted_iota(jnp.int32, (SPAN, SPAN), 0)
    cols = lax.broadcasted_iota(jnp.int32, (SPAN, SPAN), 1)
    starts = [start.astype(BF16) for start in tree_starts(ratio, width, tree_refs)]
    lefts, units = [], []
    for block in range(blocks):
        query = block_rows(got_ref, slabs[block], tokens, 0)
        key = block_rows(got_ref, slabs[block], tokens, 1)
        scores = jnp.where(rows >= cols, dot_nt(query, key), 0.0).astype(BF16)
        query_f = query.astype(F32)
        squares = jnp.sum(query_f * query_f, 1, keepdims=True)
        units.append(lax.rsqrt(squares + EPSILON) * width ** (-0.5))
        lefts.append(beside([query, scores]))
    flat = [(block, r) for block in range(blocks) for r in range(ratio)]
    rights = []
    for start, (block, r) in zip(starts, flat):
        through, reached = parts_of(dot(w_ref[block, r], start), 2)
        corrected = beside([u_ref[block, r] - through, -reached]).astype(BF16)
        rights.append(jnp.concatenate([start, corrected], axis=0))
    for right, (block, r) in zip(rights, flat):
        out = dot(lefts[block], right) * units[block]
        local_ref[r, block] = out[:, :width]
        reach_ref[r, block] = out[:, width:].astype(BF16)


def join_kernel(order, state_ref, local_ref, reach_ref, *out_refs):
    ratio, blocks, span, width = local_ref.shape
    pieces = out_refs[0].shape[1]
    along_sub, along_head = position()
    upper = along_head // (lax.axis_size("head") // 2)
    follows = lax.axis_index("outer") > 0
    states = [jnp.where(follows, state_ref[r].astype(F32), 0.0).astype(BF16) for r in range(ratio)]
    for distance, out_ref in zip(order, out_refs):
        target = along_sub ^ distance
        for kept in range(2):
            for piece in range(pieces):
                block = (target * 2 + (upper ^ (1 - kept))) * pieces + piece
                for r in range(ratio):
                    core = local_ref[r, block] + dot(reach_ref[r, block], states[r])
                    mean_square = jnp.mean(core * core, 1, keepdims=True)
                    out_ref[kept, piece, r] = (core * lax.rsqrt(mean_square + EPSILON)).astype(BF16)


def project_kernel(order, shares, kept, mine, *refs):
    parts = len(order)
    normed_refs, gate_refs = refs[:parts], refs[parts : parts + shares]
    weight_ref, *out_refs, rows_ref = refs[parts + 2 * shares :]
    unused, pieces, ratio, span, width = normed_refs[0].shape
    tokens = gate_refs[0].shape[1]
    per = span // tokens
    along_sub, along_head = position()
    for distance, normed_ref in zip(order, normed_refs):
        source = along_sub ^ distance
        for apart in range(1 - mine, shares, 2):
            share = (along_head ^ apart) & (shares - 1)
            place = pl.ds(pl.multiple_of(share // 2 * tokens, tokens), tokens)
            from_rows = pl.ds(pl.multiple_of(share % per * tokens, tokens), tokens)
            for r in range(ratio):
                lanes = pl.ds(pl.multiple_of((source * ratio + r) * width, width), width)
                normed = normed_ref[kept, share // per, r, from_rows].astype(F32)
                gate = gate_refs[apart][source * ratio + r].astype(F32)
                rows_ref[place, lanes] = (normed * gate).astype(BF16)
    first = 0
    for out_ref in out_refs:
        columns = out_ref.shape[-1]
        out = dot(rows_ref[...], weight_ref[:, first : first + columns])
        out_ref[...] = out.reshape(out_ref.shape).astype(out_ref.dtype)
        first += columns


def sum_kernel(keep_ref, *refs):
    out_ref = refs[-1]
    first = 0
    for number, got_ref in enumerate(refs[:-1]):
        columns = got_ref.shape[-1]
        if first == keep_ref.shape[-1]:
            break
        total = keep_ref[:, :, first : first + columns] + got_ref[...].astype(F32)
        for more_ref in refs[:-1]:
            if more_ref.shape[-1] == keep_ref.shape[-1] and more_ref is not got_ref:
                total = total + more_ref[:, :, first : first + columns].astype(F32)
        out_ref[:, :, first : first + columns] = total.astype(out_ref.dtype)
        first += columns


def per_device(
    outer, sub, n_head, queries, key_vectors, value_vectors, output_gate, write_strength, norm_gain, output_weight
):
    tokens, key_heads, width = queries.shape
    value_heads = value_vectors.shape[1]
    ratio = value_heads // key_heads
    sources = sub * n_head
    shard = tokens * sources
    blocks = shard // SPAN
    shard_tokens = tokens * n_head
    shape = jax.ShapeDtypeStruct

    with jax.named_scope("pack"):
        slab = ((2 + ratio) * tokens + ROW_TILE, width)
        packed = pl.pallas_call(
            pack_kernel,
            out_shape=shape((sources,) + slab, BF16),
            in_specs=[ANY] * 4,
            out_specs=ANY,
            scratch_shapes=[
                pltpu.VMEM(queries.shape, BF16),
                pltpu.VMEM(key_vectors.shape, BF16),
                pltpu.VMEM(value_vectors.shape, BF16),
                pltpu.VMEM((value_heads, tokens), BF16),
                pltpu.VMEM((sources,) + slab, BF16),
                pltpu.SemaphoreType.DMA((4,)),
                pltpu.SemaphoreType.DMA((3 + ratio,)),
            ],
            compiler_params=params(60),
        )(queries, key_vectors, value_vectors, write_strength.T)
    got = lax.all_to_all(packed, ("head", "sub"), split_axis=0, concat_axis=0, tiled=True)

    heads = sub * ratio
    with jax.named_scope("gates"):
        gates = pl.pallas_call(
            gate_kernel,
            out_shape=[shape((heads, tokens, width), BF16)] * n_head,
            in_specs=[VMEM] * 2,
            out_specs=[VMEM] * n_head,
            scratch_shapes=[pltpu.VMEM((value_heads, tokens, width), BF16)],
            compiler_params=params(),
            cost_estimate=LIGHT,
        )(output_gate, norm_gain.reshape(1, width))

    by_core = [(here, here ^ 1) for here in range(n_head)]
    gates = list(gates)
    gates[1] = lax.ppermute(gates[1], "head", by_core)

    state_type = BF16 if outer == 2 else F32
    with jax.named_scope("factors"):
        depths = []
        while blocks >> len(depths) > 1:
            depths.append(blocks >> len(depths))
        tree = []
        for depth in depths:
            tree += [shape((depth, ratio, width, width), BF16), shape((depth, ratio, width, width), F32)]
        if outer > 2:
            tree.append(shape((ratio, width, width), F32))
        out_shape = [
            shape((ratio, width, width), state_type),
            shape((blocks, ratio, SPAN, width), BF16),
            shape((blocks, ratio, SPAN, width), F32),
        ] + tree
        state, w, u, *rest = pl.pallas_call(
            functools.partial(factor_kernel, tokens, ratio, sub, n_head, outer > 2),
            out_shape=out_shape + [shape((heads, tokens, width), BF16)] * n_head,
            in_specs=[VMEM] + [ANY] * n_head,
            out_specs=[VMEM] * len(out_shape) + [ANY] * n_head,
            input_output_aliases={1 + number: len(out_shape) + number for number in range(n_head)},
            compiler_params=params(),
            cost_estimate=LIGHT,
        )(got, *gates)
        tree, gates = rest[:-n_head], rest[-n_head:]

    onward = [(here, (here + 1) % outer) for here in range(outer)]
    incoming = lax.ppermute(state, "outer", onward)
    for distance in reversed(range(2, n_head)):
        pairs = [(here, here ^ distance) for here in range(n_head)]
        gates[distance] = lax.ppermute(gates[distance], "head", pairs)
    with jax.named_scope("spread"):
        local, reach = pl.pallas_call(
            functools.partial(spread_kernel, tokens, ratio, sub),
            out_shape=[
                shape((ratio, blocks, SPAN, width), F32),
                shape((ratio, blocks, SPAN, width), BF16),
            ],
            in_specs=[VMEM] * (3 + 2 * len(depths)),
            out_specs=[VMEM] * 2,
            compiler_params=params(),
            cost_estimate=LIGHT,
        )(got, w, u, *tree[: 2 * len(depths)])
    for hop in range(outer - 2):
        incoming = jnp.where(lax.axis_index("outer") == 0, 0.0, incoming)
        turned_by = jnp.einsum("hde,hef->hdf", tree[-1], incoming, precision=lax.Precision.HIGHEST)
        incoming = lax.ppermute(state + incoming - turned_by, "outer", onward)

    pieces = shard_tokens // SPAN // 2
    columns = output_weight.shape[1]
    quarter = (n_head // 4, tokens, columns)
    half = n_head // 2
    order = [0] + sorted(range(1, sub), reverse=True)
    with jax.named_scope("join"):
        normed = pl.pallas_call(
            functools.partial(join_kernel, order),
            out_shape=[shape((2, pieces, ratio, SPAN, width), BF16)] * sub,
            in_specs=[VMEM] * 3,
            out_specs=[VMEM] * sub,
            compiler_params=params(),
            cost_estimate=LIGHT,
        )(incoming, local, reach)
    normed = [
        lax.ppermute(part, "sub", [(here, here ^ distance) for here in range(sub)]) if distance else part
        for distance, part in zip(order, normed)
    ]
    for kept in range(2):
        cuts = 1 + kept
        operands = [*normed, *gates[half * (1 - kept) :], *gates[: half * (1 - kept)], output_weight]
        results = []
        for mine in range(2):
            pieces_of = 1 if mine else cuts
            with jax.named_scope("project"):
                results += pl.pallas_call(
                    functools.partial(project_kernel, order, half, kept, mine),
                    out_shape=[shape(quarter[:-1] + (columns // pieces_of,), F32 if mine else BF16)] * pieces_of,
                    in_specs=[VMEM] * (sub + half) + [ANY] * half + [VMEM],
                    out_specs=[VMEM] * pieces_of,
                    scratch_shapes=[pltpu.VMEM((shard_tokens // 4, heads * width), BF16)],
                    compiler_params=params(),
                    cost_estimate=LIGHT,
                )(*operands)
        *sends, keep = results
        arrived = [lax.ppermute(send, "head", by_core) for send in sends]
        last = n_head == 4 and kept == 1
        with jax.named_scope("sum"):
            summed = pl.pallas_call(
                sum_kernel,
                out_shape=shape(quarter, F32 if kept and not last else BF16),
                in_specs=[VMEM] * (1 + cuts + kept),
                out_specs=VMEM,
                compiler_params=params(),
                cost_estimate=LIGHT,
            )(keep, *arrived, *([passed_on] if kept else []))
        if not kept:
            passed_on = lax.ppermute(summed, "head", [(here, here ^ half) for here in range(n_head)])
    bit = 2
    while bit < half:
        mine = (lax.axis_index("head") // bit) % 2
        split = summed.reshape((summed.shape[0] // 2, 2) + summed.shape[1:])
        send = lax.dynamic_index_in_dim(split, 1 - mine, 1, False).astype(BF16)
        keep = lax.dynamic_index_in_dim(split, mine, 1, False)
        summed = keep + lax.ppermute(send, "head", [(here, here ^ bit) for here in range(n_head)]).astype(F32)
        bit *= 2
    return summed[0].astype(BF16)


def solution(mesh):
    n_seq, n_head = mesh.shape["seq"], mesh.shape["head"]

    def run(queries, key_vectors, value_vectors, output_gate, write_strength, norm_gain, output_weight):
        sub = queries.shape[1] // n_head
        outer = n_seq // sub
        split = Mesh(mesh.devices.reshape(outer, sub, n_head), ("outer", "sub", "head"))
        every = ("outer", "sub", "head")
        placed = (
            P(every, None, None),
            P(every, None, None),
            P(every, None, None),
            P(every, None, None),
            P(every, None),
            P(),
            P("head", None),
        )
        return jax.shard_map(
            functools.partial(per_device, outer, sub, n_head),
            mesh=split,
            in_specs=placed,
            out_specs=P(every, None),
            check_vma=False,
        )(queries, key_vectors, value_vectors, output_gate, write_strength, norm_gain, output_weight)

    return run
```

```python
import functools

import jax
import jax.numpy as jnp
from jax import lax
from jax.experimental import pallas as pl
from jax.experimental.pallas import tpu as pltpu
from jax.sharding import Mesh, PartitionSpec as P

SPAN = 128
EPSILON = 1e-06
F32 = jnp.float32
BF16 = jnp.bfloat16
ROW_TILE = 16
VMEM = pl.BlockSpec(memory_space=pltpu.VMEM)
SMEM = pl.BlockSpec(memory_space=pltpu.SMEM)
ANY = pl.BlockSpec(memory_space=pl.ANY)
LIGHT = pl.CostEstimate(flops=1, bytes_accessed=1, transcendentals=0)


def dot(left, right):
    return jnp.dot(left, right, preferred_element_type=F32)


def dot_nt(left, right):
    return lax.dot_general(left, right, (((1,), (1,)), ((), ())), preferred_element_type=F32)


def params(megabytes=24):
    return pltpu.CompilerParams(vmem_limit_bytes=megabytes * 2**20)


def turned(values):
    return jnp.transpose(values, (1, 0, 2))


def split_axis(name, size):
    return tuple(f"{name}{bit}" for bit in reversed(range(size.bit_length() - 1)))


def partner_order(sub, n_head):
    heads = split_axis("head", n_head)
    return heads[-1:] + heads[:-1] + split_axis("sub", sub)


def partner(source, sub, n_head):
    axes = split_axis("sub", sub) + split_axis("head", n_head)
    bits = {name: source >> (len(axes) - 1 - number) & 1 for number, name in enumerate(axes)}
    place = 0
    for name in partner_order(sub, n_head):
        place = 2 * place + bits[name]
    return place


def position(sub, n_head):
    return lax.axis_index(split_axis("sub", sub)), lax.axis_index(split_axis("head", n_head))


def pack_kernel(sub, q_hbm, k_hbm, v_hbm, b_hbm, out_hbm, q_ref, k_ref, v_ref, b_ref, out_ref, came, left):
    tokens, key_heads, width = q_hbm.shape
    ratio = v_hbm.shape[1] // key_heads
    copies = [
        pltpu.make_async_copy(source, target, came.at[number])
        for number, (source, target) in enumerate(
            ((b_hbm, b_ref), (k_hbm, k_ref), (q_hbm, q_ref), (v_hbm, v_ref))
        )
    ]
    for copy in copies:
        copy.start()
    n_head = key_heads // sub
    heads = [head % sub * n_head + head // sub for head in range(key_heads)]
    heads = [partner(source, sub, n_head) for source in heads]
    heads = [heads.index(peer) for peer in range(key_heads)]
    leaving = []

    def leave(first, size):
        rows = pl.ds(first, size)
        leaving.append(pltpu.make_async_copy(out_ref.at[:, rows], out_hbm.at[:, rows], left.at[len(leaving)]))
        leaving[-1].start()

    copies[0].wait()
    strength = jnp.concatenate([b_ref[...].astype(F32)] * (width // tokens), axis=1)
    strength = jnp.concatenate([strength, jnp.zeros((ROW_TILE, width), F32)], axis=0)
    for peer, head in enumerate(heads):
        tile = strength[head * ratio : head * ratio + ROW_TILE]
        out_ref[peer, (2 + ratio) * tokens :] = tile.astype(BF16)
    leave((2 + ratio) * tokens, ROW_TILE)
    for place, copy, ref in ((1, copies[1], k_ref), (0, copies[2], q_ref)):
        copy.wait()
        rows = turned(ref[...])
        for peer, head in enumerate(heads):
            out_ref[peer, place * tokens : (place + 1) * tokens] = rows[head]
        leave(place * tokens, tokens)
    copies[3].wait()
    rows = turned(v_ref[...])
    for r in range(ratio):
        for peer, head in enumerate(heads):
            out_ref[peer, (2 + r) * tokens : (3 + r) * tokens] = rows[head * ratio + r]
        leave((2 + r) * tokens, tokens)
    for copy in leaving:
        copy.wait()


def gate_kernel(sub, n_head, gate_ref, gain_ref, own_ref, other_ref, *refs):
    pair_refs, gates = refs[:-1], refs[-1]
    heads = own_ref.shape[1]
    unused, along_head = position(sub, n_head)
    gate = gate_ref[...].astype(F32)
    gated = gain_ref[...].astype(F32)[:, None] * (gate / (1.0 + jnp.exp(-gate)))
    gates[...] = turned(gated.astype(BF16))

    def group(distance):
        return gates[pl.ds((along_head ^ distance) * heads, heads)]

    own_ref[0] = group(0)
    other_ref[0] = group(1)
    for number, pair_ref in enumerate(pair_refs):
        for core in range(2):
            pair_ref[core] = group(2 * number + 2 + core)


def block_slabs(blocks, sub, sources):
    places = [partner(source, sub, sources // sub) for source in range(sources)]
    per = sources // blocks
    return [places[block * per : (block + 1) * per] for block in range(blocks)]


def block_rows(got_ref, slabs, tokens, part):
    return jnp.concatenate([got_ref[slab, part * tokens : (part + 1) * tokens] for slab in slabs], axis=0)


def beside(matrices):
    return jnp.concatenate(matrices, axis=1)


def parts_of(wide, count):
    width = wide.shape[1] // count
    return [wide[:, part * width : (part + 1) * width] for part in range(count)]


def block_inverse(below):
    size = below[0].shape[0]
    rows = lax.broadcasted_iota(jnp.int32, (size, size), 0)
    cols = lax.broadcasted_iota(jnp.int32, (size, size), 1)
    zero = jnp.zeros((size, size), F32)
    step = 1
    solved = None
    while step < size:
        joins = (rows // (2 * step) == cols // (2 * step)) & (rows // step > cols // step)
        parts = [jnp.where(joins, matrix, zero) for matrix in below]
        if step == 1:
            solved = [
                jnp.where(rows == cols, jnp.ones_like(zero), -part).astype(BF16) for part in parts
            ]
        else:
            inner = [dot(part.astype(BF16), now).astype(BF16) for part, now in zip(parts, solved)]
            solved = [now - dot(now, mid).astype(BF16) for now, mid in zip(solved, inner)]
        step *= 2
    return solved


def factor_kernel(tokens, ratio, sub, total_too, got_ref, after_ref, *refs):
    state_ref, w_ref, u_ref, *tree_refs = refs
    width = got_ref.shape[-1]
    per = SPAN // tokens
    blocks = got_ref.shape[0] // per
    slabs = block_slabs(blocks, sub, got_ref.shape[0])
    rows = lax.broadcasted_iota(jnp.int32, (SPAN, SPAN), 0)
    cols = lax.broadcasted_iota(jnp.int32, (SPAN, SPAN), 1)
    lane = lax.broadcasted_iota(jnp.int32, (1, SPAN), 1)
    first = (2 + ratio) * tokens
    below, held = [], []
    for block in range(blocks):
        key = block_rows(got_ref, slabs[block], tokens, 1)
        gram = dot_nt(key, key)
        squares = jnp.where(rows == cols, gram, 0.0)
        key_row = lax.rsqrt(jnp.sum(squares, 0, keepdims=True) + EPSILON)
        key_col = lax.rsqrt(jnp.sum(squares, 1, keepdims=True) + EPSILON)
        lower = jnp.where(rows > cols, gram, 0.0) * key_row
        strengths = []
        for r in range(ratio):
            strength = jnp.zeros((1, SPAN), F32)
            for place in range(per):
                piece = got_ref[slabs[block][place], first : first + ROW_TILE].astype(F32)[r : r + 1]
                strength = jnp.where(lane // tokens == place, piece, strength)
            scaled_col = jnp.sum(jnp.where(rows == cols, strength * key_row, 0.0), 1, keepdims=True)
            below.append(lower * scaled_col)
            strengths.append(strength)
        held.append((block, key, key_col, key_row, strengths))
    solved = block_inverse(below)
    flat = [(block, r) for block in range(blocks) for r in range(ratio)]
    weighted = []
    for inverse, (block, r) in zip(solved, flat):
        unused, key, key_col, key_row, strengths = held[block]
        weighted.append(inverse.astype(F32) * key_col * strengths[r])
    for part, (block, r) in zip(weighted, flat):
        value = block_rows(got_ref, slabs[block], tokens, 2 + r)
        u_ref[block, r] = dot(part.astype(BF16), value)
    for part, (block, r) in zip(weighted, flat):
        unused, key, key_col, key_row, strengths = held[block]
        w_ref[block, r] = dot((part * key_row).astype(BF16), key).astype(BF16)
    turns, adds = [], []
    for block in range(blocks):
        key_t = held[block][1].T
        for r in range(ratio):
            turn, add = parts_of(dot(key_t, beside([w_ref[block, r], u_ref[block, r].astype(BF16)])), 2)
            turns.append(turn)
            adds.append(add)

    level = 0
    while len(adds) > ratio:
        count = len(adds) // ratio
        trans_ref, add_ref = tree_refs[2 * level : 2 * level + 2]
        for number in range(len(adds)):
            trans_ref[number // ratio, number % ratio] = turns[number].astype(BF16)
            add_ref[number // ratio, number % ratio] = adds[number]
        longer_turns, longer_adds = [], []
        for pair in range(count // 2):
            for r in range(ratio):
                left, right = 2 * pair * ratio + r, (2 * pair + 1) * ratio + r
                if count > 2 or total_too:
                    both = beside([turns[left], adds[left]])
                    turn, add = parts_of(both - dot(turns[right].astype(BF16), both.astype(BF16)), 2)
                    longer_turns.append(turns[right] + turn)
                else:
                    add = adds[left] - dot(turns[right].astype(BF16), adds[left].astype(BF16))
                longer_adds.append(add + adds[right])
        turns, adds = longer_turns, longer_adds
        level += 1
    for r in range(ratio):
        state_ref[r] = adds[r].astype(state_ref.dtype)
        if total_too:
            tree_refs[-1][r] = turns[r]


def tree_starts(ratio, width, tree_refs):
    rows = lax.broadcasted_iota(jnp.int32, (width, 2 * width), 0)
    cols = lax.broadcasted_iota(jnp.int32, (width, 2 * width), 1)
    neutral = jnp.where(cols == rows + width, 1.0, 0.0).astype(F32)
    starts = [None] * ratio
    for level in reversed(range(len(tree_refs) // 2)):
        trans_ref, add_ref = tree_refs[2 * level : 2 * level + 2]
        longer = []
        for number, start in enumerate(starts):
            place, r = 2 * (number // ratio), number % ratio
            add = beside([add_ref[place, r], jnp.zeros((width, width), F32)])
            if start is None:
                turn = beside([jnp.zeros((width, width), F32), trans_ref[place, r].astype(F32)])
                longer.append((start, neutral - turn + add))
            else:
                longer.append((start, start - dot(trans_ref[place, r], start.astype(BF16)) + add))
        starts = []
        for pair in range(len(longer) // ratio):
            for side in range(2):
                starts += [longer[pair * ratio + r][side] for r in range(ratio)]
    return [neutral if start is None else start for start in starts]


def spread_kernel(tokens, ratio, sub, passing, got_ref, w_ref, u_ref, *refs):
    refs = refs[: len(refs) - passing]
    tree_refs, (local_ref, reach_ref) = refs[: len(refs) - passing - 2], refs[-2:]
    width = got_ref.shape[-1]
    per = SPAN // tokens
    blocks = got_ref.shape[0] // per
    slabs = block_slabs(blocks, sub, got_ref.shape[0])
    rows = lax.broadcasted_iota(jnp.int32, (SPAN, SPAN), 0)
    cols = lax.broadcasted_iota(jnp.int32, (SPAN, SPAN), 1)
    starts = [start.astype(BF16) for start in tree_starts(ratio, width, tree_refs)]
    lefts, units = [], []
    for block in range(blocks):
        query = block_rows(got_ref, slabs[block], tokens, 0)
        key = block_rows(got_ref, slabs[block], tokens, 1)
        scores = jnp.where(rows >= cols, dot_nt(query, key), 0.0).astype(BF16)
        query_f = query.astype(F32)
        squares = jnp.sum(query_f * query_f, 1, keepdims=True)
        units.append(lax.rsqrt(squares + EPSILON) * width ** (-0.5))
        lefts.append(beside([query, scores]))
    flat = [(block, r) for block in range(blocks) for r in range(ratio)]
    rights = []
    for start, (block, r) in zip(starts, flat):
        through, reached = parts_of(dot(w_ref[block, r], start), 2)
        corrected = beside([u_ref[block, r] - through, -reached]).astype(BF16)
        rights.append(jnp.concatenate([start, corrected], axis=0))
    for right, (block, r) in zip(rights, flat):
        out = dot(lefts[block], right) * units[block]
        local_ref[r, block] = out[:, :width]
        reach_ref[r, block] = out[:, width:].astype(BF16)


def join_kernel(order, n_head, state_ref, local_ref, reach_ref, *out_refs):
    ratio, blocks, span, width = local_ref.shape
    pieces = out_refs[0].shape[1]
    along_sub, along_head = position(len(order), n_head)
    upper = along_head // (n_head // 2)
    follows = lax.axis_index("outer") > 0
    states = [jnp.where(follows, state_ref[r].astype(F32), 0.0).astype(BF16) for r in range(ratio)]
    for distance, out_ref in zip(order, out_refs):
        target = along_sub ^ distance
        for kept in range(2):
            for piece in range(pieces):
                block = (target * 2 + (upper ^ (1 - kept))) * pieces + piece
                for r in range(ratio):
                    core = local_ref[r, block] + dot(reach_ref[r, block], states[r])
                    mean_square = jnp.mean(core * core, 1, keepdims=True)
                    out_ref[kept, piece, r] = (core * lax.rsqrt(mean_square + EPSILON)).astype(BF16)


def project_kernel(order, shares, kept, mine, *refs):
    parts = len(order)
    normed_refs, gate_refs = refs[:parts], refs[parts : parts + shares]
    weight_ref, *out_refs, rows_ref = refs[parts + 2 * shares :]
    unused, pieces, ratio, span, width = normed_refs[0].shape
    tokens = gate_refs[0].shape[2]
    per = span // tokens
    along_sub, along_head = position(parts, 2 * shares)
    for distance, normed_ref in zip(order, normed_refs):
        source = along_sub ^ distance
        for apart in range(1 - mine, shares, 2):
            share = (along_head ^ apart) & (shares - 1)
            place = pl.ds(pl.multiple_of(share // 2 * tokens, tokens), tokens)
            from_rows = pl.ds(pl.multiple_of(share % per * tokens, tokens), tokens)
            for r in range(ratio):
                lanes = pl.ds(pl.multiple_of((source * ratio + r) * width, width), width)
                normed = normed_ref[kept, share // per, r, from_rows].astype(F32)
                gate = gate_refs[apart][0, source * ratio + r].astype(F32)
                rows_ref[place, lanes] = (normed * gate).astype(BF16)
    first = 0
    for out_ref in out_refs:
        columns = out_ref.shape[-1]
        out = dot(rows_ref[...], weight_ref[:, first : first + columns])
        out_ref[...] = out.reshape(out_ref.shape).astype(out_ref.dtype)
        first += columns


def sum_kernel(keep_ref, *refs):
    out_ref = refs[-1]
    first = 0
    for number, got_ref in enumerate(refs[:-1]):
        columns = got_ref.shape[-1]
        if first == keep_ref.shape[-1]:
            break
        total = keep_ref[:, :, first : first + columns] + got_ref[...].astype(F32)
        for more_ref in refs[:-1]:
            if more_ref.shape[-1] == keep_ref.shape[-1] and more_ref is not got_ref:
                total = total + more_ref[:, :, first : first + columns].astype(F32)
        out_ref[:, :, first : first + columns] = total.astype(out_ref.dtype)
        first += columns


def per_device(
    outer, sub, n_head, queries, key_vectors, value_vectors, output_gate, write_strength, norm_gain, output_weight
):
    tokens, key_heads, width = queries.shape
    value_heads = value_vectors.shape[1]
    ratio = value_heads // key_heads
    sources = sub * n_head
    shard = tokens * sources
    blocks = shard // SPAN
    shard_tokens = tokens * n_head
    shape = jax.ShapeDtypeStruct
    along_sub, along_head = split_axis("sub", sub), split_axis("head", n_head)

    with jax.named_scope("pack"):
        slab = ((2 + ratio) * tokens + ROW_TILE, width)
        packed = pl.pallas_call(
            functools.partial(pack_kernel, sub),
            out_shape=shape((sources,) + slab, BF16),
            in_specs=[ANY] * 4,
            out_specs=ANY,
            scratch_shapes=[
                pltpu.VMEM(queries.shape, BF16),
                pltpu.VMEM(key_vectors.shape, BF16),
                pltpu.VMEM(value_vectors.shape, BF16),
                pltpu.VMEM((value_heads, tokens), BF16),
                pltpu.VMEM((sources,) + slab, BF16),
                pltpu.SemaphoreType.DMA((4,)),
                pltpu.SemaphoreType.DMA((3 + ratio,)),
            ],
            compiler_params=params(60),
        )(queries, key_vectors, value_vectors, write_strength.T)
    got = lax.all_to_all(packed, partner_order(sub, n_head), split_axis=0, concat_axis=0, tiled=True)

    heads = sub * ratio
    by_core = [(here, here ^ 1) for here in range(n_head)]
    group = (heads, tokens, width)
    with jax.named_scope("gates"):
        own_gates, other_gates, *pair_gates = pl.pallas_call(
            functools.partial(gate_kernel, sub, n_head),
            out_shape=[shape((1,) + group, BF16)] * 2 + [shape((2,) + group, BF16)] * (n_head // 2 - 1),
            in_specs=[VMEM] * 2,
            out_specs=[VMEM] * (n_head // 2 + 1),
            scratch_shapes=[pltpu.VMEM((value_heads, tokens, width), BF16)],
            compiler_params=params(),
            cost_estimate=LIGHT,
        )(output_gate, norm_gain.reshape(1, width))
    other_gates = lax.ppermute(other_gates, along_head, by_core)

    state_type = BF16 if outer == 2 else F32
    with jax.named_scope("factors"):
        depths = []
        while blocks >> len(depths) > 1:
            depths.append(blocks >> len(depths))
        tree = []
        for depth in depths:
            tree += [shape((depth, ratio, width, width), BF16), shape((depth, ratio, width, width), F32)]
        if outer > 2:
            tree.append(shape((ratio, width, width), F32))
        out_shape = [
            shape((ratio, width, width), state_type),
            shape((blocks, ratio, SPAN, width), BF16),
            shape((blocks, ratio, SPAN, width), F32),
        ] + tree
        state, w, u, *tree = pl.pallas_call(
            functools.partial(factor_kernel, tokens, ratio, sub, outer > 2),
            out_shape=out_shape,
            in_specs=[VMEM, ANY],
            out_specs=[VMEM] * len(out_shape),
            compiler_params=params(),
            cost_estimate=LIGHT,
        )(got, other_gates)

    onward = [(here, (here + 1) % outer) for here in range(outer)]
    incoming = lax.ppermute(state, "outer", onward)
    with jax.named_scope("spread"):
        passing = len(pair_gates)
        first = 3 + 2 * len(depths)
        local, reach, *pair_gates = pl.pallas_call(
            functools.partial(spread_kernel, tokens, ratio, sub, passing),
            out_shape=[
                shape((ratio, blocks, SPAN, width), F32),
                shape((ratio, blocks, SPAN, width), BF16),
            ]
            + [shape((2,) + group, BF16)] * passing,
            in_specs=[VMEM] * first + [ANY] * passing,
            out_specs=[VMEM] * 2 + [ANY] * passing,
            input_output_aliases={first + number: 2 + number for number in range(passing)},
            compiler_params=params(),
            cost_estimate=LIGHT,
        )(got, w, u, *tree[: 2 * len(depths)], *pair_gates)
    gates = [own_gates, other_gates]
    for number, pair in enumerate(pair_gates):
        distance = 2 * number + 2
        pair = lax.ppermute(pair, along_head, [(here, here ^ distance) for here in range(n_head)])
        gates += [pair, lax.ppermute(pair[1:], along_head, by_core)]
    for hop in range(outer - 2):
        incoming = jnp.where(lax.axis_index("outer") == 0, 0.0, incoming)
        turned_by = jnp.einsum("hde,hef->hdf", tree[-1], incoming, precision=lax.Precision.HIGHEST)
        incoming = lax.ppermute(state + incoming - turned_by, "outer", onward)

    pieces = shard_tokens // SPAN // 2
    columns = output_weight.shape[1]
    quarter = (n_head // 4, tokens, columns)
    half = n_head // 2
    order = [0] + sorted(range(1, sub), reverse=True)
    with jax.named_scope("join"):
        normed = pl.pallas_call(
            functools.partial(join_kernel, order, n_head),
            out_shape=[shape((2, pieces, ratio, SPAN, width), BF16)] * sub,
            in_specs=[VMEM] * 3,
            out_specs=[VMEM] * sub,
            compiler_params=params(),
            cost_estimate=LIGHT,
        )(incoming, local, reach)
    normed = [
        lax.ppermute(part, along_sub, [(here, here ^ distance) for here in range(sub)]) if distance else part
        for distance, part in zip(order, normed)
    ]
    for kept in range(2):
        cuts = 1 + kept
        operands = [*normed, *gates[half * (1 - kept) :], *gates[: half * (1 - kept)], output_weight]
        results = []
        for mine in range(2):
            pieces_of = 1 if mine else cuts
            with jax.named_scope("project"):
                results += pl.pallas_call(
                    functools.partial(project_kernel, order, half, kept, mine),
                    out_shape=[shape(quarter[:-1] + (columns // pieces_of,), F32 if mine else BF16)] * pieces_of,
                    in_specs=[VMEM] * (sub + half) + [ANY] * half + [VMEM],
                    out_specs=[VMEM] * pieces_of,
                    scratch_shapes=[pltpu.VMEM((shard_tokens // 4, heads * width), BF16)],
                    compiler_params=params(),
                    cost_estimate=LIGHT,
                )(*operands)
        *sends, keep = results
        arrived = [lax.ppermute(send, along_head, by_core) for send in sends]
        last = n_head == 4 and kept == 1
        with jax.named_scope("sum"):
            summed = pl.pallas_call(
                sum_kernel,
                out_shape=shape(quarter, F32 if kept and not last else BF16),
                in_specs=[VMEM] * (1 + cuts + kept),
                out_specs=VMEM,
                compiler_params=params(),
                cost_estimate=LIGHT,
            )(keep, *arrived, *([passed_on] if kept else []))
        if not kept:
            passed_on = lax.ppermute(summed, along_head, [(here, here ^ half) for here in range(n_head)])
    bit = 2
    while bit < half:
        mine = (lax.axis_index(along_head) // bit) % 2
        split = summed.reshape((summed.shape[0] // 2, 2) + summed.shape[1:])
        send = lax.dynamic_index_in_dim(split, 1 - mine, 1, False).astype(BF16)
        keep = lax.dynamic_index_in_dim(split, mine, 1, False)
        summed = keep + lax.ppermute(send, along_head, [(here, here ^ bit) for here in range(n_head)]).astype(F32)
        bit *= 2
    return summed[0].astype(BF16)


def solution(mesh):
    n_seq, n_head = mesh.shape["seq"], mesh.shape["head"]

    def run(queries, key_vectors, value_vectors, output_gate, write_strength, norm_gain, output_weight):
        sub = queries.shape[1] // n_head
        outer = n_seq // sub
        along = split_axis("sub", sub) + split_axis("head", n_head)
        split = Mesh(mesh.devices.reshape((outer,) + (2,) * len(along)), ("outer",) + along)
        every = ("outer",) + along
        placed = (
            P(every, None, None),
            P(every, None, None),
            P(every, None, None),
            P(every, None, None),
            P(every, None),
            P(),
            P(split_axis("head", n_head), None),
        )
        return jax.shard_map(
            functools.partial(per_device, outer, sub, n_head),
            mesh=split,
            in_specs=placed,
            out_specs=P(every, None),
            check_vma=False,
        )(queries, key_vectors, value_vectors, output_gate, write_strength, norm_gain, output_weight)

    return run
```

```python
import functools

import jax
import jax.numpy as jnp
from jax import lax
from jax.experimental import pallas as pl
from jax.experimental.pallas import tpu as pltpu
from jax.sharding import Mesh, PartitionSpec as P

SPAN = 128
EPSILON = 1e-06
F32 = jnp.float32
BF16 = jnp.bfloat16
ROW_TILE = 16
VMEM = pl.BlockSpec(memory_space=pltpu.VMEM)
SMEM = pl.BlockSpec(memory_space=pltpu.SMEM)
ANY = pl.BlockSpec(memory_space=pl.ANY)
LIGHT = pl.CostEstimate(flops=1, bytes_accessed=1, transcendentals=0)


def dot(left, right):
    return jnp.dot(left, right, preferred_element_type=F32)


def dot_nt(left, right):
    return lax.dot_general(left, right, (((1,), (1,)), ((), ())), preferred_element_type=F32)


def params(megabytes=24):
    return pltpu.CompilerParams(vmem_limit_bytes=megabytes * 2**20)


def turned(values):
    return jnp.transpose(values, (1, 0, 2))


def split_axis(name, size):
    return tuple(f"{name}{bit}" for bit in reversed(range(size.bit_length() - 1)))


def partner_order(sub, n_head):
    heads = split_axis("head", n_head)
    return heads[-1:] + heads[:-1] + split_axis("sub", sub)


def partner(source, sub, n_head):
    axes = split_axis("sub", sub) + split_axis("head", n_head)
    bits = {name: source >> (len(axes) - 1 - number) & 1 for number, name in enumerate(axes)}
    place = 0
    for name in partner_order(sub, n_head):
        place = 2 * place + bits[name]
    return place


def position(sub, n_head):
    return lax.axis_index(split_axis("sub", sub)), lax.axis_index(split_axis("head", n_head))


def pack_kernel(sub, q_hbm, k_hbm, v_hbm, b_hbm, out_hbm, q_ref, k_ref, v_ref, b_ref, out_ref, came, left):
    tokens, key_heads, width = q_hbm.shape
    ratio = v_hbm.shape[1] // key_heads
    copies = [
        pltpu.make_async_copy(source, target, came.at[number])
        for number, (source, target) in enumerate(
            ((b_hbm, b_ref), (k_hbm, k_ref), (q_hbm, q_ref), (v_hbm, v_ref))
        )
    ]
    for copy in copies:
        copy.start()
    n_head = key_heads // sub
    heads = [head % sub * n_head + head // sub for head in range(key_heads)]
    heads = [partner(source, sub, n_head) for source in heads]
    heads = [heads.index(peer) for peer in range(key_heads)]
    leaving = []

    def leave(first, size):
        rows = pl.ds(first, size)
        leaving.append(pltpu.make_async_copy(out_ref.at[:, rows], out_hbm.at[:, rows], left.at[len(leaving)]))
        leaving[-1].start()

    copies[0].wait()
    strength = jnp.concatenate([b_ref[...].astype(F32)] * (width // tokens), axis=1)
    strength = jnp.concatenate([strength, jnp.zeros((ROW_TILE, width), F32)], axis=0)
    for peer, head in enumerate(heads):
        tile = strength[head * ratio : head * ratio + ROW_TILE]
        out_ref[peer, (2 + ratio) * tokens :] = tile.astype(BF16)
    leave((2 + ratio) * tokens, ROW_TILE)
    for place, copy, ref in ((1, copies[1], k_ref), (0, copies[2], q_ref)):
        copy.wait()
        rows = turned(ref[...])
        for peer, head in enumerate(heads):
            out_ref[peer, place * tokens : (place + 1) * tokens] = rows[head]
        leave(place * tokens, tokens)
    copies[3].wait()
    rows = turned(v_ref[...])
    for r in range(ratio):
        for peer, head in enumerate(heads):
            out_ref[peer, (2 + r) * tokens : (3 + r) * tokens] = rows[head * ratio + r]
        leave((2 + r) * tokens, tokens)
    for copy in leaving:
        copy.wait()


def gate_kernel(sub, n_head, gate_ref, gain_ref, own_ref, swap_ref, gates):
    heads = own_ref.shape[1]
    unused, along_head = position(sub, n_head)
    gate = gate_ref[...].astype(F32)
    gated = gain_ref[...].astype(F32)[:, None] * (gate / (1.0 + jnp.exp(-gate)))
    gates[...] = turned(gated.astype(BF16))
    for number in range(n_head // 2):
        own_ref[number] = gates[pl.ds((along_head ^ (2 * number)) * heads, heads)]
        swap_ref[number] = gates[pl.ds((along_head ^ (2 * number + 1)) * heads, heads)]


def pair_kernel(own_ref, swapped_ref, *pair_refs):
    for number, pair_ref in enumerate(pair_refs):
        pair_ref[0] = own_ref[number + 1]
        pair_ref[1] = swapped_ref[number + 1]


def block_slabs(blocks, sub, sources):
    places = [partner(source, sub, sources // sub) for source in range(sources)]
    per = sources // blocks
    return [places[block * per : (block + 1) * per] for block in range(blocks)]


def block_rows(got_ref, slabs, tokens, part):
    return jnp.concatenate([got_ref[slab, part * tokens : (part + 1) * tokens] for slab in slabs], axis=0)


def beside(matrices):
    return jnp.concatenate(matrices, axis=1)


def parts_of(wide, count):
    width = wide.shape[1] // count
    return [wide[:, part * width : (part + 1) * width] for part in range(count)]


def block_inverse(below):
    size = below[0].shape[0]
    rows = lax.broadcasted_iota(jnp.int32, (size, size), 0)
    cols = lax.broadcasted_iota(jnp.int32, (size, size), 1)
    zero = jnp.zeros((size, size), F32)
    step = 1
    solved = None
    while step < size:
        joins = (rows // (2 * step) == cols // (2 * step)) & (rows // step > cols // step)
        parts = [jnp.where(joins, matrix, zero) for matrix in below]
        if step == 1:
            solved = [
                jnp.where(rows == cols, jnp.ones_like(zero), -part).astype(BF16) for part in parts
            ]
        else:
            inner = [dot(part.astype(BF16), now).astype(BF16) for part, now in zip(parts, solved)]
            solved = [now - dot(now, mid).astype(BF16) for now, mid in zip(solved, inner)]
        step *= 2
    return solved


def factor_kernel(tokens, ratio, sub, passing, total_too, got_ref, *refs):
    state_ref, w_ref, u_ref, *tree_refs = refs[passing : len(refs) - passing]
    width = got_ref.shape[-1]
    per = SPAN // tokens
    blocks = got_ref.shape[0] // per
    slabs = block_slabs(blocks, sub, got_ref.shape[0])
    rows = lax.broadcasted_iota(jnp.int32, (SPAN, SPAN), 0)
    cols = lax.broadcasted_iota(jnp.int32, (SPAN, SPAN), 1)
    lane = lax.broadcasted_iota(jnp.int32, (1, SPAN), 1)
    first = (2 + ratio) * tokens
    below, held = [], []
    for block in range(blocks):
        key = block_rows(got_ref, slabs[block], tokens, 1)
        gram = dot_nt(key, key)
        squares = jnp.where(rows == cols, gram, 0.0)
        key_row = lax.rsqrt(jnp.sum(squares, 0, keepdims=True) + EPSILON)
        key_col = lax.rsqrt(jnp.sum(squares, 1, keepdims=True) + EPSILON)
        lower = jnp.where(rows > cols, gram, 0.0) * key_row
        strengths = []
        for r in range(ratio):
            strength = jnp.zeros((1, SPAN), F32)
            for place in range(per):
                piece = got_ref[slabs[block][place], first : first + ROW_TILE].astype(F32)[r : r + 1]
                strength = jnp.where(lane // tokens == place, piece, strength)
            scaled_col = jnp.sum(jnp.where(rows == cols, strength * key_row, 0.0), 1, keepdims=True)
            below.append(lower * scaled_col)
            strengths.append(strength)
        held.append((block, key, key_col, key_row, strengths))
    solved = block_inverse(below)
    flat = [(block, r) for block in range(blocks) for r in range(ratio)]
    weighted = []
    for inverse, (block, r) in zip(solved, flat):
        unused, key, key_col, key_row, strengths = held[block]
        weighted.append(inverse.astype(F32) * key_col * strengths[r])
    for part, (block, r) in zip(weighted, flat):
        value = block_rows(got_ref, slabs[block], tokens, 2 + r)
        u_ref[block, r] = dot(part.astype(BF16), value)
    for part, (block, r) in zip(weighted, flat):
        unused, key, key_col, key_row, strengths = held[block]
        w_ref[block, r] = dot((part * key_row).astype(BF16), key).astype(BF16)
    turns, adds = [], []
    for block in range(blocks):
        key_t = held[block][1].T
        for r in range(ratio):
            turn, add = parts_of(dot(key_t, beside([w_ref[block, r], u_ref[block, r].astype(BF16)])), 2)
            turns.append(turn)
            adds.append(add)

    level = 0
    while len(adds) > ratio:
        count = len(adds) // ratio
        trans_ref, add_ref = tree_refs[2 * level : 2 * level + 2]
        for number in range(len(adds)):
            trans_ref[number // ratio, number % ratio] = turns[number].astype(BF16)
            add_ref[number // ratio, number % ratio] = adds[number]
        longer_turns, longer_adds = [], []
        for pair in range(count // 2):
            for r in range(ratio):
                left, right = 2 * pair * ratio + r, (2 * pair + 1) * ratio + r
                if count > 2 or total_too:
                    both = beside([turns[left], adds[left]])
                    turn, add = parts_of(both - dot(turns[right].astype(BF16), both.astype(BF16)), 2)
                    longer_turns.append(turns[right] + turn)
                else:
                    add = adds[left] - dot(turns[right].astype(BF16), adds[left].astype(BF16))
                longer_adds.append(add + adds[right])
        turns, adds = longer_turns, longer_adds
        level += 1
    for r in range(ratio):
        state_ref[r] = adds[r].astype(state_ref.dtype)
        if total_too:
            tree_refs[-1][r] = turns[r]


def tree_starts(ratio, width, tree_refs):
    rows = lax.broadcasted_iota(jnp.int32, (width, 2 * width), 0)
    cols = lax.broadcasted_iota(jnp.int32, (width, 2 * width), 1)
    neutral = jnp.where(cols == rows + width, 1.0, 0.0).astype(F32)
    starts = [None] * ratio
    for level in reversed(range(len(tree_refs) // 2)):
        trans_ref, add_ref = tree_refs[2 * level : 2 * level + 2]
        longer = []
        for number, start in enumerate(starts):
            place, r = 2 * (number // ratio), number % ratio
            add = beside([add_ref[place, r], jnp.zeros((width, width), F32)])
            if start is None:
                turn = beside([jnp.zeros((width, width), F32), trans_ref[place, r].astype(F32)])
                longer.append((start, neutral - turn + add))
            else:
                longer.append((start, start - dot(trans_ref[place, r], start.astype(BF16)) + add))
        starts = []
        for pair in range(len(longer) // ratio):
            for side in range(2):
                starts += [longer[pair * ratio + r][side] for r in range(ratio)]
    return [neutral if start is None else start for start in starts]


def spread_kernel(tokens, ratio, sub, got_ref, w_ref, u_ref, *refs):
    tree_refs, (local_ref, reach_ref) = refs[:-2], refs[-2:]
    width = got_ref.shape[-1]
    per = SPAN // tokens
    blocks = got_ref.shape[0] // per
    slabs = block_slabs(blocks, sub, got_ref.shape[0])
    rows = lax.broadcasted_iota(jnp.int32, (SPAN, SPAN), 0)
    cols = lax.broadcasted_iota(jnp.int32, (SPAN, SPAN), 1)
    starts = [start.astype(BF16) for start in tree_starts(ratio, width, tree_refs)]
    lefts, units = [], []
    for block in range(blocks):
        query = block_rows(got_ref, slabs[block], tokens, 0)
        key = block_rows(got_ref, slabs[block], tokens, 1)
        scores = jnp.where(rows >= cols, dot_nt(query, key), 0.0).astype(BF16)
        query_f = query.astype(F32)
        squares = jnp.sum(query_f * query_f, 1, keepdims=True)
        units.append(lax.rsqrt(squares + EPSILON) * width ** (-0.5))
        lefts.append(beside([query, scores]))
    flat = [(block, r) for block in range(blocks) for r in range(ratio)]
    rights = []
    for start, (block, r) in zip(starts, flat):
        through, reached = parts_of(dot(w_ref[block, r], start), 2)
        corrected = beside([u_ref[block, r] - through, -reached]).astype(BF16)
        rights.append(jnp.concatenate([start, corrected], axis=0))
    for right, (block, r) in zip(rights, flat):
        out = dot(lefts[block], right) * units[block]
        local_ref[r, block] = out[:, :width]
        reach_ref[r, block] = out[:, width:].astype(BF16)


def join_kernel(order, n_head, state_ref, local_ref, reach_ref, *out_refs):
    ratio, blocks, span, width = local_ref.shape
    pieces = out_refs[0].shape[1]
    along_sub, along_head = position(len(order), n_head)
    upper = along_head // (n_head // 2)
    follows = lax.axis_index("outer") > 0
    states = [jnp.where(follows, state_ref[r].astype(F32), 0.0).astype(BF16) for r in range(ratio)]
    for distance, out_ref in zip(order, out_refs):
        target = along_sub ^ distance
        for kept in range(2):
            for piece in range(pieces):
                block = (target * 2 + (upper ^ (1 - kept))) * pieces + piece
                for r in range(ratio):
                    core = local_ref[r, block] + dot(reach_ref[r, block], states[r])
                    mean_square = jnp.mean(core * core, 1, keepdims=True)
                    out_ref[kept, piece, r] = (core * lax.rsqrt(mean_square + EPSILON)).astype(BF16)


def project_kernel(order, gate_places, kept, mine, *refs):
    parts, shares = len(order), len(gate_places)
    normed_refs, gate_refs = refs[:parts], refs[parts : parts + shares]
    weight_ref, *out_refs, rows_ref = refs[parts + 2 * shares :]
    unused, pieces, ratio, span, width = normed_refs[0].shape
    tokens = gate_refs[0].shape[2]
    per = span // tokens
    along_sub, along_head = position(parts, 2 * shares)
    for distance, normed_ref in zip(order, normed_refs):
        source = along_sub ^ distance
        for apart in range(1 - mine, shares, 2):
            share = (along_head ^ apart) & (shares - 1)
            place = pl.ds(pl.multiple_of(share // 2 * tokens, tokens), tokens)
            from_rows = pl.ds(pl.multiple_of(share % per * tokens, tokens), tokens)
            for r in range(ratio):
                lanes = pl.ds(pl.multiple_of((source * ratio + r) * width, width), width)
                normed = normed_ref[kept, share // per, r, from_rows].astype(F32)
                gate = gate_refs[apart][gate_places[apart], source * ratio + r].astype(F32)
                rows_ref[place, lanes] = (normed * gate).astype(BF16)
    first = 0
    for out_ref in out_refs:
        columns = out_ref.shape[-1]
        out = dot(rows_ref[...], weight_ref[:, first : first + columns])
        out_ref[...] = out.reshape(out_ref.shape).astype(out_ref.dtype)
        first += columns


def sum_kernel(keep_ref, *refs):
    out_ref = refs[-1]
    first = 0
    for number, got_ref in enumerate(refs[:-1]):
        columns = got_ref.shape[-1]
        if first == keep_ref.shape[-1]:
            break
        total = keep_ref[:, :, first : first + columns] + got_ref[...].astype(F32)
        for more_ref in refs[:-1]:
            if more_ref.shape[-1] == keep_ref.shape[-1] and more_ref is not got_ref:
                total = total + more_ref[:, :, first : first + columns].astype(F32)
        out_ref[:, :, first : first + columns] = total.astype(out_ref.dtype)
        first += columns


def per_device(
    outer, sub, n_head, queries, key_vectors, value_vectors, output_gate, write_strength, norm_gain, output_weight
):
    tokens, key_heads, width = queries.shape
    value_heads = value_vectors.shape[1]
    ratio = value_heads // key_heads
    sources = sub * n_head
    shard = tokens * sources
    blocks = shard // SPAN
    shard_tokens = tokens * n_head
    shape = jax.ShapeDtypeStruct
    along_sub, along_head = split_axis("sub", sub), split_axis("head", n_head)

    with jax.named_scope("pack"):
        slab = ((2 + ratio) * tokens + ROW_TILE, width)
        packed = pl.pallas_call(
            functools.partial(pack_kernel, sub),
            out_shape=shape((sources,) + slab, BF16),
            in_specs=[ANY] * 4,
            out_specs=ANY,
            scratch_shapes=[
                pltpu.VMEM(queries.shape, BF16),
                pltpu.VMEM(key_vectors.shape, BF16),
                pltpu.VMEM(value_vectors.shape, BF16),
                pltpu.VMEM((value_heads, tokens), BF16),
                pltpu.VMEM((sources,) + slab, BF16),
                pltpu.SemaphoreType.DMA((4,)),
                pltpu.SemaphoreType.DMA((3 + ratio,)),
            ],
            compiler_params=params(60),
        )(queries, key_vectors, value_vectors, write_strength.T)
    got = lax.all_to_all(packed, partner_order(sub, n_head), split_axis=0, concat_axis=0, tiled=True)

    heads = sub * ratio
    by_core = [(here, here ^ 1) for here in range(n_head)]
    group = (heads, tokens, width)
    half = n_head // 2
    with jax.named_scope("gates"):
        own_gates, swap = pl.pallas_call(
            functools.partial(gate_kernel, sub, n_head),
            out_shape=[shape((half,) + group, BF16)] * 2,
            in_specs=[VMEM] * 2,
            out_specs=[VMEM] * 2,
            scratch_shapes=[pltpu.VMEM((value_heads, tokens, width), BF16)],
            compiler_params=params(),
            cost_estimate=LIGHT,
        )(output_gate, norm_gain.reshape(1, width))
    swapped = lax.ppermute(swap, along_head, by_core)
    with jax.named_scope("pair"):
        pairs = pl.pallas_call(
            pair_kernel,
            out_shape=[shape((2,) + group, BF16)] * (half - 1),
            in_specs=[VMEM] * 2,
            out_specs=[VMEM] * (half - 1),
            compiler_params=params(),
            cost_estimate=LIGHT,
        )(own_gates, swapped)

    state_type = BF16 if outer == 2 else F32
    with jax.named_scope("factors"):
        depths = []
        while blocks >> len(depths) > 1:
            depths.append(blocks >> len(depths))
        tree = []
        for depth in depths:
            tree += [shape((depth, ratio, width, width), BF16), shape((depth, ratio, width, width), F32)]
        if outer > 2:
            tree.append(shape((ratio, width, width), F32))
        out_shape = [
            shape((ratio, width, width), state_type),
            shape((blocks, ratio, SPAN, width), BF16),
            shape((blocks, ratio, SPAN, width), F32),
        ] + tree
        state, w, u, *rest = pl.pallas_call(
            functools.partial(factor_kernel, tokens, ratio, sub, half - 1, outer > 2),
            out_shape=out_shape + [shape((2,) + group, BF16)] * (half - 1),
            in_specs=[VMEM] + [ANY] * (half - 1),
            out_specs=[VMEM] * len(out_shape) + [ANY] * (half - 1),
            input_output_aliases={1 + number: len(out_shape) + number for number in range(half - 1)},
            compiler_params=params(),
            cost_estimate=LIGHT,
        )(got, *pairs)
        tree, pairs = rest[: len(rest) - half + 1], rest[len(rest) - half + 1 :]

    onward = [(here, (here + 1) % outer) for here in range(outer)]
    incoming = lax.ppermute(state, "outer", onward)
    with jax.named_scope("spread"):
        local, reach = pl.pallas_call(
            functools.partial(spread_kernel, tokens, ratio, sub),
            out_shape=[
                shape((ratio, blocks, SPAN, width), F32),
                shape((ratio, blocks, SPAN, width), BF16),
            ],
            in_specs=[VMEM] * (3 + 2 * len(depths)),
            out_specs=[VMEM] * 2,
            compiler_params=params(),
            cost_estimate=LIGHT,
        )(got, w, u, *tree[: 2 * len(depths)])
    gates = [(own_gates, 0), (swapped, 0)]
    for number, pair in enumerate(pairs):
        distance = 2 * number + 2
        pair = lax.ppermute(pair, along_head, [(here, here ^ distance) for here in range(n_head)])
        gates += [(pair, 0), (pair, 1)]
    for hop in range(outer - 2):
        incoming = jnp.where(lax.axis_index("outer") == 0, 0.0, incoming)
        turned_by = jnp.einsum("hde,hef->hdf", tree[-1], incoming, precision=lax.Precision.HIGHEST)
        incoming = lax.ppermute(state + incoming - turned_by, "outer", onward)

    pieces = shard_tokens // SPAN // 2
    columns = output_weight.shape[1]
    quarter = (n_head // 4, tokens, columns)
    half = n_head // 2
    order = [0] + sorted(range(1, sub), reverse=True)
    with jax.named_scope("join"):
        normed = pl.pallas_call(
            functools.partial(join_kernel, order, n_head),
            out_shape=[shape((2, pieces, ratio, SPAN, width), BF16)] * sub,
            in_specs=[VMEM] * 3,
            out_specs=[VMEM] * sub,
            compiler_params=params(),
            cost_estimate=LIGHT,
        )(incoming, local, reach)
    normed = [
        lax.ppermute(part, along_sub, [(here, here ^ distance) for here in range(sub)]) if distance else part
        for distance, part in zip(order, normed)
    ]
    for kept in range(2):
        cuts = 1 + kept
        used, others = gates[half * (1 - kept) : half * (2 - kept)], gates[half * kept : half * (1 + kept)]
        operands = [*normed, *[array for array, unused in used + others], output_weight]
        results = []
        for mine in range(2):
            pieces_of = 1 if mine else cuts
            with jax.named_scope("project"):
                results += pl.pallas_call(
                    functools.partial(project_kernel, order, [place for unused, place in used], kept, mine),
                    out_shape=[shape(quarter[:-1] + (columns // pieces_of,), F32 if mine else BF16)] * pieces_of,
                    in_specs=[VMEM] * (sub + half) + [ANY] * half + [VMEM],
                    out_specs=[VMEM] * pieces_of,
                    scratch_shapes=[pltpu.VMEM((shard_tokens // 4, heads * width), BF16)],
                    compiler_params=params(),
                    cost_estimate=LIGHT,
                )(*operands)
        *sends, keep = results
        arrived = [lax.ppermute(send, along_head, by_core) for send in sends]
        last = n_head == 4 and kept == 1
        with jax.named_scope("sum"):
            summed = pl.pallas_call(
                sum_kernel,
                out_shape=shape(quarter, F32 if kept and not last else BF16),
                in_specs=[VMEM] * (1 + cuts + kept),
                out_specs=VMEM,
                compiler_params=params(),
                cost_estimate=LIGHT,
            )(keep, *arrived, *([passed_on] if kept else []))
        if not kept:
            passed_on = lax.ppermute(summed, along_head, [(here, here ^ half) for here in range(n_head)])
    bit = 2
    while bit < half:
        mine = (lax.axis_index(along_head) // bit) % 2
        split = summed.reshape((summed.shape[0] // 2, 2) + summed.shape[1:])
        send = lax.dynamic_index_in_dim(split, 1 - mine, 1, False).astype(BF16)
        keep = lax.dynamic_index_in_dim(split, mine, 1, False)
        summed = keep + lax.ppermute(send, along_head, [(here, here ^ bit) for here in range(n_head)]).astype(F32)
        bit *= 2
    return summed[0].astype(BF16)


def solution(mesh):
    n_seq, n_head = mesh.shape["seq"], mesh.shape["head"]

    def run(queries, key_vectors, value_vectors, output_gate, write_strength, norm_gain, output_weight):
        sub = queries.shape[1] // n_head
        outer = n_seq // sub
        along = split_axis("sub", sub) + split_axis("head", n_head)
        split = Mesh(mesh.devices.reshape((outer,) + (2,) * len(along)), ("outer",) + along)
        every = ("outer",) + along
        placed = (
            P(every, None, None),
            P(every, None, None),
            P(every, None, None),
            P(every, None, None),
            P(every, None),
            P(),
            P(split_axis("head", n_head), None),
        )
        return jax.shard_map(
            functools.partial(per_device, outer, sub, n_head),
            mesh=split,
            in_specs=placed,
            out_specs=P(every, None),
            check_vma=False,
        )(queries, key_vectors, value_vectors, output_gate, write_strength, norm_gain, output_weight)

    return run
```

```python
import functools

import jax
import jax.numpy as jnp
from jax import lax
from jax.experimental import pallas as pl
from jax.experimental.pallas import tpu as pltpu
from jax.sharding import Mesh, PartitionSpec as P

SPAN = 128
EPSILON = 1e-06
F32 = jnp.float32
BF16 = jnp.bfloat16
ROW_TILE = 16
VMEM = pl.BlockSpec(memory_space=pltpu.VMEM)
SMEM = pl.BlockSpec(memory_space=pltpu.SMEM)
ANY = pl.BlockSpec(memory_space=pl.ANY)
LIGHT = pl.CostEstimate(flops=1, bytes_accessed=1, transcendentals=0)


def dot(left, right):
    return jnp.dot(left, right, preferred_element_type=F32)


def dot_nt(left, right):
    return lax.dot_general(left, right, (((1,), (1,)), ((), ())), preferred_element_type=F32)


def params(megabytes=24):
    return pltpu.CompilerParams(vmem_limit_bytes=megabytes * 2**20)


def turned(values):
    return jnp.transpose(values, (1, 0, 2))


def split_axis(name, size):
    return tuple(f"{name}{bit}" for bit in reversed(range(size.bit_length() - 1)))


def partner_order(sub, n_head):
    heads = split_axis("head", n_head)
    return heads[-1:] + heads[:-1] + split_axis("sub", sub)


def partner(source, sub, n_head):
    axes = split_axis("sub", sub) + split_axis("head", n_head)
    bits = {name: source >> (len(axes) - 1 - number) & 1 for number, name in enumerate(axes)}
    place = 0
    for name in partner_order(sub, n_head):
        place = 2 * place + bits[name]
    return place


def position(sub, n_head):
    return lax.axis_index(split_axis("sub", sub)), lax.axis_index(split_axis("head", n_head))


def pack_kernel(sub, q_hbm, k_hbm, v_hbm, b_hbm, out_hbm, q_ref, k_ref, v_ref, b_ref, out_ref, came, left):
    tokens, key_heads, width = q_hbm.shape
    ratio = v_hbm.shape[1] // key_heads
    copies = [
        pltpu.make_async_copy(source, target, came.at[number])
        for number, (source, target) in enumerate(
            ((b_hbm, b_ref), (k_hbm, k_ref), (q_hbm, q_ref), (v_hbm, v_ref))
        )
    ]
    for copy in copies:
        copy.start()
    n_head = key_heads // sub
    heads = [head % sub * n_head + head // sub for head in range(key_heads)]
    heads = [partner(source, sub, n_head) for source in heads]
    heads = [heads.index(peer) for peer in range(key_heads)]
    leaving = []

    def leave(first, size):
        rows = pl.ds(first, size)
        leaving.append(pltpu.make_async_copy(out_ref.at[:, rows], out_hbm.at[:, rows], left.at[len(leaving)]))
        leaving[-1].start()

    copies[0].wait()
    strength = jnp.concatenate([b_ref[...].astype(F32)] * (width // tokens), axis=1)
    strength = jnp.concatenate([strength, jnp.zeros((ROW_TILE, width), F32)], axis=0)
    for peer, head in enumerate(heads):
        tile = strength[head * ratio : head * ratio + ROW_TILE]
        out_ref[peer, (2 + ratio) * tokens :] = tile.astype(BF16)
    leave((2 + ratio) * tokens, ROW_TILE)
    for place, copy, ref in ((1, copies[1], k_ref), (0, copies[2], q_ref)):
        copy.wait()
        rows = turned(ref[...])
        for peer, head in enumerate(heads):
            out_ref[peer, place * tokens : (place + 1) * tokens] = rows[head]
        leave(place * tokens, tokens)
    copies[3].wait()
    rows = turned(v_ref[...])
    for r in range(ratio):
        for peer, head in enumerate(heads):
            out_ref[peer, (2 + r) * tokens : (3 + r) * tokens] = rows[head * ratio + r]
        leave((2 + r) * tokens, tokens)
    for copy in leaving:
        copy.wait()


def gate_kernel(sub, n_head, gate_ref, gain_ref, own_ref, swap_ref, gates):
    heads = own_ref.shape[1]
    unused, along_head = position(sub, n_head)
    gate = gate_ref[...].astype(F32)
    gated = gain_ref[...].astype(F32)[:, None] * (gate / (1.0 + jnp.exp(-gate)))
    gates[...] = turned(gated.astype(BF16))
    for number in range(n_head // 2):
        own_ref[number] = gates[pl.ds((along_head ^ (2 * number)) * heads, heads)]
        swap_ref[number] = gates[pl.ds((along_head ^ (2 * number + 1)) * heads, heads)]


def pair_kernel(own_ref, swapped_ref, *pair_refs):
    for number, pair_ref in enumerate(pair_refs):
        pair_ref[0] = own_ref[number + 1]
        pair_ref[1] = swapped_ref[number + 1]


def release_kernel(*refs):
    pass


def block_slabs(blocks, sub, sources):
    places = [partner(source, sub, sources // sub) for source in range(sources)]
    per = sources // blocks
    return [places[block * per : (block + 1) * per] for block in range(blocks)]


def block_rows(got_ref, slabs, tokens, part):
    return jnp.concatenate([got_ref[slab, part * tokens : (part + 1) * tokens] for slab in slabs], axis=0)


def beside(matrices):
    return jnp.concatenate(matrices, axis=1)


def parts_of(wide, count):
    width = wide.shape[1] // count
    return [wide[:, part * width : (part + 1) * width] for part in range(count)]


def block_inverse(below):
    size = below[0].shape[0]
    rows = lax.broadcasted_iota(jnp.int32, (size, size), 0)
    cols = lax.broadcasted_iota(jnp.int32, (size, size), 1)
    zero = jnp.zeros((size, size), F32)
    step = 1
    solved = None
    while step < size:
        joins = (rows // (2 * step) == cols // (2 * step)) & (rows // step > cols // step)
        parts = [jnp.where(joins, matrix, zero) for matrix in below]
        if step == 1:
            solved = [
                jnp.where(rows == cols, jnp.ones_like(zero), -part).astype(BF16) for part in parts
            ]
        else:
            inner = [dot(part.astype(BF16), now).astype(BF16) for part, now in zip(parts, solved)]
            solved = [now - dot(now, mid).astype(BF16) for now, mid in zip(solved, inner)]
        step *= 2
    return solved


def factor_kernel(tokens, ratio, sub, passing, total_too, got_ref, *refs):
    state_ref, w_ref, u_ref, *tree_refs = refs[passing:]
    width = got_ref.shape[-1]
    per = SPAN // tokens
    blocks = got_ref.shape[0] // per
    slabs = block_slabs(blocks, sub, got_ref.shape[0])
    rows = lax.broadcasted_iota(jnp.int32, (SPAN, SPAN), 0)
    cols = lax.broadcasted_iota(jnp.int32, (SPAN, SPAN), 1)
    lane = lax.broadcasted_iota(jnp.int32, (1, SPAN), 1)
    first = (2 + ratio) * tokens
    below, held = [], []
    for block in range(blocks):
        key = block_rows(got_ref, slabs[block], tokens, 1)
        gram = dot_nt(key, key)
        squares = jnp.where(rows == cols, gram, 0.0)
        key_row = lax.rsqrt(jnp.sum(squares, 0, keepdims=True) + EPSILON)
        key_col = lax.rsqrt(jnp.sum(squares, 1, keepdims=True) + EPSILON)
        lower = jnp.where(rows > cols, gram, 0.0) * key_row
        strengths = []
        for r in range(ratio):
            strength = jnp.zeros((1, SPAN), F32)
            for place in range(per):
                piece = got_ref[slabs[block][place], first : first + ROW_TILE].astype(F32)[r : r + 1]
                strength = jnp.where(lane // tokens == place, piece, strength)
            scaled_col = jnp.sum(jnp.where(rows == cols, strength * key_row, 0.0), 1, keepdims=True)
            below.append(lower * scaled_col)
            strengths.append(strength)
        held.append((block, key, key_col, key_row, strengths))
    solved = block_inverse(below)
    flat = [(block, r) for block in range(blocks) for r in range(ratio)]
    weighted = []
    for inverse, (block, r) in zip(solved, flat):
        unused, key, key_col, key_row, strengths = held[block]
        weighted.append(inverse.astype(F32) * key_col * strengths[r])
    for part, (block, r) in zip(weighted, flat):
        value = block_rows(got_ref, slabs[block], tokens, 2 + r)
        u_ref[block, r] = dot(part.astype(BF16), value)
    for part, (block, r) in zip(weighted, flat):
        unused, key, key_col, key_row, strengths = held[block]
        w_ref[block, r] = dot((part * key_row).astype(BF16), key).astype(BF16)
    turns, adds = [], []
    for block in range(blocks):
        key_t = held[block][1].T
        for r in range(ratio):
            turn, add = parts_of(dot(key_t, beside([w_ref[block, r], u_ref[block, r].astype(BF16)])), 2)
            turns.append(turn)
            adds.append(add)

    level = 0
    while len(adds) > ratio:
        count = len(adds) // ratio
        trans_ref, add_ref = tree_refs[2 * level : 2 * level + 2]
        for number in range(len(adds)):
            trans_ref[number // ratio, number % ratio] = turns[number].astype(BF16)
            add_ref[number // ratio, number % ratio] = adds[number]
        longer_turns, longer_adds = [], []
        for pair in range(count // 2):
            for r in range(ratio):
                left, right = 2 * pair * ratio + r, (2 * pair + 1) * ratio + r
                if count > 2 or total_too:
                    both = beside([turns[left], adds[left]])
                    turn, add = parts_of(both - dot(turns[right].astype(BF16), both.astype(BF16)), 2)
                    longer_turns.append(turns[right] + turn)
                else:
                    add = adds[left] - dot(turns[right].astype(BF16), adds[left].astype(BF16))
                longer_adds.append(add + adds[right])
        turns, adds = longer_turns, longer_adds
        level += 1
    for r in range(ratio):
        state_ref[r] = adds[r].astype(state_ref.dtype)
        if total_too:
            tree_refs[-1][r] = turns[r]


def tree_starts(ratio, width, tree_refs):
    rows = lax.broadcasted_iota(jnp.int32, (width, 2 * width), 0)
    cols = lax.broadcasted_iota(jnp.int32, (width, 2 * width), 1)
    neutral = jnp.where(cols == rows + width, 1.0, 0.0).astype(F32)
    starts = [None] * ratio
    for level in reversed(range(len(tree_refs) // 2)):
        trans_ref, add_ref = tree_refs[2 * level : 2 * level + 2]
        longer = []
        for number, start in enumerate(starts):
            place, r = 2 * (number // ratio), number % ratio
            add = beside([add_ref[place, r], jnp.zeros((width, width), F32)])
            if start is None:
                turn = beside([jnp.zeros((width, width), F32), trans_ref[place, r].astype(F32)])
                longer.append((start, neutral - turn + add))
            else:
                longer.append((start, start - dot(trans_ref[place, r], start.astype(BF16)) + add))
        starts = []
        for pair in range(len(longer) // ratio):
            for side in range(2):
                starts += [longer[pair * ratio + r][side] for r in range(ratio)]
    return [neutral if start is None else start for start in starts]


def spread_kernel(tokens, ratio, sub, got_ref, w_ref, u_ref, *refs):
    tree_refs, (local_ref, reach_ref) = refs[:-2], refs[-2:]
    width = got_ref.shape[-1]
    per = SPAN // tokens
    blocks = got_ref.shape[0] // per
    slabs = block_slabs(blocks, sub, got_ref.shape[0])
    rows = lax.broadcasted_iota(jnp.int32, (SPAN, SPAN), 0)
    cols = lax.broadcasted_iota(jnp.int32, (SPAN, SPAN), 1)
    starts = [start.astype(BF16) for start in tree_starts(ratio, width, tree_refs)]
    lefts, units = [], []
    for block in range(blocks):
        query = block_rows(got_ref, slabs[block], tokens, 0)
        key = block_rows(got_ref, slabs[block], tokens, 1)
        scores = jnp.where(rows >= cols, dot_nt(query, key), 0.0).astype(BF16)
        query_f = query.astype(F32)
        squares = jnp.sum(query_f * query_f, 1, keepdims=True)
        units.append(lax.rsqrt(squares + EPSILON) * width ** (-0.5))
        lefts.append(beside([query, scores]))
    flat = [(block, r) for block in range(blocks) for r in range(ratio)]
    rights = []
    for start, (block, r) in zip(starts, flat):
        through, reached = parts_of(dot(w_ref[block, r], start), 2)
        corrected = beside([u_ref[block, r] - through, -reached]).astype(BF16)
        rights.append(jnp.concatenate([start, corrected], axis=0))
    for right, (block, r) in zip(rights, flat):
        out = dot(lefts[block], right) * units[block]
        local_ref[r, block] = out[:, :width]
        reach_ref[r, block] = out[:, width:].astype(BF16)


def join_kernel(order, n_head, state_ref, local_ref, reach_ref, *out_refs):
    ratio, blocks, span, width = local_ref.shape
    pieces = out_refs[0].shape[1]
    along_sub, along_head = position(len(order), n_head)
    upper = along_head // (n_head // 2)
    follows = lax.axis_index("outer") > 0
    states = [jnp.where(follows, state_ref[r].astype(F32), 0.0).astype(BF16) for r in range(ratio)]
    for distance, out_ref in zip(order, out_refs):
        target = along_sub ^ distance
        for kept in range(2):
            for piece in range(pieces):
                block = (target * 2 + (upper ^ (1 - kept))) * pieces + piece
                for r in range(ratio):
                    core = local_ref[r, block] + dot(reach_ref[r, block], states[r])
                    mean_square = jnp.mean(core * core, 1, keepdims=True)
                    out_ref[kept, piece, r] = (core * lax.rsqrt(mean_square + EPSILON)).astype(BF16)


def project_kernel(order, gate_places, kept, *refs):
    parts, shares = len(order), len(gate_places)
    normed_refs, gate_refs = refs[:parts], refs[parts : parts + shares]
    weight_ref, *send_refs, keep_ref, rows_ref = refs[parts + 2 * shares :]
    unused, pieces, ratio, span, width = normed_refs[0].shape
    tokens = gate_refs[0].shape[2]
    per = span // tokens
    along_sub, along_head = position(parts, 2 * shares)
    for distance, normed_ref in zip(order, normed_refs):
        source = along_sub ^ distance
        for apart, gate_ref in enumerate(gate_refs):
            share = (along_head ^ apart) & (shares - 1)
            first = ((1 - apart % 2) * (shares // 2) + share // 2) * tokens
            place = pl.ds(pl.multiple_of(first, tokens), tokens)
            from_rows = pl.ds(pl.multiple_of(share % per * tokens, tokens), tokens)
            for r in range(ratio):
                lanes = pl.ds(pl.multiple_of((source * ratio + r) * width, width), width)
                normed = normed_ref[kept, share // per, r, from_rows].astype(F32)
                gate = gate_ref[gate_places[apart], source * ratio + r].astype(F32)
                rows_ref[place, lanes] = (normed * gate).astype(BF16)
    out = dot(rows_ref[...], weight_ref[...]).reshape((2,) + keep_ref.shape)
    first = 0
    for send_ref in send_refs:
        columns = send_ref.shape[-1]
        send_ref[...] = out[0, :, :, first : first + columns].astype(BF16)
        first += columns
    keep_ref[...] = out[1]


def sum_kernel(keep_ref, *refs):
    out_ref = refs[-1]
    first = 0
    for number, got_ref in enumerate(refs[:-1]):
        columns = got_ref.shape[-1]
        if first == keep_ref.shape[-1]:
            break
        total = keep_ref[:, :, first : first + columns] + got_ref[...].astype(F32)
        for more_ref in refs[:-1]:
            if more_ref.shape[-1] == keep_ref.shape[-1] and more_ref is not got_ref:
                total = total + more_ref[:, :, first : first + columns].astype(F32)
        out_ref[:, :, first : first + columns] = total.astype(out_ref.dtype)
        first += columns


def per_device(
    outer, sub, n_head, queries, key_vectors, value_vectors, output_gate, write_strength, norm_gain, output_weight
):
    tokens, key_heads, width = queries.shape
    value_heads = value_vectors.shape[1]
    ratio = value_heads // key_heads
    sources = sub * n_head
    shard = tokens * sources
    blocks = shard // SPAN
    shard_tokens = tokens * n_head
    shape = jax.ShapeDtypeStruct
    along_sub, along_head = split_axis("sub", sub), split_axis("head", n_head)

    with jax.named_scope("pack"):
        slab = ((2 + ratio) * tokens + ROW_TILE, width)
        packed = pl.pallas_call(
            functools.partial(pack_kernel, sub),
            out_shape=shape((sources,) + slab, BF16),
            in_specs=[ANY] * 4,
            out_specs=ANY,
            scratch_shapes=[
                pltpu.VMEM(queries.shape, BF16),
                pltpu.VMEM(key_vectors.shape, BF16),
                pltpu.VMEM(value_vectors.shape, BF16),
                pltpu.VMEM((value_heads, tokens), BF16),
                pltpu.VMEM((sources,) + slab, BF16),
                pltpu.SemaphoreType.DMA((4,)),
                pltpu.SemaphoreType.DMA((3 + ratio,)),
            ],
            compiler_params=params(60),
        )(queries, key_vectors, value_vectors, write_strength.T)
    got = lax.all_to_all(packed, partner_order(sub, n_head), split_axis=0, concat_axis=0, tiled=True)

    heads = sub * ratio
    by_core = [(here, here ^ 1) for here in range(n_head)]
    group = (heads, tokens, width)
    half = n_head // 2
    with jax.named_scope("gates"):
        own_gates, swap = pl.pallas_call(
            functools.partial(gate_kernel, sub, n_head),
            out_shape=[shape((half,) + group, BF16)] * 2,
            in_specs=[VMEM] * 2,
            out_specs=[VMEM] * 2,
            scratch_shapes=[pltpu.VMEM((value_heads, tokens, width), BF16)],
            compiler_params=params(),
            cost_estimate=LIGHT,
        )(output_gate, norm_gain.reshape(1, width))
    swapped = lax.ppermute(swap, along_head, by_core)
    with jax.named_scope("pair"):
        pairs = pl.pallas_call(
            pair_kernel,
            out_shape=[shape((2,) + group, BF16)] * (half - 1),
            in_specs=[VMEM] * 2,
            out_specs=[VMEM] * (half - 1),
            compiler_params=params(),
            cost_estimate=LIGHT,
        )(own_gates, swapped)

    state_type = BF16 if outer == 2 else F32
    with jax.named_scope("factors"):
        depths = []
        while blocks >> len(depths) > 1:
            depths.append(blocks >> len(depths))
        tree = []
        for depth in depths:
            tree += [shape((depth, ratio, width, width), BF16), shape((depth, ratio, width, width), F32)]
        if outer > 2:
            tree.append(shape((ratio, width, width), F32))
        out_shape = [
            shape((ratio, width, width), state_type),
            shape((blocks, ratio, SPAN, width), BF16),
            shape((blocks, ratio, SPAN, width), F32),
        ] + tree
        state, w, u, *tree = pl.pallas_call(
            functools.partial(factor_kernel, tokens, ratio, sub, half - 1, outer > 2),
            out_shape=out_shape,
            in_specs=[VMEM] + [ANY] * (half - 1),
            out_specs=[VMEM] * len(out_shape),
            compiler_params=params(),
            cost_estimate=LIGHT,
        )(got, *pairs)

    onward = [(here, (here + 1) % outer) for here in range(outer)]
    incoming = lax.ppermute(state, "outer", onward)
    with jax.named_scope("spread"):
        local, reach = pl.pallas_call(
            functools.partial(spread_kernel, tokens, ratio, sub),
            out_shape=[
                shape((ratio, blocks, SPAN, width), F32),
                shape((ratio, blocks, SPAN, width), BF16),
            ],
            in_specs=[VMEM] * (3 + 2 * len(depths)),
            out_specs=[VMEM] * 2,
            compiler_params=params(),
            cost_estimate=LIGHT,
        )(got, w, u, *tree[: 2 * len(depths)])
    with jax.named_scope("release"):
        pairs = pl.pallas_call(
            release_kernel,
            out_shape=[shape((2,) + group, BF16)] * (half - 1),
            in_specs=[ANY] * half,
            out_specs=[ANY] * (half - 1),
            input_output_aliases={1 + number: number for number in range(half - 1)},
            compiler_params=params(),
            cost_estimate=LIGHT,
        )(state, *pairs)
    gates = [(own_gates, 0), (swapped, 0)]
    for number, pair in enumerate(pairs):
        distance = 2 * number + 2
        pair = lax.ppermute(pair, along_head, [(here, here ^ distance) for here in range(n_head)])
        gates += [(pair, 0), (pair, 1)]
    for hop in range(outer - 2):
        incoming = jnp.where(lax.axis_index("outer") == 0, 0.0, incoming)
        turned_by = jnp.einsum("hde,hef->hdf", tree[-1], incoming, precision=lax.Precision.HIGHEST)
        incoming = lax.ppermute(state + incoming - turned_by, "outer", onward)

    pieces = shard_tokens // SPAN // 2
    columns = output_weight.shape[1]
    quarter = (n_head // 4, tokens, columns)
    half = n_head // 2
    order = [0] + sorted(range(1, sub), reverse=True)
    with jax.named_scope("join"):
        normed = pl.pallas_call(
            functools.partial(join_kernel, order, n_head),
            out_shape=[shape((2, pieces, ratio, SPAN, width), BF16)] * sub,
            in_specs=[VMEM] * 3,
            out_specs=[VMEM] * sub,
            compiler_params=params(),
            cost_estimate=pl.CostEstimate(flops=2 * 10**9, bytes_accessed=1, transcendentals=0),
        )(incoming, local, reach)
    normed = [
        lax.ppermute(part, along_sub, [(here, here ^ distance) for here in range(sub)]) if distance else part
        for distance, part in zip(order, normed)
    ]
    for kept in range(2):
        cuts = 1 + kept
        used, others = gates[half * (1 - kept) : half * (2 - kept)], gates[half * kept : half * (1 + kept)]
        operands = [*normed, *[array for array, unused in used + others], output_weight]
        with jax.named_scope("project"):
            *sends, keep = pl.pallas_call(
                functools.partial(project_kernel, order, [place for unused, place in used], kept),
                out_shape=[shape(quarter[:-1] + (columns // cuts,), BF16)] * cuts + [shape(quarter, F32)],
                in_specs=[VMEM] * (sub + half) + [ANY] * half + [VMEM],
                out_specs=[VMEM] * (cuts + 1),
                scratch_shapes=[pltpu.VMEM((shard_tokens // 2, heads * width), BF16)],
                compiler_params=params(),
                cost_estimate=LIGHT,
            )(*operands)
        arrived = [lax.ppermute(send, along_head, by_core) for send in sends]
        last = n_head == 4 and kept == 1
        with jax.named_scope("sum"):
            summed = pl.pallas_call(
                sum_kernel,
                out_shape=shape(quarter, F32 if kept and not last else BF16),
                in_specs=[VMEM] * (1 + cuts + kept),
                out_specs=VMEM,
                compiler_params=params(),
                cost_estimate=LIGHT,
            )(keep, *arrived, *([passed_on] if kept else []))
        if not kept:
            passed_on = lax.ppermute(summed, along_head, [(here, here ^ half) for here in range(n_head)])
    bit = 2
    while bit < half:
        mine = (lax.axis_index(along_head) // bit) % 2
        split = summed.reshape((summed.shape[0] // 2, 2) + summed.shape[1:])
        send = lax.dynamic_index_in_dim(split, 1 - mine, 1, False).astype(BF16)
        keep = lax.dynamic_index_in_dim(split, mine, 1, False)
        summed = keep + lax.ppermute(send, along_head, [(here, here ^ bit) for here in range(n_head)]).astype(F32)
        bit *= 2
    return summed[0].astype(BF16)


def solution(mesh):
    n_seq, n_head = mesh.shape["seq"], mesh.shape["head"]

    def run(queries, key_vectors, value_vectors, output_gate, write_strength, norm_gain, output_weight):
        sub = queries.shape[1] // n_head
        outer = n_seq // sub
        along = split_axis("sub", sub) + split_axis("head", n_head)
        split = Mesh(mesh.devices.reshape((outer,) + (2,) * len(along)), ("outer",) + along)
        every = ("outer",) + along
        placed = (
            P(every, None, None),
            P(every, None, None),
            P(every, None, None),
            P(every, None, None),
            P(every, None),
            P(),
            P(split_axis("head", n_head), None),
        )
        return jax.shard_map(
            functools.partial(per_device, outer, sub, n_head),
            mesh=split,
            in_specs=placed,
            out_specs=P(every, None),
            check_vma=False,
        )(queries, key_vectors, value_vectors, output_gate, write_strength, norm_gain, output_weight)

    return run
```

```python
import functools

import jax
import jax.numpy as jnp
from jax import lax
from jax.experimental import pallas as pl
from jax.experimental.pallas import tpu as pltpu
from jax.sharding import Mesh, PartitionSpec as P

SPAN = 128
EPSILON = 1e-06
F32 = jnp.float32
BF16 = jnp.bfloat16
ROW_TILE = 16
VMEM = pl.BlockSpec(memory_space=pltpu.VMEM)
SMEM = pl.BlockSpec(memory_space=pltpu.SMEM)
ANY = pl.BlockSpec(memory_space=pl.ANY)
LIGHT = pl.CostEstimate(flops=1, bytes_accessed=1, transcendentals=0)


def dot(left, right):
    return jnp.dot(left, right, preferred_element_type=F32)


def dot_nt(left, right):
    return lax.dot_general(left, right, (((1,), (1,)), ((), ())), preferred_element_type=F32)


def params(megabytes=24):
    return pltpu.CompilerParams(vmem_limit_bytes=megabytes * 2**20)


def turned(values):
    return jnp.transpose(values, (1, 0, 2))


def split_axis(name, size):
    return tuple(f"{name}{bit}" for bit in reversed(range(size.bit_length() - 1)))


def partner_order(sub, n_head):
    heads = split_axis("head", n_head)
    return heads[-1:] + heads[:-1] + split_axis("sub", sub)


def partner(source, sub, n_head):
    axes = split_axis("sub", sub) + split_axis("head", n_head)
    bits = {name: source >> (len(axes) - 1 - number) & 1 for number, name in enumerate(axes)}
    place = 0
    for name in partner_order(sub, n_head):
        place = 2 * place + bits[name]
    return place


def position(sub, n_head):
    return lax.axis_index(split_axis("sub", sub)), lax.axis_index(split_axis("head", n_head))


def pack_kernel(sub, q_hbm, k_hbm, v_hbm, b_hbm, out_hbm, q_ref, k_ref, v_ref, b_ref, out_ref, came, left):
    tokens, key_heads, width = q_hbm.shape
    ratio = v_hbm.shape[1] // key_heads
    copies = [
        pltpu.make_async_copy(source, target, came.at[number])
        for number, (source, target) in enumerate(
            ((b_hbm, b_ref), (k_hbm, k_ref), (q_hbm, q_ref), (v_hbm, v_ref))
        )
    ]
    for copy in copies:
        copy.start()
    n_head = key_heads // sub
    heads = [head % sub * n_head + head // sub for head in range(key_heads)]
    heads = [partner(source, sub, n_head) for source in heads]
    heads = [heads.index(peer) for peer in range(key_heads)]
    leaving = []

    def leave(first, size):
        rows = pl.ds(first, size)
        leaving.append(pltpu.make_async_copy(out_ref.at[:, rows], out_hbm.at[:, rows], left.at[len(leaving)]))
        leaving[-1].start()

    copies[0].wait()
    strength = jnp.concatenate([b_ref[...].astype(F32)] * (width // tokens), axis=1)
    strength = jnp.concatenate([strength, jnp.zeros((ROW_TILE, width), F32)], axis=0)
    for peer, head in enumerate(heads):
        tile = strength[head * ratio : head * ratio + ROW_TILE]
        out_ref[peer, (2 + ratio) * tokens :] = tile.astype(BF16)
    leave((2 + ratio) * tokens, ROW_TILE)
    for place, copy, ref in ((1, copies[1], k_ref), (0, copies[2], q_ref)):
        copy.wait()
        rows = turned(ref[...])
        for peer, head in enumerate(heads):
            out_ref[peer, place * tokens : (place + 1) * tokens] = rows[head]
        leave(place * tokens, tokens)
    copies[3].wait()
    rows = turned(v_ref[...])
    for r in range(ratio):
        for peer, head in enumerate(heads):
            out_ref[peer, (2 + r) * tokens : (3 + r) * tokens] = rows[head * ratio + r]
        leave((2 + r) * tokens, tokens)
    for copy in leaving:
        copy.wait()


def gate_kernel(sub, n_head, gate_ref, gain_ref, own_ref, swap_ref, gates):
    heads = own_ref.shape[1]
    unused, along_head = position(sub, n_head)
    gate = gate_ref[...].astype(F32)
    gated = gain_ref[...].astype(F32)[:, None] * (gate / (1.0 + jnp.exp(-gate)))
    gates[...] = turned(gated.astype(BF16))
    for number in range(n_head // 2):
        own_ref[number] = gates[pl.ds((along_head ^ (2 * number)) * heads, heads)]
        swap_ref[number] = gates[pl.ds((along_head ^ (2 * number + 1)) * heads, heads)]


def pair_kernel(own_ref, swapped_ref, *pair_refs):
    for number, pair_ref in enumerate(pair_refs):
        pair_ref[0] = own_ref[number + 1]
        pair_ref[1] = swapped_ref[number + 1]


def block_slabs(blocks, sub, sources):
    places = [partner(source, sub, sources // sub) for source in range(sources)]
    per = sources // blocks
    return [places[block * per : (block + 1) * per] for block in range(blocks)]


def block_rows(got_ref, slabs, tokens, part):
    return jnp.concatenate([got_ref[slab, part * tokens : (part + 1) * tokens] for slab in slabs], axis=0)


def beside(matrices):
    return jnp.concatenate(matrices, axis=1)


def parts_of(wide, count):
    width = wide.shape[1] // count
    return [wide[:, part * width : (part + 1) * width] for part in range(count)]


def block_inverse(below):
    size = below[0].shape[0]
    rows = lax.broadcasted_iota(jnp.int32, (size, size), 0)
    cols = lax.broadcasted_iota(jnp.int32, (size, size), 1)
    zero = jnp.zeros((size, size), F32)
    step = 1
    solved = None
    while step < size:
        joins = (rows // (2 * step) == cols // (2 * step)) & (rows // step > cols // step)
        parts = [jnp.where(joins, matrix, zero) for matrix in below]
        if step == 1:
            solved = [
                jnp.where(rows == cols, jnp.ones_like(zero), -part).astype(BF16) for part in parts
            ]
        else:
            inner = [dot(part.astype(BF16), now).astype(BF16) for part, now in zip(parts, solved)]
            solved = [now - dot(now, mid).astype(BF16) for now, mid in zip(solved, inner)]
        step *= 2
    return solved


def factor_kernel(tokens, ratio, sub, passing, total_too, got_ref, *refs):
    state_ref, w_ref, u_ref, *tree_refs = refs[passing:]
    width = got_ref.shape[-1]
    per = SPAN // tokens
    blocks = got_ref.shape[0] // per
    slabs = block_slabs(blocks, sub, got_ref.shape[0])
    rows = lax.broadcasted_iota(jnp.int32, (SPAN, SPAN), 0)
    cols = lax.broadcasted_iota(jnp.int32, (SPAN, SPAN), 1)
    lane = lax.broadcasted_iota(jnp.int32, (1, SPAN), 1)
    first = (2 + ratio) * tokens
    below, held = [], []
    for block in range(blocks):
        key = block_rows(got_ref, slabs[block], tokens, 1)
        gram = dot_nt(key, key)
        squares = jnp.where(rows == cols, gram, 0.0)
        key_row = lax.rsqrt(jnp.sum(squares, 0, keepdims=True) + EPSILON)
        key_col = lax.rsqrt(jnp.sum(squares, 1, keepdims=True) + EPSILON)
        lower = jnp.where(rows > cols, gram, 0.0) * key_row
        strengths = []
        for r in range(ratio):
            strength = jnp.zeros((1, SPAN), F32)
            for place in range(per):
                piece = got_ref[slabs[block][place], first : first + ROW_TILE].astype(F32)[r : r + 1]
                strength = jnp.where(lane // tokens == place, piece, strength)
            scaled_col = jnp.sum(jnp.where(rows == cols, strength * key_row, 0.0), 1, keepdims=True)
            below.append(lower * scaled_col)
            strengths.append(strength)
        held.append((block, key, key_col, key_row, strengths))
    solved = block_inverse(below)
    flat = [(block, r) for block in range(blocks) for r in range(ratio)]
    weighted = []
    for inverse, (block, r) in zip(solved, flat):
        unused, key, key_col, key_row, strengths = held[block]
        weighted.append(inverse.astype(F32) * key_col * strengths[r])
    for part, (block, r) in zip(weighted, flat):
        value = block_rows(got_ref, slabs[block], tokens, 2 + r)
        u_ref[block, r] = dot(part.astype(BF16), value)
    for part, (block, r) in zip(weighted, flat):
        unused, key, key_col, key_row, strengths = held[block]
        w_ref[block, r] = dot((part * key_row).astype(BF16), key).astype(BF16)
    turns, adds = [], []
    for block in range(blocks):
        key_t = held[block][1].T
        for r in range(ratio):
            turn, add = parts_of(dot(key_t, beside([w_ref[block, r], u_ref[block, r].astype(BF16)])), 2)
            turns.append(turn)
            adds.append(add)

    level = 0
    while len(adds) > ratio:
        count = len(adds) // ratio
        trans_ref, add_ref = tree_refs[2 * level : 2 * level + 2]
        for number in range(len(adds)):
            trans_ref[number // ratio, number % ratio] = turns[number].astype(BF16)
            add_ref[number // ratio, number % ratio] = adds[number]
        longer_turns, longer_adds = [], []
        for pair in range(count // 2):
            for r in range(ratio):
                left, right = 2 * pair * ratio + r, (2 * pair + 1) * ratio + r
                if count > 2 or total_too:
                    both = beside([turns[left], adds[left]])
                    turn, add = parts_of(both - dot(turns[right].astype(BF16), both.astype(BF16)), 2)
                    longer_turns.append(turns[right] + turn)
                else:
                    add = adds[left] - dot(turns[right].astype(BF16), adds[left].astype(BF16))
                longer_adds.append(add + adds[right])
        turns, adds = longer_turns, longer_adds
        level += 1
    for r in range(ratio):
        state_ref[r] = adds[r].astype(state_ref.dtype)
        if total_too:
            tree_refs[-1][r] = turns[r]


def tree_starts(ratio, width, tree_refs):
    rows = lax.broadcasted_iota(jnp.int32, (width, 2 * width), 0)
    cols = lax.broadcasted_iota(jnp.int32, (width, 2 * width), 1)
    neutral = jnp.where(cols == rows + width, 1.0, 0.0).astype(F32)
    starts = [None] * ratio
    for level in reversed(range(len(tree_refs) // 2)):
        trans_ref, add_ref = tree_refs[2 * level : 2 * level + 2]
        longer = []
        for number, start in enumerate(starts):
            place, r = 2 * (number // ratio), number % ratio
            add = beside([add_ref[place, r], jnp.zeros((width, width), F32)])
            if start is None:
                turn = beside([jnp.zeros((width, width), F32), trans_ref[place, r].astype(F32)])
                longer.append((start, neutral - turn + add))
            else:
                longer.append((start, start - dot(trans_ref[place, r], start.astype(BF16)) + add))
        starts = []
        for pair in range(len(longer) // ratio):
            for side in range(2):
                starts += [longer[pair * ratio + r][side] for r in range(ratio)]
    return [neutral if start is None else start for start in starts]


def spread_kernel(tokens, ratio, sub, passing, got_ref, w_ref, u_ref, *refs):
    refs = refs[: len(refs) - passing]
    tree_refs, (local_ref, reach_ref) = refs[: len(refs) - passing - 2], refs[-2:]
    width = got_ref.shape[-1]
    per = SPAN // tokens
    blocks = got_ref.shape[0] // per
    slabs = block_slabs(blocks, sub, got_ref.shape[0])
    rows = lax.broadcasted_iota(jnp.int32, (SPAN, SPAN), 0)
    cols = lax.broadcasted_iota(jnp.int32, (SPAN, SPAN), 1)
    starts = [start.astype(BF16) for start in tree_starts(ratio, width, tree_refs)]
    lefts, units = [], []
    for block in range(blocks):
        query = block_rows(got_ref, slabs[block], tokens, 0)
        key = block_rows(got_ref, slabs[block], tokens, 1)
        scores = jnp.where(rows >= cols, dot_nt(query, key), 0.0).astype(BF16)
        query_f = query.astype(F32)
        squares = jnp.sum(query_f * query_f, 1, keepdims=True)
        units.append(lax.rsqrt(squares + EPSILON) * width ** (-0.5))
        lefts.append(beside([query, scores]))
    flat = [(block, r) for block in range(blocks) for r in range(ratio)]
    rights = []
    for start, (block, r) in zip(starts, flat):
        through, reached = parts_of(dot(w_ref[block, r], start), 2)
        corrected = beside([u_ref[block, r] - through, -reached]).astype(BF16)
        rights.append(jnp.concatenate([start, corrected], axis=0))
    for right, (block, r) in zip(rights, flat):
        out = dot(lefts[block], right) * units[block]
        local_ref[r, block] = out[:, :width]
        reach_ref[r, block] = out[:, width:].astype(BF16)


def join_kernel(order, n_head, state_ref, local_ref, reach_ref, *out_refs):
    ratio, blocks, span, width = local_ref.shape
    pieces = out_refs[0].shape[1]
    along_sub, along_head = position(len(order), n_head)
    upper = along_head // (n_head // 2)
    follows = lax.axis_index("outer") > 0
    states = [jnp.where(follows, state_ref[r].astype(F32), 0.0).astype(BF16) for r in range(ratio)]
    for distance, out_ref in zip(order, out_refs):
        target = along_sub ^ distance
        for kept in range(2):
            for piece in range(pieces):
                block = (target * 2 + (upper ^ (1 - kept))) * pieces + piece
                for r in range(ratio):
                    core = local_ref[r, block] + dot(reach_ref[r, block], states[r])
                    mean_square = jnp.mean(core * core, 1, keepdims=True)
                    out_ref[kept, piece, r] = (core * lax.rsqrt(mean_square + EPSILON)).astype(BF16)


def project_kernel(order, gate_places, kept, *refs):
    parts, shares = len(order), len(gate_places)
    normed_refs, gate_refs = refs[:parts], refs[parts : parts + shares]
    weight_ref, *out_refs, rows_ref = refs[parts + 2 * shares :]
    unused, pieces, ratio, span, width = normed_refs[0].shape
    tokens = gate_refs[0].shape[2]
    per = span // tokens
    along_sub, along_head = position(parts, 2 * shares)
    for distance, normed_ref in zip(order, normed_refs):
        source = along_sub ^ distance
        for apart, gate_ref in enumerate(gate_refs):
            share = (along_head ^ apart) & (shares - 1)
            first = ((1 - apart % 2) * (shares // 2) + share // 2) * tokens
            place = pl.ds(pl.multiple_of(first, tokens), tokens)
            from_rows = pl.ds(pl.multiple_of(share % per * tokens, tokens), tokens)
            for r in range(ratio):
                lanes = pl.ds(pl.multiple_of((source * ratio + r) * width, width), width)
                normed = normed_ref[kept, share // per, r, from_rows].astype(F32)
                gate = gate_ref[gate_places[apart], source * ratio + r].astype(F32)
                rows_ref[place, lanes] = (normed * gate).astype(BF16)
    multiply(0, rows_ref[...], weight_ref, out_refs)


def multiply(first, rows, weight_ref, out_refs):
    *send_refs, keep_ref = out_refs
    every = keep_ref.shape[-1]
    out = dot(rows, weight_ref[:, first : first + every]).reshape((2,) + keep_ref.shape)
    start = 0
    for send_ref in send_refs:
        columns = send_ref.shape[-1]
        send_ref[...] = out[0, :, :, start : start + columns].astype(BF16)
        start += columns
    keep_ref[...] = out[1]


def more_kernel(first, rows_ref, weight_ref, *out_refs):
    multiply(first, rows_ref[...], weight_ref, out_refs)


def sum_kernel(keep_ref, *refs):
    *got_refs, out_ref = refs
    every = keep_ref.shape[-1]
    placed, start = [], 0
    for got_ref in got_refs:
        placed.append((start, got_ref))
        start = (start + got_ref.shape[-1]) % every
    cuts = sorted({first for first, unused in placed} | {every})
    for first, last in zip(cuts, cuts[1:]):
        total = keep_ref[:, :, first:last]
        for start, got_ref in placed:
            if start <= first and last <= start + got_ref.shape[-1]:
                total = total + got_ref[:, :, first - start : last - start].astype(F32)
        out_ref[:, :, first:last] = total.astype(out_ref.dtype)


def per_device(
    outer, sub, n_head, queries, key_vectors, value_vectors, output_gate, write_strength, norm_gain, output_weight
):
    tokens, key_heads, width = queries.shape
    value_heads = value_vectors.shape[1]
    ratio = value_heads // key_heads
    sources = sub * n_head
    shard = tokens * sources
    blocks = shard // SPAN
    shard_tokens = tokens * n_head
    shape = jax.ShapeDtypeStruct
    along_sub, along_head = split_axis("sub", sub), split_axis("head", n_head)

    with jax.named_scope("pack"):
        slab = ((2 + ratio) * tokens + ROW_TILE, width)
        packed = pl.pallas_call(
            functools.partial(pack_kernel, sub),
            out_shape=shape((sources,) + slab, BF16),
            in_specs=[ANY] * 4,
            out_specs=ANY,
            scratch_shapes=[
                pltpu.VMEM(queries.shape, BF16),
                pltpu.VMEM(key_vectors.shape, BF16),
                pltpu.VMEM(value_vectors.shape, BF16),
                pltpu.VMEM((value_heads, tokens), BF16),
                pltpu.VMEM((sources,) + slab, BF16),
                pltpu.SemaphoreType.DMA((4,)),
                pltpu.SemaphoreType.DMA((3 + ratio,)),
            ],
            compiler_params=params(60),
        )(queries, key_vectors, value_vectors, write_strength.T)
    got = lax.all_to_all(packed, partner_order(sub, n_head), split_axis=0, concat_axis=0, tiled=True)

    heads = sub * ratio
    by_core = [(here, here ^ 1) for here in range(n_head)]
    group = (heads, tokens, width)
    half = n_head // 2
    with jax.named_scope("gates"):
        own_gates, swap = pl.pallas_call(
            functools.partial(gate_kernel, sub, n_head),
            out_shape=[shape((half,) + group, BF16)] * 2,
            in_specs=[VMEM] * 2,
            out_specs=[VMEM] * 2,
            scratch_shapes=[pltpu.VMEM((value_heads, tokens, width), BF16)],
            compiler_params=params(),
            cost_estimate=LIGHT,
        )(output_gate, norm_gain.reshape(1, width))
    swapped = lax.ppermute(swap, along_head, by_core)
    with jax.named_scope("pair"):
        pairs = pl.pallas_call(
            pair_kernel,
            out_shape=[shape((2,) + group, BF16)] * (half - 1),
            in_specs=[VMEM] * 2,
            out_specs=[VMEM] * (half - 1),
            compiler_params=params(),
            cost_estimate=LIGHT,
        )(own_gates, swapped)

    state_type = BF16 if outer == 2 else F32
    with jax.named_scope("factors"):
        depths = []
        while blocks >> len(depths) > 1:
            depths.append(blocks >> len(depths))
        tree = []
        for depth in depths:
            tree += [shape((depth, ratio, width, width), BF16), shape((depth, ratio, width, width), F32)]
        if outer > 2:
            tree.append(shape((ratio, width, width), F32))
        out_shape = [
            shape((ratio, width, width), state_type),
            shape((blocks, ratio, SPAN, width), BF16),
            shape((blocks, ratio, SPAN, width), F32),
        ] + tree
        state, w, u, *tree = pl.pallas_call(
            functools.partial(factor_kernel, tokens, ratio, sub, half - 1, outer > 2),
            out_shape=out_shape,
            in_specs=[VMEM] + [ANY] * (half - 1),
            out_specs=[VMEM] * len(out_shape),
            compiler_params=params(),
            cost_estimate=LIGHT,
        )(got, *pairs)

    onward = [(here, (here + 1) % outer) for here in range(outer)]
    incoming = lax.ppermute(state, "outer", onward)
    with jax.named_scope("spread"):
        read = 3 + 2 * len(depths)
        local, reach, *pairs = pl.pallas_call(
            functools.partial(spread_kernel, tokens, ratio, sub, half - 1),
            out_shape=[
                shape((ratio, blocks, SPAN, width), F32),
                shape((ratio, blocks, SPAN, width), BF16),
            ]
            + [shape((2,) + group, BF16)] * (half - 1),
            in_specs=[VMEM] * read + [ANY] * (half - 1),
            out_specs=[VMEM] * 2 + [ANY] * (half - 1),
            input_output_aliases={read + number: 2 + number for number in range(half - 1)},
            compiler_params=params(),
            cost_estimate=LIGHT,
        )(got, w, u, *tree[: 2 * len(depths)], *pairs)
    gates = [(own_gates, 0), (swapped, 0)]
    for number, pair in enumerate(pairs):
        distance = 2 * number + 2
        pair = lax.ppermute(pair, along_head, [(here, here ^ distance) for here in range(n_head)])
        gates += [(pair, 0), (pair, 1)]
    for hop in range(outer - 2):
        incoming = jnp.where(lax.axis_index("outer") == 0, 0.0, incoming)
        turned_by = jnp.einsum("hde,hef->hdf", tree[-1], incoming, precision=lax.Precision.HIGHEST)
        incoming = lax.ppermute(state + incoming - turned_by, "outer", onward)

    pieces = shard_tokens // SPAN // 2
    columns = output_weight.shape[1]
    quarter = (n_head // 4, tokens, columns)
    half = n_head // 2
    order = [0] + sorted(range(1, sub), reverse=True)
    with jax.named_scope("join"):
        normed = pl.pallas_call(
            functools.partial(join_kernel, order, n_head),
            out_shape=[shape((2, pieces, ratio, SPAN, width), BF16)] * sub,
            in_specs=[VMEM] * 3,
            out_specs=[VMEM] * sub,
            compiler_params=params(),
            cost_estimate=pl.CostEstimate(flops=2 * 10**9, bytes_accessed=1, transcendentals=0),
        )(incoming, local, reach)
    normed = [
        lax.ppermute(part, along_sub, [(here, here ^ distance) for here in range(sub)]) if distance else part
        for distance, part in zip(order, normed)
    ]
    across = [(here, here ^ half) for here in range(n_head)]

    def project(kept, pieces, every, rows_too):
        used, others = gates[half * (1 - kept) : half * (2 - kept)], gates[half * kept : half * (1 + kept)]
        rows = pltpu.VMEM((shard_tokens // 2, heads * width), BF16)
        with jax.named_scope("project"):
            return pl.pallas_call(
                functools.partial(project_kernel, order, [place for unused, place in used], kept),
                out_shape=[shape(quarter[:-1] + (piece,), BF16) for piece in pieces]
                + [shape(quarter[:-1] + (every,), F32)]
                + [shape(rows.shape, BF16)] * rows_too,
                in_specs=[VMEM] * (sub + half) + [ANY] * half + [VMEM],
                out_specs=[VMEM] * (len(pieces) + 1 + rows_too),
                scratch_shapes=[rows] * (1 - rows_too),
                compiler_params=params(),
                cost_estimate=LIGHT,
            )(*normed, *[array for array, unused in used + others], output_weight)

    def add(keep, arrived, kind):
        with jax.named_scope("sum"):
            return pl.pallas_call(
                sum_kernel,
                out_shape=shape(keep.shape, kind),
                in_specs=[VMEM] * (1 + len(arrived)),
                out_specs=VMEM,
                compiler_params=params(),
                cost_estimate=LIGHT,
            )(keep, *arrived)

    cuts = 2
    every = columns // cuts
    passed_on = []
    for cut in range(cuts):
        if cut == 0:
            send, keep, rows = project(0, [every], every, 1)
        else:
            with jax.named_scope("project_more"):
                send, keep = pl.pallas_call(
                    functools.partial(more_kernel, cut * every),
                    out_shape=[shape(quarter[:-1] + (every,), BF16), shape(quarter[:-1] + (every,), F32)],
                    in_specs=[VMEM] * 2,
                    out_specs=[VMEM] * 2,
                    compiler_params=params(),
                    cost_estimate=LIGHT,
                )(rows, output_weight)
        summed = add(keep, [lax.ppermute(send, along_head, by_core)], BF16)
        passed_on.append(lax.ppermute(summed, along_head, across))
    third = columns // 3 // width * width
    *sends, keep = project(1, [columns - 2 * third, third, third], columns, 0)
    arrived = [lax.ppermute(send, along_head, by_core) for send in sends]
    summed = add(keep, arrived + passed_on, BF16 if n_head == 4 else F32)
    bit = 2
    while bit < half:
        mine = (lax.axis_index(along_head) // bit) % 2
        split = summed.reshape((summed.shape[0] // 2, 2) + summed.shape[1:])
        send = lax.dynamic_index_in_dim(split, 1 - mine, 1, False).astype(BF16)
        keep = lax.dynamic_index_in_dim(split, mine, 1, False)
        summed = keep + lax.ppermute(send, along_head, [(here, here ^ bit) for here in range(n_head)]).astype(F32)
        bit *= 2
    return summed[0].astype(BF16)


def solution(mesh):
    n_seq, n_head = mesh.shape["seq"], mesh.shape["head"]

    def run(queries, key_vectors, value_vectors, output_gate, write_strength, norm_gain, output_weight):
        sub = queries.shape[1] // n_head
        outer = n_seq // sub
        along = split_axis("sub", sub) + split_axis("head", n_head)
        split = Mesh(mesh.devices.reshape((outer,) + (2,) * len(along)), ("outer",) + along)
        every = ("outer",) + along
        placed = (
            P(every, None, None),
            P(every, None, None),
            P(every, None, None),
            P(every, None, None),
            P(every, None),
            P(),
            P(split_axis("head", n_head), None),
        )
        return jax.shard_map(
            functools.partial(per_device, outer, sub, n_head),
            mesh=split,
            in_specs=placed,
            out_specs=P(every, None),
            check_vma=False,
        )(queries, key_vectors, value_vectors, output_gate, write_strength, norm_gain, output_weight)

    return run
```

```python
import functools

import jax
import jax.numpy as jnp
from jax import lax
from jax.experimental import pallas as pl
from jax.experimental.pallas import tpu as pltpu
from jax.sharding import Mesh, PartitionSpec as P

SPAN = 128
EPSILON = 1e-06
F32 = jnp.float32
BF16 = jnp.bfloat16
ROW_TILE = 16
VMEM = pl.BlockSpec(memory_space=pltpu.VMEM)
SMEM = pl.BlockSpec(memory_space=pltpu.SMEM)
ANY = pl.BlockSpec(memory_space=pl.ANY)
LIGHT = pl.CostEstimate(flops=1, bytes_accessed=1, transcendentals=0)


def dot(left, right):
    return jnp.dot(left, right, preferred_element_type=F32)


def dot_nt(left, right):
    return lax.dot_general(left, right, (((1,), (1,)), ((), ())), preferred_element_type=F32)


def params(megabytes=24):
    return pltpu.CompilerParams(vmem_limit_bytes=megabytes * 2**20)


def turned(values):
    return jnp.transpose(values, (1, 0, 2))


def split_axis(name, size):
    return tuple(f"{name}{bit}" for bit in reversed(range(size.bit_length() - 1)))


def partner_order(sub, n_head):
    heads = split_axis("head", n_head)
    return heads[-1:] + heads[:-1] + split_axis("sub", sub)


def partner(source, sub, n_head):
    axes = split_axis("sub", sub) + split_axis("head", n_head)
    bits = {name: source >> (len(axes) - 1 - number) & 1 for number, name in enumerate(axes)}
    place = 0
    for name in partner_order(sub, n_head):
        place = 2 * place + bits[name]
    return place


def position(sub, n_head):
    return lax.axis_index(split_axis("sub", sub)), lax.axis_index(split_axis("head", n_head))


def pack_kernel(sub, q_hbm, k_hbm, v_hbm, b_hbm, out_hbm, q_ref, k_ref, v_ref, b_ref, out_ref, came, left):
    tokens, key_heads, width = q_hbm.shape
    ratio = v_hbm.shape[1] // key_heads
    copies = [
        pltpu.make_async_copy(source, target, came.at[number])
        for number, (source, target) in enumerate(
            ((b_hbm, b_ref), (k_hbm, k_ref), (q_hbm, q_ref), (v_hbm, v_ref))
        )
    ]
    for copy in copies:
        copy.start()
    n_head = key_heads // sub
    heads = [head % sub * n_head + head // sub for head in range(key_heads)]
    heads = [partner(source, sub, n_head) for source in heads]
    heads = [heads.index(peer) for peer in range(key_heads)]
    leaving = []

    def leave(first, size):
        rows = pl.ds(first, size)
        leaving.append(pltpu.make_async_copy(out_ref.at[:, rows], out_hbm.at[:, rows], left.at[len(leaving)]))
        leaving[-1].start()

    copies[0].wait()
    strength = jnp.concatenate([b_ref[...].astype(F32)] * (width // tokens), axis=1)
    strength = jnp.concatenate([strength, jnp.zeros((ROW_TILE, width), F32)], axis=0)
    for peer, head in enumerate(heads):
        tile = strength[head * ratio : head * ratio + ROW_TILE]
        out_ref[peer, (2 + ratio) * tokens :] = tile.astype(BF16)
    leave((2 + ratio) * tokens, ROW_TILE)
    for place, copy, ref in ((1, copies[1], k_ref), (0, copies[2], q_ref)):
        copy.wait()
        rows = turned(ref[...])
        for peer, head in enumerate(heads):
            out_ref[peer, place * tokens : (place + 1) * tokens] = rows[head]
        leave(place * tokens, tokens)
    copies[3].wait()
    rows = turned(v_ref[...])
    for r in range(ratio):
        for peer, head in enumerate(heads):
            out_ref[peer, (2 + r) * tokens : (3 + r) * tokens] = rows[head * ratio + r]
        leave((2 + r) * tokens, tokens)
    for copy in leaving:
        copy.wait()


def gate_kernel(sub, n_head, gate_ref, gain_ref, own_ref, swap_ref, gates):
    heads = own_ref.shape[1]
    unused, along_head = position(sub, n_head)
    gate = gate_ref[...].astype(F32)
    gated = gain_ref[...].astype(F32)[:, None] * (gate / (1.0 + jnp.exp(-gate)))
    gates[...] = turned(gated.astype(BF16))
    for number in range(n_head // 2):
        own_ref[number] = gates[pl.ds((along_head ^ (2 * number)) * heads, heads)]
        swap_ref[number] = gates[pl.ds((along_head ^ (2 * number + 1)) * heads, heads)]


def pair_kernel(own_ref, swapped_ref, *pair_refs):
    for number, pair_ref in enumerate(pair_refs):
        pair_ref[0] = own_ref[number + 1]
        pair_ref[1] = swapped_ref[number + 1]


def block_slabs(blocks, sub, sources):
    places = [partner(source, sub, sources // sub) for source in range(sources)]
    per = sources // blocks
    return [places[block * per : (block + 1) * per] for block in range(blocks)]


def block_rows(got_ref, slabs, tokens, part):
    return jnp.concatenate([got_ref[slab, part * tokens : (part + 1) * tokens] for slab in slabs], axis=0)


def beside(matrices):
    return jnp.concatenate(matrices, axis=1)


def parts_of(wide, count):
    width = wide.shape[1] // count
    return [wide[:, part * width : (part + 1) * width] for part in range(count)]


def odd_rows(matrix, step):
    return jnp.concatenate([matrix[first : first + step] for first in range(step, matrix.shape[0], 2 * step)], axis=0)


def between_zeros(rows, step):
    zero = jnp.zeros((step, rows.shape[1]), rows.dtype)
    groups = []
    for first in range(0, rows.shape[0], step):
        groups += [zero, rows[first : first + step]]
    return jnp.concatenate(groups, axis=0)


def block_inverse(below):
    size = below[0].shape[0]
    rows = lax.broadcasted_iota(jnp.int32, (size, size), 0)
    cols = lax.broadcasted_iota(jnp.int32, (size, size), 1)
    step = 1
    solved = None
    while step < size:
        joins = (rows // (2 * step) == cols // (2 * step)) & (rows // step > cols // step)
        if step == 1:
            solved = [
                jnp.where(rows == cols, 1.0, -jnp.where(joins, matrix, 0.0)).astype(BF16) for matrix in below
            ]
        elif step < ROW_TILE:
            parts = [jnp.where(joins, matrix, 0.0).astype(BF16) for matrix in below]
            inner = [dot(part, now).astype(BF16) for part, now in zip(parts, solved)]
            solved = [now - dot(now, mid).astype(BF16) for now, mid in zip(solved, inner)]
        else:
            joins = odd_rows(jnp.where(joins, 1, 0), step) > 0
            parts = [jnp.where(joins, odd_rows(matrix, step), 0.0).astype(BF16) for matrix in below]
            inner = [dot(part, now).astype(BF16) for part, now in zip(parts, solved)]
            inner = [between_zeros(mid, step) for mid in inner]
            outer = [dot(odd_rows(now, step), mid).astype(BF16) for now, mid in zip(solved, inner)]
            solved = [now - between_zeros(part, step) for now, part in zip(solved, outer)]
        step *= 2
    return solved


def factor_kernel(tokens, ratio, sub, passing, total_too, got_ref, *refs):
    state_ref, w_ref, u_ref, *tree_refs = refs[passing:]
    width = got_ref.shape[-1]
    per = SPAN // tokens
    blocks = got_ref.shape[0] // per
    slabs = block_slabs(blocks, sub, got_ref.shape[0])
    rows = lax.broadcasted_iota(jnp.int32, (SPAN, SPAN), 0)
    cols = lax.broadcasted_iota(jnp.int32, (SPAN, SPAN), 1)
    lane = lax.broadcasted_iota(jnp.int32, (1, SPAN), 1)
    first = (2 + ratio) * tokens
    below, held = [], []
    for block in range(blocks):
        key = block_rows(got_ref, slabs[block], tokens, 1)
        gram = dot_nt(key, key)
        squares = jnp.where(rows == cols, gram, 0.0)
        key_row = lax.rsqrt(jnp.sum(squares, 0, keepdims=True) + EPSILON)
        key_col = lax.rsqrt(jnp.sum(squares, 1, keepdims=True) + EPSILON)
        lower = jnp.where(rows > cols, gram, 0.0) * key_row
        strengths = []
        for r in range(ratio):
            strength = jnp.zeros((1, SPAN), F32)
            for place in range(per):
                piece = got_ref[slabs[block][place], first : first + ROW_TILE].astype(F32)[r : r + 1]
                strength = jnp.where(lane // tokens == place, piece, strength)
            scaled_col = jnp.sum(jnp.where(rows == cols, strength * key_row, 0.0), 1, keepdims=True)
            below.append(lower * scaled_col)
            strengths.append(strength)
        held.append((block, key, key_col, key_row, strengths))
    solved = block_inverse(below)
    flat = [(block, r) for block in range(blocks) for r in range(ratio)]
    weighted = []
    for inverse, (block, r) in zip(solved, flat):
        unused, key, key_col, key_row, strengths = held[block]
        weighted.append(inverse.astype(F32) * key_col * strengths[r])
    for part, (block, r) in zip(weighted, flat):
        value = block_rows(got_ref, slabs[block], tokens, 2 + r)
        u_ref[block, r] = dot(part.astype(BF16), value)
    for part, (block, r) in zip(weighted, flat):
        unused, key, key_col, key_row, strengths = held[block]
        w_ref[block, r] = dot((part * key_row).astype(BF16), key).astype(BF16)
    turns, adds = [], []
    for block in range(blocks):
        key_t = held[block][1].T
        for r in range(ratio):
            turn, add = parts_of(dot(key_t, beside([w_ref[block, r], u_ref[block, r].astype(BF16)])), 2)
            turns.append(turn)
            adds.append(add)

    level = 0
    while len(adds) > ratio:
        count = len(adds) // ratio
        trans_ref, add_ref = tree_refs[2 * level : 2 * level + 2]
        for number in range(len(adds)):
            trans_ref[number // ratio, number % ratio] = turns[number].astype(BF16)
            add_ref[number // ratio, number % ratio] = adds[number]
        longer_turns, longer_adds = [], []
        for pair in range(count // 2):
            for r in range(ratio):
                left, right = 2 * pair * ratio + r, (2 * pair + 1) * ratio + r
                if count > 2 or total_too:
                    both = beside([turns[left], adds[left]])
                    turn, add = parts_of(both - dot(turns[right].astype(BF16), both.astype(BF16)), 2)
                    longer_turns.append(turns[right] + turn)
                else:
                    add = adds[left] - dot(turns[right].astype(BF16), adds[left].astype(BF16))
                longer_adds.append(add + adds[right])
        turns, adds = longer_turns, longer_adds
        level += 1
    for r in range(ratio):
        state_ref[r] = adds[r].astype(state_ref.dtype)
        if total_too:
            tree_refs[-1][r] = turns[r]


def tree_starts(ratio, width, tree_refs):
    rows = lax.broadcasted_iota(jnp.int32, (width, 2 * width), 0)
    cols = lax.broadcasted_iota(jnp.int32, (width, 2 * width), 1)
    neutral = jnp.where(cols == rows + width, 1.0, 0.0).astype(F32)
    starts = [None] * ratio
    for level in reversed(range(len(tree_refs) // 2)):
        trans_ref, add_ref = tree_refs[2 * level : 2 * level + 2]
        longer = []
        for number, start in enumerate(starts):
            place, r = 2 * (number // ratio), number % ratio
            add = beside([add_ref[place, r], jnp.zeros((width, width), F32)])
            if start is None:
                turn = beside([jnp.zeros((width, width), F32), trans_ref[place, r].astype(F32)])
                longer.append((start, neutral - turn + add))
            else:
                longer.append((start, start - dot(trans_ref[place, r], start.astype(BF16)) + add))
        starts = []
        for pair in range(len(longer) // ratio):
            for side in range(2):
                starts += [longer[pair * ratio + r][side] for r in range(ratio)]
    return [neutral if start is None else start for start in starts]


def spread_kernel(tokens, ratio, sub, passing, got_ref, w_ref, u_ref, *refs):
    refs = refs[: len(refs) - passing]
    tree_refs, (local_ref, reach_ref) = refs[: len(refs) - passing - 2], refs[-2:]
    width = got_ref.shape[-1]
    per = SPAN // tokens
    blocks = got_ref.shape[0] // per
    slabs = block_slabs(blocks, sub, got_ref.shape[0])
    rows = lax.broadcasted_iota(jnp.int32, (SPAN, SPAN), 0)
    cols = lax.broadcasted_iota(jnp.int32, (SPAN, SPAN), 1)
    starts = [start.astype(BF16) for start in tree_starts(ratio, width, tree_refs)]
    lefts, units = [], []
    for block in range(blocks):
        query = block_rows(got_ref, slabs[block], tokens, 0)
        key = block_rows(got_ref, slabs[block], tokens, 1)
        scores = jnp.where(rows >= cols, dot_nt(query, key), 0.0).astype(BF16)
        query_f = query.astype(F32)
        squares = jnp.sum(query_f * query_f, 1, keepdims=True)
        units.append(lax.rsqrt(squares + EPSILON) * width ** (-0.5))
        lefts.append(beside([query, scores]))
    flat = [(block, r) for block in range(blocks) for r in range(ratio)]
    rights = []
    for start, (block, r) in zip(starts, flat):
        through, reached = parts_of(dot(w_ref[block, r], start), 2)
        corrected = beside([u_ref[block, r] - through, -reached]).astype(BF16)
        rights.append(jnp.concatenate([start, corrected], axis=0))
    for right, (block, r) in zip(rights, flat):
        out = dot(lefts[block], right) * units[block]
        local_ref[r, block] = out[:, :width]
        reach_ref[r, block] = out[:, width:].astype(BF16)


def join_kernel(order, n_head, state_ref, local_ref, reach_ref, *out_refs):
    ratio, blocks, span, width = local_ref.shape
    pieces = out_refs[0].shape[1]
    along_sub, along_head = position(len(order), n_head)
    upper = along_head // (n_head // 2)
    follows = lax.axis_index("outer") > 0
    states = [jnp.where(follows, state_ref[r].astype(F32), 0.0).astype(BF16) for r in range(ratio)]
    for distance, out_ref in zip(order, out_refs):
        target = along_sub ^ distance
        for kept in range(2):
            for piece in range(pieces):
                block = (target * 2 + (upper ^ (1 - kept))) * pieces + piece
                for r in range(ratio):
                    core = local_ref[r, block] + dot(reach_ref[r, block], states[r])
                    mean_square = jnp.mean(core * core, 1, keepdims=True)
                    out_ref[kept, piece, r] = (core * lax.rsqrt(mean_square + EPSILON)).astype(BF16)


def project_kernel(order, gate_places, kept, *refs):
    parts, shares = len(order), len(gate_places)
    normed_refs, gate_refs = refs[:parts], refs[parts : parts + shares]
    weight_ref, *out_refs, rows_ref = refs[parts + 2 * shares :]
    unused, pieces, ratio, span, width = normed_refs[0].shape
    tokens = gate_refs[0].shape[2]
    per = span // tokens
    along_sub, along_head = position(parts, 2 * shares)
    for distance, normed_ref in zip(order, normed_refs):
        source = along_sub ^ distance
        for apart, gate_ref in enumerate(gate_refs):
            share = (along_head ^ apart) & (shares - 1)
            first = ((1 - apart % 2) * (shares // 2) + share // 2) * tokens
            place = pl.ds(pl.multiple_of(first, tokens), tokens)
            from_rows = pl.ds(pl.multiple_of(share % per * tokens, tokens), tokens)
            for r in range(ratio):
                lanes = pl.ds(pl.multiple_of((source * ratio + r) * width, width), width)
                normed = normed_ref[kept, share // per, r, from_rows].astype(F32)
                gate = gate_ref[gate_places[apart], source * ratio + r].astype(F32)
                rows_ref[place, lanes] = (normed * gate).astype(BF16)
    multiply(0, rows_ref[...], weight_ref, out_refs)


def multiply(first, rows, weight_ref, out_refs):
    *send_refs, keep_ref = out_refs
    every = keep_ref.shape[-1]
    out = dot(rows, weight_ref[:, first : first + every]).reshape((2,) + keep_ref.shape)
    start = 0
    for send_ref in send_refs:
        columns = send_ref.shape[-1]
        send_ref[...] = out[0, :, :, start : start + columns].astype(BF16)
        start += columns
    keep_ref[...] = out[1]


def more_kernel(first, rows_ref, weight_ref, *out_refs):
    multiply(first, rows_ref[...], weight_ref, out_refs)


def sum_kernel(keep_ref, *refs):
    *got_refs, out_ref = refs
    every = keep_ref.shape[-1]
    placed, start = [], 0
    for got_ref in got_refs:
        placed.append((start, got_ref))
        start = (start + got_ref.shape[-1]) % every
    cuts = sorted({first for first, unused in placed} | {every})
    for first, last in zip(cuts, cuts[1:]):
        total = keep_ref[:, :, first:last]
        for start, got_ref in placed:
            if start <= first and last <= start + got_ref.shape[-1]:
                total = total + got_ref[:, :, first - start : last - start].astype(F32)
        out_ref[:, :, first:last] = total.astype(out_ref.dtype)


def per_device(
    outer, sub, n_head, queries, key_vectors, value_vectors, output_gate, write_strength, norm_gain, output_weight
):
    tokens, key_heads, width = queries.shape
    value_heads = value_vectors.shape[1]
    ratio = value_heads // key_heads
    sources = sub * n_head
    shard = tokens * sources
    blocks = shard // SPAN
    shard_tokens = tokens * n_head
    shape = jax.ShapeDtypeStruct
    along_sub, along_head = split_axis("sub", sub), split_axis("head", n_head)

    with jax.named_scope("pack"):
        slab = ((2 + ratio) * tokens + ROW_TILE, width)
        packed = pl.pallas_call(
            functools.partial(pack_kernel, sub),
            out_shape=shape((sources,) + slab, BF16),
            in_specs=[ANY] * 4,
            out_specs=ANY,
            scratch_shapes=[
                pltpu.VMEM(queries.shape, BF16),
                pltpu.VMEM(key_vectors.shape, BF16),
                pltpu.VMEM(value_vectors.shape, BF16),
                pltpu.VMEM((value_heads, tokens), BF16),
                pltpu.VMEM((sources,) + slab, BF16),
                pltpu.SemaphoreType.DMA((4,)),
                pltpu.SemaphoreType.DMA((3 + ratio,)),
            ],
            compiler_params=params(60),
        )(queries, key_vectors, value_vectors, write_strength.T)
    got = lax.all_to_all(packed, partner_order(sub, n_head), split_axis=0, concat_axis=0, tiled=True)

    heads = sub * ratio
    by_core = [(here, here ^ 1) for here in range(n_head)]
    group = (heads, tokens, width)
    half = n_head // 2
    with jax.named_scope("gates"):
        own_gates, swap = pl.pallas_call(
            functools.partial(gate_kernel, sub, n_head),
            out_shape=[shape((half,) + group, BF16)] * 2,
            in_specs=[VMEM] * 2,
            out_specs=[VMEM] * 2,
            scratch_shapes=[pltpu.VMEM((value_heads, tokens, width), BF16)],
            compiler_params=params(),
            cost_estimate=LIGHT,
        )(output_gate, norm_gain.reshape(1, width))
    swapped = lax.ppermute(swap, along_head, by_core)
    with jax.named_scope("pair"):
        pairs = pl.pallas_call(
            pair_kernel,
            out_shape=[shape((2,) + group, BF16)] * (half - 1),
            in_specs=[VMEM] * 2,
            out_specs=[VMEM] * (half - 1),
            compiler_params=params(),
            cost_estimate=LIGHT,
        )(own_gates, swapped)

    state_type = BF16 if outer == 2 else F32
    with jax.named_scope("factors"):
        depths = []
        while blocks >> len(depths) > 1:
            depths.append(blocks >> len(depths))
        tree = []
        for depth in depths:
            tree += [shape((depth, ratio, width, width), BF16), shape((depth, ratio, width, width), F32)]
        if outer > 2:
            tree.append(shape((ratio, width, width), F32))
        out_shape = [
            shape((ratio, width, width), state_type),
            shape((blocks, ratio, SPAN, width), BF16),
            shape((blocks, ratio, SPAN, width), F32),
        ] + tree
        state, w, u, *tree = pl.pallas_call(
            functools.partial(factor_kernel, tokens, ratio, sub, half - 1, outer > 2),
            out_shape=out_shape,
            in_specs=[VMEM] + [ANY] * (half - 1),
            out_specs=[VMEM] * len(out_shape),
            compiler_params=params(),
            cost_estimate=LIGHT,
        )(got, *pairs)

    onward = [(here, (here + 1) % outer) for here in range(outer)]
    incoming = lax.ppermute(state, "outer", onward)
    with jax.named_scope("spread"):
        read = 3 + 2 * len(depths)
        local, reach, *pairs = pl.pallas_call(
            functools.partial(spread_kernel, tokens, ratio, sub, half - 1),
            out_shape=[
                shape((ratio, blocks, SPAN, width), F32),
                shape((ratio, blocks, SPAN, width), BF16),
            ]
            + [shape((2,) + group, BF16)] * (half - 1),
            in_specs=[VMEM] * read + [ANY] * (half - 1),
            out_specs=[VMEM] * 2 + [ANY] * (half - 1),
            input_output_aliases={read + number: 2 + number for number in range(half - 1)},
            compiler_params=params(),
            cost_estimate=LIGHT,
        )(got, w, u, *tree[: 2 * len(depths)], *pairs)
    gates = [(own_gates, 0), (swapped, 0)]
    for number, pair in enumerate(pairs):
        distance = 2 * number + 2
        pair = lax.ppermute(pair, along_head, [(here, here ^ distance) for here in range(n_head)])
        gates += [(pair, 0), (pair, 1)]
    for hop in range(outer - 2):
        incoming = jnp.where(lax.axis_index("outer") == 0, 0.0, incoming)
        turned_by = jnp.einsum("hde,hef->hdf", tree[-1], incoming, precision=lax.Precision.HIGHEST)
        incoming = lax.ppermute(state + incoming - turned_by, "outer", onward)

    pieces = shard_tokens // SPAN // 2
    columns = output_weight.shape[1]
    quarter = (n_head // 4, tokens, columns)
    half = n_head // 2
    order = [0] + sorted(range(1, sub), reverse=True)
    with jax.named_scope("join"):
        normed = pl.pallas_call(
            functools.partial(join_kernel, order, n_head),
            out_shape=[shape((2, pieces, ratio, SPAN, width), BF16)] * sub,
            in_specs=[VMEM] * 3,
            out_specs=[VMEM] * sub,
            compiler_params=params(),
            cost_estimate=pl.CostEstimate(flops=2 * 10**9, bytes_accessed=1, transcendentals=0),
        )(incoming, local, reach)
    normed = [
        lax.ppermute(part, along_sub, [(here, here ^ distance) for here in range(sub)]) if distance else part
        for distance, part in zip(order, normed)
    ]
    across = [(here, here ^ half) for here in range(n_head)]

    def project(kept, pieces, every, rows_too):
        used, others = gates[half * (1 - kept) : half * (2 - kept)], gates[half * kept : half * (1 + kept)]
        rows = pltpu.VMEM((shard_tokens // 2, heads * width), BF16)
        with jax.named_scope("project"):
            return pl.pallas_call(
                functools.partial(project_kernel, order, [place for unused, place in used], kept),
                out_shape=[shape(quarter[:-1] + (piece,), BF16) for piece in pieces]
                + [shape(quarter[:-1] + (every,), F32)]
                + [shape(rows.shape, BF16)] * rows_too,
                in_specs=[VMEM] * (sub + half) + [ANY] * half + [VMEM],
                out_specs=[VMEM] * (len(pieces) + 1 + rows_too),
                scratch_shapes=[rows] * (1 - rows_too),
                compiler_params=params(),
                cost_estimate=LIGHT,
            )(*normed, *[array for array, unused in used + others], output_weight)

    def add(keep, arrived, kind):
        with jax.named_scope("sum"):
            return pl.pallas_call(
                sum_kernel,
                out_shape=shape(keep.shape, kind),
                in_specs=[VMEM] * (1 + len(arrived)),
                out_specs=VMEM,
                compiler_params=params(),
                cost_estimate=LIGHT,
            )(keep, *arrived)

    cuts = 2
    every = columns // cuts
    passed_on = []
    for cut in range(cuts):
        if cut == 0:
            send, keep, rows = project(0, [every], every, 1)
        else:
            with jax.named_scope("project_more"):
                send, keep = pl.pallas_call(
                    functools.partial(more_kernel, cut * every),
                    out_shape=[shape(quarter[:-1] + (every,), BF16), shape(quarter[:-1] + (every,), F32)],
                    in_specs=[VMEM] * 2,
                    out_specs=[VMEM] * 2,
                    compiler_params=params(),
                    cost_estimate=LIGHT,
                )(rows, output_weight)
        summed = add(keep, [lax.ppermute(send, along_head, by_core)], BF16)
        passed_on.append(lax.ppermute(summed, along_head, across))
    third = columns // 3 // width * width
    *sends, keep = project(1, [columns - 2 * third, third, third], columns, 0)
    arrived = [lax.ppermute(send, along_head, by_core) for send in sends]
    summed = add(keep, arrived + passed_on, BF16 if n_head == 4 else F32)
    bit = 2
    while bit < half:
        mine = (lax.axis_index(along_head) // bit) % 2
        split = summed.reshape((summed.shape[0] // 2, 2) + summed.shape[1:])
        send = lax.dynamic_index_in_dim(split, 1 - mine, 1, False).astype(BF16)
        keep = lax.dynamic_index_in_dim(split, mine, 1, False)
        summed = keep + lax.ppermute(send, along_head, [(here, here ^ bit) for here in range(n_head)]).astype(F32)
        bit *= 2
    return summed[0].astype(BF16)


def solution(mesh):
    n_seq, n_head = mesh.shape["seq"], mesh.shape["head"]

    def run(queries, key_vectors, value_vectors, output_gate, write_strength, norm_gain, output_weight):
        sub = queries.shape[1] // n_head
        outer = n_seq // sub
        along = split_axis("sub", sub) + split_axis("head", n_head)
        split = Mesh(mesh.devices.reshape((outer,) + (2,) * len(along)), ("outer",) + along)
        every = ("outer",) + along
        placed = (
            P(every, None, None),
            P(every, None, None),
            P(every, None, None),
            P(every, None, None),
            P(every, None),
            P(),
            P(split_axis("head", n_head), None),
        )
        return jax.shard_map(
            functools.partial(per_device, outer, sub, n_head),
            mesh=split,
            in_specs=placed,
            out_specs=P(every, None),
            check_vma=False,
        )(queries, key_vectors, value_vectors, output_gate, write_strength, norm_gain, output_weight)

    return run
```

```python
import functools

import jax
import jax.numpy as jnp
from jax import lax
from jax.experimental import pallas as pl
from jax.experimental.pallas import tpu as pltpu
from jax.sharding import Mesh, PartitionSpec as P

SPAN = 128
EPSILON = 1e-06
F32 = jnp.float32
BF16 = jnp.bfloat16
ROW_TILE = 16
VMEM = pl.BlockSpec(memory_space=pltpu.VMEM)
SMEM = pl.BlockSpec(memory_space=pltpu.SMEM)
ANY = pl.BlockSpec(memory_space=pl.ANY)
LIGHT = pl.CostEstimate(flops=1, bytes_accessed=1, transcendentals=0)


def dot(left, right):
    return jnp.dot(left, right, preferred_element_type=F32)


def dot_nt(left, right):
    return lax.dot_general(left, right, (((1,), (1,)), ((), ())), preferred_element_type=F32)


def params(megabytes=24):
    return pltpu.CompilerParams(vmem_limit_bytes=megabytes * 2**20)


def turned(values):
    return jnp.transpose(values, (1, 0, 2))


def split_axis(name, size):
    return tuple(f"{name}{bit}" for bit in reversed(range(size.bit_length() - 1)))


def partner_order(sub, n_head):
    heads = split_axis("head", n_head)
    return heads[-1:] + heads[:-1] + split_axis("sub", sub)


def partner(source, sub, n_head):
    axes = split_axis("sub", sub) + split_axis("head", n_head)
    bits = {name: source >> (len(axes) - 1 - number) & 1 for number, name in enumerate(axes)}
    place = 0
    for name in partner_order(sub, n_head):
        place = 2 * place + bits[name]
    return place


def position(sub, n_head):
    return lax.axis_index(split_axis("sub", sub)), lax.axis_index(split_axis("head", n_head))


def pack_kernel(sub, q_hbm, k_hbm, v_hbm, b_hbm, out_hbm, q_ref, k_ref, v_ref, b_ref, out_ref, came, left):
    tokens, key_heads, width = q_hbm.shape
    ratio = v_hbm.shape[1] // key_heads
    copies = [
        pltpu.make_async_copy(source, target, came.at[number])
        for number, (source, target) in enumerate(
            ((b_hbm, b_ref), (k_hbm, k_ref), (q_hbm, q_ref), (v_hbm, v_ref))
        )
    ]
    for copy in copies:
        copy.start()
    n_head = key_heads // sub
    heads = [head % sub * n_head + head // sub for head in range(key_heads)]
    heads = [partner(source, sub, n_head) for source in heads]
    heads = [heads.index(peer) for peer in range(key_heads)]
    leaving = []

    def leave(first, size):
        rows = pl.ds(first, size)
        leaving.append(pltpu.make_async_copy(out_ref.at[:, rows], out_hbm.at[:, rows], left.at[len(leaving)]))
        leaving[-1].start()

    copies[0].wait()
    strength = jnp.concatenate([b_ref[...].astype(F32)] * (width // tokens), axis=1)
    strength = jnp.concatenate([strength, jnp.zeros((ROW_TILE, width), F32)], axis=0)
    for peer, head in enumerate(heads):
        tile = strength[head * ratio : head * ratio + ROW_TILE]
        out_ref[peer, (2 + ratio) * tokens :] = tile.astype(BF16)
    leave((2 + ratio) * tokens, ROW_TILE)
    for place, copy, ref in ((1, copies[1], k_ref), (0, copies[2], q_ref)):
        copy.wait()
        rows = turned(ref[...])
        for peer, head in enumerate(heads):
            out_ref[peer, place * tokens : (place + 1) * tokens] = rows[head]
        leave(place * tokens, tokens)
    copies[3].wait()
    rows = turned(v_ref[...])
    for r in range(ratio):
        for peer, head in enumerate(heads):
            out_ref[peer, (2 + r) * tokens : (3 + r) * tokens] = rows[head * ratio + r]
        leave((2 + r) * tokens, tokens)
    for copy in leaving:
        copy.wait()


def gate_kernel(sub, n_head, gate_ref, gain_ref, own_ref, swap_ref, gates):
    heads = own_ref.shape[1]
    unused, along_head = position(sub, n_head)
    gate = gate_ref[...].astype(F32)
    gated = gain_ref[...].astype(F32)[:, None] * (gate / (1.0 + jnp.exp(-gate)))
    gates[...] = turned(gated.astype(BF16))
    for number in range(n_head // 2):
        own_ref[number] = gates[pl.ds((along_head ^ (2 * number)) * heads, heads)]
        swap_ref[number] = gates[pl.ds((along_head ^ (2 * number + 1)) * heads, heads)]


def pair_kernel(own_ref, swapped_ref, *pair_refs):
    for number, pair_ref in enumerate(pair_refs):
        pair_ref[0] = own_ref[number + 1]
        pair_ref[1] = swapped_ref[number + 1]


def block_slabs(blocks, sub, sources):
    places = [partner(source, sub, sources // sub) for source in range(sources)]
    per = sources // blocks
    return [places[block * per : (block + 1) * per] for block in range(blocks)]


def block_rows(got_ref, slabs, tokens, part):
    return jnp.concatenate([got_ref[slab, part * tokens : (part + 1) * tokens] for slab in slabs], axis=0)


def beside(matrices):
    return jnp.concatenate(matrices, axis=1)


def parts_of(wide, count):
    width = wide.shape[1] // count
    return [wide[:, part * width : (part + 1) * width] for part in range(count)]


def block_inverse(below):
    size = below[0].shape[0]
    rows = lax.broadcasted_iota(jnp.int32, (size, size), 0)
    cols = lax.broadcasted_iota(jnp.int32, (size, size), 1)
    zero = jnp.zeros((size, size), F32)
    step = 1
    solved = None
    while step < size:
        joins = (rows // (2 * step) == cols // (2 * step)) & (rows // step > cols // step)
        parts = [jnp.where(joins, matrix, zero) for matrix in below]
        if step == 1:
            solved = [
                jnp.where(rows == cols, jnp.ones_like(zero), -part).astype(BF16) for part in parts
            ]
        else:
            inner = [dot(part.astype(BF16), now).astype(BF16) for part, now in zip(parts, solved)]
            solved = [now - dot(now, mid).astype(BF16) for now, mid in zip(solved, inner)]
        step *= 2
    return solved


def dot_two(left, right):
    high = left.astype(BF16)
    low = (left - high.astype(F32)).astype(BF16)
    both = dot(jnp.concatenate([high, low], axis=0), right)
    return both[: left.shape[0]] + both[left.shape[0] :]


def refined(below, solved):
    size = below[0].shape[0]
    rows = lax.broadcasted_iota(jnp.int32, (size, size), 0)
    cols = lax.broadcasted_iota(jnp.int32, (size, size), 1)
    identity = jnp.where(rows == cols, 1.0, 0.0)
    left_over = [
        (identity - now.astype(F32) - dot_two(matrix, now)).astype(BF16) for matrix, now in zip(below, solved)
    ]
    return [now.astype(F32) + dot(now, rest) for now, rest in zip(solved, left_over)]


def factor_kernel(tokens, ratio, sub, passing, total_too, got_ref, *refs):
    state_ref, w_ref, u_ref, *tree_refs = refs[passing:]
    width = got_ref.shape[-1]
    per = SPAN // tokens
    blocks = got_ref.shape[0] // per
    slabs = block_slabs(blocks, sub, got_ref.shape[0])
    rows = lax.broadcasted_iota(jnp.int32, (SPAN, SPAN), 0)
    cols = lax.broadcasted_iota(jnp.int32, (SPAN, SPAN), 1)
    lane = lax.broadcasted_iota(jnp.int32, (1, SPAN), 1)
    first = (2 + ratio) * tokens
    below, held = [], []
    for block in range(blocks):
        key = block_rows(got_ref, slabs[block], tokens, 1)
        gram = dot_nt(key, key)
        squares = jnp.where(rows == cols, gram, 0.0)
        key_row = lax.rsqrt(jnp.sum(squares, 0, keepdims=True) + EPSILON)
        key_col = lax.rsqrt(jnp.sum(squares, 1, keepdims=True) + EPSILON)
        lower = jnp.where(rows > cols, gram, 0.0) * key_row
        strengths = []
        for r in range(ratio):
            strength = jnp.zeros((1, SPAN), F32)
            for place in range(per):
                piece = got_ref[slabs[block][place], first : first + ROW_TILE].astype(F32)[r : r + 1]
                strength = jnp.where(lane // tokens == place, piece, strength)
            scaled_col = jnp.sum(jnp.where(rows == cols, strength * key_row, 0.0), 1, keepdims=True)
            below.append(lower * scaled_col)
            strengths.append(strength)
        held.append((block, key, key_col, key_row, strengths))
    solved = refined(below, block_inverse(below))
    flat = [(block, r) for block in range(blocks) for r in range(ratio)]
    weighted = []
    for inverse, (block, r) in zip(solved, flat):
        unused, key, key_col, key_row, strengths = held[block]
        weighted.append(inverse * key_col * strengths[r])
    for part, (block, r) in zip(weighted, flat):
        value = block_rows(got_ref, slabs[block], tokens, 2 + r)
        u_ref[block, r] = dot_two(part, value)
    for part, (block, r) in zip(weighted, flat):
        unused, key, key_col, key_row, strengths = held[block]
        w_ref[block, r] = dot_two(part * key_row, key).astype(BF16)
    turns, adds = [], []
    for block in range(blocks):
        key_t = held[block][1].T
        for r in range(ratio):
            turn, add = parts_of(dot(key_t, beside([w_ref[block, r], u_ref[block, r].astype(BF16)])), 2)
            turns.append(turn)
            adds.append(add)

    level = 0
    while len(adds) > ratio:
        count = len(adds) // ratio
        trans_ref, add_ref = tree_refs[2 * level : 2 * level + 2]
        for number in range(len(adds)):
            trans_ref[number // ratio, number % ratio] = turns[number].astype(BF16)
            add_ref[number // ratio, number % ratio] = adds[number]
        longer_turns, longer_adds = [], []
        for pair in range(count // 2):
            for r in range(ratio):
                left, right = 2 * pair * ratio + r, (2 * pair + 1) * ratio + r
                if count > 2 or total_too:
                    both = beside([turns[left], adds[left]])
                    turn, add = parts_of(both - dot(turns[right].astype(BF16), both.astype(BF16)), 2)
                    longer_turns.append(turns[right] + turn)
                else:
                    add = adds[left] - dot(turns[right].astype(BF16), adds[left].astype(BF16))
                longer_adds.append(add + adds[right])
        turns, adds = longer_turns, longer_adds
        level += 1
    for r in range(ratio):
        state_ref[r] = adds[r].astype(state_ref.dtype)
        if total_too:
            tree_refs[-1][r] = turns[r]


def tree_starts(ratio, width, tree_refs):
    rows = lax.broadcasted_iota(jnp.int32, (width, 2 * width), 0)
    cols = lax.broadcasted_iota(jnp.int32, (width, 2 * width), 1)
    neutral = jnp.where(cols == rows + width, 1.0, 0.0).astype(F32)
    starts = [None] * ratio
    for level in reversed(range(len(tree_refs) // 2)):
        trans_ref, add_ref = tree_refs[2 * level : 2 * level + 2]
        longer = []
        for number, start in enumerate(starts):
            place, r = 2 * (number // ratio), number % ratio
            add = beside([add_ref[place, r], jnp.zeros((width, width), F32)])
            if start is None:
                turn = beside([jnp.zeros((width, width), F32), trans_ref[place, r].astype(F32)])
                longer.append((start, neutral - turn + add))
            else:
                longer.append((start, start - dot(trans_ref[place, r], start.astype(BF16)) + add))
        starts = []
        for pair in range(len(longer) // ratio):
            for side in range(2):
                starts += [longer[pair * ratio + r][side] for r in range(ratio)]
    return [neutral if start is None else start for start in starts]


def spread_kernel(tokens, ratio, sub, passing, got_ref, w_ref, u_ref, *refs):
    refs = refs[: len(refs) - passing]
    tree_refs, (local_ref, reach_ref) = refs[: len(refs) - passing - 2], refs[-2:]
    width = got_ref.shape[-1]
    per = SPAN // tokens
    blocks = got_ref.shape[0] // per
    slabs = block_slabs(blocks, sub, got_ref.shape[0])
    rows = lax.broadcasted_iota(jnp.int32, (SPAN, SPAN), 0)
    cols = lax.broadcasted_iota(jnp.int32, (SPAN, SPAN), 1)
    starts = [start.astype(BF16) for start in tree_starts(ratio, width, tree_refs)]
    lefts, units = [], []
    for block in range(blocks):
        query = block_rows(got_ref, slabs[block], tokens, 0)
        key = block_rows(got_ref, slabs[block], tokens, 1)
        scores = jnp.where(rows >= cols, dot_nt(query, key), 0.0).astype(BF16)
        query_f = query.astype(F32)
        squares = jnp.sum(query_f * query_f, 1, keepdims=True)
        units.append(lax.rsqrt(squares + EPSILON) * width ** (-0.5))
        lefts.append(beside([query, scores]))
    flat = [(block, r) for block in range(blocks) for r in range(ratio)]
    rights = []
    for start, (block, r) in zip(starts, flat):
        through, reached = parts_of(dot(w_ref[block, r], start), 2)
        corrected = beside([u_ref[block, r] - through, -reached]).astype(BF16)
        rights.append(jnp.concatenate([start, corrected], axis=0))
    for right, (block, r) in zip(rights, flat):
        out = dot(lefts[block], right) * units[block]
        local_ref[r, block] = out[:, :width]
        reach_ref[r, block] = out[:, width:].astype(BF16)


def join_kernel(order, n_head, state_ref, local_ref, reach_ref, *out_refs):
    ratio, blocks, span, width = local_ref.shape
    pieces = out_refs[0].shape[1]
    along_sub, along_head = position(len(order), n_head)
    upper = along_head // (n_head // 2)
    follows = lax.axis_index("outer") > 0
    states = [jnp.where(follows, state_ref[r].astype(F32), 0.0).astype(BF16) for r in range(ratio)]
    for distance, out_ref in zip(order, out_refs):
        target = along_sub ^ distance
        for kept in range(2):
            for piece in range(pieces):
                block = (target * 2 + (upper ^ (1 - kept))) * pieces + piece
                for r in range(ratio):
                    core = local_ref[r, block] + dot(reach_ref[r, block], states[r])
                    mean_square = jnp.mean(core * core, 1, keepdims=True)
                    out_ref[kept, piece, r] = (core * lax.rsqrt(mean_square + EPSILON)).astype(BF16)


def project_kernel(order, gate_places, kept, *refs):
    parts, shares = len(order), len(gate_places)
    normed_refs, gate_refs = refs[:parts], refs[parts : parts + shares]
    weight_ref, *out_refs, rows_ref = refs[parts + 2 * shares :]
    unused, pieces, ratio, span, width = normed_refs[0].shape
    tokens = gate_refs[0].shape[2]
    per = span // tokens
    along_sub, along_head = position(parts, 2 * shares)
    for distance, normed_ref in zip(order, normed_refs):
        source = along_sub ^ distance
        for apart, gate_ref in enumerate(gate_refs):
            share = (along_head ^ apart) & (shares - 1)
            first = ((1 - apart % 2) * (shares // 2) + share // 2) * tokens
            place = pl.ds(pl.multiple_of(first, tokens), tokens)
            from_rows = pl.ds(pl.multiple_of(share % per * tokens, tokens), tokens)
            for r in range(ratio):
                lanes = pl.ds(pl.multiple_of((source * ratio + r) * width, width), width)
                normed = normed_ref[kept, share // per, r, from_rows].astype(F32)
                gate = gate_ref[gate_places[apart], source * ratio + r].astype(F32)
                rows_ref[place, lanes] = (normed * gate).astype(BF16)
    multiply(0, rows_ref[...], weight_ref, out_refs)


def multiply(first, rows, weight_ref, out_refs):
    *send_refs, keep_ref = out_refs
    every = keep_ref.shape[-1]
    out = dot(rows, weight_ref[:, first : first + every]).reshape((2,) + keep_ref.shape)
    start = 0
    for send_ref in send_refs:
        columns = send_ref.shape[-1]
        send_ref[...] = out[0, :, :, start : start + columns].astype(BF16)
        start += columns
    keep_ref[...] = out[1]


def more_kernel(first, rows_ref, weight_ref, *out_refs):
    multiply(first, rows_ref[...], weight_ref, out_refs)


def sum_kernel(keep_ref, *refs):
    *got_refs, out_ref = refs
    every = keep_ref.shape[-1]
    placed, start = [], 0
    for got_ref in got_refs:
        placed.append((start, got_ref))
        start = (start + got_ref.shape[-1]) % every
    cuts = sorted({first for first, unused in placed} | {every})
    for first, last in zip(cuts, cuts[1:]):
        total = keep_ref[:, :, first:last]
        for start, got_ref in placed:
            if start <= first and last <= start + got_ref.shape[-1]:
                total = total + got_ref[:, :, first - start : last - start].astype(F32)
        out_ref[:, :, first:last] = total.astype(out_ref.dtype)


def per_device(
    outer, sub, n_head, queries, key_vectors, value_vectors, output_gate, write_strength, norm_gain, output_weight
):
    tokens, key_heads, width = queries.shape
    value_heads = value_vectors.shape[1]
    ratio = value_heads // key_heads
    sources = sub * n_head
    shard = tokens * sources
    blocks = shard // SPAN
    shard_tokens = tokens * n_head
    shape = jax.ShapeDtypeStruct
    along_sub, along_head = split_axis("sub", sub), split_axis("head", n_head)

    with jax.named_scope("pack"):
        slab = ((2 + ratio) * tokens + ROW_TILE, width)
        packed = pl.pallas_call(
            functools.partial(pack_kernel, sub),
            out_shape=shape((sources,) + slab, BF16),
            in_specs=[ANY] * 4,
            out_specs=ANY,
            scratch_shapes=[
                pltpu.VMEM(queries.shape, BF16),
                pltpu.VMEM(key_vectors.shape, BF16),
                pltpu.VMEM(value_vectors.shape, BF16),
                pltpu.VMEM((value_heads, tokens), BF16),
                pltpu.VMEM((sources,) + slab, BF16),
                pltpu.SemaphoreType.DMA((4,)),
                pltpu.SemaphoreType.DMA((3 + ratio,)),
            ],
            compiler_params=params(60),
        )(queries, key_vectors, value_vectors, write_strength.T)
    got = lax.all_to_all(packed, partner_order(sub, n_head), split_axis=0, concat_axis=0, tiled=True)

    heads = sub * ratio
    by_core = [(here, here ^ 1) for here in range(n_head)]
    group = (heads, tokens, width)
    half = n_head // 2
    with jax.named_scope("gates"):
        own_gates, swap = pl.pallas_call(
            functools.partial(gate_kernel, sub, n_head),
            out_shape=[shape((half,) + group, BF16)] * 2,
            in_specs=[VMEM] * 2,
            out_specs=[VMEM] * 2,
            scratch_shapes=[pltpu.VMEM((value_heads, tokens, width), BF16)],
            compiler_params=params(),
            cost_estimate=LIGHT,
        )(output_gate, norm_gain.reshape(1, width))
    swapped = lax.ppermute(swap, along_head, by_core)
    with jax.named_scope("pair"):
        pairs = pl.pallas_call(
            pair_kernel,
            out_shape=[shape((2,) + group, BF16)] * (half - 1),
            in_specs=[VMEM] * 2,
            out_specs=[VMEM] * (half - 1),
            compiler_params=params(),
            cost_estimate=LIGHT,
        )(own_gates, swapped)

    state_type = BF16 if outer == 2 else F32
    with jax.named_scope("factors"):
        depths = []
        while blocks >> len(depths) > 1:
            depths.append(blocks >> len(depths))
        tree = []
        for depth in depths:
            tree += [shape((depth, ratio, width, width), BF16), shape((depth, ratio, width, width), F32)]
        if outer > 2:
            tree.append(shape((ratio, width, width), F32))
        out_shape = [
            shape((ratio, width, width), state_type),
            shape((blocks, ratio, SPAN, width), BF16),
            shape((blocks, ratio, SPAN, width), F32),
        ] + tree
        state, w, u, *tree = pl.pallas_call(
            functools.partial(factor_kernel, tokens, ratio, sub, half - 1, outer > 2),
            out_shape=out_shape,
            in_specs=[VMEM] + [ANY] * (half - 1),
            out_specs=[VMEM] * len(out_shape),
            compiler_params=params(),
            cost_estimate=LIGHT,
        )(got, *pairs)

    onward = [(here, (here + 1) % outer) for here in range(outer)]
    incoming = lax.ppermute(state, "outer", onward)
    with jax.named_scope("spread"):
        read = 3 + 2 * len(depths)
        local, reach, *pairs = pl.pallas_call(
            functools.partial(spread_kernel, tokens, ratio, sub, half - 1),
            out_shape=[
                shape((ratio, blocks, SPAN, width), F32),
                shape((ratio, blocks, SPAN, width), BF16),
            ]
            + [shape((2,) + group, BF16)] * (half - 1),
            in_specs=[VMEM] * read + [ANY] * (half - 1),
            out_specs=[VMEM] * 2 + [ANY] * (half - 1),
            input_output_aliases={read + number: 2 + number for number in range(half - 1)},
            compiler_params=params(),
            cost_estimate=LIGHT,
        )(got, w, u, *tree[: 2 * len(depths)], *pairs)
    gates = [(own_gates, 0), (swapped, 0)]
    for number, pair in enumerate(pairs):
        distance = 2 * number + 2
        pair = lax.ppermute(pair, along_head, [(here, here ^ distance) for here in range(n_head)])
        gates += [(pair, 0), (pair, 1)]
    for hop in range(outer - 2):
        incoming = jnp.where(lax.axis_index("outer") == 0, 0.0, incoming)
        turned_by = jnp.einsum("hde,hef->hdf", tree[-1], incoming, precision=lax.Precision.HIGHEST)
        incoming = lax.ppermute(state + incoming - turned_by, "outer", onward)

    pieces = shard_tokens // SPAN // 2
    columns = output_weight.shape[1]
    quarter = (n_head // 4, tokens, columns)
    half = n_head // 2
    order = [0] + sorted(range(1, sub), reverse=True)
    with jax.named_scope("join"):
        normed = pl.pallas_call(
            functools.partial(join_kernel, order, n_head),
            out_shape=[shape((2, pieces, ratio, SPAN, width), BF16)] * sub,
            in_specs=[VMEM] * 3,
            out_specs=[VMEM] * sub,
            compiler_params=params(),
            cost_estimate=pl.CostEstimate(flops=2 * 10**9, bytes_accessed=1, transcendentals=0),
        )(incoming, local, reach)
    normed = [
        lax.ppermute(part, along_sub, [(here, here ^ distance) for here in range(sub)]) if distance else part
        for distance, part in zip(order, normed)
    ]
    across = [(here, here ^ half) for here in range(n_head)]

    def project(kept, pieces, every, rows_too):
        used, others = gates[half * (1 - kept) : half * (2 - kept)], gates[half * kept : half * (1 + kept)]
        rows = pltpu.VMEM((shard_tokens // 2, heads * width), BF16)
        with jax.named_scope("project"):
            return pl.pallas_call(
                functools.partial(project_kernel, order, [place for unused, place in used], kept),
                out_shape=[shape(quarter[:-1] + (piece,), BF16) for piece in pieces]
                + [shape(quarter[:-1] + (every,), F32)]
                + [shape(rows.shape, BF16)] * rows_too,
                in_specs=[VMEM] * (sub + half) + [ANY] * half + [VMEM],
                out_specs=[VMEM] * (len(pieces) + 1 + rows_too),
                scratch_shapes=[rows] * (1 - rows_too),
                compiler_params=params(),
                cost_estimate=LIGHT,
            )(*normed, *[array for array, unused in used + others], output_weight)

    def add(keep, arrived, kind):
        with jax.named_scope("sum"):
            return pl.pallas_call(
                sum_kernel,
                out_shape=shape(keep.shape, kind),
                in_specs=[VMEM] * (1 + len(arrived)),
                out_specs=VMEM,
                compiler_params=params(),
                cost_estimate=LIGHT,
            )(keep, *arrived)

    cuts = 2
    every = columns // cuts
    passed_on = []
    for cut in range(cuts):
        if cut == 0:
            send, keep, rows = project(0, [every], every, 1)
        else:
            with jax.named_scope("project_more"):
                send, keep = pl.pallas_call(
                    functools.partial(more_kernel, cut * every),
                    out_shape=[shape(quarter[:-1] + (every,), BF16), shape(quarter[:-1] + (every,), F32)],
                    in_specs=[VMEM] * 2,
                    out_specs=[VMEM] * 2,
                    compiler_params=params(),
                    cost_estimate=LIGHT,
                )(rows, output_weight)
        summed = add(keep, [lax.ppermute(send, along_head, by_core)], BF16)
        passed_on.append(lax.ppermute(summed, along_head, across))
    third = columns // 3 // width * width
    *sends, keep = project(1, [columns - 2 * third, third, third], columns, 0)
    arrived = [lax.ppermute(send, along_head, by_core) for send in sends]
    summed = add(keep, arrived + passed_on, BF16 if n_head == 4 else F32)
    bit = 2
    while bit < half:
        mine = (lax.axis_index(along_head) // bit) % 2
        split = summed.reshape((summed.shape[0] // 2, 2) + summed.shape[1:])
        send = lax.dynamic_index_in_dim(split, 1 - mine, 1, False).astype(BF16)
        keep = lax.dynamic_index_in_dim(split, mine, 1, False)
        summed = keep + lax.ppermute(send, along_head, [(here, here ^ bit) for here in range(n_head)]).astype(F32)
        bit *= 2
    return summed[0].astype(BF16)


def solution(mesh):
    n_seq, n_head = mesh.shape["seq"], mesh.shape["head"]

    def run(queries, key_vectors, value_vectors, output_gate, write_strength, norm_gain, output_weight):
        sub = queries.shape[1] // n_head
        outer = n_seq // sub
        along = split_axis("sub", sub) + split_axis("head", n_head)
        split = Mesh(mesh.devices.reshape((outer,) + (2,) * len(along)), ("outer",) + along)
        every = ("outer",) + along
        placed = (
            P(every, None, None),
            P(every, None, None),
            P(every, None, None),
            P(every, None, None),
            P(every, None),
            P(),
            P(split_axis("head", n_head), None),
        )
        return jax.shard_map(
            functools.partial(per_device, outer, sub, n_head),
            mesh=split,
            in_specs=placed,
            out_specs=P(every, None),
            check_vma=False,
        )(queries, key_vectors, value_vectors, output_gate, write_strength, norm_gain, output_weight)

    return run
```

```python
import functools

import jax
import jax.numpy as jnp
from jax import lax
from jax.experimental import pallas as pl
from jax.experimental.pallas import tpu as pltpu
from jax.sharding import Mesh, PartitionSpec as P

SPAN = 128
EPSILON = 1e-06
F32 = jnp.float32
BF16 = jnp.bfloat16
ROW_TILE = 16
VMEM = pl.BlockSpec(memory_space=pltpu.VMEM)
SMEM = pl.BlockSpec(memory_space=pltpu.SMEM)
ANY = pl.BlockSpec(memory_space=pl.ANY)
LIGHT = pl.CostEstimate(flops=1, bytes_accessed=1, transcendentals=0)


def dot(left, right):
    return jnp.dot(left, right, preferred_element_type=F32)


def dot_nt(left, right):
    return lax.dot_general(left, right, (((1,), (1,)), ((), ())), preferred_element_type=F32)


def params(megabytes=24):
    return pltpu.CompilerParams(vmem_limit_bytes=megabytes * 2**20)


def turned(values):
    return jnp.transpose(values, (1, 0, 2))


def split_axis(name, size):
    return tuple(f"{name}{bit}" for bit in reversed(range(size.bit_length() - 1)))


def partner_order(sub, n_head):
    heads = split_axis("head", n_head)
    return heads[-1:] + heads[:-1] + split_axis("sub", sub)


def partner(source, sub, n_head):
    axes = split_axis("sub", sub) + split_axis("head", n_head)
    bits = {name: source >> (len(axes) - 1 - number) & 1 for number, name in enumerate(axes)}
    place = 0
    for name in partner_order(sub, n_head):
        place = 2 * place + bits[name]
    return place


def position(sub, n_head):
    return lax.axis_index(split_axis("sub", sub)), lax.axis_index(split_axis("head", n_head))


def pack_kernel(sub, q_hbm, k_hbm, v_hbm, b_hbm, out_hbm, q_ref, k_ref, v_ref, b_ref, out_ref, came, left):
    tokens, key_heads, width = q_hbm.shape
    ratio = v_hbm.shape[1] // key_heads
    copies = [
        pltpu.make_async_copy(source, target, came.at[number])
        for number, (source, target) in enumerate(
            ((b_hbm, b_ref), (k_hbm, k_ref), (q_hbm, q_ref), (v_hbm, v_ref))
        )
    ]
    for copy in copies:
        copy.start()
    n_head = key_heads // sub
    heads = [head % sub * n_head + head // sub for head in range(key_heads)]
    heads = [partner(source, sub, n_head) for source in heads]
    heads = [heads.index(peer) for peer in range(key_heads)]
    leaving = []

    def leave(first, size):
        rows = pl.ds(first, size)
        leaving.append(pltpu.make_async_copy(out_ref.at[:, rows], out_hbm.at[:, rows], left.at[len(leaving)]))
        leaving[-1].start()

    copies[0].wait()
    strength = jnp.concatenate([b_ref[...].astype(F32)] * (width // tokens), axis=1)
    strength = jnp.concatenate([strength, jnp.zeros((ROW_TILE, width), F32)], axis=0)
    for peer, head in enumerate(heads):
        tile = strength[head * ratio : head * ratio + ROW_TILE]
        out_ref[peer, (2 + ratio) * tokens :] = tile.astype(BF16)
    leave((2 + ratio) * tokens, ROW_TILE)
    for place, copy, ref in ((1, copies[1], k_ref), (0, copies[2], q_ref)):
        copy.wait()
        rows = turned(ref[...])
        for peer, head in enumerate(heads):
            out_ref[peer, place * tokens : (place + 1) * tokens] = rows[head]
        leave(place * tokens, tokens)
    copies[3].wait()
    rows = turned(v_ref[...])
    for r in range(ratio):
        for peer, head in enumerate(heads):
            out_ref[peer, (2 + r) * tokens : (3 + r) * tokens] = rows[head * ratio + r]
        leave((2 + r) * tokens, tokens)
    for copy in leaving:
        copy.wait()


def gate_kernel(sub, n_head, gate_ref, gain_ref, own_ref, swap_ref, gates):
    heads = own_ref.shape[1]
    unused, along_head = position(sub, n_head)
    gate = gate_ref[...].astype(F32)
    gated = gain_ref[...].astype(F32)[:, None] * (gate / (1.0 + jnp.exp(-gate)))
    gates[...] = turned(gated.astype(BF16))
    for number in range(n_head // 2):
        own_ref[number] = gates[pl.ds((along_head ^ (2 * number)) * heads, heads)]
        swap_ref[number] = gates[pl.ds((along_head ^ (2 * number + 1)) * heads, heads)]


def pair_kernel(own_ref, swapped_ref, *pair_refs):
    for number, pair_ref in enumerate(pair_refs):
        pair_ref[0] = own_ref[number + 1]
        pair_ref[1] = swapped_ref[number + 1]


def block_slabs(blocks, sub, sources):
    places = [partner(source, sub, sources // sub) for source in range(sources)]
    per = sources // blocks
    return [places[block * per : (block + 1) * per] for block in range(blocks)]


def block_rows(got_ref, slabs, tokens, part):
    return jnp.concatenate([got_ref[slab, part * tokens : (part + 1) * tokens] for slab in slabs], axis=0)


def beside(matrices):
    return jnp.concatenate(matrices, axis=1)


def parts_of(wide, count):
    width = wide.shape[1] // count
    return [wide[:, part * width : (part + 1) * width] for part in range(count)]


def block_inverse(below):
    size = below[0].shape[0]
    rows = lax.broadcasted_iota(jnp.int32, (size, size), 0)
    cols = lax.broadcasted_iota(jnp.int32, (size, size), 1)
    apart = rows ^ cols
    solved = None
    for level in range(size.bit_length() - 2):
        joins = (apart >> level) == 1
        parts = [jnp.where(joins, matrix, 0.0) for matrix in below]
        if level == 0:
            solved = [jnp.where(apart == 0, 1.0, -part).astype(BF16) for part in parts]
        else:
            inner = [dot(part.astype(BF16), now).astype(BF16) for part, now in zip(parts, solved)]
            solved = [now - dot(now, mid).astype(BF16) for now, mid in zip(solved, inner)]
    return solved


def dot_two(left, right):
    high = left.astype(BF16)
    low = (left - high.astype(F32)).astype(BF16)
    both = dot(jnp.concatenate([high, low], axis=0), right)
    return both[: left.shape[0]] + both[left.shape[0] :]


def refined(below, solved):
    size = below[0].shape[0]
    rows = lax.broadcasted_iota(jnp.int32, (size, size), 0)
    cols = lax.broadcasted_iota(jnp.int32, (size, size), 1)
    identity = jnp.where(rows == cols, 1.0, 0.0)
    left_over = [
        (identity - now.astype(F32) - dot_two(matrix, now)).astype(BF16) for matrix, now in zip(below, solved)
    ]
    return [now.astype(F32) + dot(now, rest) for now, rest in zip(solved, left_over)]


def factor_kernel(tokens, ratio, sub, passing, total_too, got_ref, *refs):
    state_ref, w_ref, u_ref, *tree_refs = refs[passing:]
    width = got_ref.shape[-1]
    per = SPAN // tokens
    blocks = got_ref.shape[0] // per
    slabs = block_slabs(blocks, sub, got_ref.shape[0])
    rows = lax.broadcasted_iota(jnp.int32, (SPAN, SPAN), 0)
    cols = lax.broadcasted_iota(jnp.int32, (SPAN, SPAN), 1)
    lane = lax.broadcasted_iota(jnp.int32, (1, SPAN), 1)
    first = (2 + ratio) * tokens
    below, held = [], []
    for block in range(blocks):
        key = block_rows(got_ref, slabs[block], tokens, 1)
        gram = dot_nt(key, key)
        squares = jnp.where(rows == cols, gram, 0.0)
        key_row = lax.rsqrt(jnp.sum(squares, 0, keepdims=True) + EPSILON)
        key_col = lax.rsqrt(jnp.sum(squares, 1, keepdims=True) + EPSILON)
        lower = jnp.where(rows > cols, gram, 0.0) * key_row
        strengths = []
        for r in range(ratio):
            strength = jnp.zeros((1, SPAN), F32)
            for place in range(per):
                piece = got_ref[slabs[block][place], first : first + ROW_TILE].astype(F32)[r : r + 1]
                strength = jnp.where(lane // tokens == place, piece, strength)
            scaled_col = jnp.sum(jnp.where(rows == cols, strength * key_row, 0.0), 1, keepdims=True)
            below.append(lower * scaled_col)
            strengths.append(strength)
        held.append((block, key, key_col, key_row, strengths))
    solved = refined(below, block_inverse(below))
    flat = [(block, r) for block in range(blocks) for r in range(ratio)]
    weighted = []
    for inverse, (block, r) in zip(solved, flat):
        unused, key, key_col, key_row, strengths = held[block]
        weighted.append(inverse * key_col * strengths[r])
    for part, (block, r) in zip(weighted, flat):
        value = block_rows(got_ref, slabs[block], tokens, 2 + r)
        u_ref[block, r] = dot_two(part, value)
    for part, (block, r) in zip(weighted, flat):
        unused, key, key_col, key_row, strengths = held[block]
        w_ref[block, r] = dot_two(part * key_row, key).astype(BF16)
    turns, adds = [], []
    for block in range(blocks):
        key_t = held[block][1].T
        for r in range(ratio):
            turn, add = parts_of(dot(key_t, beside([w_ref[block, r], u_ref[block, r].astype(BF16)])), 2)
            turns.append(turn)
            adds.append(add)

    level = 0
    while len(adds) > ratio:
        count = len(adds) // ratio
        trans_ref, add_ref = tree_refs[2 * level : 2 * level + 2]
        for number in range(len(adds)):
            trans_ref[number // ratio, number % ratio] = turns[number].astype(BF16)
            add_ref[number // ratio, number % ratio] = adds[number]
        longer_turns, longer_adds = [], []
        for pair in range(count // 2):
            for r in range(ratio):
                left, right = 2 * pair * ratio + r, (2 * pair + 1) * ratio + r
                if count > 2 or total_too:
                    both = beside([turns[left], adds[left]])
                    turn, add = parts_of(both - dot(turns[right].astype(BF16), both.astype(BF16)), 2)
                    longer_turns.append(turns[right] + turn)
                else:
                    add = adds[left] - dot(turns[right].astype(BF16), adds[left].astype(BF16))
                longer_adds.append(add + adds[right])
        turns, adds = longer_turns, longer_adds
        level += 1
    for r in range(ratio):
        state_ref[r] = adds[r].astype(state_ref.dtype)
        if total_too:
            tree_refs[-1][r] = turns[r]


def tree_starts(ratio, width, tree_refs):
    rows = lax.broadcasted_iota(jnp.int32, (width, 2 * width), 0)
    cols = lax.broadcasted_iota(jnp.int32, (width, 2 * width), 1)
    neutral = jnp.where(cols == rows + width, 1.0, 0.0).astype(F32)
    starts = [None] * ratio
    for level in reversed(range(len(tree_refs) // 2)):
        trans_ref, add_ref = tree_refs[2 * level : 2 * level + 2]
        longer = []
        for number, start in enumerate(starts):
            place, r = 2 * (number // ratio), number % ratio
            add = beside([add_ref[place, r], jnp.zeros((width, width), F32)])
            if start is None:
                turn = beside([jnp.zeros((width, width), F32), trans_ref[place, r].astype(F32)])
                longer.append((start, neutral - turn + add))
            else:
                longer.append((start, start - dot(trans_ref[place, r], start.astype(BF16)) + add))
        starts = []
        for pair in range(len(longer) // ratio):
            for side in range(2):
                starts += [longer[pair * ratio + r][side] for r in range(ratio)]
    return [neutral if start is None else start for start in starts]


def spread_kernel(tokens, ratio, sub, passing, got_ref, w_ref, u_ref, *refs):
    refs = refs[: len(refs) - passing]
    tree_refs, (local_ref, reach_ref) = refs[: len(refs) - passing - 2], refs[-2:]
    width = got_ref.shape[-1]
    per = SPAN // tokens
    blocks = got_ref.shape[0] // per
    slabs = block_slabs(blocks, sub, got_ref.shape[0])
    rows = lax.broadcasted_iota(jnp.int32, (SPAN, SPAN), 0)
    cols = lax.broadcasted_iota(jnp.int32, (SPAN, SPAN), 1)
    starts = [start.astype(BF16) for start in tree_starts(ratio, width, tree_refs)]
    lefts, units = [], []
    for block in range(blocks):
        query = block_rows(got_ref, slabs[block], tokens, 0)
        key = block_rows(got_ref, slabs[block], tokens, 1)
        scores = jnp.where(rows >= cols, dot_nt(query, key), 0.0).astype(BF16)
        query_f = query.astype(F32)
        squares = jnp.sum(query_f * query_f, 1, keepdims=True)
        units.append(lax.rsqrt(squares + EPSILON) * width ** (-0.5))
        lefts.append(beside([query, scores]))
    flat = [(block, r) for block in range(blocks) for r in range(ratio)]
    rights = []
    for start, (block, r) in zip(starts, flat):
        through, reached = parts_of(dot(w_ref[block, r], start), 2)
        corrected = beside([u_ref[block, r] - through, -reached]).astype(BF16)
        rights.append(jnp.concatenate([start, corrected], axis=0))
    for right, (block, r) in zip(rights, flat):
        out = dot(lefts[block], right) * units[block]
        local_ref[r, block] = out[:, :width]
        reach_ref[r, block] = out[:, width:].astype(BF16)


def join_kernel(order, n_head, state_ref, local_ref, reach_ref, *out_refs):
    ratio, blocks, span, width = local_ref.shape
    pieces = out_refs[0].shape[1]
    along_sub, along_head = position(len(order), n_head)
    upper = along_head // (n_head // 2)
    follows = lax.axis_index("outer") > 0
    states = [jnp.where(follows, state_ref[r].astype(F32), 0.0).astype(BF16) for r in range(ratio)]
    for distance, out_ref in zip(order, out_refs):
        target = along_sub ^ distance
        for kept in range(2):
            for piece in range(pieces):
                block = (target * 2 + (upper ^ (1 - kept))) * pieces + piece
                for r in range(ratio):
                    core = local_ref[r, block] + dot(reach_ref[r, block], states[r])
                    mean_square = jnp.mean(core * core, 1, keepdims=True)
                    out_ref[kept, piece, r] = (core * lax.rsqrt(mean_square + EPSILON)).astype(BF16)


def project_kernel(order, gate_places, kept, *refs):
    parts, shares = len(order), len(gate_places)
    normed_refs, gate_refs = refs[:parts], refs[parts : parts + shares]
    weight_ref, *out_refs, rows_ref = refs[parts + 2 * shares :]
    unused, pieces, ratio, span, width = normed_refs[0].shape
    tokens = gate_refs[0].shape[2]
    per = span // tokens
    along_sub, along_head = position(parts, 2 * shares)
    for distance, normed_ref in zip(order, normed_refs):
        source = along_sub ^ distance
        for apart, gate_ref in enumerate(gate_refs):
            share = (along_head ^ apart) & (shares - 1)
            first = ((1 - apart % 2) * (shares // 2) + share // 2) * tokens
            place = pl.ds(pl.multiple_of(first, tokens), tokens)
            from_rows = pl.ds(pl.multiple_of(share % per * tokens, tokens), tokens)
            for r in range(ratio):
                lanes = pl.ds(pl.multiple_of((source * ratio + r) * width, width), width)
                normed = normed_ref[kept, share // per, r, from_rows].astype(F32)
                gate = gate_ref[gate_places[apart], source * ratio + r].astype(F32)
                rows_ref[place, lanes] = (normed * gate).astype(BF16)
    multiply(0, rows_ref[...], weight_ref, out_refs)


def multiply(first, rows, weight_ref, out_refs):
    *send_refs, keep_ref = out_refs
    every = keep_ref.shape[-1]
    out = dot(rows, weight_ref[:, first : first + every]).reshape((2,) + keep_ref.shape)
    start = 0
    for send_ref in send_refs:
        columns = send_ref.shape[-1]
        send_ref[...] = out[0, :, :, start : start + columns].astype(BF16)
        start += columns
    keep_ref[...] = out[1]


def more_kernel(first, rows_ref, weight_ref, *out_refs):
    multiply(first, rows_ref[...], weight_ref, out_refs)


def sum_kernel(keep_ref, *refs):
    *got_refs, out_ref = refs
    every = keep_ref.shape[-1]
    placed, start = [], 0
    for got_ref in got_refs:
        placed.append((start, got_ref))
        start = (start + got_ref.shape[-1]) % every
    cuts = sorted({first for first, unused in placed} | {every})
    for first, last in zip(cuts, cuts[1:]):
        total = keep_ref[:, :, first:last]
        for start, got_ref in placed:
            if start <= first and last <= start + got_ref.shape[-1]:
                total = total + got_ref[:, :, first - start : last - start].astype(F32)
        out_ref[:, :, first:last] = total.astype(out_ref.dtype)


def per_device(
    outer, sub, n_head, queries, key_vectors, value_vectors, output_gate, write_strength, norm_gain, output_weight
):
    tokens, key_heads, width = queries.shape
    value_heads = value_vectors.shape[1]
    ratio = value_heads // key_heads
    sources = sub * n_head
    shard = tokens * sources
    blocks = shard // SPAN
    shard_tokens = tokens * n_head
    shape = jax.ShapeDtypeStruct
    along_sub, along_head = split_axis("sub", sub), split_axis("head", n_head)

    with jax.named_scope("pack"):
        slab = ((2 + ratio) * tokens + ROW_TILE, width)
        packed = pl.pallas_call(
            functools.partial(pack_kernel, sub),
            out_shape=shape((sources,) + slab, BF16),
            in_specs=[ANY] * 4,
            out_specs=ANY,
            scratch_shapes=[
                pltpu.VMEM(queries.shape, BF16),
                pltpu.VMEM(key_vectors.shape, BF16),
                pltpu.VMEM(value_vectors.shape, BF16),
                pltpu.VMEM((value_heads, tokens), BF16),
                pltpu.VMEM((sources,) + slab, BF16),
                pltpu.SemaphoreType.DMA((4,)),
                pltpu.SemaphoreType.DMA((3 + ratio,)),
            ],
            compiler_params=params(60),
        )(queries, key_vectors, value_vectors, write_strength.T)
    got = lax.all_to_all(packed, partner_order(sub, n_head), split_axis=0, concat_axis=0, tiled=True)

    heads = sub * ratio
    by_core = [(here, here ^ 1) for here in range(n_head)]
    group = (heads, tokens, width)
    half = n_head // 2
    with jax.named_scope("gates"):
        own_gates, swap = pl.pallas_call(
            functools.partial(gate_kernel, sub, n_head),
            out_shape=[shape((half,) + group, BF16)] * 2,
            in_specs=[VMEM] * 2,
            out_specs=[VMEM] * 2,
            scratch_shapes=[pltpu.VMEM((value_heads, tokens, width), BF16)],
            compiler_params=params(),
            cost_estimate=LIGHT,
        )(output_gate, norm_gain.reshape(1, width))
    swapped = lax.ppermute(swap, along_head, by_core)
    with jax.named_scope("pair"):
        pairs = pl.pallas_call(
            pair_kernel,
            out_shape=[shape((2,) + group, BF16)] * (half - 1),
            in_specs=[VMEM] * 2,
            out_specs=[VMEM] * (half - 1),
            compiler_params=params(),
            cost_estimate=LIGHT,
        )(own_gates, swapped)

    state_type = BF16 if outer == 2 else F32
    with jax.named_scope("factors"):
        depths = []
        while blocks >> len(depths) > 1:
            depths.append(blocks >> len(depths))
        tree = []
        for depth in depths:
            tree += [shape((depth, ratio, width, width), BF16), shape((depth, ratio, width, width), F32)]
        if outer > 2:
            tree.append(shape((ratio, width, width), F32))
        out_shape = [
            shape((ratio, width, width), state_type),
            shape((blocks, ratio, SPAN, width), BF16),
            shape((blocks, ratio, SPAN, width), F32),
        ] + tree
        state, w, u, *tree = pl.pallas_call(
            functools.partial(factor_kernel, tokens, ratio, sub, half - 1, outer > 2),
            out_shape=out_shape,
            in_specs=[VMEM] + [ANY] * (half - 1),
            out_specs=[VMEM] * len(out_shape),
            compiler_params=params(),
            cost_estimate=LIGHT,
        )(got, *pairs)

    onward = [(here, (here + 1) % outer) for here in range(outer)]
    incoming = lax.ppermute(state, "outer", onward)
    with jax.named_scope("spread"):
        read = 3 + 2 * len(depths)
        local, reach, *pairs = pl.pallas_call(
            functools.partial(spread_kernel, tokens, ratio, sub, half - 1),
            out_shape=[
                shape((ratio, blocks, SPAN, width), F32),
                shape((ratio, blocks, SPAN, width), BF16),
            ]
            + [shape((2,) + group, BF16)] * (half - 1),
            in_specs=[VMEM] * read + [ANY] * (half - 1),
            out_specs=[VMEM] * 2 + [ANY] * (half - 1),
            input_output_aliases={read + number: 2 + number for number in range(half - 1)},
            compiler_params=params(),
            cost_estimate=LIGHT,
        )(got, w, u, *tree[: 2 * len(depths)], *pairs)
    gates = [(own_gates, 0), (swapped, 0)]
    for number, pair in enumerate(pairs):
        distance = 2 * number + 2
        pair = lax.ppermute(pair, along_head, [(here, here ^ distance) for here in range(n_head)])
        gates += [(pair, 0), (pair, 1)]
    for hop in range(outer - 2):
        incoming = jnp.where(lax.axis_index("outer") == 0, 0.0, incoming)
        turned_by = jnp.einsum("hde,hef->hdf", tree[-1], incoming, precision=lax.Precision.HIGHEST)
        incoming = lax.ppermute(state + incoming - turned_by, "outer", onward)

    pieces = shard_tokens // SPAN // 2
    columns = output_weight.shape[1]
    quarter = (n_head // 4, tokens, columns)
    half = n_head // 2
    order = [0] + sorted(range(1, sub), reverse=True)
    with jax.named_scope("join"):
        normed = pl.pallas_call(
            functools.partial(join_kernel, order, n_head),
            out_shape=[shape((2, pieces, ratio, SPAN, width), BF16)] * sub,
            in_specs=[VMEM] * 3,
            out_specs=[VMEM] * sub,
            compiler_params=params(),
            cost_estimate=pl.CostEstimate(flops=2 * 10**9, bytes_accessed=1, transcendentals=0),
        )(incoming, local, reach)
    normed = [
        lax.ppermute(part, along_sub, [(here, here ^ distance) for here in range(sub)]) if distance else part
        for distance, part in zip(order, normed)
    ]
    across = [(here, here ^ half) for here in range(n_head)]

    def project(kept, pieces, every, rows_too):
        used, others = gates[half * (1 - kept) : half * (2 - kept)], gates[half * kept : half * (1 + kept)]
        rows = pltpu.VMEM((shard_tokens // 2, heads * width), BF16)
        with jax.named_scope("project"):
            return pl.pallas_call(
                functools.partial(project_kernel, order, [place for unused, place in used], kept),
                out_shape=[shape(quarter[:-1] + (piece,), BF16) for piece in pieces]
                + [shape(quarter[:-1] + (every,), F32)]
                + [shape(rows.shape, BF16)] * rows_too,
                in_specs=[VMEM] * (sub + half) + [ANY] * half + [VMEM],
                out_specs=[VMEM] * (len(pieces) + 1 + rows_too),
                scratch_shapes=[rows] * (1 - rows_too),
                compiler_params=params(),
                cost_estimate=LIGHT,
            )(*normed, *[array for array, unused in used + others], output_weight)

    def add(keep, arrived, kind):
        with jax.named_scope("sum"):
            return pl.pallas_call(
                sum_kernel,
                out_shape=shape(keep.shape, kind),
                in_specs=[VMEM] * (1 + len(arrived)),
                out_specs=VMEM,
                compiler_params=params(),
                cost_estimate=LIGHT,
            )(keep, *arrived)

    cuts = 2
    every = columns // cuts
    passed_on = []
    for cut in range(cuts):
        if cut == 0:
            send, keep, rows = project(0, [every], every, 1)
        else:
            with jax.named_scope("project_more"):
                send, keep = pl.pallas_call(
                    functools.partial(more_kernel, cut * every),
                    out_shape=[shape(quarter[:-1] + (every,), BF16), shape(quarter[:-1] + (every,), F32)],
                    in_specs=[VMEM] * 2,
                    out_specs=[VMEM] * 2,
                    compiler_params=params(),
                    cost_estimate=LIGHT,
                )(rows, output_weight)
        summed = add(keep, [lax.ppermute(send, along_head, by_core)], BF16)
        passed_on.append(lax.ppermute(summed, along_head, across))
    third = columns // 3 // width * width
    *sends, keep = project(1, [columns - 2 * third, third, third], columns, 0)
    arrived = [lax.ppermute(send, along_head, by_core) for send in sends]
    summed = add(keep, arrived + passed_on, BF16 if n_head == 4 else F32)
    bit = 2
    while bit < half:
        mine = (lax.axis_index(along_head) // bit) % 2
        split = summed.reshape((summed.shape[0] // 2, 2) + summed.shape[1:])
        send = lax.dynamic_index_in_dim(split, 1 - mine, 1, False).astype(BF16)
        keep = lax.dynamic_index_in_dim(split, mine, 1, False)
        summed = keep + lax.ppermute(send, along_head, [(here, here ^ bit) for here in range(n_head)]).astype(F32)
        bit *= 2
    return summed[0].astype(BF16)


def solution(mesh):
    n_seq, n_head = mesh.shape["seq"], mesh.shape["head"]

    def run(queries, key_vectors, value_vectors, output_gate, write_strength, norm_gain, output_weight):
        sub = queries.shape[1] // n_head
        outer = n_seq // sub
        along = split_axis("sub", sub) + split_axis("head", n_head)
        split = Mesh(mesh.devices.reshape((outer,) + (2,) * len(along)), ("outer",) + along)
        every = ("outer",) + along
        placed = (
            P(every, None, None),
            P(every, None, None),
            P(every, None, None),
            P(every, None, None),
            P(every, None),
            P(),
            P(split_axis("head", n_head), None),
        )
        return jax.shard_map(
            functools.partial(per_device, outer, sub, n_head),
            mesh=split,
            in_specs=placed,
            out_specs=P(every, None),
            check_vma=False,
        )(queries, key_vectors, value_vectors, output_gate, write_strength, norm_gain, output_weight)

    return run
```

```python
import functools

import jax
import jax.numpy as jnp
from jax import lax
from jax.experimental import pallas as pl
from jax.experimental.pallas import tpu as pltpu
from jax.sharding import Mesh, PartitionSpec as P

SPAN = 128
EPSILON = 1e-06
F32 = jnp.float32
BF16 = jnp.bfloat16
ROW_TILE = 16
VMEM = pl.BlockSpec(memory_space=pltpu.VMEM)
SMEM = pl.BlockSpec(memory_space=pltpu.SMEM)
ANY = pl.BlockSpec(memory_space=pl.ANY)
LIGHT = pl.CostEstimate(flops=1, bytes_accessed=1, transcendentals=0)


def dot(left, right):
    return jnp.dot(left, right, preferred_element_type=F32)


def dot_nt(left, right):
    return lax.dot_general(left, right, (((1,), (1,)), ((), ())), preferred_element_type=F32)


def params(megabytes=24):
    return pltpu.CompilerParams(vmem_limit_bytes=megabytes * 2**20)


def turned(values):
    return jnp.transpose(values, (1, 0, 2))


def split_axis(name, size):
    return tuple(f"{name}{bit}" for bit in reversed(range(size.bit_length() - 1)))


def partner_order(sub, n_head):
    heads = split_axis("head", n_head)
    return heads[-1:] + heads[:-1] + split_axis("sub", sub)


def partner(source, sub, n_head):
    axes = split_axis("sub", sub) + split_axis("head", n_head)
    bits = {name: source >> (len(axes) - 1 - number) & 1 for number, name in enumerate(axes)}
    place = 0
    for name in partner_order(sub, n_head):
        place = 2 * place + bits[name]
    return place


def position(sub, n_head):
    return lax.axis_index(split_axis("sub", sub)), lax.axis_index(split_axis("head", n_head))


def pack_kernel(sub, q_hbm, k_hbm, v_hbm, b_hbm, out_hbm, q_ref, k_ref, v_ref, b_ref, out_ref, came, left):
    tokens, key_heads, width = q_hbm.shape
    ratio = v_hbm.shape[1] // key_heads
    copies = [
        pltpu.make_async_copy(source, target, came.at[number])
        for number, (source, target) in enumerate(
            ((b_hbm, b_ref), (k_hbm, k_ref), (q_hbm, q_ref), (v_hbm, v_ref))
        )
    ]
    for copy in copies:
        copy.start()
    n_head = key_heads // sub
    heads = [head % sub * n_head + head // sub for head in range(key_heads)]
    heads = [partner(source, sub, n_head) for source in heads]
    heads = [heads.index(peer) for peer in range(key_heads)]
    leaving = []

    def leave(first, size):
        rows = pl.ds(first, size)
        leaving.append(pltpu.make_async_copy(out_ref.at[:, rows], out_hbm.at[:, rows], left.at[len(leaving)]))
        leaving[-1].start()

    copies[0].wait()
    strength = jnp.concatenate([b_ref[...].astype(F32)] * (width // tokens), axis=1)
    strength = jnp.concatenate([strength, jnp.zeros((ROW_TILE, width), F32)], axis=0)
    for peer, head in enumerate(heads):
        tile = strength[head * ratio : head * ratio + ROW_TILE]
        out_ref[peer, (2 + ratio) * tokens :] = tile.astype(BF16)
    leave((2 + ratio) * tokens, ROW_TILE)
    for place, copy, ref in ((1, copies[1], k_ref), (0, copies[2], q_ref)):
        copy.wait()
        rows = turned(ref[...])
        for peer, head in enumerate(heads):
            out_ref[peer, place * tokens : (place + 1) * tokens] = rows[head]
        leave(place * tokens, tokens)
    copies[3].wait()
    rows = turned(v_ref[...])
    for r in range(ratio):
        for peer, head in enumerate(heads):
            out_ref[peer, (2 + r) * tokens : (3 + r) * tokens] = rows[head * ratio + r]
        leave((2 + r) * tokens, tokens)
    for copy in leaving:
        copy.wait()


def gate_kernel(sub, n_head, gate_ref, gain_ref, own_ref, swap_ref, gates):
    heads = own_ref.shape[1]
    unused, along_head = position(sub, n_head)
    gate = gate_ref[...].astype(F32)
    gated = gain_ref[...].astype(F32)[:, None] * (gate / (1.0 + jnp.exp(-gate)))
    gates[...] = turned(gated.astype(BF16))
    for number in range(n_head // 2):
        own_ref[number] = gates[pl.ds((along_head ^ (2 * number)) * heads, heads)]
        swap_ref[number] = gates[pl.ds((along_head ^ (2 * number + 1)) * heads, heads)]


def pair_kernel(own_ref, swapped_ref, *pair_refs):
    for number, pair_ref in enumerate(pair_refs):
        pair_ref[0] = own_ref[number + 1]
        pair_ref[1] = swapped_ref[number + 1]


def hold_kernel(weight_hbm, after_ref, weight_ref, done):
    copy = pltpu.make_async_copy(weight_hbm, weight_ref, done)
    copy.start()
    copy.wait()


def block_slabs(blocks, sub, sources):
    places = [partner(source, sub, sources // sub) for source in range(sources)]
    per = sources // blocks
    return [places[block * per : (block + 1) * per] for block in range(blocks)]


def block_rows(got_ref, slabs, tokens, part):
    return jnp.concatenate([got_ref[slab, part * tokens : (part + 1) * tokens] for slab in slabs], axis=0)


def beside(matrices):
    return jnp.concatenate(matrices, axis=1)


def parts_of(wide, count):
    width = wide.shape[1] // count
    return [wide[:, part * width : (part + 1) * width] for part in range(count)]


def block_inverse(below):
    size = below[0].shape[0]
    rows = lax.broadcasted_iota(jnp.int32, (size, size), 0)
    cols = lax.broadcasted_iota(jnp.int32, (size, size), 1)
    apart = rows ^ cols
    below = [matrix.astype(BF16) for matrix in below]
    solved = [jnp.where(apart == 0, 1.0, 0.0).astype(BF16)] * len(below)
    for level in range(size.bit_length() - 2):
        joins = jnp.where((apart >> level) == 1, 1.0, 0.0).astype(BF16)
        parts = [matrix * joins for matrix in below]
        if level == 0:
            solved = [now - part for part, now in zip(parts, solved)]
        else:
            inner = [dot(part, now).astype(BF16) for part, now in zip(parts, solved)]
            solved = [now - dot(now, mid).astype(BF16) for now, mid in zip(solved, inner)]
    return solved


def dot_two(left, right):
    high = left.astype(BF16)
    low = (left - high.astype(F32)).astype(BF16)
    both = dot(jnp.concatenate([high, low], axis=0), right)
    return both[: left.shape[0]] + both[left.shape[0] :]


def refined(below, solved):
    size = below[0].shape[0]
    rows = lax.broadcasted_iota(jnp.int32, (size, size), 0)
    cols = lax.broadcasted_iota(jnp.int32, (size, size), 1)
    identity = jnp.where(rows == cols, 1.0, 0.0)
    left_over = [
        (identity - now.astype(F32) - dot_two(matrix, now)).astype(BF16) for matrix, now in zip(below, solved)
    ]
    return [now.astype(F32) + dot(now, rest) for now, rest in zip(solved, left_over)]


def factor_kernel(tokens, ratio, sub, passing, total_too, got_ref, *refs):
    state_ref, w_ref, u_ref, *tree_refs = refs[passing:]
    width = got_ref.shape[-1]
    per = SPAN // tokens
    blocks = got_ref.shape[0] // per
    slabs = block_slabs(blocks, sub, got_ref.shape[0])
    rows = lax.broadcasted_iota(jnp.int32, (SPAN, SPAN), 0)
    cols = lax.broadcasted_iota(jnp.int32, (SPAN, SPAN), 1)
    lane = lax.broadcasted_iota(jnp.int32, (1, SPAN), 1)
    first = (2 + ratio) * tokens
    below, held = [], []
    for block in range(blocks):
        key = block_rows(got_ref, slabs[block], tokens, 1)
        gram = dot_nt(key, key)
        squares = jnp.where(rows == cols, gram, 0.0)
        key_row = lax.rsqrt(jnp.sum(squares, 0, keepdims=True) + EPSILON)
        key_col = lax.rsqrt(jnp.sum(squares, 1, keepdims=True) + EPSILON)
        lower = jnp.where(rows > cols, gram, 0.0) * key_row
        strengths = []
        for r in range(ratio):
            strength = jnp.zeros((1, SPAN), F32)
            for place in range(per):
                piece = got_ref[slabs[block][place], first : first + ROW_TILE].astype(F32)[r : r + 1]
                strength = jnp.where(lane // tokens == place, piece, strength)
            scaled_col = jnp.sum(jnp.where(rows == cols, strength * key_row, 0.0), 1, keepdims=True)
            below.append(lower * scaled_col)
            strengths.append(strength)
        held.append((block, key, key_col, key_row, strengths))
    solved = refined(below, block_inverse(below))
    flat = [(block, r) for block in range(blocks) for r in range(ratio)]
    weighted = []
    for inverse, (block, r) in zip(solved, flat):
        unused, key, key_col, key_row, strengths = held[block]
        weighted.append(inverse * key_col * strengths[r])
    for part, (block, r) in zip(weighted, flat):
        value = block_rows(got_ref, slabs[block], tokens, 2 + r)
        u_ref[block, r] = dot_two(part, value)
    for part, (block, r) in zip(weighted, flat):
        unused, key, key_col, key_row, strengths = held[block]
        w_ref[block, r] = dot_two(part * key_row, key).astype(BF16)
    turns, adds = [], []
    for block in range(blocks):
        key_t = held[block][1].T
        for r in range(ratio):
            turn, add = parts_of(dot(key_t, beside([w_ref[block, r], u_ref[block, r].astype(BF16)])), 2)
            turns.append(turn)
            adds.append(add)

    level = 0
    while len(adds) > ratio:
        count = len(adds) // ratio
        trans_ref, add_ref = tree_refs[2 * level : 2 * level + 2]
        for number in range(len(adds)):
            trans_ref[number // ratio, number % ratio] = turns[number].astype(BF16)
            add_ref[number // ratio, number % ratio] = adds[number]
        longer_turns, longer_adds = [], []
        for pair in range(count // 2):
            for r in range(ratio):
                left, right = 2 * pair * ratio + r, (2 * pair + 1) * ratio + r
                if count > 2 or total_too:
                    both = beside([turns[left], adds[left]])
                    turn, add = parts_of(both - dot(turns[right].astype(BF16), both.astype(BF16)), 2)
                    longer_turns.append(turns[right] + turn)
                else:
                    add = adds[left] - dot(turns[right].astype(BF16), adds[left].astype(BF16))
                longer_adds.append(add + adds[right])
        turns, adds = longer_turns, longer_adds
        level += 1
    for r in range(ratio):
        state_ref[r] = adds[r].astype(state_ref.dtype)
        if total_too:
            tree_refs[-1][r] = turns[r]


def tree_starts(ratio, width, tree_refs):
    rows = lax.broadcasted_iota(jnp.int32, (width, 2 * width), 0)
    cols = lax.broadcasted_iota(jnp.int32, (width, 2 * width), 1)
    neutral = jnp.where(cols == rows + width, 1.0, 0.0).astype(F32)
    starts = [None] * ratio
    for level in reversed(range(len(tree_refs) // 2)):
        trans_ref, add_ref = tree_refs[2 * level : 2 * level + 2]
        longer = []
        for number, start in enumerate(starts):
            place, r = 2 * (number // ratio), number % ratio
            add = beside([add_ref[place, r], jnp.zeros((width, width), F32)])
            if start is None:
                turn = beside([jnp.zeros((width, width), F32), trans_ref[place, r].astype(F32)])
                longer.append((start, neutral - turn + add))
            else:
                longer.append((start, start - dot(trans_ref[place, r], start.astype(BF16)) + add))
        starts = []
        for pair in range(len(longer) // ratio):
            for side in range(2):
                starts += [longer[pair * ratio + r][side] for r in range(ratio)]
    return [neutral if start is None else start for start in starts]


def spread_kernel(tokens, ratio, sub, passing, got_ref, w_ref, u_ref, *refs):
    refs = refs[: len(refs) - passing]
    tree_refs, (local_ref, reach_ref) = refs[: len(refs) - passing - 2], refs[-2:]
    width = got_ref.shape[-1]
    per = SPAN // tokens
    blocks = got_ref.shape[0] // per
    slabs = block_slabs(blocks, sub, got_ref.shape[0])
    rows = lax.broadcasted_iota(jnp.int32, (SPAN, SPAN), 0)
    cols = lax.broadcasted_iota(jnp.int32, (SPAN, SPAN), 1)
    starts = [start.astype(BF16) for start in tree_starts(ratio, width, tree_refs)]
    lefts, units = [], []
    for block in range(blocks):
        query = block_rows(got_ref, slabs[block], tokens, 0)
        key = block_rows(got_ref, slabs[block], tokens, 1)
        scores = jnp.where(rows >= cols, dot_nt(query, key), 0.0).astype(BF16)
        query_f = query.astype(F32)
        squares = jnp.sum(query_f * query_f, 1, keepdims=True)
        units.append(lax.rsqrt(squares + EPSILON) * width ** (-0.5))
        lefts.append(beside([query, scores]))
    flat = [(block, r) for block in range(blocks) for r in range(ratio)]
    rights = []
    for start, (block, r) in zip(starts, flat):
        through, reached = parts_of(dot(w_ref[block, r], start), 2)
        corrected = beside([u_ref[block, r] - through, -reached]).astype(BF16)
        rights.append(jnp.concatenate([start, corrected], axis=0))
    for right, (block, r) in zip(rights, flat):
        out = dot(lefts[block], right) * units[block]
        local_ref[r, block] = out[:, :width]
        reach_ref[r, block] = out[:, width:].astype(BF16)


def join_kernel(order, n_head, state_ref, local_ref, reach_ref, *out_refs):
    ratio, blocks, span, width = local_ref.shape
    pieces = out_refs[0].shape[1]
    along_sub, along_head = position(len(order), n_head)
    upper = along_head // (n_head // 2)
    follows = lax.axis_index("outer") > 0
    states = [jnp.where(follows, state_ref[r].astype(F32), 0.0).astype(BF16) for r in range(ratio)]
    for distance, out_ref in zip(order, out_refs):
        target = along_sub ^ distance
        for kept in range(2):
            for piece in range(pieces):
                block = (target * 2 + (upper ^ (1 - kept))) * pieces + piece
                for r in range(ratio):
                    core = local_ref[r, block] + dot(reach_ref[r, block], states[r])
                    mean_square = jnp.mean(core * core, 1, keepdims=True)
                    out_ref[kept, piece, r] = (core * lax.rsqrt(mean_square + EPSILON)).astype(BF16)


def project_kernel(order, gate_places, kept, *refs):
    parts, shares = len(order), len(gate_places)
    normed_refs, gate_refs = refs[:parts], refs[parts : parts + shares]
    weight_ref, *out_refs, rows_ref = refs[parts + 2 * shares :]
    unused, pieces, ratio, span, width = normed_refs[0].shape
    tokens = gate_refs[0].shape[2]
    per = span // tokens
    along_sub, along_head = position(parts, 2 * shares)
    for distance, normed_ref in zip(order, normed_refs):
        source = along_sub ^ distance
        for apart, gate_ref in enumerate(gate_refs):
            share = (along_head ^ apart) & (shares - 1)
            first = ((1 - apart % 2) * (shares // 2) + share // 2) * tokens
            place = pl.ds(pl.multiple_of(first, tokens), tokens)
            from_rows = pl.ds(pl.multiple_of(share % per * tokens, tokens), tokens)
            for r in range(ratio):
                lanes = pl.ds(pl.multiple_of((source * ratio + r) * width, width), width)
                normed = normed_ref[kept, share // per, r, from_rows].astype(F32)
                gate = gate_ref[gate_places[apart], source * ratio + r].astype(F32)
                rows_ref[place, lanes] = (normed * gate).astype(BF16)
    multiply(0, rows_ref[...], weight_ref, out_refs)


def multiply(first, rows, weight_ref, out_refs):
    *send_refs, keep_ref = out_refs
    every = keep_ref.shape[-1]
    out = dot(rows, weight_ref[:, first : first + every]).reshape((2,) + keep_ref.shape)
    start = 0
    for send_ref in send_refs:
        columns = send_ref.shape[-1]
        send_ref[...] = out[0, :, :, start : start + columns].astype(BF16)
        start += columns
    keep_ref[...] = out[1]


def more_kernel(first, rows_ref, weight_ref, *out_refs):
    multiply(first, rows_ref[...], weight_ref, out_refs)


def sum_kernel(keep_ref, *refs):
    *got_refs, out_ref = refs
    every = keep_ref.shape[-1]
    placed, start = [], 0
    for got_ref in got_refs:
        placed.append((start, got_ref))
        start = (start + got_ref.shape[-1]) % every
    cuts = sorted({first for first, unused in placed} | {every})
    for first, last in zip(cuts, cuts[1:]):
        total = keep_ref[:, :, first:last]
        for start, got_ref in placed:
            if start <= first and last <= start + got_ref.shape[-1]:
                total = total + got_ref[:, :, first - start : last - start].astype(F32)
        out_ref[:, :, first:last] = total.astype(out_ref.dtype)


def per_device(
    outer, sub, n_head, queries, key_vectors, value_vectors, output_gate, write_strength, norm_gain, output_weight
):
    tokens, key_heads, width = queries.shape
    value_heads = value_vectors.shape[1]
    ratio = value_heads // key_heads
    sources = sub * n_head
    shard = tokens * sources
    blocks = shard // SPAN
    shard_tokens = tokens * n_head
    shape = jax.ShapeDtypeStruct
    along_sub, along_head = split_axis("sub", sub), split_axis("head", n_head)

    with jax.named_scope("pack"):
        slab = ((2 + ratio) * tokens + ROW_TILE, width)
        packed = pl.pallas_call(
            functools.partial(pack_kernel, sub),
            out_shape=shape((sources,) + slab, BF16),
            in_specs=[ANY] * 4,
            out_specs=ANY,
            scratch_shapes=[
                pltpu.VMEM(queries.shape, BF16),
                pltpu.VMEM(key_vectors.shape, BF16),
                pltpu.VMEM(value_vectors.shape, BF16),
                pltpu.VMEM((value_heads, tokens), BF16),
                pltpu.VMEM((sources,) + slab, BF16),
                pltpu.SemaphoreType.DMA((4,)),
                pltpu.SemaphoreType.DMA((3 + ratio,)),
            ],
            compiler_params=params(60),
        )(queries, key_vectors, value_vectors, write_strength.T)
    got = lax.all_to_all(packed, partner_order(sub, n_head), split_axis=0, concat_axis=0, tiled=True)

    heads = sub * ratio
    by_core = [(here, here ^ 1) for here in range(n_head)]
    group = (heads, tokens, width)
    half = n_head // 2
    with jax.named_scope("gates"):
        own_gates, swap = pl.pallas_call(
            functools.partial(gate_kernel, sub, n_head),
            out_shape=[shape((half,) + group, BF16)] * 2,
            in_specs=[VMEM] * 2,
            out_specs=[VMEM] * 2,
            scratch_shapes=[pltpu.VMEM((value_heads, tokens, width), BF16)],
            compiler_params=params(),
            cost_estimate=LIGHT,
        )(output_gate, norm_gain.reshape(1, width))
    swapped = lax.ppermute(swap, along_head, by_core)
    with jax.named_scope("pair"):
        pairs = pl.pallas_call(
            pair_kernel,
            out_shape=[shape((2,) + group, BF16)] * (half - 1),
            in_specs=[VMEM] * 2,
            out_specs=[VMEM] * (half - 1),
            compiler_params=params(),
            cost_estimate=LIGHT,
        )(own_gates, swapped)

    with jax.named_scope("hold"):
        held_weight = pl.pallas_call(
            hold_kernel,
            out_shape=shape(output_weight.shape, BF16),
            in_specs=[ANY] * 2,
            out_specs=VMEM,
            scratch_shapes=[pltpu.SemaphoreType.DMA],
            compiler_params=params(),
            cost_estimate=LIGHT,
        )(output_weight, own_gates)

    state_type = BF16 if outer == 2 else F32
    with jax.named_scope("factors"):
        depths = []
        while blocks >> len(depths) > 1:
            depths.append(blocks >> len(depths))
        tree = []
        for depth in depths:
            tree += [shape((depth, ratio, width, width), BF16), shape((depth, ratio, width, width), F32)]
        if outer > 2:
            tree.append(shape((ratio, width, width), F32))
        out_shape = [
            shape((ratio, width, width), state_type),
            shape((blocks, ratio, SPAN, width), BF16),
            shape((blocks, ratio, SPAN, width), F32),
        ] + tree
        state, w, u, *tree = pl.pallas_call(
            functools.partial(factor_kernel, tokens, ratio, sub, half, outer > 2),
            out_shape=out_shape,
            in_specs=[VMEM] + [ANY] * half,
            out_specs=[VMEM] * len(out_shape),
            compiler_params=params(),
            cost_estimate=LIGHT,
        )(got, held_weight, *pairs)

    onward = [(here, (here + 1) % outer) for here in range(outer)]
    incoming = lax.ppermute(state, "outer", onward)
    with jax.named_scope("spread"):
        read = 3 + 2 * len(depths)
        local, reach, *pairs = pl.pallas_call(
            functools.partial(spread_kernel, tokens, ratio, sub, half - 1),
            out_shape=[
                shape((ratio, blocks, SPAN, width), F32),
                shape((ratio, blocks, SPAN, width), BF16),
            ]
            + [shape((2,) + group, BF16)] * (half - 1),
            in_specs=[VMEM] * read + [ANY] * (half - 1),
            out_specs=[VMEM] * 2 + [ANY] * (half - 1),
            input_output_aliases={read + number: 2 + number for number in range(half - 1)},
            compiler_params=params(),
            cost_estimate=LIGHT,
        )(got, w, u, *tree[: 2 * len(depths)], *pairs)
    gates = [(own_gates, 0), (swapped, 0)]
    for number, pair in enumerate(pairs):
        distance = 2 * number + 2
        pair = lax.ppermute(pair, along_head, [(here, here ^ distance) for here in range(n_head)])
        gates += [(pair, 0), (pair, 1)]
    for hop in range(outer - 2):
        incoming = jnp.where(lax.axis_index("outer") == 0, 0.0, incoming)
        turned_by = jnp.einsum("hde,hef->hdf", tree[-1], incoming, precision=lax.Precision.HIGHEST)
        incoming = lax.ppermute(state + incoming - turned_by, "outer", onward)

    pieces = shard_tokens // SPAN // 2
    columns = output_weight.shape[1]
    quarter = (n_head // 4, tokens, columns)
    half = n_head // 2
    order = [0] + sorted(range(1, sub), reverse=True)
    with jax.named_scope("join"):
        normed = pl.pallas_call(
            functools.partial(join_kernel, order, n_head),
            out_shape=[shape((2, pieces, ratio, SPAN, width), BF16)] * sub,
            in_specs=[VMEM] * 3,
            out_specs=[VMEM] * sub,
            compiler_params=params(),
            cost_estimate=pl.CostEstimate(flops=2 * 10**9, bytes_accessed=1, transcendentals=0),
        )(incoming, local, reach)
    normed = [
        lax.ppermute(part, along_sub, [(here, here ^ distance) for here in range(sub)]) if distance else part
        for distance, part in zip(order, normed)
    ]
    across = [(here, here ^ half) for here in range(n_head)]

    def project(kept, pieces, every, rows_too):
        used, others = gates[half * (1 - kept) : half * (2 - kept)], gates[half * kept : half * (1 + kept)]
        rows = pltpu.VMEM((shard_tokens // 2, heads * width), BF16)
        with jax.named_scope("project"):
            return pl.pallas_call(
                functools.partial(project_kernel, order, [place for unused, place in used], kept),
                out_shape=[shape(quarter[:-1] + (piece,), BF16) for piece in pieces]
                + [shape(quarter[:-1] + (every,), F32)]
                + [shape(rows.shape, BF16)] * rows_too,
                in_specs=[VMEM] * (sub + half) + [ANY] * half + [VMEM],
                out_specs=[VMEM] * (len(pieces) + 1 + rows_too),
                scratch_shapes=[rows] * (1 - rows_too),
                compiler_params=params(),
                cost_estimate=LIGHT,
            )(*normed, *[array for array, unused in used + others], held_weight)

    def add(keep, arrived, kind):
        with jax.named_scope("sum"):
            return pl.pallas_call(
                sum_kernel,
                out_shape=shape(keep.shape, kind),
                in_specs=[VMEM] * (1 + len(arrived)),
                out_specs=VMEM,
                compiler_params=params(),
                cost_estimate=LIGHT,
            )(keep, *arrived)

    cuts = 2
    every = columns // cuts
    passed_on = []
    for cut in range(cuts):
        if cut == 0:
            send, keep, rows = project(0, [every], every, 1)
        else:
            with jax.named_scope("project_more"):
                send, keep = pl.pallas_call(
                    functools.partial(more_kernel, cut * every),
                    out_shape=[shape(quarter[:-1] + (every,), BF16), shape(quarter[:-1] + (every,), F32)],
                    in_specs=[VMEM] * 2,
                    out_specs=[VMEM] * 2,
                    compiler_params=params(),
                    cost_estimate=LIGHT,
                )(rows, held_weight)
        summed = add(keep, [lax.ppermute(send, along_head, by_core)], BF16)
        passed_on.append(lax.ppermute(summed, along_head, across))
    third = columns // 3 // width * width
    *sends, keep = project(1, [columns - 2 * third, third, third], columns, 0)
    arrived = [lax.ppermute(send, along_head, by_core) for send in sends]
    summed = add(keep, arrived + passed_on, BF16 if n_head == 4 else F32)
    bit = 2
    while bit < half:
        mine = (lax.axis_index(along_head) // bit) % 2
        split = summed.reshape((summed.shape[0] // 2, 2) + summed.shape[1:])
        send = lax.dynamic_index_in_dim(split, 1 - mine, 1, False).astype(BF16)
        keep = lax.dynamic_index_in_dim(split, mine, 1, False)
        summed = keep + lax.ppermute(send, along_head, [(here, here ^ bit) for here in range(n_head)]).astype(F32)
        bit *= 2
    return summed[0].astype(BF16)


def solution(mesh):
    n_seq, n_head = mesh.shape["seq"], mesh.shape["head"]

    def run(queries, key_vectors, value_vectors, output_gate, write_strength, norm_gain, output_weight):
        sub = queries.shape[1] // n_head
        outer = n_seq // sub
        along = split_axis("sub", sub) + split_axis("head", n_head)
        split = Mesh(mesh.devices.reshape((outer,) + (2,) * len(along)), ("outer",) + along)
        every = ("outer",) + along
        placed = (
            P(every, None, None),
            P(every, None, None),
            P(every, None, None),
            P(every, None, None),
            P(every, None),
            P(),
            P(split_axis("head", n_head), None),
        )
        return jax.shard_map(
            functools.partial(per_device, outer, sub, n_head),
            mesh=split,
            in_specs=placed,
            out_specs=P(every, None),
            check_vma=False,
        )(queries, key_vectors, value_vectors, output_gate, write_strength, norm_gain, output_weight)

    return run
```

```python
import functools

import jax
import jax.numpy as jnp
from jax import lax
from jax.experimental import pallas as pl
from jax.experimental.pallas import tpu as pltpu
from jax.sharding import Mesh, PartitionSpec as P

SPAN = 128
EPSILON = 1e-06
F32 = jnp.float32
BF16 = jnp.bfloat16
ROW_TILE = 16
VMEM = pl.BlockSpec(memory_space=pltpu.VMEM)
SMEM = pl.BlockSpec(memory_space=pltpu.SMEM)
ANY = pl.BlockSpec(memory_space=pl.ANY)
LIGHT = pl.CostEstimate(flops=1, bytes_accessed=1, transcendentals=0)


def dot(left, right):
    return jnp.dot(left, right, preferred_element_type=F32)


def dot_nt(left, right):
    return lax.dot_general(left, right, (((1,), (1,)), ((), ())), preferred_element_type=F32)


def params(megabytes=24):
    return pltpu.CompilerParams(vmem_limit_bytes=megabytes * 2**20)


def turned(values):
    return jnp.transpose(values, (1, 0, 2))


def split_axis(name, size):
    return tuple(f"{name}{bit}" for bit in reversed(range(size.bit_length() - 1)))


def partner_order(sub, n_head):
    heads = split_axis("head", n_head)
    return heads[-1:] + heads[:-1] + split_axis("sub", sub)


def partner(source, sub, n_head):
    axes = split_axis("sub", sub) + split_axis("head", n_head)
    bits = {name: source >> (len(axes) - 1 - number) & 1 for number, name in enumerate(axes)}
    place = 0
    for name in partner_order(sub, n_head):
        place = 2 * place + bits[name]
    return place


def position(sub, n_head):
    return lax.axis_index(split_axis("sub", sub)), lax.axis_index(split_axis("head", n_head))


def pack_kernel(sub, q_hbm, k_hbm, v_hbm, b_hbm, out_hbm, q_ref, k_ref, v_ref, b_ref, out_ref, came, left):
    tokens, key_heads, width = q_hbm.shape
    ratio = v_hbm.shape[1] // key_heads
    copies = [
        pltpu.make_async_copy(source, target, came.at[number])
        for number, (source, target) in enumerate(
            ((b_hbm, b_ref), (k_hbm, k_ref), (q_hbm, q_ref), (v_hbm, v_ref))
        )
    ]
    for copy in copies:
        copy.start()
    n_head = key_heads // sub
    heads = [head % sub * n_head + head // sub for head in range(key_heads)]
    heads = [partner(source, sub, n_head) for source in heads]
    heads = [heads.index(peer) for peer in range(key_heads)]
    leaving = []

    def leave(first, size):
        rows = pl.ds(first, size)
        leaving.append(pltpu.make_async_copy(out_ref.at[:, rows], out_hbm.at[:, rows], left.at[len(leaving)]))
        leaving[-1].start()

    copies[0].wait()
    strength = jnp.concatenate([b_ref[...].astype(F32)] * (width // tokens), axis=1)
    strength = jnp.concatenate([strength, jnp.zeros((ROW_TILE, width), F32)], axis=0)
    for peer, head in enumerate(heads):
        tile = strength[head * ratio : head * ratio + ROW_TILE]
        out_ref[peer, (2 + ratio) * tokens :] = tile.astype(BF16)
    leave((2 + ratio) * tokens, ROW_TILE)
    for place, copy, ref in ((1, copies[1], k_ref), (0, copies[2], q_ref)):
        copy.wait()
        rows = turned(ref[...])
        for peer, head in enumerate(heads):
            out_ref[peer, place * tokens : (place + 1) * tokens] = rows[head]
        leave(place * tokens, tokens)
    copies[3].wait()
    rows = turned(v_ref[...])
    for r in range(ratio):
        for peer, head in enumerate(heads):
            out_ref[peer, (2 + r) * tokens : (3 + r) * tokens] = rows[head * ratio + r]
        leave((2 + r) * tokens, tokens)
    for copy in leaving:
        copy.wait()


def gate_kernel(sub, n_head, gate_ref, gain_ref, own_ref, swap_ref, gates):
    heads = own_ref.shape[1]
    unused, along_head = position(sub, n_head)
    gate = gate_ref[...].astype(F32)
    gated = gain_ref[...].astype(F32)[:, None] * (gate / (1.0 + jnp.exp(-gate)))
    gates[...] = turned(gated.astype(BF16))
    for number in range(n_head // 2):
        own_ref[number] = gates[pl.ds((along_head ^ (2 * number)) * heads, heads)]
        swap_ref[number] = gates[pl.ds((along_head ^ (2 * number + 1)) * heads, heads)]


def pair_kernel(own_ref, swapped_ref, *pair_refs):
    for number, pair_ref in enumerate(pair_refs):
        pair_ref[0] = own_ref[number + 1]
        pair_ref[1] = swapped_ref[number + 1]


def block_slabs(blocks, sub, sources):
    places = [partner(source, sub, sources // sub) for source in range(sources)]
    per = sources // blocks
    return [places[block * per : (block + 1) * per] for block in range(blocks)]


def block_rows(got_ref, slabs, tokens, part):
    return jnp.concatenate([got_ref[slab, part * tokens : (part + 1) * tokens] for slab in slabs], axis=0)


def beside(matrices):
    return jnp.concatenate(matrices, axis=1)


def parts_of(wide, count):
    width = wide.shape[1] // count
    return [wide[:, part * width : (part + 1) * width] for part in range(count)]


def block_inverse(below):
    size = below[0].shape[0]
    rows = lax.broadcasted_iota(jnp.int32, (size, size), 0)
    cols = lax.broadcasted_iota(jnp.int32, (size, size), 1)
    apart = rows ^ cols
    below = [matrix.astype(BF16) for matrix in below]
    solved = [jnp.where(apart == 0, 1.0, 0.0).astype(BF16)] * len(below)
    for level in range(size.bit_length() - 2):
        joins = jnp.where((apart >> level) == 1, 1.0, 0.0).astype(BF16)
        parts = [matrix * joins for matrix in below]
        if level == 0:
            solved = [now - part for part, now in zip(parts, solved)]
        else:
            inner = [dot(part, now).astype(BF16) for part, now in zip(parts, solved)]
            solved = [now - dot(now, mid).astype(BF16) for now, mid in zip(solved, inner)]
    return solved


def dot_two(left, right):
    high = left.astype(BF16)
    low = (left - high.astype(F32)).astype(BF16)
    both = dot(jnp.concatenate([high, low], axis=0), right)
    return both[: left.shape[0]] + both[left.shape[0] :]


def refined(below, solved):
    size = below[0].shape[0]
    rows = lax.broadcasted_iota(jnp.int32, (size, size), 0)
    cols = lax.broadcasted_iota(jnp.int32, (size, size), 1)
    identity = jnp.where(rows == cols, 1.0, 0.0)
    left_over = [
        (identity - now.astype(F32) - dot_two(matrix, now)).astype(BF16) for matrix, now in zip(below, solved)
    ]
    return [now.astype(F32) + dot(now, rest) for now, rest in zip(solved, left_over)]


def factor_kernel(tokens, ratio, sub, passing, total_too, got_ref, *refs):
    state_ref, w_ref, u_ref, *tree_refs = refs[passing:]
    width = got_ref.shape[-1]
    per = SPAN // tokens
    blocks = got_ref.shape[0] // per
    slabs = block_slabs(blocks, sub, got_ref.shape[0])
    rows = lax.broadcasted_iota(jnp.int32, (SPAN, SPAN), 0)
    cols = lax.broadcasted_iota(jnp.int32, (SPAN, SPAN), 1)
    lane = lax.broadcasted_iota(jnp.int32, (1, SPAN), 1)
    first = (2 + ratio) * tokens
    below, held = [], []
    for block in range(blocks):
        key = block_rows(got_ref, slabs[block], tokens, 1)
        gram = dot_nt(key, key)
        squares = jnp.where(rows == cols, gram, 0.0)
        key_row = lax.rsqrt(jnp.sum(squares, 0, keepdims=True) + EPSILON)
        key_col = lax.rsqrt(jnp.sum(squares, 1, keepdims=True) + EPSILON)
        lower = jnp.where(rows > cols, gram, 0.0) * key_row
        strengths = []
        for r in range(ratio):
            strength = jnp.zeros((1, SPAN), F32)
            for place in range(per):
                piece = got_ref[slabs[block][place], first : first + ROW_TILE].astype(F32)[r : r + 1]
                strength = jnp.where(lane // tokens == place, piece, strength)
            scaled_col = jnp.sum(jnp.where(rows == cols, strength * key_row, 0.0), 1, keepdims=True)
            below.append(lower * scaled_col)
            strengths.append(strength)
        held.append((block, key, key_col, key_row, strengths))
    solved = refined(below, block_inverse(below))
    flat = [(block, r) for block in range(blocks) for r in range(ratio)]
    weighted = []
    for inverse, (block, r) in zip(solved, flat):
        unused, key, key_col, key_row, strengths = held[block]
        weighted.append(inverse * key_col * strengths[r])
    for part, (block, r) in zip(weighted, flat):
        value = block_rows(got_ref, slabs[block], tokens, 2 + r)
        u_ref[block, r] = dot_two(part, value)
    for part, (block, r) in zip(weighted, flat):
        unused, key, key_col, key_row, strengths = held[block]
        w_ref[block, r] = dot_two(part * key_row, key).astype(BF16)
    turns, adds = [], []
    for block in range(blocks):
        key_t = held[block][1].T
        for r in range(ratio):
            turn, add = parts_of(dot(key_t, beside([w_ref[block, r], u_ref[block, r].astype(BF16)])), 2)
            turns.append(turn)
            adds.append(add)

    level = 0
    while len(adds) > ratio:
        count = len(adds) // ratio
        trans_ref, add_ref = tree_refs[2 * level : 2 * level + 2]
        for number in range(len(adds)):
            trans_ref[number // ratio, number % ratio] = turns[number].astype(BF16)
            add_ref[number // ratio, number % ratio] = adds[number]
        longer_turns, longer_adds = [], []
        for pair in range(count // 2):
            for r in range(ratio):
                left, right = 2 * pair * ratio + r, (2 * pair + 1) * ratio + r
                if count > 2 or total_too:
                    both = beside([turns[left], adds[left]])
                    turn, add = parts_of(both - dot(turns[right].astype(BF16), both.astype(BF16)), 2)
                    longer_turns.append(turns[right] + turn)
                else:
                    add = adds[left] - dot(turns[right].astype(BF16), adds[left].astype(BF16))
                longer_adds.append(add + adds[right])
        turns, adds = longer_turns, longer_adds
        level += 1
    for r in range(ratio):
        state_ref[r] = adds[r].astype(state_ref.dtype)
        if total_too:
            tree_refs[-1][r] = turns[r]


def tree_starts(ratio, width, tree_refs):
    rows = lax.broadcasted_iota(jnp.int32, (width, 2 * width), 0)
    cols = lax.broadcasted_iota(jnp.int32, (width, 2 * width), 1)
    neutral = jnp.where(cols == rows + width, 1.0, 0.0).astype(F32)
    starts = [None] * ratio
    for level in reversed(range(len(tree_refs) // 2)):
        trans_ref, add_ref = tree_refs[2 * level : 2 * level + 2]
        longer = []
        for number, start in enumerate(starts):
            place, r = 2 * (number // ratio), number % ratio
            add = beside([add_ref[place, r], jnp.zeros((width, width), F32)])
            if start is None:
                turn = beside([jnp.zeros((width, width), F32), trans_ref[place, r].astype(F32)])
                longer.append((start, neutral - turn + add))
            else:
                longer.append((start, start - dot(trans_ref[place, r], start.astype(BF16)) + add))
        starts = []
        for pair in range(len(longer) // ratio):
            for side in range(2):
                starts += [longer[pair * ratio + r][side] for r in range(ratio)]
    return [neutral if start is None else start for start in starts]


def spread_kernel(tokens, ratio, sub, passing, got_ref, w_ref, u_ref, *refs):
    refs = refs[: len(refs) - passing]
    tree_refs, (local_ref, reach_ref) = refs[: len(refs) - passing - 2], refs[-2:]
    width = got_ref.shape[-1]
    per = SPAN // tokens
    blocks = got_ref.shape[0] // per
    slabs = block_slabs(blocks, sub, got_ref.shape[0])
    rows = lax.broadcasted_iota(jnp.int32, (SPAN, SPAN), 0)
    cols = lax.broadcasted_iota(jnp.int32, (SPAN, SPAN), 1)
    starts = [start.astype(BF16) for start in tree_starts(ratio, width, tree_refs)]
    lefts, units = [], []
    for block in range(blocks):
        query = block_rows(got_ref, slabs[block], tokens, 0)
        key = block_rows(got_ref, slabs[block], tokens, 1)
        scores = jnp.where(rows >= cols, dot_nt(query, key), 0.0).astype(BF16)
        query_f = query.astype(F32)
        squares = jnp.sum(query_f * query_f, 1, keepdims=True)
        units.append(lax.rsqrt(squares + EPSILON) * width ** (-0.5))
        lefts.append(beside([query, scores]))
    flat = [(block, r) for block in range(blocks) for r in range(ratio)]
    rights = []
    for start, (block, r) in zip(starts, flat):
        through, reached = parts_of(dot(w_ref[block, r], start), 2)
        corrected = beside([u_ref[block, r] - through, -reached]).astype(BF16)
        rights.append(jnp.concatenate([start, corrected], axis=0))
    for right, (block, r) in zip(rights, flat):
        out = dot(lefts[block], right) * units[block]
        local_ref[r, block] = out[:, :width]
        reach_ref[r, block] = out[:, width:].astype(BF16)


def join_kernel(order, n_head, state_ref, local_ref, reach_ref, *out_refs):
    ratio, blocks, span, width = local_ref.shape
    pieces = out_refs[0].shape[1]
    along_sub, along_head = position(len(order), n_head)
    upper = along_head // (n_head // 2)
    follows = lax.axis_index("outer") > 0
    states = [jnp.where(follows, state_ref[r].astype(F32), 0.0).astype(BF16) for r in range(ratio)]
    for distance, out_ref in zip(order, out_refs):
        target = along_sub ^ distance
        for kept in range(2):
            for piece in range(pieces):
                block = (target * 2 + (upper ^ (1 - kept))) * pieces + piece
                for r in range(ratio):
                    core = local_ref[r, block] + dot(reach_ref[r, block], states[r])
                    mean_square = jnp.mean(core * core, 1, keepdims=True)
                    out_ref[kept, piece, r] = (core * lax.rsqrt(mean_square + EPSILON)).astype(BF16)


def project_kernel(order, gate_places, kept, *refs):
    parts, shares = len(order), len(gate_places)
    normed_refs, gate_refs = refs[:parts], refs[parts : parts + shares]
    weight_ref, *out_refs, rows_ref = refs[parts + 2 * shares :]
    unused, pieces, ratio, span, width = normed_refs[0].shape
    tokens = gate_refs[0].shape[2]
    per = span // tokens
    along_sub, along_head = position(parts, 2 * shares)
    for distance, normed_ref in zip(order, normed_refs):
        source = along_sub ^ distance
        for apart, gate_ref in enumerate(gate_refs):
            share = (along_head ^ apart) & (shares - 1)
            first = ((1 - apart % 2) * (shares // 2) + share // 2) * tokens
            place = pl.ds(pl.multiple_of(first, tokens), tokens)
            from_rows = pl.ds(pl.multiple_of(share % per * tokens, tokens), tokens)
            for r in range(ratio):
                lanes = pl.ds(pl.multiple_of((source * ratio + r) * width, width), width)
                normed = normed_ref[kept, share // per, r, from_rows].astype(F32)
                gate = gate_ref[gate_places[apart], source * ratio + r].astype(F32)
                rows_ref[place, lanes] = (normed * gate).astype(BF16)
    multiply(0, rows_ref[...], weight_ref, out_refs)


def multiply(first, rows, weight_ref, out_refs):
    *send_refs, keep_ref = out_refs
    every = keep_ref.shape[-1]
    out = dot(rows, weight_ref[:, first : first + every]).reshape((2,) + keep_ref.shape)
    start = 0
    for send_ref in send_refs:
        columns = send_ref.shape[-1]
        send_ref[...] = out[0, :, :, start : start + columns].astype(BF16)
        start += columns
    keep_ref[...] = out[1]


def more_kernel(first, rows_ref, weight_ref, *out_refs):
    multiply(first, rows_ref[...], weight_ref, out_refs)


def sum_kernel(keep_ref, *refs):
    *got_refs, out_ref = refs
    every = keep_ref.shape[-1]
    placed, start = [], 0
    for got_ref in got_refs:
        placed.append((start, got_ref))
        start = (start + got_ref.shape[-1]) % every
    cuts = sorted({first for first, unused in placed} | {every})
    for first, last in zip(cuts, cuts[1:]):
        total = keep_ref[:, :, first:last]
        for start, got_ref in placed:
            if start <= first and last <= start + got_ref.shape[-1]:
                total = total + got_ref[:, :, first - start : last - start].astype(F32)
        out_ref[:, :, first:last] = total.astype(out_ref.dtype)


def per_device(
    outer, sub, n_head, queries, key_vectors, value_vectors, output_gate, write_strength, norm_gain, output_weight
):
    tokens, key_heads, width = queries.shape
    value_heads = value_vectors.shape[1]
    ratio = value_heads // key_heads
    sources = sub * n_head
    shard = tokens * sources
    blocks = shard // SPAN
    shard_tokens = tokens * n_head
    shape = jax.ShapeDtypeStruct
    along_sub, along_head = split_axis("sub", sub), split_axis("head", n_head)

    with jax.named_scope("pack"):
        slab = ((2 + ratio) * tokens + ROW_TILE, width)
        packed = pl.pallas_call(
            functools.partial(pack_kernel, sub),
            out_shape=shape((sources,) + slab, BF16),
            in_specs=[ANY] * 4,
            out_specs=ANY,
            scratch_shapes=[
                pltpu.VMEM(queries.shape, BF16),
                pltpu.VMEM(key_vectors.shape, BF16),
                pltpu.VMEM(value_vectors.shape, BF16),
                pltpu.VMEM((value_heads, tokens), BF16),
                pltpu.VMEM((sources,) + slab, BF16),
                pltpu.SemaphoreType.DMA((4,)),
                pltpu.SemaphoreType.DMA((3 + ratio,)),
            ],
            compiler_params=params(60),
        )(queries, key_vectors, value_vectors, write_strength.T)
    got = lax.all_to_all(packed, partner_order(sub, n_head), split_axis=0, concat_axis=0, tiled=True)

    heads = sub * ratio
    by_core = [(here, here ^ 1) for here in range(n_head)]
    group = (heads, tokens, width)
    half = n_head // 2
    with jax.named_scope("gates"):
        own_gates, swap = pl.pallas_call(
            functools.partial(gate_kernel, sub, n_head),
            out_shape=[shape((half,) + group, BF16)] * 2,
            in_specs=[VMEM] * 2,
            out_specs=[VMEM] * 2,
            scratch_shapes=[pltpu.VMEM((value_heads, tokens, width), BF16)],
            compiler_params=params(),
            cost_estimate=LIGHT,
        )(output_gate, norm_gain.reshape(1, width))
    swapped = lax.ppermute(swap, along_head, by_core)
    with jax.named_scope("pair"):
        pairs = pl.pallas_call(
            pair_kernel,
            out_shape=[shape((2,) + group, BF16)] * (half - 1),
            in_specs=[VMEM] * 2,
            out_specs=[VMEM] * (half - 1),
            compiler_params=params(),
            cost_estimate=LIGHT,
        )(own_gates, swapped)

    state_type = BF16 if outer == 2 else F32
    with jax.named_scope("factors"):
        depths = []
        while blocks >> len(depths) > 1:
            depths.append(blocks >> len(depths))
        tree = []
        for depth in depths:
            tree += [shape((depth, ratio, width, width), BF16), shape((depth, ratio, width, width), F32)]
        if outer > 2:
            tree.append(shape((ratio, width, width), F32))
        out_shape = [
            shape((ratio, width, width), state_type),
            shape((blocks, ratio, SPAN, width), BF16),
            shape((blocks, ratio, SPAN, width), F32),
        ] + tree
        state, w, u, *tree = pl.pallas_call(
            functools.partial(factor_kernel, tokens, ratio, sub, half - 1, outer > 2),
            out_shape=out_shape,
            in_specs=[VMEM] + [ANY] * (half - 1),
            out_specs=[VMEM] * len(out_shape),
            compiler_params=params(),
            cost_estimate=LIGHT,
        )(got, *pairs)

    onward = [(here, (here + 1) % outer) for here in range(outer)]
    incoming = lax.ppermute(state, "outer", onward)
    with jax.named_scope("spread"):
        read = 3 + 2 * len(depths)
        local, reach, *pairs = pl.pallas_call(
            functools.partial(spread_kernel, tokens, ratio, sub, half - 1),
            out_shape=[
                shape((ratio, blocks, SPAN, width), F32),
                shape((ratio, blocks, SPAN, width), BF16),
            ]
            + [shape((2,) + group, BF16)] * (half - 1),
            in_specs=[VMEM] * read + [ANY] * (half - 1),
            out_specs=[VMEM] * 2 + [ANY] * (half - 1),
            input_output_aliases={read + number: 2 + number for number in range(half - 1)},
            compiler_params=params(),
            cost_estimate=LIGHT,
        )(got, w, u, *tree[: 2 * len(depths)], *pairs)
    gates = [(own_gates, 0), (swapped, 0)]
    for number, pair in enumerate(pairs):
        distance = 2 * number + 2
        pair = lax.ppermute(pair, along_head, [(here, here ^ distance) for here in range(n_head)])
        gates += [(pair, 0), (pair, 1)]
    for hop in range(outer - 2):
        incoming = jnp.where(lax.axis_index("outer") == 0, 0.0, incoming)
        turned_by = jnp.einsum("hde,hef->hdf", tree[-1], incoming, precision=lax.Precision.HIGHEST)
        incoming = lax.ppermute(state + incoming - turned_by, "outer", onward)

    pieces = shard_tokens // SPAN // 2
    columns = output_weight.shape[1]
    quarter = (n_head // 4, tokens, columns)
    half = n_head // 2
    order = list(range(sub))
    with jax.named_scope("join"):
        normed = pl.pallas_call(
            functools.partial(join_kernel, order, n_head),
            out_shape=[shape((2, pieces, ratio, SPAN, width), BF16)] * sub,
            in_specs=[VMEM] * 3,
            out_specs=[VMEM] * sub,
            compiler_params=params(),
            cost_estimate=pl.CostEstimate(flops=2 * 10**9, bytes_accessed=1, transcendentals=0),
        )(incoming, local, reach)
    normed = [
        lax.ppermute(part, along_sub, [(here, here ^ distance) for here in range(sub)]) if distance else part
        for distance, part in zip(order, normed)
    ]
    across = [(here, here ^ half) for here in range(n_head)]

    def project(kept, pieces, every, rows_too):
        used, others = gates[half * (1 - kept) : half * (2 - kept)], gates[half * kept : half * (1 + kept)]
        rows = pltpu.VMEM((shard_tokens // 2, heads * width), BF16)
        with jax.named_scope("project"):
            return pl.pallas_call(
                functools.partial(project_kernel, order, [place for unused, place in used], kept),
                out_shape=[shape(quarter[:-1] + (piece,), BF16) for piece in pieces]
                + [shape(quarter[:-1] + (every,), F32)]
                + [shape(rows.shape, BF16)] * rows_too,
                in_specs=[VMEM] * (sub + half) + [ANY] * half + [VMEM],
                out_specs=[VMEM] * (len(pieces) + 1 + rows_too),
                scratch_shapes=[rows] * (1 - rows_too),
                compiler_params=params(),
                cost_estimate=LIGHT,
            )(*normed, *[array for array, unused in used + others], output_weight)

    def add(keep, arrived, kind):
        with jax.named_scope("sum"):
            return pl.pallas_call(
                sum_kernel,
                out_shape=shape(keep.shape, kind),
                in_specs=[VMEM] * (1 + len(arrived)),
                out_specs=VMEM,
                compiler_params=params(),
                cost_estimate=LIGHT,
            )(keep, *arrived)

    cuts = 2
    every = columns // cuts
    passed_on = []
    for cut in range(cuts):
        if cut == 0:
            send, keep, rows = project(0, [every], every, 1)
        else:
            with jax.named_scope("project_more"):
                send, keep = pl.pallas_call(
                    functools.partial(more_kernel, cut * every),
                    out_shape=[shape(quarter[:-1] + (every,), BF16), shape(quarter[:-1] + (every,), F32)],
                    in_specs=[VMEM] * 2,
                    out_specs=[VMEM] * 2,
                    compiler_params=params(),
                    cost_estimate=LIGHT,
                )(rows, output_weight)
        summed = add(keep, [lax.ppermute(send, along_head, by_core)], BF16)
        passed_on.append(lax.ppermute(summed, along_head, across))
    third = columns // 3 // width * width
    *sends, keep = project(1, [columns - 2 * third, third, third], columns, 0)
    arrived = [lax.ppermute(send, along_head, by_core) for send in sends]
    summed = add(keep, arrived + passed_on, BF16 if n_head == 4 else F32)
    bit = 2
    while bit < half:
        mine = (lax.axis_index(along_head) // bit) % 2
        split = summed.reshape((summed.shape[0] // 2, 2) + summed.shape[1:])
        send = lax.dynamic_index_in_dim(split, 1 - mine, 1, False).astype(BF16)
        keep = lax.dynamic_index_in_dim(split, mine, 1, False)
        summed = keep + lax.ppermute(send, along_head, [(here, here ^ bit) for here in range(n_head)]).astype(F32)
        bit *= 2
    return summed[0].astype(BF16)


def solution(mesh):
    n_seq, n_head = mesh.shape["seq"], mesh.shape["head"]

    def run(queries, key_vectors, value_vectors, output_gate, write_strength, norm_gain, output_weight):
        sub = queries.shape[1] // n_head
        outer = n_seq // sub
        along = split_axis("sub", sub) + split_axis("head", n_head)
        split = Mesh(mesh.devices.reshape((outer,) + (2,) * len(along)), ("outer",) + along)
        every = ("outer",) + along
        placed = (
            P(every, None, None),
            P(every, None, None),
            P(every, None, None),
            P(every, None, None),
            P(every, None),
            P(),
            P(split_axis("head", n_head), None),
        )
        return jax.shard_map(
            functools.partial(per_device, outer, sub, n_head),
            mesh=split,
            in_specs=placed,
            out_specs=P(every, None),
            check_vma=False,
        )(queries, key_vectors, value_vectors, output_gate, write_strength, norm_gain, output_weight)

    return run
```

```python
import functools

import jax
import jax.numpy as jnp
from jax import lax
from jax.experimental import pallas as pl
from jax.experimental.pallas import tpu as pltpu
from jax.sharding import Mesh, PartitionSpec as P

SPAN = 128
EPSILON = 1e-06
F32 = jnp.float32
BF16 = jnp.bfloat16
ROW_TILE = 16
VMEM = pl.BlockSpec(memory_space=pltpu.VMEM)
SMEM = pl.BlockSpec(memory_space=pltpu.SMEM)
ANY = pl.BlockSpec(memory_space=pl.ANY)
LIGHT = pl.CostEstimate(flops=1, bytes_accessed=1, transcendentals=0)


def dot(left, right):
    return jnp.dot(left, right, preferred_element_type=F32)


def dot_nt(left, right):
    return lax.dot_general(left, right, (((1,), (1,)), ((), ())), preferred_element_type=F32)


def params(megabytes=24):
    return pltpu.CompilerParams(vmem_limit_bytes=megabytes * 2**20)


def turned(values):
    return jnp.transpose(values, (1, 0, 2))


def split_axis(name, size):
    return tuple(f"{name}{bit}" for bit in reversed(range(size.bit_length() - 1)))


def partner_order(sub, n_head):
    heads = split_axis("head", n_head)
    return heads[-1:] + heads[:-1] + split_axis("sub", sub)


def partner(source, sub, n_head):
    axes = split_axis("sub", sub) + split_axis("head", n_head)
    bits = {name: source >> (len(axes) - 1 - number) & 1 for number, name in enumerate(axes)}
    place = 0
    for name in partner_order(sub, n_head):
        place = 2 * place + bits[name]
    return place


def position(sub, n_head):
    return lax.axis_index(split_axis("sub", sub)), lax.axis_index(split_axis("head", n_head))


def pack_kernel(sub, q_hbm, k_hbm, v_hbm, b_hbm, out_hbm, q_ref, k_ref, v_ref, b_ref, out_ref, came, left):
    tokens, key_heads, width = q_hbm.shape
    ratio = v_hbm.shape[1] // key_heads
    copies = [
        pltpu.make_async_copy(source, target, came.at[number])
        for number, (source, target) in enumerate(
            ((b_hbm, b_ref), (k_hbm, k_ref), (q_hbm, q_ref), (v_hbm, v_ref))
        )
    ]
    for copy in copies:
        copy.start()
    n_head = key_heads // sub
    heads = [head % sub * n_head + head // sub for head in range(key_heads)]
    heads = [partner(source, sub, n_head) for source in heads]
    heads = [heads.index(peer) for peer in range(key_heads)]
    leaving = []

    def leave(first, size):
        rows = pl.ds(first, size)
        leaving.append(pltpu.make_async_copy(out_ref.at[:, rows], out_hbm.at[:, rows], left.at[len(leaving)]))
        leaving[-1].start()

    copies[0].wait()
    strength = jnp.concatenate([b_ref[...].astype(F32)] * (width // tokens), axis=1)
    strength = jnp.concatenate([strength, jnp.zeros((ROW_TILE, width), F32)], axis=0)
    for peer, head in enumerate(heads):
        tile = strength[head * ratio : head * ratio + ROW_TILE]
        out_ref[peer, (2 + ratio) * tokens :] = tile.astype(BF16)
    leave((2 + ratio) * tokens, ROW_TILE)
    for place, copy, ref in ((1, copies[1], k_ref), (0, copies[2], q_ref)):
        copy.wait()
        rows = turned(ref[...])
        for peer, head in enumerate(heads):
            out_ref[peer, place * tokens : (place + 1) * tokens] = rows[head]
        leave(place * tokens, tokens)
    copies[3].wait()
    rows = turned(v_ref[...])
    for r in range(ratio):
        for peer, head in enumerate(heads):
            out_ref[peer, (2 + r) * tokens : (3 + r) * tokens] = rows[head * ratio + r]
        leave((2 + r) * tokens, tokens)
    for copy in leaving:
        copy.wait()


def gate_kernel(sub, n_head, gate_ref, gain_ref, own_ref, swap_ref, gates):
    heads = own_ref.shape[1]
    unused, along_head = position(sub, n_head)
    gate = gate_ref[...].astype(F32)
    gated = gain_ref[...].astype(F32)[:, None] * (gate / (1.0 + jnp.exp(-gate)))
    gates[...] = turned(gated.astype(BF16))
    for number in range(n_head // 2):
        own_ref[number] = gates[pl.ds((along_head ^ (2 * number)) * heads, heads)]
        swap_ref[number] = gates[pl.ds((along_head ^ (2 * number + 1)) * heads, heads)]


def pair_kernel(own_ref, swapped_ref, *pair_refs):
    for number, pair_ref in enumerate(pair_refs):
        pair_ref[0] = own_ref[number + 1]
        pair_ref[1] = swapped_ref[number + 1]


def block_slabs(blocks, sub, sources):
    places = [partner(source, sub, sources // sub) for source in range(sources)]
    per = sources // blocks
    return [places[block * per : (block + 1) * per] for block in range(blocks)]


def block_rows(got_ref, slabs, tokens, part):
    return jnp.concatenate([got_ref[slab, part * tokens : (part + 1) * tokens] for slab in slabs], axis=0)


def beside(matrices):
    return jnp.concatenate(matrices, axis=1)


def parts_of(wide, count):
    width = wide.shape[1] // count
    return [wide[:, part * width : (part + 1) * width] for part in range(count)]


def block_inverse(below):
    size = below[0].shape[0]
    rows = lax.broadcasted_iota(jnp.int32, (size, size), 0)
    cols = lax.broadcasted_iota(jnp.int32, (size, size), 1)
    apart = rows ^ cols
    below = [matrix.astype(BF16) for matrix in below]
    solved = [jnp.where(apart == 0, 1.0, 0.0).astype(BF16)] * len(below)
    for level in range(size.bit_length() - 2):
        joins = jnp.where((apart >> level) == 1, 1.0, 0.0).astype(BF16)
        parts = [matrix * joins for matrix in below]
        if level == 0:
            solved = [now - part for part, now in zip(parts, solved)]
        else:
            inner = [dot(part, now).astype(BF16) for part, now in zip(parts, solved)]
            solved = [now - dot(now, mid).astype(BF16) for now, mid in zip(solved, inner)]
    return solved


def dot_two(left, right):
    high = left.astype(BF16)
    low = (left - high.astype(F32)).astype(BF16)
    both = dot(jnp.concatenate([high, low], axis=0), right)
    return both[: left.shape[0]] + both[left.shape[0] :]


def refined(below, solved):
    size = below[0].shape[0]
    rows = lax.broadcasted_iota(jnp.int32, (size, size), 0)
    cols = lax.broadcasted_iota(jnp.int32, (size, size), 1)
    identity = jnp.where(rows == cols, 1.0, 0.0)
    left_over = [
        (identity - now.astype(F32) - dot_two(matrix, now)).astype(BF16) for matrix, now in zip(below, solved)
    ]
    return [now.astype(F32) + dot(now, rest) for now, rest in zip(solved, left_over)]


def factor_kernel(tokens, ratio, sub, passing, total_too, got_ref, *refs):
    state_ref, w_ref, u_ref, *tree_refs = refs[passing:]
    width = got_ref.shape[-1]
    per = SPAN // tokens
    blocks = got_ref.shape[0] // per
    slabs = block_slabs(blocks, sub, got_ref.shape[0])
    rows = lax.broadcasted_iota(jnp.int32, (SPAN, SPAN), 0)
    cols = lax.broadcasted_iota(jnp.int32, (SPAN, SPAN), 1)
    lane = lax.broadcasted_iota(jnp.int32, (1, SPAN), 1)
    first = (2 + ratio) * tokens
    below, held = [], []
    for block in range(blocks):
        key = block_rows(got_ref, slabs[block], tokens, 1)
        gram = dot_nt(key, key)
        squares = jnp.where(rows == cols, gram, 0.0)
        key_row = lax.rsqrt(jnp.sum(squares, 0, keepdims=True) + EPSILON)
        key_col = lax.rsqrt(jnp.sum(squares, 1, keepdims=True) + EPSILON)
        lower = jnp.where(rows > cols, gram, 0.0) * key_row
        strengths = []
        for r in range(ratio):
            strength = jnp.zeros((1, SPAN), F32)
            for place in range(per):
                piece = got_ref[slabs[block][place], first : first + ROW_TILE].astype(F32)[r : r + 1]
                strength = jnp.where(lane // tokens == place, piece, strength)
            scaled_col = jnp.sum(jnp.where(rows == cols, strength * key_row, 0.0), 1, keepdims=True)
            below.append(lower * scaled_col)
            strengths.append(strength)
        held.append((block, key, key_col, key_row, strengths))
    solved = refined(below, block_inverse(below))
    flat = [(block, r) for block in range(blocks) for r in range(ratio)]
    weighted = []
    for inverse, (block, r) in zip(solved, flat):
        unused, key, key_col, key_row, strengths = held[block]
        weighted.append(inverse * key_col * strengths[r])
    for part, (block, r) in zip(weighted, flat):
        value = block_rows(got_ref, slabs[block], tokens, 2 + r)
        u_ref[block, r] = dot(part.astype(BF16), value)
    for part, (block, r) in zip(weighted, flat):
        unused, key, key_col, key_row, strengths = held[block]
        w_ref[block, r] = dot((part * key_row).astype(BF16), key).astype(BF16)
    turns, adds = [], []
    for block in range(blocks):
        key_t = held[block][1].T
        for r in range(ratio):
            turn, add = parts_of(dot(key_t, beside([w_ref[block, r], u_ref[block, r].astype(BF16)])), 2)
            turns.append(turn)
            adds.append(add)

    level = 0
    while len(adds) > ratio:
        count = len(adds) // ratio
        trans_ref, add_ref = tree_refs[2 * level : 2 * level + 2]
        for number in range(len(adds)):
            trans_ref[number // ratio, number % ratio] = turns[number].astype(BF16)
            add_ref[number // ratio, number % ratio] = adds[number]
        longer_turns, longer_adds = [], []
        for pair in range(count // 2):
            for r in range(ratio):
                left, right = 2 * pair * ratio + r, (2 * pair + 1) * ratio + r
                if count > 2 or total_too:
                    both = beside([turns[left], adds[left]])
                    turn, add = parts_of(both - dot(turns[right].astype(BF16), both.astype(BF16)), 2)
                    longer_turns.append(turns[right] + turn)
                else:
                    add = adds[left] - dot(turns[right].astype(BF16), adds[left].astype(BF16))
                longer_adds.append(add + adds[right])
        turns, adds = longer_turns, longer_adds
        level += 1
    for r in range(ratio):
        state_ref[r] = adds[r].astype(state_ref.dtype)
        if total_too:
            tree_refs[-1][r] = turns[r]


def tree_starts(ratio, width, tree_refs):
    rows = lax.broadcasted_iota(jnp.int32, (width, 2 * width), 0)
    cols = lax.broadcasted_iota(jnp.int32, (width, 2 * width), 1)
    neutral = jnp.where(cols == rows + width, 1.0, 0.0).astype(F32)
    starts = [None] * ratio
    for level in reversed(range(len(tree_refs) // 2)):
        trans_ref, add_ref = tree_refs[2 * level : 2 * level + 2]
        longer = []
        for number, start in enumerate(starts):
            place, r = 2 * (number // ratio), number % ratio
            add = beside([add_ref[place, r], jnp.zeros((width, width), F32)])
            if start is None:
                turn = beside([jnp.zeros((width, width), F32), trans_ref[place, r].astype(F32)])
                longer.append((start, neutral - turn + add))
            else:
                longer.append((start, start - dot(trans_ref[place, r], start.astype(BF16)) + add))
        starts = []
        for pair in range(len(longer) // ratio):
            for side in range(2):
                starts += [longer[pair * ratio + r][side] for r in range(ratio)]
    return [neutral if start is None else start for start in starts]


def spread_kernel(tokens, ratio, sub, passing, got_ref, w_ref, u_ref, *refs):
    refs = refs[: len(refs) - passing]
    tree_refs, (local_ref, reach_ref) = refs[: len(refs) - passing - 2], refs[-2:]
    width = got_ref.shape[-1]
    per = SPAN // tokens
    blocks = got_ref.shape[0] // per
    slabs = block_slabs(blocks, sub, got_ref.shape[0])
    rows = lax.broadcasted_iota(jnp.int32, (SPAN, SPAN), 0)
    cols = lax.broadcasted_iota(jnp.int32, (SPAN, SPAN), 1)
    starts = [start.astype(BF16) for start in tree_starts(ratio, width, tree_refs)]
    lefts, units = [], []
    for block in range(blocks):
        query = block_rows(got_ref, slabs[block], tokens, 0)
        key = block_rows(got_ref, slabs[block], tokens, 1)
        scores = jnp.where(rows >= cols, dot_nt(query, key), 0.0).astype(BF16)
        query_f = query.astype(F32)
        squares = jnp.sum(query_f * query_f, 1, keepdims=True)
        units.append(lax.rsqrt(squares + EPSILON) * width ** (-0.5))
        lefts.append(beside([query, scores]))
    flat = [(block, r) for block in range(blocks) for r in range(ratio)]
    rights = []
    for start, (block, r) in zip(starts, flat):
        through, reached = parts_of(dot(w_ref[block, r], start), 2)
        corrected = beside([u_ref[block, r] - through, -reached]).astype(BF16)
        rights.append(jnp.concatenate([start, corrected], axis=0))
    for right, (block, r) in zip(rights, flat):
        out = dot(lefts[block], right) * units[block]
        local_ref[r, block] = out[:, :width]
        reach_ref[r, block] = out[:, width:].astype(BF16)


def join_kernel(order, n_head, state_ref, local_ref, reach_ref, *out_refs):
    ratio, blocks, span, width = local_ref.shape
    pieces = out_refs[0].shape[1]
    along_sub, along_head = position(len(order), n_head)
    upper = along_head // (n_head // 2)
    follows = lax.axis_index("outer") > 0
    states = [jnp.where(follows, state_ref[r].astype(F32), 0.0).astype(BF16) for r in range(ratio)]
    for distance, out_ref in zip(order, out_refs):
        target = along_sub ^ distance
        for kept in range(2):
            for piece in range(pieces):
                block = (target * 2 + (upper ^ (1 - kept))) * pieces + piece
                for r in range(ratio):
                    core = local_ref[r, block] + dot(reach_ref[r, block], states[r])
                    mean_square = jnp.mean(core * core, 1, keepdims=True)
                    out_ref[kept, piece, r] = (core * lax.rsqrt(mean_square + EPSILON)).astype(BF16)


def project_kernel(order, gate_places, kept, *refs):
    parts, shares = len(order), len(gate_places)
    normed_refs, gate_refs = refs[:parts], refs[parts : parts + shares]
    weight_ref, *out_refs, rows_ref = refs[parts + 2 * shares :]
    unused, pieces, ratio, span, width = normed_refs[0].shape
    tokens = gate_refs[0].shape[2]
    per = span // tokens
    along_sub, along_head = position(parts, 2 * shares)
    for distance, normed_ref in zip(order, normed_refs):
        source = along_sub ^ distance
        for apart, gate_ref in enumerate(gate_refs):
            share = (along_head ^ apart) & (shares - 1)
            first = ((1 - apart % 2) * (shares // 2) + share // 2) * tokens
            place = pl.ds(pl.multiple_of(first, tokens), tokens)
            from_rows = pl.ds(pl.multiple_of(share % per * tokens, tokens), tokens)
            for r in range(ratio):
                lanes = pl.ds(pl.multiple_of((source * ratio + r) * width, width), width)
                normed = normed_ref[kept, share // per, r, from_rows].astype(F32)
                gate = gate_ref[gate_places[apart], source * ratio + r].astype(F32)
                rows_ref[place, lanes] = (normed * gate).astype(BF16)
    multiply(0, rows_ref[...], weight_ref, out_refs)


def multiply(first, rows, weight_ref, out_refs):
    *send_refs, keep_ref = out_refs
    every = keep_ref.shape[-1]
    out = dot(rows, weight_ref[:, first : first + every]).reshape((2,) + keep_ref.shape)
    start = 0
    for send_ref in send_refs:
        columns = send_ref.shape[-1]
        send_ref[...] = out[0, :, :, start : start + columns].astype(BF16)
        start += columns
    keep_ref[...] = out[1]


def more_kernel(first, rows_ref, weight_ref, *out_refs):
    multiply(first, rows_ref[...], weight_ref, out_refs)


def sum_kernel(keep_ref, *refs):
    *got_refs, out_ref = refs
    every = keep_ref.shape[-1]
    placed, start = [], 0
    for got_ref in got_refs:
        placed.append((start, got_ref))
        start = (start + got_ref.shape[-1]) % every
    cuts = sorted({first for first, unused in placed} | {every})
    for first, last in zip(cuts, cuts[1:]):
        total = keep_ref[:, :, first:last]
        for start, got_ref in placed:
            if start <= first and last <= start + got_ref.shape[-1]:
                total = total + got_ref[:, :, first - start : last - start].astype(F32)
        out_ref[:, :, first:last] = total.astype(out_ref.dtype)


def per_device(
    outer, sub, n_head, queries, key_vectors, value_vectors, output_gate, write_strength, norm_gain, output_weight
):
    tokens, key_heads, width = queries.shape
    value_heads = value_vectors.shape[1]
    ratio = value_heads // key_heads
    sources = sub * n_head
    shard = tokens * sources
    blocks = shard // SPAN
    shard_tokens = tokens * n_head
    shape = jax.ShapeDtypeStruct
    along_sub, along_head = split_axis("sub", sub), split_axis("head", n_head)

    with jax.named_scope("pack"):
        slab = ((2 + ratio) * tokens + ROW_TILE, width)
        packed = pl.pallas_call(
            functools.partial(pack_kernel, sub),
            out_shape=shape((sources,) + slab, BF16),
            in_specs=[ANY] * 4,
            out_specs=ANY,
            scratch_shapes=[
                pltpu.VMEM(queries.shape, BF16),
                pltpu.VMEM(key_vectors.shape, BF16),
                pltpu.VMEM(value_vectors.shape, BF16),
                pltpu.VMEM((value_heads, tokens), BF16),
                pltpu.VMEM((sources,) + slab, BF16),
                pltpu.SemaphoreType.DMA((4,)),
                pltpu.SemaphoreType.DMA((3 + ratio,)),
            ],
            compiler_params=params(60),
        )(queries, key_vectors, value_vectors, write_strength.T)
    got = lax.all_to_all(packed, partner_order(sub, n_head), split_axis=0, concat_axis=0, tiled=True)

    heads = sub * ratio
    by_core = [(here, here ^ 1) for here in range(n_head)]
    group = (heads, tokens, width)
    half = n_head // 2
    with jax.named_scope("gates"):
        own_gates, swap = pl.pallas_call(
            functools.partial(gate_kernel, sub, n_head),
            out_shape=[shape((half,) + group, BF16)] * 2,
            in_specs=[VMEM] * 2,
            out_specs=[VMEM] * 2,
            scratch_shapes=[pltpu.VMEM((value_heads, tokens, width), BF16)],
            compiler_params=params(),
            cost_estimate=LIGHT,
        )(output_gate, norm_gain.reshape(1, width))
    swapped = lax.ppermute(swap, along_head, by_core)
    with jax.named_scope("pair"):
        pairs = pl.pallas_call(
            pair_kernel,
            out_shape=[shape((2,) + group, BF16)] * (half - 1),
            in_specs=[VMEM] * 2,
            out_specs=[VMEM] * (half - 1),
            compiler_params=params(),
            cost_estimate=LIGHT,
        )(own_gates, swapped)

    state_type = BF16 if outer == 2 else F32
    with jax.named_scope("factors"):
        depths = []
        while blocks >> len(depths) > 1:
            depths.append(blocks >> len(depths))
        tree = []
        for depth in depths:
            tree += [shape((depth, ratio, width, width), BF16), shape((depth, ratio, width, width), F32)]
        if outer > 2:
            tree.append(shape((ratio, width, width), F32))
        out_shape = [
            shape((ratio, width, width), state_type),
            shape((blocks, ratio, SPAN, width), BF16),
            shape((blocks, ratio, SPAN, width), F32),
        ] + tree
        state, w, u, *tree = pl.pallas_call(
            functools.partial(factor_kernel, tokens, ratio, sub, half - 1, outer > 2),
            out_shape=out_shape,
            in_specs=[VMEM] + [ANY] * (half - 1),
            out_specs=[VMEM] * len(out_shape),
            compiler_params=params(),
            cost_estimate=LIGHT,
        )(got, *pairs)

    onward = [(here, (here + 1) % outer) for here in range(outer)]
    incoming = lax.ppermute(state, "outer", onward)
    with jax.named_scope("spread"):
        read = 3 + 2 * len(depths)
        local, reach, *pairs = pl.pallas_call(
            functools.partial(spread_kernel, tokens, ratio, sub, half - 1),
            out_shape=[
                shape((ratio, blocks, SPAN, width), F32),
                shape((ratio, blocks, SPAN, width), BF16),
            ]
            + [shape((2,) + group, BF16)] * (half - 1),
            in_specs=[VMEM] * read + [ANY] * (half - 1),
            out_specs=[VMEM] * 2 + [ANY] * (half - 1),
            input_output_aliases={read + number: 2 + number for number in range(half - 1)},
            compiler_params=params(),
            cost_estimate=LIGHT,
        )(got, w, u, *tree[: 2 * len(depths)], *pairs)
    gates = [(own_gates, 0), (swapped, 0)]
    for number, pair in enumerate(pairs):
        distance = 2 * number + 2
        pair = lax.ppermute(pair, along_head, [(here, here ^ distance) for here in range(n_head)])
        gates += [(pair, 0), (pair, 1)]
    for hop in range(outer - 2):
        incoming = jnp.where(lax.axis_index("outer") == 0, 0.0, incoming)
        turned_by = jnp.einsum("hde,hef->hdf", tree[-1], incoming, precision=lax.Precision.HIGHEST)
        incoming = lax.ppermute(state + incoming - turned_by, "outer", onward)

    pieces = shard_tokens // SPAN // 2
    columns = output_weight.shape[1]
    quarter = (n_head // 4, tokens, columns)
    half = n_head // 2
    order = [0] + sorted(range(1, sub), reverse=True)
    with jax.named_scope("join"):
        normed = pl.pallas_call(
            functools.partial(join_kernel, order, n_head),
            out_shape=[shape((2, pieces, ratio, SPAN, width), BF16)] * sub,
            in_specs=[VMEM] * 3,
            out_specs=[VMEM] * sub,
            compiler_params=params(),
            cost_estimate=pl.CostEstimate(flops=2 * 10**9, bytes_accessed=1, transcendentals=0),
        )(incoming, local, reach)
    normed = [
        lax.ppermute(part, along_sub, [(here, here ^ distance) for here in range(sub)]) if distance else part
        for distance, part in zip(order, normed)
    ]
    across = [(here, here ^ half) for here in range(n_head)]

    def project(kept, pieces, every, rows_too):
        used, others = gates[half * (1 - kept) : half * (2 - kept)], gates[half * kept : half * (1 + kept)]
        rows = pltpu.VMEM((shard_tokens // 2, heads * width), BF16)
        with jax.named_scope("project"):
            return pl.pallas_call(
                functools.partial(project_kernel, order, [place for unused, place in used], kept),
                out_shape=[shape(quarter[:-1] + (piece,), BF16) for piece in pieces]
                + [shape(quarter[:-1] + (every,), F32)]
                + [shape(rows.shape, BF16)] * rows_too,
                in_specs=[VMEM] * (sub + half) + [ANY] * half + [VMEM],
                out_specs=[VMEM] * (len(pieces) + 1 + rows_too),
                scratch_shapes=[rows] * (1 - rows_too),
                compiler_params=params(),
                cost_estimate=LIGHT,
            )(*normed, *[array for array, unused in used + others], output_weight)

    def add(keep, arrived, kind):
        with jax.named_scope("sum"):
            return pl.pallas_call(
                sum_kernel,
                out_shape=shape(keep.shape, kind),
                in_specs=[VMEM] * (1 + len(arrived)),
                out_specs=VMEM,
                compiler_params=params(),
                cost_estimate=LIGHT,
            )(keep, *arrived)

    cuts = 2
    every = columns // cuts
    passed_on = []
    for cut in range(cuts):
        if cut == 0:
            send, keep, rows = project(0, [every], every, 1)
        else:
            with jax.named_scope("project_more"):
                send, keep = pl.pallas_call(
                    functools.partial(more_kernel, cut * every),
                    out_shape=[shape(quarter[:-1] + (every,), BF16), shape(quarter[:-1] + (every,), F32)],
                    in_specs=[VMEM] * 2,
                    out_specs=[VMEM] * 2,
                    compiler_params=params(),
                    cost_estimate=LIGHT,
                )(rows, output_weight)
        summed = add(keep, [lax.ppermute(send, along_head, by_core)], BF16)
        passed_on.append(lax.ppermute(summed, along_head, across))
    third = columns // 3 // width * width
    *sends, keep = project(1, [columns - 2 * third, third, third], columns, 0)
    arrived = [lax.ppermute(send, along_head, by_core) for send in sends]
    summed = add(keep, arrived + passed_on, BF16 if n_head == 4 else F32)
    bit = 2
    while bit < half:
        mine = (lax.axis_index(along_head) // bit) % 2
        split = summed.reshape((summed.shape[0] // 2, 2) + summed.shape[1:])
        send = lax.dynamic_index_in_dim(split, 1 - mine, 1, False).astype(BF16)
        keep = lax.dynamic_index_in_dim(split, mine, 1, False)
        summed = keep + lax.ppermute(send, along_head, [(here, here ^ bit) for here in range(n_head)]).astype(F32)
        bit *= 2
    return summed[0].astype(BF16)


def solution(mesh):
    n_seq, n_head = mesh.shape["seq"], mesh.shape["head"]

    def run(queries, key_vectors, value_vectors, output_gate, write_strength, norm_gain, output_weight):
        sub = queries.shape[1] // n_head
        outer = n_seq // sub
        along = split_axis("sub", sub) + split_axis("head", n_head)
        split = Mesh(mesh.devices.reshape((outer,) + (2,) * len(along)), ("outer",) + along)
        every = ("outer",) + along
        placed = (
            P(every, None, None),
            P(every, None, None),
            P(every, None, None),
            P(every, None, None),
            P(every, None),
            P(),
            P(split_axis("head", n_head), None),
        )
        return jax.shard_map(
            functools.partial(per_device, outer, sub, n_head),
            mesh=split,
            in_specs=placed,
            out_specs=P(every, None),
            check_vma=False,
        )(queries, key_vectors, value_vectors, output_gate, write_strength, norm_gain, output_weight)

    return run
```

```python
import functools

import jax
import jax.numpy as jnp
from jax import lax
from jax.experimental import pallas as pl
from jax.experimental.pallas import tpu as pltpu
from jax.sharding import Mesh, PartitionSpec as P

SPAN = 128
EPSILON = 1e-06
F32 = jnp.float32
BF16 = jnp.bfloat16
ROW_TILE = 16
VMEM = pl.BlockSpec(memory_space=pltpu.VMEM)
SMEM = pl.BlockSpec(memory_space=pltpu.SMEM)
ANY = pl.BlockSpec(memory_space=pl.ANY)
LIGHT = pl.CostEstimate(flops=1, bytes_accessed=1, transcendentals=0)


def dot(left, right):
    return jnp.dot(left, right, preferred_element_type=F32)


def dot_nt(left, right):
    return lax.dot_general(left, right, (((1,), (1,)), ((), ())), preferred_element_type=F32)


def params(megabytes=24):
    return pltpu.CompilerParams(vmem_limit_bytes=megabytes * 2**20)


def turned(values):
    return jnp.transpose(values, (1, 0, 2))


def split_axis(name, size):
    return tuple(f"{name}{bit}" for bit in reversed(range(size.bit_length() - 1)))


def partner_order(sub, n_head):
    heads = split_axis("head", n_head)
    return heads[-1:] + split_axis("sub", sub) + heads[:-1]


def partner(source, sub, n_head):
    axes = split_axis("sub", sub) + split_axis("head", n_head)
    bits = {name: source >> (len(axes) - 1 - number) & 1 for number, name in enumerate(axes)}
    place = 0
    for name in partner_order(sub, n_head):
        place = 2 * place + bits[name]
    return place


def position(sub, n_head):
    return lax.axis_index(split_axis("sub", sub)), lax.axis_index(split_axis("head", n_head))


def pack_kernel(sub, q_hbm, k_hbm, v_hbm, b_hbm, out_hbm, q_ref, k_ref, v_ref, b_ref, out_ref, came, left):
    tokens, key_heads, width = q_hbm.shape
    ratio = v_hbm.shape[1] // key_heads
    copies = [
        pltpu.make_async_copy(source, target, came.at[number])
        for number, (source, target) in enumerate(
            ((b_hbm, b_ref), (k_hbm, k_ref), (q_hbm, q_ref), (v_hbm, v_ref))
        )
    ]
    for copy in copies:
        copy.start()
    n_head = key_heads // sub
    heads = [head % sub * n_head + head // sub for head in range(key_heads)]
    heads = [partner(source, sub, n_head) for source in heads]
    heads = [heads.index(peer) for peer in range(key_heads)]
    leaving = []

    def leave(first, size):
        rows = pl.ds(first, size)
        leaving.append(pltpu.make_async_copy(out_ref.at[:, rows], out_hbm.at[:, rows], left.at[len(leaving)]))
        leaving[-1].start()

    copies[0].wait()
    strength = jnp.concatenate([b_ref[...].astype(F32)] * (width // tokens), axis=1)
    strength = jnp.concatenate([strength, jnp.zeros((ROW_TILE, width), F32)], axis=0)
    for peer, head in enumerate(heads):
        tile = strength[head * ratio : head * ratio + ROW_TILE]
        out_ref[peer, (2 + ratio) * tokens :] = tile.astype(BF16)
    leave((2 + ratio) * tokens, ROW_TILE)
    for place, copy, ref in ((1, copies[1], k_ref), (0, copies[2], q_ref)):
        copy.wait()
        rows = turned(ref[...])
        for peer, head in enumerate(heads):
            out_ref[peer, place * tokens : (place + 1) * tokens] = rows[head]
        leave(place * tokens, tokens)
    copies[3].wait()
    rows = turned(v_ref[...])
    for r in range(ratio):
        for peer, head in enumerate(heads):
            out_ref[peer, (2 + r) * tokens : (3 + r) * tokens] = rows[head * ratio + r]
        leave((2 + r) * tokens, tokens)
    for copy in leaving:
        copy.wait()


def gate_kernel(sub, n_head, gate_ref, gain_ref, own_ref, swap_ref, gates):
    heads = own_ref.shape[1]
    unused, along_head = position(sub, n_head)
    gate = gate_ref[...].astype(F32)
    gated = gain_ref[...].astype(F32)[:, None] * (gate / (1.0 + jnp.exp(-gate)))
    gates[...] = turned(gated.astype(BF16))
    for number in range(n_head // 2):
        own_ref[number] = gates[pl.ds((along_head ^ (2 * number)) * heads, heads)]
        swap_ref[number] = gates[pl.ds((along_head ^ (2 * number + 1)) * heads, heads)]


def pair_kernel(own_ref, swapped_ref, *pair_refs):
    for number, pair_ref in enumerate(pair_refs):
        pair_ref[0] = own_ref[number + 1]
        pair_ref[1] = swapped_ref[number + 1]


def block_slabs(blocks, sub, sources):
    places = [partner(source, sub, sources // sub) for source in range(sources)]
    per = sources // blocks
    return [places[block * per : (block + 1) * per] for block in range(blocks)]


def block_rows(got_ref, slabs, tokens, part):
    return jnp.concatenate([got_ref[slab, part * tokens : (part + 1) * tokens] for slab in slabs], axis=0)


def beside(matrices):
    return jnp.concatenate(matrices, axis=1)


def parts_of(wide, count):
    width = wide.shape[1] // count
    return [wide[:, part * width : (part + 1) * width] for part in range(count)]


def block_inverse(below):
    size = below[0].shape[0]
    rows = lax.broadcasted_iota(jnp.int32, (size, size), 0)
    cols = lax.broadcasted_iota(jnp.int32, (size, size), 1)
    apart = rows ^ cols
    below = [matrix.astype(BF16) for matrix in below]
    solved = [jnp.where(apart == 0, 1.0, 0.0).astype(BF16)] * len(below)
    for level in range(size.bit_length() - 2):
        joins = jnp.where((apart >> level) == 1, 1.0, 0.0).astype(BF16)
        parts = [matrix * joins for matrix in below]
        if level == 0:
            solved = [now - part for part, now in zip(parts, solved)]
        else:
            inner = [dot(part, now).astype(BF16) for part, now in zip(parts, solved)]
            solved = [now - dot(now, mid).astype(BF16) for now, mid in zip(solved, inner)]
    return solved


def dot_two(left, right):
    high = left.astype(BF16)
    low = (left - high.astype(F32)).astype(BF16)
    both = dot(jnp.concatenate([high, low], axis=0), right)
    return both[: left.shape[0]] + both[left.shape[0] :]


def refined(below, solved):
    size = below[0].shape[0]
    rows = lax.broadcasted_iota(jnp.int32, (size, size), 0)
    cols = lax.broadcasted_iota(jnp.int32, (size, size), 1)
    identity = jnp.where(rows == cols, 1.0, 0.0)
    left_over = [
        (identity - now.astype(F32) - dot_two(matrix, now)).astype(BF16) for matrix, now in zip(below, solved)
    ]
    return [now.astype(F32) + dot(now, rest) for now, rest in zip(solved, left_over)]


def factor_kernel(tokens, ratio, sub, passing, total_too, got_ref, *refs):
    state_ref, w_ref, u_ref, *tree_refs = refs[passing:]
    width = got_ref.shape[-1]
    per = SPAN // tokens
    blocks = got_ref.shape[0] // per
    slabs = block_slabs(blocks, sub, got_ref.shape[0])
    rows = lax.broadcasted_iota(jnp.int32, (SPAN, SPAN), 0)
    cols = lax.broadcasted_iota(jnp.int32, (SPAN, SPAN), 1)
    lane = lax.broadcasted_iota(jnp.int32, (1, SPAN), 1)
    first = (2 + ratio) * tokens
    below, held = [], []
    for block in range(blocks):
        key = block_rows(got_ref, slabs[block], tokens, 1)
        gram = dot_nt(key, key)
        squares = jnp.where(rows == cols, gram, 0.0)
        key_row = lax.rsqrt(jnp.sum(squares, 0, keepdims=True) + EPSILON)
        key_col = lax.rsqrt(jnp.sum(squares, 1, keepdims=True) + EPSILON)
        lower = jnp.where(rows > cols, gram, 0.0) * key_row
        strengths = []
        for r in range(ratio):
            strength = jnp.zeros((1, SPAN), F32)
            for place in range(per):
                piece = got_ref[slabs[block][place], first : first + ROW_TILE].astype(F32)[r : r + 1]
                strength = jnp.where(lane // tokens == place, piece, strength)
            scaled_col = jnp.sum(jnp.where(rows == cols, strength * key_row, 0.0), 1, keepdims=True)
            below.append(lower * scaled_col)
            strengths.append(strength)
        held.append((block, key, key_col, key_row, strengths))
    solved = refined(below, block_inverse(below))
    flat = [(block, r) for block in range(blocks) for r in range(ratio)]
    weighted = []
    for inverse, (block, r) in zip(solved, flat):
        unused, key, key_col, key_row, strengths = held[block]
        weighted.append(inverse * key_col * strengths[r])
    for part, (block, r) in zip(weighted, flat):
        value = block_rows(got_ref, slabs[block], tokens, 2 + r)
        u_ref[block, r] = dot(part.astype(BF16), value)
    for part, (block, r) in zip(weighted, flat):
        unused, key, key_col, key_row, strengths = held[block]
        w_ref[block, r] = dot((part * key_row).astype(BF16), key).astype(BF16)
    turns, adds = [], []
    for block in range(blocks):
        key_t = held[block][1].T
        for r in range(ratio):
            turn, add = parts_of(dot(key_t, beside([w_ref[block, r], u_ref[block, r].astype(BF16)])), 2)
            turns.append(turn)
            adds.append(add)

    level = 0
    while len(adds) > ratio:
        count = len(adds) // ratio
        trans_ref, add_ref = tree_refs[2 * level : 2 * level + 2]
        for number in range(len(adds)):
            trans_ref[number // ratio, number % ratio] = turns[number].astype(BF16)
            add_ref[number // ratio, number % ratio] = adds[number]
        longer_turns, longer_adds = [], []
        for pair in range(count // 2):
            for r in range(ratio):
                left, right = 2 * pair * ratio + r, (2 * pair + 1) * ratio + r
                if count > 2 or total_too:
                    both = beside([turns[left], adds[left]])
                    turn, add = parts_of(both - dot(turns[right].astype(BF16), both.astype(BF16)), 2)
                    longer_turns.append(turns[right] + turn)
                else:
                    add = adds[left] - dot(turns[right].astype(BF16), adds[left].astype(BF16))
                longer_adds.append(add + adds[right])
        turns, adds = longer_turns, longer_adds
        level += 1
    for r in range(ratio):
        state_ref[r] = adds[r].astype(state_ref.dtype)
        if total_too:
            tree_refs[-1][r] = turns[r]


def tree_starts(ratio, width, tree_refs):
    rows = lax.broadcasted_iota(jnp.int32, (width, 2 * width), 0)
    cols = lax.broadcasted_iota(jnp.int32, (width, 2 * width), 1)
    neutral = jnp.where(cols == rows + width, 1.0, 0.0).astype(F32)
    starts = [None] * ratio
    for level in reversed(range(len(tree_refs) // 2)):
        trans_ref, add_ref = tree_refs[2 * level : 2 * level + 2]
        longer = []
        for number, start in enumerate(starts):
            place, r = 2 * (number // ratio), number % ratio
            add = beside([add_ref[place, r], jnp.zeros((width, width), F32)])
            if start is None:
                turn = beside([jnp.zeros((width, width), F32), trans_ref[place, r].astype(F32)])
                longer.append((start, neutral - turn + add))
            else:
                longer.append((start, start - dot(trans_ref[place, r], start.astype(BF16)) + add))
        starts = []
        for pair in range(len(longer) // ratio):
            for side in range(2):
                starts += [longer[pair * ratio + r][side] for r in range(ratio)]
    return [neutral if start is None else start for start in starts]


def spread_kernel(tokens, ratio, sub, passing, got_ref, w_ref, u_ref, *refs):
    refs = refs[: len(refs) - passing]
    tree_refs, (local_ref, reach_ref) = refs[: len(refs) - passing - 2], refs[-2:]
    width = got_ref.shape[-1]
    per = SPAN // tokens
    blocks = got_ref.shape[0] // per
    slabs = block_slabs(blocks, sub, got_ref.shape[0])
    rows = lax.broadcasted_iota(jnp.int32, (SPAN, SPAN), 0)
    cols = lax.broadcasted_iota(jnp.int32, (SPAN, SPAN), 1)
    starts = [start.astype(BF16) for start in tree_starts(ratio, width, tree_refs)]
    lefts, units = [], []
    for block in range(blocks):
        query = block_rows(got_ref, slabs[block], tokens, 0)
        key = block_rows(got_ref, slabs[block], tokens, 1)
        scores = jnp.where(rows >= cols, dot_nt(query, key), 0.0).astype(BF16)
        query_f = query.astype(F32)
        squares = jnp.sum(query_f * query_f, 1, keepdims=True)
        units.append(lax.rsqrt(squares + EPSILON) * width ** (-0.5))
        lefts.append(beside([query, scores]))
    flat = [(block, r) for block in range(blocks) for r in range(ratio)]
    rights = []
    for start, (block, r) in zip(starts, flat):
        through, reached = parts_of(dot(w_ref[block, r], start), 2)
        corrected = beside([u_ref[block, r] - through, -reached]).astype(BF16)
        rights.append(jnp.concatenate([start, corrected], axis=0))
    for right, (block, r) in zip(rights, flat):
        out = dot(lefts[block], right) * units[block]
        local_ref[r, block] = out[:, :width]
        reach_ref[r, block] = out[:, width:].astype(BF16)


def join_kernel(order, n_head, state_ref, local_ref, reach_ref, *out_refs):
    ratio, blocks, span, width = local_ref.shape
    pieces = out_refs[0].shape[1]
    along_sub, along_head = position(len(order), n_head)
    upper = along_head // (n_head // 2)
    follows = lax.axis_index("outer") > 0
    states = [jnp.where(follows, state_ref[r].astype(F32), 0.0).astype(BF16) for r in range(ratio)]
    for distance, out_ref in zip(order, out_refs):
        target = along_sub ^ distance
        for kept in range(2):
            for piece in range(pieces):
                block = (target * 2 + (upper ^ (1 - kept))) * pieces + piece
                for r in range(ratio):
                    core = local_ref[r, block] + dot(reach_ref[r, block], states[r])
                    mean_square = jnp.mean(core * core, 1, keepdims=True)
                    out_ref[kept, piece, r] = (core * lax.rsqrt(mean_square + EPSILON)).astype(BF16)


def project_kernel(order, gate_places, kept, *refs):
    parts, shares = len(order), len(gate_places)
    normed_refs, gate_refs = refs[:parts], refs[parts : parts + shares]
    weight_ref, *out_refs, rows_ref = refs[parts + 2 * shares :]
    unused, pieces, ratio, span, width = normed_refs[0].shape
    tokens = gate_refs[0].shape[2]
    per = span // tokens
    along_sub, along_head = position(parts, 2 * shares)
    for distance, normed_ref in zip(order, normed_refs):
        source = along_sub ^ distance
        for apart, gate_ref in enumerate(gate_refs):
            share = (along_head ^ apart) & (shares - 1)
            first = ((1 - apart % 2) * (shares // 2) + share // 2) * tokens
            place = pl.ds(pl.multiple_of(first, tokens), tokens)
            from_rows = pl.ds(pl.multiple_of(share % per * tokens, tokens), tokens)
            for r in range(ratio):
                lanes = pl.ds(pl.multiple_of((source * ratio + r) * width, width), width)
                normed = normed_ref[kept, share // per, r, from_rows].astype(F32)
                gate = gate_ref[gate_places[apart], source * ratio + r].astype(F32)
                rows_ref[place, lanes] = (normed * gate).astype(BF16)
    multiply(0, rows_ref[...], weight_ref, out_refs)


def multiply(first, rows, weight_ref, out_refs):
    *send_refs, keep_ref = out_refs
    every = keep_ref.shape[-1]
    out = dot(rows, weight_ref[:, first : first + every]).reshape((2,) + keep_ref.shape)
    start = 0
    for send_ref in send_refs:
        columns = send_ref.shape[-1]
        send_ref[...] = out[0, :, :, start : start + columns].astype(BF16)
        start += columns
    keep_ref[...] = out[1]


def more_kernel(first, rows_ref, weight_ref, *out_refs):
    multiply(first, rows_ref[...], weight_ref, out_refs)


def sum_kernel(keep_ref, *refs):
    *got_refs, out_ref = refs
    every = keep_ref.shape[-1]
    placed, start = [], 0
    for got_ref in got_refs:
        placed.append((start, got_ref))
        start = (start + got_ref.shape[-1]) % every
    cuts = sorted({first for first, unused in placed} | {every})
    for first, last in zip(cuts, cuts[1:]):
        total = keep_ref[:, :, first:last]
        for start, got_ref in placed:
            if start <= first and last <= start + got_ref.shape[-1]:
                total = total + got_ref[:, :, first - start : last - start].astype(F32)
        out_ref[:, :, first:last] = total.astype(out_ref.dtype)


def per_device(
    outer, sub, n_head, queries, key_vectors, value_vectors, output_gate, write_strength, norm_gain, output_weight
):
    tokens, key_heads, width = queries.shape
    value_heads = value_vectors.shape[1]
    ratio = value_heads // key_heads
    sources = sub * n_head
    shard = tokens * sources
    blocks = shard // SPAN
    shard_tokens = tokens * n_head
    shape = jax.ShapeDtypeStruct
    along_sub, along_head = split_axis("sub", sub), split_axis("head", n_head)

    with jax.named_scope("pack"):
        slab = ((2 + ratio) * tokens + ROW_TILE, width)
        packed = pl.pallas_call(
            functools.partial(pack_kernel, sub),
            out_shape=shape((sources,) + slab, BF16),
            in_specs=[ANY] * 4,
            out_specs=ANY,
            scratch_shapes=[
                pltpu.VMEM(queries.shape, BF16),
                pltpu.VMEM(key_vectors.shape, BF16),
                pltpu.VMEM(value_vectors.shape, BF16),
                pltpu.VMEM((value_heads, tokens), BF16),
                pltpu.VMEM((sources,) + slab, BF16),
                pltpu.SemaphoreType.DMA((4,)),
                pltpu.SemaphoreType.DMA((3 + ratio,)),
            ],
            compiler_params=params(60),
        )(queries, key_vectors, value_vectors, write_strength.T)
    got = lax.all_to_all(packed, partner_order(sub, n_head), split_axis=0, concat_axis=0, tiled=True)

    heads = sub * ratio
    by_core = [(here, here ^ 1) for here in range(n_head)]
    group = (heads, tokens, width)
    half = n_head // 2
    with jax.named_scope("gates"):
        own_gates, swap = pl.pallas_call(
            functools.partial(gate_kernel, sub, n_head),
            out_shape=[shape((half,) + group, BF16)] * 2,
            in_specs=[VMEM] * 2,
            out_specs=[VMEM] * 2,
            scratch_shapes=[pltpu.VMEM((value_heads, tokens, width), BF16)],
            compiler_params=params(),
            cost_estimate=LIGHT,
        )(output_gate, norm_gain.reshape(1, width))
    swapped = lax.ppermute(swap, along_head, by_core)
    with jax.named_scope("pair"):
        pairs = pl.pallas_call(
            pair_kernel,
            out_shape=[shape((2,) + group, BF16)] * (half - 1),
            in_specs=[VMEM] * 2,
            out_specs=[VMEM] * (half - 1),
            compiler_params=params(),
            cost_estimate=LIGHT,
        )(own_gates, swapped)

    state_type = BF16 if outer == 2 else F32
    with jax.named_scope("factors"):
        depths = []
        while blocks >> len(depths) > 1:
            depths.append(blocks >> len(depths))
        tree = []
        for depth in depths:
            tree += [shape((depth, ratio, width, width), BF16), shape((depth, ratio, width, width), F32)]
        if outer > 2:
            tree.append(shape((ratio, width, width), F32))
        out_shape = [
            shape((ratio, width, width), state_type),
            shape((blocks, ratio, SPAN, width), BF16),
            shape((blocks, ratio, SPAN, width), F32),
        ] + tree
        state, w, u, *tree = pl.pallas_call(
            functools.partial(factor_kernel, tokens, ratio, sub, half - 1, outer > 2),
            out_shape=out_shape,
            in_specs=[VMEM] + [ANY] * (half - 1),
            out_specs=[VMEM] * len(out_shape),
            compiler_params=params(),
            cost_estimate=LIGHT,
        )(got, *pairs)

    onward = [(here, (here + 1) % outer) for here in range(outer)]
    incoming = lax.ppermute(state, "outer", onward)
    with jax.named_scope("spread"):
        read = 3 + 2 * len(depths)
        local, reach, *pairs = pl.pallas_call(
            functools.partial(spread_kernel, tokens, ratio, sub, half - 1),
            out_shape=[
                shape((ratio, blocks, SPAN, width), F32),
                shape((ratio, blocks, SPAN, width), BF16),
            ]
            + [shape((2,) + group, BF16)] * (half - 1),
            in_specs=[VMEM] * read + [ANY] * (half - 1),
            out_specs=[VMEM] * 2 + [ANY] * (half - 1),
            input_output_aliases={read + number: 2 + number for number in range(half - 1)},
            compiler_params=params(),
            cost_estimate=LIGHT,
        )(got, w, u, *tree[: 2 * len(depths)], *pairs)
    gates = [(own_gates, 0), (swapped, 0)]
    for number, pair in enumerate(pairs):
        distance = 2 * number + 2
        pair = lax.ppermute(pair, along_head, [(here, here ^ distance) for here in range(n_head)])
        gates += [(pair, 0), (pair, 1)]
    for hop in range(outer - 2):
        incoming = jnp.where(lax.axis_index("outer") == 0, 0.0, incoming)
        turned_by = jnp.einsum("hde,hef->hdf", tree[-1], incoming, precision=lax.Precision.HIGHEST)
        incoming = lax.ppermute(state + incoming - turned_by, "outer", onward)

    pieces = shard_tokens // SPAN // 2
    columns = output_weight.shape[1]
    quarter = (n_head // 4, tokens, columns)
    half = n_head // 2
    order = [0] + sorted(range(1, sub), reverse=True)
    with jax.named_scope("join"):
        normed = pl.pallas_call(
            functools.partial(join_kernel, order, n_head),
            out_shape=[shape((2, pieces, ratio, SPAN, width), BF16)] * sub,
            in_specs=[VMEM] * 3,
            out_specs=[VMEM] * sub,
            compiler_params=params(),
            cost_estimate=pl.CostEstimate(flops=2 * 10**9, bytes_accessed=1, transcendentals=0),
        )(incoming, local, reach)
    normed = [
        lax.ppermute(part, along_sub, [(here, here ^ distance) for here in range(sub)]) if distance else part
        for distance, part in zip(order, normed)
    ]
    across = [(here, here ^ half) for here in range(n_head)]

    def project(kept, pieces, every, rows_too):
        used, others = gates[half * (1 - kept) : half * (2 - kept)], gates[half * kept : half * (1 + kept)]
        rows = pltpu.VMEM((shard_tokens // 2, heads * width), BF16)
        with jax.named_scope("project"):
            return pl.pallas_call(
                functools.partial(project_kernel, order, [place for unused, place in used], kept),
                out_shape=[shape(quarter[:-1] + (piece,), BF16) for piece in pieces]
                + [shape(quarter[:-1] + (every,), F32)]
                + [shape(rows.shape, BF16)] * rows_too,
                in_specs=[VMEM] * (sub + half) + [ANY] * half + [VMEM],
                out_specs=[VMEM] * (len(pieces) + 1 + rows_too),
                scratch_shapes=[rows] * (1 - rows_too),
                compiler_params=params(),
                cost_estimate=LIGHT,
            )(*normed, *[array for array, unused in used + others], output_weight)

    def add(keep, arrived, kind):
        with jax.named_scope("sum"):
            return pl.pallas_call(
                sum_kernel,
                out_shape=shape(keep.shape, kind),
                in_specs=[VMEM] * (1 + len(arrived)),
                out_specs=VMEM,
                compiler_params=params(),
                cost_estimate=LIGHT,
            )(keep, *arrived)

    cuts = 2
    every = columns // cuts
    passed_on = []
    for cut in range(cuts):
        if cut == 0:
            send, keep, rows = project(0, [every], every, 1)
        else:
            with jax.named_scope("project_more"):
                send, keep = pl.pallas_call(
                    functools.partial(more_kernel, cut * every),
                    out_shape=[shape(quarter[:-1] + (every,), BF16), shape(quarter[:-1] + (every,), F32)],
                    in_specs=[VMEM] * 2,
                    out_specs=[VMEM] * 2,
                    compiler_params=params(),
                    cost_estimate=LIGHT,
                )(rows, output_weight)
        summed = add(keep, [lax.ppermute(send, along_head, by_core)], BF16)
        passed_on.append(lax.ppermute(summed, along_head, across))
    third = columns // 3 // width * width
    *sends, keep = project(1, [columns - 2 * third, third, third], columns, 0)
    arrived = [lax.ppermute(send, along_head, by_core) for send in sends]
    summed = add(keep, arrived + passed_on, BF16 if n_head == 4 else F32)
    bit = 2
    while bit < half:
        mine = (lax.axis_index(along_head) // bit) % 2
        split = summed.reshape((summed.shape[0] // 2, 2) + summed.shape[1:])
        send = lax.dynamic_index_in_dim(split, 1 - mine, 1, False).astype(BF16)
        keep = lax.dynamic_index_in_dim(split, mine, 1, False)
        summed = keep + lax.ppermute(send, along_head, [(here, here ^ bit) for here in range(n_head)]).astype(F32)
        bit *= 2
    return summed[0].astype(BF16)


def solution(mesh):
    n_seq, n_head = mesh.shape["seq"], mesh.shape["head"]

    def run(queries, key_vectors, value_vectors, output_gate, write_strength, norm_gain, output_weight):
        sub = queries.shape[1] // n_head
        outer = n_seq // sub
        along = split_axis("sub", sub) + split_axis("head", n_head)
        split = Mesh(mesh.devices.reshape((outer,) + (2,) * len(along)), ("outer",) + along)
        every = ("outer",) + along
        placed = (
            P(every, None, None),
            P(every, None, None),
            P(every, None, None),
            P(every, None, None),
            P(every, None),
            P(),
            P(split_axis("head", n_head), None),
        )
        return jax.shard_map(
            functools.partial(per_device, outer, sub, n_head),
            mesh=split,
            in_specs=placed,
            out_specs=P(every, None),
            check_vma=False,
        )(queries, key_vectors, value_vectors, output_gate, write_strength, norm_gain, output_weight)

    return run
```
